32 devices in a mesh: dp: 4 (over y, core), seq: 8 (over z, x).
Axes of the slice: x: 2, y: 2, z: 4, core: 2. Of those that a mesh axis runs over, the one named last changes fastest.
Arguments:
- frames: bfloat16 [4, 2048, 512], P('dp', 'seq'), may hold values from -6 to 6
- cotangent: float32 [4, 2048, 512], P('dp', 'seq'), may hold values from -6 to 6
- segment_ids: int32 [4, 2048], P('dp', 'seq'), may hold values from 0 to 3, as said below
- code_index: int32 [4, 256, 2, 2], P('dp', 'seq'), may hold values from 0 to 1023, as said below
- codebooks: float32 [2, 2, 1024, 256], replicated, may hold values from -3 to 3
- dead_codes: int32 [2, 2, 1024], P(None, None, 'seq'), may hold values 0 or 1
- code_slots: int32 [2, 2, 1024], P(None, None, 'seq'), may hold values from 0 to 511
- buffered: float32 [2, 512, 256], replicated, may hold values from -3 to 3
- encoder_dilated: float32 [3, 7, 512, 256], P(None, None, 'seq'), may hold values from -0.09375 to 0.09375
- encoder_pointwise: float32 [3, 512, 256], P(None, 'seq'), may hold values from -0.375 to 0.375
- down_weight: float32 [8, 512, 512], P(None, 'seq'), may hold values from -0.09375 to 0.09375
- group_in: float32 [2, 256, 256], P(None, 'seq'), may hold values from -0.375 to 0.375
- group_out: float32 [2, 256, 256], P(None, 'seq'), may hold values from -0.375 to 0.375
- up_weight: float32 [8, 512, 512], P(None, 'seq'), may hold values from -0.25 to 0.25
- decoder_dilated: float32 [3, 7, 512, 256], P(None, None, 'seq'), may hold values from -0.09375 to 0.09375
- decoder_pointwise: float32 [3, 512, 256], P(None, 'seq'), may hold values from -0.375 to 0.375
- encoder_dilated_moment: float32 [3, 7, 512, 256], P(None, None, 'seq'), may hold values from -160 to 160
- encoder_pointwise_moment: float32 [3, 512, 256], P(None, 'seq'), may hold values from -160 to 160
- down_moment: float32 [8, 512, 512], P(None, 'seq'), may hold values from -56 to 56
- group_in_moment: float32 [2, 256, 256], P(None, 'seq'), may hold values from -56 to 56
- group_out_moment: float32 [2, 256, 256], P(None, 'seq'), may hold values from -56 to 56
- up_moment: float32 [8, 512, 512], P(None, 'seq'), may hold values from -56 to 56
- decoder_dilated_moment: float32 [3, 7, 512, 256], P(None, None, 'seq'), may hold values from -160 to 160
- decoder_pointwise_moment: float32 [3, 512, 256], P(None, 'seq'), may hold values from -160 to 160
Outputs:
- decoded: bfloat16 [4, 2048, 512], P('dp', 'seq')
- frames_grad: float32 [4, 2048, 512], P('dp', 'seq')
- new_codebooks: float32 [2, 2, 1024, 256], P(None, None, 'seq')
- encoder_dilated_velocity: float32 [3, 7, 512, 256], P(None, None, 'seq')
- encoder_pointwise_velocity: float32 [3, 512, 256], P(None, 'seq')
- down_velocity: float32 [8, 512, 512], P(None, 'seq')
- group_in_velocity: float32 [2, 256, 256], P(None, 'seq')
- group_out_velocity: float32 [2, 256, 256], P(None, 'seq')
- up_velocity: float32 [8, 512, 512], P(None, 'seq')
- decoder_dilated_velocity: float32 [3, 7, 512, 256], P(None, None, 'seq')
- decoder_pointwise_velocity: float32 [3, 512, 256], P(None, 'seq')
- encoder_dilated_next: float32 [3, 7, 512, 256], P(None, None, 'seq')
- encoder_pointwise_next: float32 [3, 512, 256], P(None, 'seq')
- down_next: float32 [8, 512, 512], P(None, 'seq')
- group_in_next: float32 [2, 256, 256], P(None, 'seq')
- group_out_next: float32 [2, 256, 256], P(None, 'seq')
- up_next: float32 [8, 512, 512], P(None, 'seq')
- decoder_dilated_next: float32 [3, 7, 512, 256], P(None, None, 'seq')
- decoder_pointwise_next: float32 [3, 512, 256], P(None, 'seq')
The draws below stay inside these ranges and needn't reach their ends.
Inputs may be any that keep to these rules, and one draw needn't show every extreme that they name: `segment_ids`: segment ids never fall along a row and change only at multiples of 8 frames. In every row one segment runs from the first device of seq to a boundary within the first 24 frames of device 8 // 2, and the next from there to the last device. `code_index`: in each group and level at most 896 distinct codes are chosen, 0 and 1023 among them.
All inputs are finite; a program needn't handle non-finite values. No bound on the sum of `dead_codes` on one device may be relied on, other than what follows from the above.
Results may differ from the reference program's by a relative error of at most 0.019.
Values may be sent and summed in bfloat16 or wider, within the bound.
A program may use at most 256 MiB of HBM per device.

```python
import functools
import jax
import jax.numpy as jnp
from jax import lax

C = 512
H = 256
CODES = 1024
GROUPS = 2
LEVELS = 2
KERNEL = 7
STRIDE = 8
NS_STEPS = 5
TL = 256
BUF = 512
Z = 256
ROWS = 4
TIME = 2048
LAT = 256


def draw_segment_ids(key, part):
    key = jax.random.fold_in(key, 11)
    first_key, second_key, third_key = jax.random.split(key, 3)
    lat_dev = TL // STRIDE
    latent_all = TIME // STRIDE
    device_total = TIME // TL
    early = jax.random.randint(first_key, (ROWS, 1), 1, lat_dev)
    middle = device_total // 2 * lat_dev + jax.random.randint(second_key, (ROWS, 1), 1, 4)
    late = jax.random.randint(third_key, (ROWS, 1), latent_all - lat_dev + 1, latent_all)
    latent_pos = (jnp.arange(TIME, dtype=jnp.int32) // STRIDE)[None, :]
    total = (latent_pos >= early).astype(jnp.int32) + (latent_pos >= middle).astype(jnp.int32)
    total = total + (latent_pos >= late).astype(jnp.int32)
    return total.astype(jnp.int32)


def draw_code_index(key, part):
    key = jax.random.fold_in(key, 23)
    in_use = CODES - CODES // 8
    frame_total = ROWS * LAT
    positions = jnp.arange(frame_total, dtype=jnp.int32)
    columns = []
    for pair_number in range(GROUPS * LEVELS):
        pair_key = jax.random.fold_in(key, pair_number)
        perm_key, pick_key, spot_key, step_key = jax.random.split(pair_key, 4)
        middle = jax.random.permutation(perm_key, CODES - 2).astype(jnp.int32) + 1
        table = jnp.concatenate([jnp.array([0, CODES - 1], dtype=jnp.int32), middle[:in_use - 2]])
        picks = jax.random.randint(pick_key, (frame_total,), 0, in_use)
        spot_low = jax.random.randint(spot_key, (), 0, frame_total)
        spot_high = (spot_low + 1 + jax.random.randint(step_key, (), 0, frame_total - 1)) % frame_total
        picks = jnp.where(positions == spot_low, 0, picks)
        picks = jnp.where(positions == spot_high, 1, picks)
        columns.append(jnp.take(table, picks, axis=0))
    stacked = jnp.stack(columns, axis=1)
    return stacked.reshape(ROWS, LAT, GROUPS, LEVELS).astype(jnp.int32)


def with_ends(entries, own_key, least, high):
    longest = entries.shape.index(max(entries.shape))
    spots = []
    for shift in (0, 1):
        where = [jax.random.randint(jax.random.fold_in(own_key, axis), (), 0, length) for axis, length in enumerate(entries.shape)]
        where[longest] = (where[longest] + shift) % entries.shape[longest]
        spots.append(tuple(where))
    return entries.at[spots[0]].set(least).at[spots[1]].set(high)


def block_scale(rng, shape, cuts, smallest, high):
    level, own = 1.0, jax.random.fold_in(rng, 6)
    for dim, blocks in cuts:
        heights = jnp.exp(jax.random.uniform(jax.random.fold_in(own, dim), (blocks,), jnp.float32, smallest / len(cuts), high / len(cuts)))
        level = level * jnp.repeat(heights, shape[dim] // blocks).reshape([-1 if axis == dim else 1 for axis in range(len(shape))])
    return level


def normal_values(rng, extent, scale, reach, cuts=(), kind=jnp.bfloat16):
    loudness = block_scale(rng, extent, cuts, -0.22, 0.18) if cuts else 1.0
    result = jax.random.normal(rng, extent, jnp.float32) * scale * loudness
    return jnp.minimum(jnp.maximum(result, -reach), reach).astype(kind)


def setup_inputs(seed: int = 0) -> dict:
    arg_keys = jax.random.split(jax.random.key(seed), 25)
    return {
        "frames": normal_values(arg_keys[0], (ROWS, TIME, C), 1.0, 6.0, ((0, 4), (1, 8))),
        "cotangent": normal_values(arg_keys[1], (ROWS, TIME, C), 1.0, 6.0, ((0, 4), (1, 8)), jnp.float32),
        "segment_ids": draw_segment_ids(jax.random.fold_in(arg_keys[24], 71), 0),
        "code_index": draw_code_index(jax.random.fold_in(arg_keys[24], 71), 0),
        "codebooks": normal_values(arg_keys[4], (GROUPS, LEVELS, CODES, Z), 0.5, 3.0, (), jnp.float32),
        "dead_codes": with_ends((jax.random.randint(arg_keys[5], (GROUPS, LEVELS, CODES), 0, 8) < 1).astype(jnp.int32), jax.random.fold_in(arg_keys[5], 1), 0, 1),
        "code_slots": with_ends(jax.random.randint(arg_keys[6], (GROUPS, LEVELS, CODES), 0, BUF), jax.random.fold_in(arg_keys[6], 1), 0, BUF - 1).astype(jnp.int32),
        "buffered": normal_values(arg_keys[7], (GROUPS, BUF, Z), 0.5, 3.0, (), jnp.float32),
        "encoder_dilated": normal_values(arg_keys[8], (3, KERNEL, C, H), (KERNEL * C) ** -0.5, 0.09375, ((2, 8),), jnp.float32),
        "encoder_pointwise": normal_values(arg_keys[9], (3, C, H), H ** -0.5, 0.375, ((1, 8),), jnp.float32),
        "down_weight": normal_values(arg_keys[10], (STRIDE, C, C), (STRIDE * C) ** -0.5, 0.09375, ((1, 8),), jnp.float32),
        "group_in": normal_values(arg_keys[11], (GROUPS, Z, Z), Z ** -0.5, 0.375, ((1, 8),), jnp.float32),
        "group_out": normal_values(arg_keys[12], (GROUPS, Z, Z), Z ** -0.5, 0.375, ((1, 8),), jnp.float32),
        "up_weight": normal_values(arg_keys[13], (STRIDE, C, C), C ** -0.5, 0.25, ((1, 8),), jnp.float32),
        "decoder_dilated": normal_values(arg_keys[14], (3, KERNEL, C, H), (KERNEL * C) ** -0.5, 0.09375, ((2, 8),), jnp.float32),
        "decoder_pointwise": normal_values(arg_keys[15], (3, C, H), H ** -0.5, 0.375, ((1, 8),), jnp.float32),
        "encoder_dilated_moment": normal_values(arg_keys[16], (3, KERNEL, C, H), (0.3 * (ROWS * TIME) ** 0.5), 160.0, ((2, 8),), jnp.float32),
        "encoder_pointwise_moment": normal_values(arg_keys[17], (3, C, H), (0.3 * (ROWS * TIME) ** 0.5), 160.0, ((1, 8),), jnp.float32),
        "down_moment": normal_values(arg_keys[18], (STRIDE, C, C), (0.3 * (ROWS * LAT) ** 0.5), 56.0, ((1, 8),), jnp.float32),
        "group_in_moment": normal_values(arg_keys[19], (GROUPS, Z, Z), (0.3 * (ROWS * LAT) ** 0.5), 56.0, ((1, 8),), jnp.float32),
        "group_out_moment": normal_values(arg_keys[20], (GROUPS, Z, Z), (0.3 * (ROWS * LAT) ** 0.5), 56.0, ((1, 8),), jnp.float32),
        "up_moment": normal_values(arg_keys[21], (STRIDE, C, C), (0.3 * (ROWS * LAT) ** 0.5), 56.0, ((1, 8),), jnp.float32),
        "decoder_dilated_moment": normal_values(arg_keys[22], (3, KERNEL, C, H), (0.3 * (ROWS * TIME) ** 0.5), 160.0, ((2, 8),), jnp.float32),
        "decoder_pointwise_moment": normal_values(arg_keys[23], (3, C, H), (0.3 * (ROWS * TIME) ** 0.5), 160.0, ((1, 8),), jnp.float32),
    }


@jax.custom_vjp
def low(v):
    return lax.optimization_barrier(v.astype(jnp.bfloat16)).astype(jnp.float32)

@jax.custom_vjp
def low_back(v):
    return v

def low_keep(v):
    return (low(v), None)

def low_pass(kept, grad):
    return (grad,)

def back_keep(v):
    return (v, None)

def back_low(kept, grad):
    return (low(grad),)
low.defvjp(low_keep, low_pass)
low_back.defvjp(back_keep, back_low)
highest = lax.Precision.HIGHEST
dilation_list = (1, 3, 9)
stacked_flags = (True, True, False, True, True, False, True, True)
coef_first = 3.4445
coef_second = -4.775
coef_third = 2.0315
commit_weight = 0.25
moment_decay = 0.5
update_rate = 0.5
code_rate = 0.5
norm_floor = 1e-07

def unit_forward(stream, segment_ids, dilated, pointwise, dilation):
    length = stream.shape[1]
    reach_frames = KERNEL // 2 * dilation
    active = low(jax.nn.elu(stream))
    padded = jnp.pad(active, ((0, 0), (reach_frames, reach_frames), (0, 0)))
    padded_ids = jnp.pad(segment_ids, ((0, 0), (reach_frames, reach_frames)), constant_values=-1)
    hidden = jnp.zeros((stream.shape[0], length, dilated.shape[2]), jnp.float32)
    for kernel_tap in range(KERNEL):
        offset = reach_frames + (kernel_tap - KERNEL // 2) * dilation
        window = padded[:, offset:offset + length, :]
        matched = (padded_ids[:, offset:offset + length] == segment_ids).astype(jnp.float32)
        hidden = hidden + jnp.einsum('btc,ch->bth', window * matched[:, :, None], dilated[kernel_tap], precision=highest)
    hidden = low_back(hidden)
    excited = low(jax.nn.elu(hidden))
    branch = low_back(jnp.einsum('bth,ch->btc', excited, pointwise, precision=highest))
    return stream + branch

def run_units(stream, segment_ids, dilated_stack, pointwise_stack):
    for position, dilation in enumerate(dilation_list):
        unit = jax.checkpoint(functools.partial(unit_forward, dilation=dilation))
        stream = unit(stream, segment_ids, dilated_stack[position], pointwise_stack[position])
    return stream

def encode(lowered, frames, segment_ids):
    stream = run_units(frames, segment_ids, lowered[0], lowered[1])
    active = low(jax.nn.elu(stream))
    row_count, length, channels = active.shape
    blocks = active.reshape(row_count, length // STRIDE, STRIDE * channels)
    latent = low(low_back(jnp.einsum('btk,kc->btc', blocks, lowered[2].reshape(STRIDE * channels, channels), precision=highest)))
    firsts = [low_back(jnp.einsum('btc,cd->btd', latent[:, :, group_index * Z:(group_index + 1) * Z], lowered[3][group_index], precision=highest)) for group_index in range(GROUPS)]
    return jnp.stack(firsts)

def decode(lowered, quantized, segment_ids):
    parts = [jnp.einsum('btd,de->bte', low(quantized[group_index]), lowered[4][group_index], precision=highest) for group_index in range(GROUPS)]
    mixed = low_back(jnp.concatenate(parts, axis=2))
    active = low(jax.nn.elu(mixed))
    row_count, latent_len, channels = active.shape
    spread = jnp.einsum('btc,kc->btk', active, lowered[5].reshape(STRIDE * channels, channels), precision=highest)
    stream = low_back(spread.reshape(row_count, latent_len * STRIDE, channels))
    return run_units(stream, segment_ids, lowered[6], lowered[7])

def forward(weights, frames, segment_ids, chosen, shift):
    lowered = tuple((low(weight) for weight in weights))
    firsts = encode(lowered, frames, segment_ids)
    seconds = firsts - chosen[:, 0]
    commit = commit_weight * (jnp.sum((firsts - chosen[:, 0]) ** 2) + jnp.sum((seconds - chosen[:, 1]) ** 2))
    decoded = decode(lowered, firsts + shift, segment_ids)
    return ((decoded, commit), firsts)

def orthogonalize(matrix):
    norm_value = jnp.sqrt(jnp.sum(matrix * matrix))
    current = matrix / (norm_value + norm_floor)
    for repeat in range(NS_STEPS):
        gram = jnp.dot(current.T, current, precision=highest)
        mixing = coef_second * gram + coef_third * jnp.dot(gram, gram, precision=highest)
        current = coef_first * current + jnp.dot(current, mixing, precision=highest)
    return current

def reference(frames, cotangent, segment_ids, code_index, codebooks, dead_codes, code_slots, buffered, encoder_dilated, encoder_pointwise, down_weight, group_in, group_out, up_weight, decoder_dilated, decoder_pointwise, encoder_dilated_moment, encoder_pointwise_moment, down_moment, group_in_moment, group_out_moment, up_moment, decoder_dilated_moment, decoder_pointwise_moment):
    weights = (encoder_dilated, encoder_pointwise, down_weight, group_in, group_out, up_weight, decoder_dilated, decoder_pointwise)
    olds = (encoder_dilated_moment, encoder_pointwise_moment, down_moment, group_in_moment, group_out_moment, up_moment, decoder_dilated_moment, decoder_pointwise_moment)
    frames_float = frames.astype(jnp.float32)
    chosen = jnp.stack([jnp.stack([jnp.take(codebooks[group_index, level_index], code_index[:, :, group_index, level_index], axis=0) for level_index in range(LEVELS)]) for group_index in range(GROUPS)])
    plain = encode(tuple((low(weight) for weight in weights)), frames_float, segment_ids)
    shift = chosen[:, 0] + chosen[:, 1] - plain
    function = functools.partial(forward, segment_ids=segment_ids, chosen=chosen, shift=shift)
    outputs, pullback, firsts = jax.vjp(function, weights, frames_float, has_aux=True)
    decoded, commit = outputs
    grads, frames_grad = pullback((cotangent.astype(decoded.dtype), jnp.ones_like(commit)))
    residuals = jnp.stack([firsts, firsts - chosen[:, 0]], axis=1)
    sum_rows = []
    count_rows = []
    for group_index in range(GROUPS):
        for level_index in range(LEVELS):
            flat_index = code_index[:, :, group_index, level_index].reshape(-1)
            sum_rows.append(jax.ops.segment_sum(residuals[group_index, level_index].reshape(-1, Z), flat_index, num_segments=CODES))
            count_rows.append(jax.ops.segment_sum(jnp.ones(flat_index.shape, jnp.float32), flat_index, num_segments=CODES))
    code_sums = jnp.stack(sum_rows).reshape(GROUPS, LEVELS, CODES, Z)
    code_counts = jnp.stack(count_rows).reshape(GROUPS, LEVELS, CODES)
    code_means = code_sums / jnp.maximum(code_counts, 1.0)[..., None]
    code_used = jnp.minimum(code_counts, 1.0)[..., None]
    updated = codebooks + code_rate * code_used * (code_means - codebooks)
    replaced = jnp.stack([jnp.stack([jnp.take(buffered[group_index], code_slots[group_index, level_index], axis=0) for level_index in range(LEVELS)]) for group_index in range(GROUPS)])
    new_codebooks = jnp.where(dead_codes[..., None] == 1, replaced, updated)
    velocities = []
    nexts = []
    for position in range(8):
        velocity = moment_decay * olds[position] + grads[position]
        leading = velocity.shape[0] if stacked_flags[position] else 1
        view = velocity.reshape(leading, -1, velocity.shape[-1])
        ortho = jax.vmap(orthogonalize)(view).reshape(velocity.shape)
        velocities.append(velocity)
        nexts.append(weights[position] - update_rate * ortho)
    return (decoded.astype(jnp.bfloat16), frames_grad, new_codebooks, velocities[0], velocities[1], velocities[2], velocities[3], velocities[4], velocities[5], velocities[6], velocities[7], nexts[0], nexts[1], nexts[2], nexts[3], nexts[4], nexts[5], nexts[6], nexts[7])
```

```python
import jax
import jax.numpy as jnp
from jax import lax
from jax.sharding import PartitionSpec as P

GROUPS = 2
LEVELS = 2
KERNEL = 7
STRIDE = 8
NS_STEPS = 5


highest = lax.Precision.HIGHEST
dilation_list = (1, 3, 9)
stacked_flags = (True, True, False, True, True, False, True, True)
coef_first = 3.4445
coef_second = -4.775
coef_third = 2.0315
commit_weight = 0.25
moment_decay = 0.5
update_rate = 0.5
code_rate = 0.5
norm_floor = 1e-07
widest = 27


def extended(block, sides, width):
    for axis, dim in sides:
        count = lax.axis_size(axis)
        forward = [(i, i + 1) for i in range(count - 1)]
        backward = [(target, source) for source, target in forward]
        low = lax.ppermute(
            lax.slice_in_dim(block, block.shape[dim] - width, None, axis=dim), axis, forward
        )
        high = lax.ppermute(lax.slice_in_dim(block, 0, width, axis=dim), axis, backward)
        block = jnp.concatenate([low, block, high], axis=dim)
    return block


def elu_slope(values):
    return jnp.where(values > 0, 1.0, jnp.exp(jnp.minimum(values, 0.0)))


def contract_rows(left, right):
    return lax.dot_general(
        left, right, (((0,), (0,)), ((), ())), preferred_element_type=jnp.float32
    )


def contract_last(left, right):
    return lax.dot_general(
        left, right, (((1,), (1,)), ((), ())), preferred_element_type=jnp.float32
    )


def unit_forward(stream, segment_rim, dilation, dilated, pointwise):
    row_count, length, channels = stream.shape
    reach_frames = KERNEL // 2 * dilation
    active = jax.nn.elu(stream).astype(jnp.bfloat16)
    padded = extended(active, (("seq", 1),), reach_frames)
    own_ids = segment_rim[:, widest : widest + length]
    masks = []
    pieces = []
    for kernel_tap in range(KERNEL):
        shift_by = (kernel_tap - KERNEL // 2) * dilation
        matched = (
            segment_rim[:, widest + shift_by : widest + shift_by + length] == own_ids
        ).astype(jnp.bfloat16)[:, :, None]
        masks.append(matched)
        pieces.append(
            padded[:, reach_frames + shift_by : reach_frames + shift_by + length, :] * matched
        )
    columns = jnp.concatenate(pieces, axis=2).reshape(row_count * length, KERNEL * channels)
    hidden = jnp.dot(
        columns, dilated.reshape(KERNEL * channels, -1), preferred_element_type=jnp.float32
    )
    excited = jax.nn.elu(hidden).astype(jnp.bfloat16)
    branch = contract_last(excited, pointwise)
    output = stream + branch.reshape(row_count, length, channels)
    return (output, (stream, masks, columns, hidden, excited))


def unit_backward(grad_out, kept, dilation, dilated, pointwise):
    stream, masks, columns, hidden, excited = kept
    row_count, length, channels = stream.shape
    reach_frames = KERNEL // 2 * dilation
    grad_branch = grad_out.reshape(row_count * length, channels).astype(jnp.bfloat16)
    point_grad = contract_rows(grad_branch, excited)
    grad_excited = jnp.dot(grad_branch, pointwise, preferred_element_type=jnp.float32)
    grad_hidden = (grad_excited * elu_slope(hidden)).astype(jnp.bfloat16)
    dilated_matrix = dilated.reshape(KERNEL * channels, -1)
    dilated_grad = contract_rows(columns, grad_hidden).reshape(dilated.shape)
    grad_columns = contract_last(grad_hidden, dilated_matrix).reshape(
        row_count, length, KERNEL, channels
    )
    grad_padded = jnp.zeros((row_count, length + 2 * reach_frames, channels), jnp.float32)
    for kernel_tap in range(KERNEL):
        offset = reach_frames + (kernel_tap - KERNEL // 2) * dilation
        grad_padded = grad_padded.at[:, offset : offset + length, :].add(
            grad_columns[:, :, kernel_tap, :] * masks[kernel_tap]
        )
    rims = jnp.concatenate(
        [grad_padded[:, :reach_frames], grad_padded[:, reach_frames + length :]], axis=1
    )
    arrived = extended(rims, (("seq", 1),), reach_frames)
    grad_active = grad_padded[:, reach_frames : reach_frames + length]
    grad_active = grad_active.at[:, :reach_frames].add(arrived[:, :reach_frames])
    grad_active = grad_active.at[:, length - reach_frames :].add(arrived[:, 3 * reach_frames :])
    grad_stream = grad_out + grad_active * elu_slope(stream)
    return (grad_stream, dilated_grad, point_grad)


def solve_mixing(gram):
    norm = jnp.sqrt(jnp.trace(gram, axis1=1, axis2=2)) + norm_floor
    scale = 1.0 / norm
    current = gram * (scale * scale)[:, None, None]
    eye = jnp.eye(gram.shape[-1], dtype=jnp.float32)[None]
    total = None
    for repeat in range(NS_STEPS):
        square = jnp.einsum("ncd,nde->nce", current, current, precision=highest)
        factor = coef_first * eye + coef_second * current + coef_third * square
        if total is None:
            total = factor
        else:
            total = jnp.einsum("ncd,nde->nce", total, factor, precision=highest)
        if repeat < NS_STEPS - 1:
            half = jnp.einsum("ncd,nde->nce", current, factor, precision=highest)
            current = jnp.einsum("ncd,nde->nce", half, factor, precision=highest)
    return total * scale[:, None, None]


def pack_rows(parts):
    return jnp.concatenate([part.reshape(-1, part.shape[-1]) for part in parts], axis=0)


def shard_rows(array, axis, count):
    shape = array.shape
    split = array.reshape(shape[:axis] + (count, shape[axis] // count) + shape[axis + 1 :])
    return jnp.moveaxis(split, axis, 0).reshape(count, -1, shape[-1])


def unshard_rows(rows, shape, axis):
    count = rows.shape[0]
    split = rows.reshape((count,) + shape[:axis] + (shape[axis] // count,) + shape[axis + 1 :])
    return jnp.moveaxis(split, 0, axis).reshape(shape)


narrow = (0, 1, 3, 4, 6, 7)
wide = (2, 5)
shard_axis = (2, 1, 1, 1, 1, 1, 2, 1)


def per_device(
    frames,
    cotangent,
    segment_ids,
    code_index,
    codebooks,
    dead_codes,
    code_slots,
    buffered,
    encoder_dilated,
    encoder_pointwise,
    down_weight,
    group_in,
    group_out,
    up_weight,
    decoder_dilated,
    decoder_pointwise,
    encoder_dilated_moment,
    encoder_pointwise_moment,
    down_moment,
    group_in_moment,
    group_out_moment,
    up_moment,
    decoder_dilated_moment,
    decoder_pointwise_moment,
):
    masters = (
        encoder_dilated,
        encoder_pointwise,
        down_weight,
        group_in,
        group_out,
        up_weight,
        decoder_dilated,
        decoder_pointwise,
    )
    olds = (
        encoder_dilated_moment,
        encoder_pointwise_moment,
        down_moment,
        group_in_moment,
        group_out_moment,
        up_moment,
        decoder_dilated_moment,
        decoder_pointwise_moment,
    )
    lowered = [weight.astype(jnp.bfloat16) for weight in masters]
    count = lax.axis_size("seq")
    full = [None] * 8
    for members in (narrow, wide):
        packed = lax.all_gather(pack_rows([lowered[i] for i in members]), "seq", axis=0)
        start = 0
        for i in members:
            rows = lowered[i].size // lowered[i].shape[-1]
            shape = list(lowered[i].shape)
            shape[shard_axis[i]] *= count
            full[i] = unshard_rows(packed[:, start : start + rows], tuple(shape), shard_axis[i])
            start += rows
    row_count, length, channels = frames.shape
    latent_len = length // STRIDE
    tokens = row_count * latent_len
    segment_rim = extended(segment_ids + 1, (("seq", 1),), widest)
    stream = frames.astype(jnp.float32)
    encoder_kept = []
    for position, dilation in enumerate(dilation_list):
        stream, kept = unit_forward(
            stream, segment_rim, dilation, full[0][position], full[1][position]
        )
        encoder_kept.append(kept)
    before_down = stream
    down_active = jax.nn.elu(stream).astype(jnp.bfloat16).reshape(tokens, STRIDE * channels)
    down_matrix = full[2].reshape(STRIDE * channels, channels)
    latent = jnp.dot(down_active, down_matrix, preferred_element_type=jnp.float32)
    latent_low = latent.astype(jnp.bfloat16)
    group_width = channels // GROUPS
    code_range = lax.broadcasted_iota(jnp.int32, (1, codebooks.shape[2]), 1)
    firsts = []
    seconds = []
    quantized = []
    onehots = []
    last_picks = []
    for group_index in range(GROUPS):
        latent_slice = latent_low[:, group_index * group_width : (group_index + 1) * group_width]
        first_part = jnp.dot(latent_slice, full[3][group_index], preferred_element_type=jnp.float32)
        picked = []
        for level_index in range(LEVELS):
            onehot = (
                code_index[:, :, group_index, level_index].reshape(-1, 1) == code_range
            ).astype(jnp.float32)
            onehots.append(onehot)
            picked.append(jnp.dot(onehot, codebooks[group_index, level_index], precision=highest))
        firsts.append(first_part)
        seconds.append(first_part - picked[0])
        quantized.append((picked[0] + picked[1]).astype(jnp.bfloat16))
        last_picks.append(picked[1])
    mixed = jnp.concatenate(
        [
            jnp.dot(
                quantized[group_index], full[4][group_index], preferred_element_type=jnp.float32
            )
            for group_index in range(GROUPS)
        ],
        axis=1,
    )
    lifted = jax.nn.elu(mixed).astype(jnp.bfloat16)
    up_matrix = full[5].reshape(STRIDE * channels, channels)
    stream = contract_last(lifted, up_matrix).reshape(row_count, length, channels)
    decoder_kept = []
    for position, dilation in enumerate(dilation_list):
        stream, kept = unit_forward(
            stream, segment_rim, dilation, full[6][position], full[7][position]
        )
        decoder_kept.append(kept)
    decoded = stream.astype(jnp.bfloat16)
    grad = cotangent
    decoder_dilated_grads = [None, None, None]
    decoder_point_grads = [None, None, None]
    for position in (2, 1, 0):
        grad, dilated_grad, point_grad = unit_backward(
            grad,
            decoder_kept[position],
            dilation_list[position],
            full[6][position],
            full[7][position],
        )
        decoder_dilated_grads[position] = dilated_grad
        decoder_point_grads[position] = point_grad
    grad_up = grad.reshape(tokens, STRIDE * channels).astype(jnp.bfloat16)
    up_grad = contract_rows(grad_up, lifted).reshape(full[5].shape)
    grad_lifted = jnp.dot(grad_up, up_matrix, preferred_element_type=jnp.float32)
    grad_mixed = (grad_lifted * elu_slope(mixed)).astype(jnp.bfloat16)
    group_out_grads = []
    group_in_grads = []
    grad_latent_parts = []
    for group_index in range(GROUPS):
        grad_slice = grad_mixed[:, group_index * group_width : (group_index + 1) * group_width]
        group_out_grads.append(contract_rows(quantized[group_index], grad_slice))
        grad_quant = contract_last(grad_slice, full[4][group_index])
        grad_first = grad_quant + 2.0 * commit_weight * (
            seconds[group_index] + (seconds[group_index] - last_picks[group_index])
        )
        grad_first_low = grad_first.astype(jnp.bfloat16)
        latent_slice = latent_low[:, group_index * group_width : (group_index + 1) * group_width]
        group_in_grads.append(contract_rows(latent_slice, grad_first_low))
        grad_latent_parts.append(contract_last(grad_first_low, full[3][group_index]))
    grad_latent = jnp.concatenate(grad_latent_parts, axis=1).astype(jnp.bfloat16)
    down_grad = contract_rows(down_active, grad_latent).reshape(full[2].shape)
    grad_blocks = contract_last(grad_latent, down_matrix).reshape(row_count, length, channels)
    grad = grad_blocks * elu_slope(before_down)
    encoder_dilated_grads = [None, None, None]
    encoder_point_grads = [None, None, None]
    for position in (2, 1, 0):
        grad, dilated_grad, point_grad = unit_backward(
            grad,
            encoder_kept[position],
            dilation_list[position],
            full[0][position],
            full[1][position],
        )
        encoder_dilated_grads[position] = dilated_grad
        encoder_point_grads[position] = point_grad
    everyone = ("dp", "seq")
    all_rows = lax.all_gather(
        jnp.concatenate([firsts[0], seconds[0], firsts[1], seconds[1]], axis=1),
        everyone,
        axis=0,
        tiled=True,
    )
    all_codes = lax.all_gather(
        code_index.reshape(tokens, GROUPS * LEVELS), everyone, axis=0, tiled=True
    )
    code_share = dead_codes.shape[2]
    own_range = lax.broadcasted_iota(
        jnp.int32, (1, code_share), 1
    ) + code_share * lax.axis_index("seq")
    sum_list = []
    count_list = []
    for entry in range(GROUPS * LEVELS):
        own_hot = (all_codes[:, entry : entry + 1] == own_range).astype(jnp.float32)
        sum_list.append(
            lax.dot_general(
                own_hot,
                all_rows[:, entry * group_width : (entry + 1) * group_width],
                (((0,), (0,)), ((), ())),
                precision=highest,
            )
        )
        count_list.append(jnp.sum(own_hot, axis=0))
    total_sums = jnp.stack(sum_list).reshape(GROUPS, LEVELS, code_share, group_width)
    total_counts = jnp.stack(count_list).reshape(GROUPS, LEVELS, code_share)
    full_grads = (
        jnp.stack(encoder_dilated_grads),
        jnp.stack(encoder_point_grads),
        down_grad,
        jnp.stack(group_in_grads),
        jnp.stack(group_out_grads),
        up_grad,
        jnp.stack(decoder_dilated_grads),
        jnp.stack(decoder_point_grads),
    )
    reduced = [None] * 8
    for members in (narrow, wide):
        packed = jnp.concatenate(
            [shard_rows(full_grads[i], shard_axis[i], count) for i in members], axis=1
        )
        share = lax.psum_scatter(packed, "seq", scatter_dimension=0, tiled=False)
        share = lax.psum(share, "dp")
        start = 0
        for i in members:
            rows = masters[i].size // masters[i].shape[-1]
            reduced[i] = share[start : start + rows].reshape(masters[i].shape)
            start += rows
    own_codes = lax.dynamic_slice_in_dim(
        codebooks, lax.axis_index("seq") * code_share, code_share, 2
    )
    code_means = total_sums / jnp.maximum(total_counts, 1.0)[..., None]
    code_used = jnp.minimum(total_counts, 1.0)[..., None]
    updated = own_codes + code_rate * code_used * (code_means - own_codes)
    slot_range = lax.broadcasted_iota(jnp.int32, (1, 1, 1, buffered.shape[1]), 3)
    slot_onehot = (code_slots[..., None] == slot_range).astype(jnp.float32)
    replaced = jnp.einsum("glsb,gbz->glsz", slot_onehot, buffered, precision=highest)
    new_codebooks = jnp.where(dead_codes[..., None] == 1, replaced, updated)
    velocities = tuple((moment_decay * olds[position] + reduced[position] for position in range(8)))
    views = tuple(
        (
            velocities[position].reshape(
                velocities[position].shape[0] if stacked_flags[position] else 1,
                -1,
                velocities[position].shape[-1],
            )
            for position in range(8)
        )
    )
    current = [None] * 8
    for members in (narrow, wide):
        grams = lax.psum(
            jnp.concatenate(
                [
                    jnp.einsum("nrc,nrd->ncd", views[i], views[i], precision=highest)
                    for i in members
                ]
            ),
            "seq",
        )
        mixing = solve_mixing(grams)
        start = 0
        for i in members:
            stop = start + views[i].shape[0]
            current[i] = jnp.einsum(
                "nrc,ncd->nrd", views[i], mixing[start:stop], precision=highest
            )
            start = stop
    shaped = tuple((current[position].reshape(masters[position].shape) for position in range(8)))
    nexts = tuple((masters[position] - update_rate * shaped[position] for position in range(8)))
    return (
        decoded,
        grad,
        new_codebooks,
        velocities[0],
        velocities[1],
        velocities[2],
        velocities[3],
        velocities[4],
        velocities[5],
        velocities[6],
        velocities[7],
        nexts[0],
        nexts[1],
        nexts[2],
        nexts[3],
        nexts[4],
        nexts[5],
        nexts[6],
        nexts[7],
    )


def solution(mesh):
    in_specs = (
        P("dp", "seq", None),
        P("dp", "seq", None),
        P("dp", "seq"),
        P("dp", "seq", None, None),
        P(),
        P(None, None, "seq"),
        P(None, None, "seq"),
        P(),
        P(None, None, "seq", None),
        P(None, "seq", None),
        P(None, "seq", None),
        P(None, "seq", None),
        P(None, "seq", None),
        P(None, "seq", None),
        P(None, None, "seq", None),
        P(None, "seq", None),
        P(None, None, "seq", None),
        P(None, "seq", None),
        P(None, "seq", None),
        P(None, "seq", None),
        P(None, "seq", None),
        P(None, "seq", None),
        P(None, None, "seq", None),
        P(None, "seq", None),
    )
    out_specs = (
        P("dp", "seq", None),
        P("dp", "seq", None),
        P(None, None, "seq", None),
        P(None, None, "seq", None),
        P(None, "seq", None),
        P(None, "seq", None),
        P(None, "seq", None),
        P(None, "seq", None),
        P(None, "seq", None),
        P(None, None, "seq", None),
        P(None, "seq", None),
        P(None, None, "seq", None),
        P(None, "seq", None),
        P(None, "seq", None),
        P(None, "seq", None),
        P(None, "seq", None),
        P(None, "seq", None),
        P(None, None, "seq", None),
        P(None, "seq", None),
    )
    return jax.shard_map(
        per_device, mesh=mesh, in_specs=in_specs, out_specs=out_specs, check_vma=False
    )
```

```python
import functools

import jax
import jax.numpy as jnp
from jax import lax
from jax.experimental import pallas as pl
from jax.experimental.pallas import tpu as pltpu
from jax.sharding import PartitionSpec as P

GROUPS = 2
LEVELS = 2
KERNEL = 7
STRIDE = 8
NS_STEPS = 5


highest = lax.Precision.HIGHEST
dilation_list = (1, 3, 9)
stacked_flags = (True, True, False, True, True, False, True, True)
coef_first = 3.4445
coef_second = -4.775
coef_third = 2.0315
commit_weight = 0.25
moment_decay = 0.5
update_rate = 0.5
code_rate = 0.5
norm_floor = 1e-07
widest = 27


def extended(block, sides, width):
    for axis, dim in sides:
        count = lax.axis_size(axis)
        forward = [(i, i + 1) for i in range(count - 1)]
        backward = [(target, source) for source, target in forward]
        low = lax.ppermute(
            lax.slice_in_dim(block, block.shape[dim] - width, None, axis=dim), axis, forward
        )
        high = lax.ppermute(lax.slice_in_dim(block, 0, width, axis=dim), axis, backward)
        block = jnp.concatenate([low, block, high], axis=dim)
    return block


def elu_slope(values):
    return jnp.where(values > 0, 1.0, jnp.exp(jnp.minimum(values, 0.0)))


def contract_rows(left, right):
    return lax.dot_general(
        left, right, (((0,), (0,)), ((), ())), preferred_element_type=jnp.float32
    )


def contract_last(left, right):
    return lax.dot_general(
        left, right, (((1,), (1,)), ((), ())), preferred_element_type=jnp.float32
    )


def unit_forward(stream, segment_rim, dilation, dilated, pointwise):
    row_count, length, channels = stream.shape
    reach_frames = KERNEL // 2 * dilation
    active = jax.nn.elu(stream).astype(jnp.bfloat16)
    padded = extended(active, (("seq", 1),), reach_frames)
    own_ids = segment_rim[:, widest : widest + length]
    masks = []
    pieces = []
    for kernel_tap in range(KERNEL):
        shift_by = (kernel_tap - KERNEL // 2) * dilation
        matched = (
            segment_rim[:, widest + shift_by : widest + shift_by + length] == own_ids
        ).astype(jnp.bfloat16)[:, :, None]
        masks.append(matched)
        pieces.append(
            padded[:, reach_frames + shift_by : reach_frames + shift_by + length, :] * matched
        )
    columns = jnp.concatenate(pieces, axis=2).reshape(row_count * length, KERNEL * channels)
    hidden = jnp.dot(
        columns, dilated.reshape(KERNEL * channels, -1), preferred_element_type=jnp.float32
    )
    excited = jax.nn.elu(hidden).astype(jnp.bfloat16)
    branch = contract_last(excited, pointwise)
    output = stream + branch.reshape(row_count, length, channels)
    return (output, (stream, masks, columns, hidden, excited))


def unit_backward(grad_out, kept, dilation, dilated, pointwise):
    stream, masks, columns, hidden, excited = kept
    row_count, length, channels = stream.shape
    reach_frames = KERNEL // 2 * dilation
    grad_branch = grad_out.reshape(row_count * length, channels).astype(jnp.bfloat16)
    point_grad = contract_rows(grad_branch, excited)
    grad_excited = jnp.dot(grad_branch, pointwise, preferred_element_type=jnp.float32)
    grad_hidden = (grad_excited * elu_slope(hidden)).astype(jnp.bfloat16)
    dilated_matrix = dilated.reshape(KERNEL * channels, -1)
    dilated_grad = contract_rows(columns, grad_hidden).reshape(dilated.shape)
    grad_columns = contract_last(grad_hidden, dilated_matrix).reshape(
        row_count, length, KERNEL, channels
    )
    grad_padded = jnp.zeros((row_count, length + 2 * reach_frames, channels), jnp.float32)
    for kernel_tap in range(KERNEL):
        offset = reach_frames + (kernel_tap - KERNEL // 2) * dilation
        grad_padded = grad_padded.at[:, offset : offset + length, :].add(
            grad_columns[:, :, kernel_tap, :] * masks[kernel_tap]
        )
    rims = jnp.concatenate(
        [grad_padded[:, :reach_frames], grad_padded[:, reach_frames + length :]], axis=1
    )
    arrived = extended(rims, (("seq", 1),), reach_frames)
    grad_active = grad_padded[:, reach_frames : reach_frames + length]
    grad_active = grad_active.at[:, :reach_frames].add(arrived[:, :reach_frames])
    grad_active = grad_active.at[:, length - reach_frames :].add(arrived[:, 3 * reach_frames :])
    grad_stream = grad_out + grad_active * elu_slope(stream)
    return (grad_stream, dilated_grad, point_grad)


def solve_mixing(gram):
    norm = jnp.sqrt(jnp.trace(gram, axis1=1, axis2=2)) + norm_floor
    scale = 1.0 / norm
    current = gram * (scale * scale)[:, None, None]
    eye = jnp.eye(gram.shape[-1], dtype=jnp.float32)[None]
    total = None
    for repeat in range(NS_STEPS):
        square = jnp.einsum("ncd,nde->nce", current, current, precision=highest)
        factor = coef_first * eye + coef_second * current + coef_third * square
        if total is None:
            total = factor
        else:
            total = jnp.einsum("ncd,nde->nce", total, factor, precision=highest)
        if repeat < NS_STEPS - 1:
            half = jnp.einsum("ncd,nde->nce", current, factor, precision=highest)
            current = jnp.einsum("ncd,nde->nce", half, factor, precision=highest)
    return total * scale[:, None, None]


def halves(array):
    width = array.shape[-1] // 2
    split = array.reshape(array.shape[:-1] + (2, width))
    return jnp.moveaxis(split, -2, 0)


def whole_rows(rows, high):
    unit = 32 * high
    return -(-rows // unit) * unit


def pack_side(dilated, pointwise, group, strided, high, lead):
    parts = [dilated, pointwise, group, strided]
    kept = dilated.shape[:lead]
    flat = [part.reshape(kept + (-1, part.shape[-1])) for part in parts]
    rows = sum(part.shape[lead] for part in flat)
    extra = whole_rows(rows, high) - rows
    if extra:
        flat.append(jnp.zeros(kept + (extra, flat[0].shape[-1]), flat[0].dtype))
    return jnp.concatenate(flat, axis=lead)


def by_owner(array, axis, count):
    shape = array.shape
    split = array.reshape(shape[:axis] + (count, shape[axis] // count) + shape[axis + 1 :])
    return jnp.moveaxis(split, axis, 0)


def take_side(rows, shapes):
    found = []
    start = 0
    for shape in shapes:
        size = 1
        for extent in shape[:-1]:
            size *= extent
        found.append(rows[..., start : start + size, :].reshape(rows.shape[:-2] + shape))
        start += size
    return found


def joined(array, axis):
    moved = jnp.moveaxis(array, 0, axis)
    shape = moved.shape
    return moved.reshape(shape[:axis] + (shape[axis] * shape[axis + 1],) + shape[axis + 2 :])


MESH = pl.DeviceIdType.MESH


def line_sizes(seq, dp):
    across = 1
    while (2 * across) * (2 * across) <= seq:
        across *= 2
    return across, dp // 2, seq // across


def place(sizes):
    wide, high, _ = sizes
    row = lax.axis_index("dp")
    part = lax.axis_index("seq")
    return part % wide, row // 2, part // wide, row % 2


def greet(sizes):
    wide, high, deep = sizes
    x, y, z, c = place(sizes)
    barrier = pltpu.get_barrier_semaphore()
    others = [(y * 2 + 1 - c, z * wide + x)]
    others += [(y * 2 + c, z * wide + (x + k) % wide) for k in range(1, wide)]
    others += [((y + k) % high * 2 + c, z * wide + x) for k in range(1, high)]
    others += [(y * 2 + c, (z + k) % deep * wide + x) for k in range(1, deep)]
    for other in others:
        pl.semaphore_signal(barrier, inc=1, device_id=other, device_id_type=MESH)
    pl.semaphore_wait(barrier, len(others))


def gather_kernel(sizes, in_ref, out_ref, send_sem, recv_sem, local_sem):
    wide, high, deep = sizes
    x, y, z, c = place(sizes)
    greet(sizes)
    own = pltpu.make_async_copy(in_ref, out_ref.at[z, x], local_sem)
    own.start()
    sent = []

    def send(zs, xs, ys, h, to, source=None):
        spot = out_ref.at[zs, xs, c, ys, h]
        copy = pltpu.make_async_remote_copy(
            src_ref=spot if source is None else source,
            dst_ref=spot,
            send_sem=send_sem.at[len(sent)],
            recv_sem=recv_sem.at[zs, xs, c, ys, h],
            device_id=to,
            device_id_type=MESH,
        )
        copy.start()
        sent.append(copy)

    def arrive(zs, xs, cs, ys, h):
        spot = out_ref.at[zs, xs, cs, ys, h]
        pltpu.make_async_remote_copy(
            src_ref=spot,
            dst_ref=spot,
            send_sem=send_sem.at[0],
            recv_sem=recv_sem.at[zs, xs, cs, ys, h],
            device_id=(y * 2 + 1 - c, z * wide + x),
            device_id_type=MESH,
        ).wait_recv()

    def to_x(zs, xs, ys, h, source=None):
        for k in range(1, wide):
            send(zs, xs, ys, h, (y * 2 + c, z * wide + (x + k) % wide), source)

    def to_y(zs, xs, ys, h):
        for k in range(1, high):
            send(zs, xs, ys, h, ((y + k) % high * 2 + c, z * wide + x))

    def to_core(zs, xs, ys, h):
        send(zs, xs, ys, h, (y * 2 + 1 - c, z * wide + x))

    for k in range(deep - 1, 0, -1):
        for h in range(2):
            send(z, x, y, h, (y * 2 + c, (z + k) % deep * wide + x), in_ref.at[c, y, h])
    to_x(z, x, y, 0, in_ref.at[c, y, 0])
    for j in range(high):
        ys = (y + j) % high
        to_x(z, x, ys, 1, in_ref.at[c, ys, 1])
    for k in range(1, deep):
        zs = (z + k) % deep
        arrive(zs, x, c, y, 0)
        to_x(zs, x, y, 0)
        to_y(zs, x, y, 0)
        to_core(zs, x, y, 0)
        arrive(zs, x, c, y, 1)
        to_y(zs, x, y, 1)
        to_x(zs, x, y, 1)
        to_core(zs, x, y, 1)
    for k in range(deep):
        zs = (z + k) % deep
        for i in range(1, wide):
            xs = (x + i) % wide
            arrive(zs, xs, c, y, 0)
            to_y(zs, xs, y, 0)
            to_core(zs, xs, y, 0)
        if k > 0:
            for j in range(1, high):
                ys = (y + j) % high
                arrive(zs, x, c, ys, 1)
                to_x(zs, x, ys, 1)
                to_core(zs, x, ys, 1)
    for k in range(deep):
        zs = (z + k) % deep
        for i in range(wide):
            xs = (x + i) % wide
            if k == 0 and i == 0:
                continue
            for j in range(1, high):
                ys = (y + j) % high
                arrive(zs, xs, c, ys, 0)
                to_core(zs, xs, ys, 0)
            if i > 0:
                for j in range(high):
                    ys = (y + j) % high
                    arrive(zs, xs, c, ys, 1)
                    to_core(zs, xs, ys, 1)
    for k in range(deep):
        zs = (z + k) % deep
        for i in range(wide):
            xs = (x + i) % wide
            if k == 0 and i == 0:
                continue
            for j in range(high):
                for h in range(2):
                    arrive(zs, xs, 1 - c, (y + j) % high, h)
    for copy in sent:
        copy.wait_send()
    own.wait()


def gather_sends(sizes):
    wide, high, deep = sizes
    n = (deep - 1) * 2 + (wide - 1) * (1 + high)
    n += (deep - 1) * 2 * (wide - 1 + high - 1 + 1)
    n += deep * (wide - 1) * high + (deep - 1) * (high - 1) * wide
    n += (deep * wide - 1) * (high - 1) + deep * (wide - 1) * high
    return n


def gather_rows(shard, sizes, collective_id):
    wide, high, deep = sizes
    total, width = shard.shape
    rows = total // (4 * high)
    block = shard.reshape(2, high, 2, rows, width)
    out = pl.pallas_call(
        functools.partial(gather_kernel, sizes),
        out_shape=jax.ShapeDtypeStruct((deep, wide) + block.shape, block.dtype),
        in_specs=[pl.BlockSpec(memory_space=pl.ANY)],
        out_specs=pl.BlockSpec(memory_space=pl.ANY),
        scratch_shapes=[
            pltpu.SemaphoreType.DMA((gather_sends(sizes),)),
            pltpu.SemaphoreType.DMA((deep, wide, 2, high, 2)),
            pltpu.SemaphoreType.DMA,
        ],
        compiler_params=pltpu.CompilerParams(collective_id=collective_id, has_side_effects=True),
    )(block)
    return out.reshape(deep * wide, total, width)


def reduce_kernel(
    sizes,
    in_ref,
    out_ref,
    held,
    from_core,
    from_x_a,
    from_y_b,
    from_y_a,
    from_x_b,
    from_z,
    final,
    send_sem,
    local_sem,
    core_sem,
    xa_sem,
    yb_sem,
    ya_sem,
    xb_sem,
    z_sem,
    done_sem,
):
    wide, high, deep = sizes
    x, y, z, c = place(sizes)
    greet(sizes)
    partner = (y * 2 + 1 - c, z * wide + x)
    sent = []

    def send(src, dst, recv, to):
        copy = pltpu.make_async_remote_copy(
            src_ref=src,
            dst_ref=dst,
            send_sem=send_sem.at[len(sent)],
            recv_sem=recv,
            device_id=to,
            device_id_type=MESH,
        )
        copy.start()
        sent.append(copy)
        return copy

    def arrive(dst, recv):
        pltpu.make_async_remote_copy(
            src_ref=dst,
            dst_ref=dst,
            send_sem=send_sem.at[0],
            recv_sem=recv,
            device_id=partner,
            device_id_type=MESH,
        ).wait_recv()

    def merge(target, extras):
        total = target[...].astype(jnp.float32)
        for extra in extras:
            total = total + extra[...].astype(jnp.float32)
        target[...] = total.astype(target.dtype)

    order = [(z + k) % deep for k in range(deep // 2, deep)] + [
        (z + k) % deep for k in range(deep // 2 - 1, 0, -1)
    ] + [z]
    local = []
    for step, zt in enumerate(order):
        copy = pltpu.make_async_copy(in_ref.at[zt, :, c], held.at[step], local_sem.at[step])
        copy.start()
        local.append(copy)
        send(in_ref.at[zt, :, 1 - c], from_core.at[step], core_sem.at[step], partner)

    def first(step):
        local[step].wait()
        arrive(from_core.at[step], core_sem.at[step])

        def body(i, carry):
            xi, yi, hi = i // (2 * high), i // 2 % high, i % 2
            merge(held.at[step, xi, yi, hi], [from_core.at[step, xi, yi, hi]])
            return carry

        lax.fori_loop(0, wide * high * 2, body, 0)
        for k in range(1, wide):
            xt = (x + k) % wide
            send(
                held.at[step, xt, :, 0],
                from_x_a.at[k - 1, step],
                xa_sem.at[k - 1, step],
                (y * 2 + c, z * wide + xt),
            )
        for k in range(1, high):
            yt = (y + k) % high
            send(
                held.at[step, :, yt, 1],
                from_y_b.at[k - 1, step],
                yb_sem.at[k - 1, step],
                (yt * 2 + c, z * wide + x),
            )

    def second(step):
        for k in range(1, wide):
            arrive(from_x_a.at[k - 1, step], xa_sem.at[k - 1, step])

        def body_a(i, carry):
            yt = (y + 1 + i) % high
            merge(held.at[step, x, yt, 0], [from_x_a.at[k, step, yt] for k in range(wide - 1)])
            return carry

        lax.fori_loop(0, high, body_a, 0)
        for k in range(1, high):
            yt = (y + k) % high
            send(
                held.at[step, x, yt, 0],
                from_y_a.at[k - 1, step],
                ya_sem.at[k - 1, step],
                (yt * 2 + c, z * wide + x),
            )
        for k in range(1, high):
            arrive(from_y_b.at[k - 1, step], yb_sem.at[k - 1, step])

        def body_b(i, carry):
            xt = (x + 1 + i) % wide
            merge(held.at[step, xt, y, 1], [from_y_b.at[k, step, xt] for k in range(high - 1)])
            return carry

        lax.fori_loop(0, wide, body_b, 0)
        for k in range(1, wide):
            xt = (x + k) % wide
            send(
                held.at[step, xt, y, 1],
                from_x_b.at[k - 1, step],
                xb_sem.at[k - 1, step],
                (y * 2 + c, z * wide + xt),
            )

    def third(step):
        for k in range(1, high):
            arrive(from_y_a.at[k - 1, step], ya_sem.at[k - 1, step])
        merge(held.at[step, x, y, 0], [from_y_a.at[k, step] for k in range(high - 1)])
        for k in range(1, wide):
            arrive(from_x_b.at[k - 1, step], xb_sem.at[k - 1, step])
        merge(held.at[step, x, y, 1], [from_x_b.at[k, step] for k in range(wide - 1)])
        if step < deep - 1:
            send(
                held.at[step, x, y],
                from_z.at[step],
                z_sem.at[step],
                (y * 2 + c, order[step] * wide + x),
            )

    for turn in range(deep + 2):
        if turn < deep:
            first(turn)
        if 0 <= turn - 1 < deep:
            second(turn - 1)
        if 0 <= turn - 2 < deep:
            third(turn - 2)
    for step in range(deep - 1):
        arrive(from_z.at[step], z_sem.at[step])
    for h in range(2):
        total = held[deep - 1, x, y, h].astype(jnp.float32)
        for step in range(deep - 1):
            total = total + from_z[step, h].astype(jnp.float32)
        final[h] = total.astype(final.dtype)
    own = pltpu.make_async_copy(final, out_ref.at[c, y], local_sem.at[deep])
    own.start()
    for k in range(1, high):
        send(final, out_ref.at[c, y], done_sem.at[c, y], ((y + k) % high * 2 + c, z * wide + x))
    send(final, out_ref.at[c, y], done_sem.at[c, y], partner)
    for k in range(1, high):
        yt = (y + k) % high
        arrive(out_ref.at[c, yt], done_sem.at[c, yt])
        send(out_ref.at[c, yt], out_ref.at[c, yt], done_sem.at[c, yt], partner)
    for k in range(high):
        yt = (y + k) % high
        arrive(out_ref.at[1 - c, yt], done_sem.at[1 - c, yt])
    for copy in sent:
        copy.wait_send()
    own.wait()


def reduce_rows(partial, sizes, collective_id):
    wide, high, deep = sizes
    _, total, width = partial.shape
    rows = total // (4 * high)
    kind = partial.dtype
    block = partial.reshape(deep, wide, 2, high, 2, rows, width)
    tail = (rows, width)
    dma = pltpu.SemaphoreType.DMA
    sends = deep + deep * 2 * (wide - 1 + high - 1) + deep - 1 + 2 * (high - 1) + 1
    out = pl.pallas_call(
        functools.partial(reduce_kernel, sizes),
        out_shape=jax.ShapeDtypeStruct((2, high, 2, rows, width), kind),
        in_specs=[pl.BlockSpec(memory_space=pl.ANY)],
        out_specs=pl.BlockSpec(memory_space=pl.ANY),
        scratch_shapes=[
            pltpu.VMEM((deep, wide, high, 2) + tail, kind),
            pltpu.VMEM((deep, wide, high, 2) + tail, kind),
            pltpu.VMEM((wide - 1, deep, high) + tail, kind),
            pltpu.VMEM((high - 1, deep, wide) + tail, kind),
            pltpu.VMEM((high - 1, deep) + tail, kind),
            pltpu.VMEM((wide - 1, deep) + tail, kind),
            pltpu.VMEM((deep - 1, 2) + tail, kind),
            pltpu.VMEM((2,) + tail, kind),
            dma((sends,)),
            dma((deep + 1,)),
            dma((deep,)),
            dma((wide - 1, deep)),
            dma((high - 1, deep)),
            dma((high - 1, deep)),
            dma((wide - 1, deep)),
            dma((deep - 1,)),
            dma((2, high)),
        ],
        compiler_params=pltpu.CompilerParams(
            collective_id=collective_id, has_side_effects=True, vmem_limit_bytes=60 * 2**20
        ),
    )(block)
    return out.reshape(total, width)


narrow = (0, 1, 3, 4, 6, 7)
wide = (2, 5)

def per_device(
    frames,
    cotangent,
    segment_ids,
    code_index,
    codebooks,
    dead_codes,
    code_slots,
    buffered,
    encoder_dilated,
    encoder_pointwise,
    down_weight,
    group_in,
    group_out,
    up_weight,
    decoder_dilated,
    decoder_pointwise,
    encoder_dilated_moment,
    encoder_pointwise_moment,
    down_moment,
    group_in_moment,
    group_out_moment,
    up_moment,
    decoder_dilated_moment,
    decoder_pointwise_moment,
):
    masters = (
        encoder_dilated,
        encoder_pointwise,
        down_weight,
        group_in,
        group_out,
        up_weight,
        decoder_dilated,
        decoder_pointwise,
    )
    olds = (
        encoder_dilated_moment,
        encoder_pointwise_moment,
        down_moment,
        group_in_moment,
        group_out_moment,
        up_moment,
        decoder_dilated_moment,
        decoder_pointwise_moment,
    )
    lowered = [weight.astype(jnp.bfloat16) for weight in masters]
    count = lax.axis_size("seq")
    sizes = line_sizes(count, lax.axis_size("dp"))
    sides = ((0, 1, 3, 2), (6, 7, 4, 5))
    packed = []
    for side in sides:
        parts = [lowered[i] for i in side[:3]] + [halves(lowered[side[3]])]
        packed.append(pack_side(*parts, sizes[1], 0))
    side_rows = packed[0].shape[0]
    gathered = gather_rows(jnp.concatenate(packed), sizes, 0)
    full = [None] * 8
    part_shapes = []
    for at, side in enumerate(sides):
        shapes = [masters[i].shape for i in side[:3]]
        taps, share, width = masters[side[3]].shape
        shapes.append((2, taps, share, width // 2))
        part_shapes.append(shapes)
        parts = take_side(gathered[:, at * side_rows : (at + 1) * side_rows], shapes)
        for i, part, axis in zip(side[:3], parts, (2, 1, 1)):
            full[i] = joined(part, axis)
        strided = joined(parts[3], 2)
        full[side[3]] = jnp.concatenate([strided[0], strided[1]], axis=-1)
    row_count, length, channels = frames.shape
    latent_len = length // STRIDE
    tokens = row_count * latent_len
    segment_rim = extended(segment_ids + 1, (("seq", 1),), widest)
    stream = frames.astype(jnp.float32)
    encoder_kept = []
    for position, dilation in enumerate(dilation_list):
        stream, kept = unit_forward(
            stream, segment_rim, dilation, full[0][position], full[1][position]
        )
        encoder_kept.append(kept)
    before_down = stream
    down_active = jax.nn.elu(stream).astype(jnp.bfloat16).reshape(tokens, STRIDE * channels)
    down_matrix = full[2].reshape(STRIDE * channels, channels)
    latent = jnp.dot(down_active, down_matrix, preferred_element_type=jnp.float32)
    latent_low = latent.astype(jnp.bfloat16)
    group_width = channels // GROUPS
    code_range = lax.broadcasted_iota(jnp.int32, (1, codebooks.shape[2]), 1)
    firsts = []
    seconds = []
    quantized = []
    onehots = []
    last_picks = []
    for group_index in range(GROUPS):
        latent_slice = latent_low[:, group_index * group_width : (group_index + 1) * group_width]
        first_part = jnp.dot(latent_slice, full[3][group_index], preferred_element_type=jnp.float32)
        picked = []
        for level_index in range(LEVELS):
            onehot = (
                code_index[:, :, group_index, level_index].reshape(-1, 1) == code_range
            ).astype(jnp.float32)
            onehots.append(onehot)
            picked.append(jnp.dot(onehot, codebooks[group_index, level_index], precision=highest))
        firsts.append(first_part)
        seconds.append(first_part - picked[0])
        quantized.append((picked[0] + picked[1]).astype(jnp.bfloat16))
        last_picks.append(picked[1])
    mixed = jnp.concatenate(
        [
            jnp.dot(
                quantized[group_index], full[4][group_index], preferred_element_type=jnp.float32
            )
            for group_index in range(GROUPS)
        ],
        axis=1,
    )
    lifted = jax.nn.elu(mixed).astype(jnp.bfloat16)
    up_matrix = full[5].reshape(STRIDE * channels, channels)
    stream = contract_last(lifted, up_matrix).reshape(row_count, length, channels)
    decoder_kept = []
    for position, dilation in enumerate(dilation_list):
        stream, kept = unit_forward(
            stream, segment_rim, dilation, full[6][position], full[7][position]
        )
        decoder_kept.append(kept)
    decoded = stream.astype(jnp.bfloat16)
    grad = cotangent
    decoder_dilated_grads = [None, None, None]
    decoder_point_grads = [None, None, None]
    for position in (2, 1, 0):
        grad, dilated_grad, point_grad = unit_backward(
            grad,
            decoder_kept[position],
            dilation_list[position],
            full[6][position],
            full[7][position],
        )
        decoder_dilated_grads[position] = dilated_grad
        decoder_point_grads[position] = point_grad
    grad_up = grad.reshape(tokens, STRIDE * channels).astype(jnp.bfloat16)
    up_grad = contract_rows(grad_up, lifted).reshape(full[5].shape)
    grad_lifted = jnp.dot(grad_up, up_matrix, preferred_element_type=jnp.float32)
    grad_mixed = (grad_lifted * elu_slope(mixed)).astype(jnp.bfloat16)
    group_out_grads = []
    group_in_grads = []
    grad_latent_parts = []
    for group_index in range(GROUPS):
        grad_slice = grad_mixed[:, group_index * group_width : (group_index + 1) * group_width]
        group_out_grads.append(contract_rows(quantized[group_index], grad_slice))
        grad_quant = contract_last(grad_slice, full[4][group_index])
        grad_first = grad_quant + 2.0 * commit_weight * (
            seconds[group_index] + (seconds[group_index] - last_picks[group_index])
        )
        grad_first_low = grad_first.astype(jnp.bfloat16)
        latent_slice = latent_low[:, group_index * group_width : (group_index + 1) * group_width]
        group_in_grads.append(contract_rows(latent_slice, grad_first_low))
        grad_latent_parts.append(contract_last(grad_first_low, full[3][group_index]))
    grad_latent = jnp.concatenate(grad_latent_parts, axis=1).astype(jnp.bfloat16)
    down_grad = contract_rows(down_active, grad_latent).reshape(full[2].shape)
    grad_blocks = contract_last(grad_latent, down_matrix).reshape(row_count, length, channels)
    grad = grad_blocks * elu_slope(before_down)
    encoder_dilated_grads = [None, None, None]
    encoder_point_grads = [None, None, None]
    for position in (2, 1, 0):
        grad, dilated_grad, point_grad = unit_backward(
            grad,
            encoder_kept[position],
            dilation_list[position],
            full[0][position],
            full[1][position],
        )
        encoder_dilated_grads[position] = dilated_grad
        encoder_point_grads[position] = point_grad
    everyone = ("dp", "seq")
    all_rows = lax.all_gather(
        jnp.concatenate([firsts[0], seconds[0], firsts[1], seconds[1]], axis=1),
        everyone,
        axis=0,
        tiled=True,
    )
    all_codes = lax.all_gather(
        code_index.reshape(tokens, GROUPS * LEVELS), everyone, axis=0, tiled=True
    )
    code_share = dead_codes.shape[2]
    own_range = lax.broadcasted_iota(
        jnp.int32, (1, code_share), 1
    ) + code_share * lax.axis_index("seq")
    sum_list = []
    count_list = []
    for entry in range(GROUPS * LEVELS):
        own_hot = (all_codes[:, entry : entry + 1] == own_range).astype(jnp.float32)
        sum_list.append(
            lax.dot_general(
                own_hot,
                all_rows[:, entry * group_width : (entry + 1) * group_width],
                (((0,), (0,)), ((), ())),
                precision=highest,
            )
        )
        count_list.append(jnp.sum(own_hot, axis=0))
    total_sums = jnp.stack(sum_list).reshape(GROUPS, LEVELS, code_share, group_width)
    total_counts = jnp.stack(count_list).reshape(GROUPS, LEVELS, code_share)
    full_grads = (
        jnp.stack(encoder_dilated_grads),
        jnp.stack(encoder_point_grads),
        down_grad,
        jnp.stack(group_in_grads),
        jnp.stack(group_out_grads),
        up_grad,
        jnp.stack(decoder_dilated_grads),
        jnp.stack(decoder_point_grads),
    )
    packed = []
    for side in sides:
        parts = [
            by_owner(full_grads[i].astype(jnp.bfloat16), axis, count)
            for i, axis in zip(side[:3], (2, 1, 1))
        ]
        strided = by_owner(full_grads[side[3]].astype(jnp.bfloat16), 1, count)
        parts.append(jnp.moveaxis(halves(strided), 0, 1))
        packed.append(pack_side(*parts, sizes[1], 1))
    share = reduce_rows(jnp.concatenate(packed, axis=1), sizes, 1)
    reduced = [None] * 8
    for at, side in enumerate(sides):
        parts = take_side(share[at * side_rows : (at + 1) * side_rows], part_shapes[at])
        for i, part in zip(side[:3], parts):
            reduced[i] = part.astype(jnp.float32)
        reduced[side[3]] = jnp.concatenate([parts[3][0], parts[3][1]], axis=-1).astype(jnp.float32)
    own_codes = lax.dynamic_slice_in_dim(
        codebooks, lax.axis_index("seq") * code_share, code_share, 2
    )
    code_means = total_sums / jnp.maximum(total_counts, 1.0)[..., None]
    code_used = jnp.minimum(total_counts, 1.0)[..., None]
    updated = own_codes + code_rate * code_used * (code_means - own_codes)
    slot_range = lax.broadcasted_iota(jnp.int32, (1, 1, 1, buffered.shape[1]), 3)
    slot_onehot = (code_slots[..., None] == slot_range).astype(jnp.float32)
    replaced = jnp.einsum("glsb,gbz->glsz", slot_onehot, buffered, precision=highest)
    new_codebooks = jnp.where(dead_codes[..., None] == 1, replaced, updated)
    velocities = tuple((moment_decay * olds[position] + reduced[position] for position in range(8)))
    views = tuple(
        (
            velocities[position].reshape(
                velocities[position].shape[0] if stacked_flags[position] else 1,
                -1,
                velocities[position].shape[-1],
            )
            for position in range(8)
        )
    )
    current = [None] * 8
    for members in (narrow, wide):
        grams = lax.psum(
            jnp.concatenate(
                [
                    jnp.einsum("nrc,nrd->ncd", views[i], views[i], precision=highest)
                    for i in members
                ]
            ),
            "seq",
        )
        mixing = solve_mixing(grams)
        start = 0
        for i in members:
            stop = start + views[i].shape[0]
            current[i] = jnp.einsum(
                "nrc,ncd->nrd", views[i], mixing[start:stop], precision=highest
            )
            start = stop
    shaped = tuple((current[position].reshape(masters[position].shape) for position in range(8)))
    nexts = tuple((masters[position] - update_rate * shaped[position] for position in range(8)))
    return (
        decoded,
        grad,
        new_codebooks,
        velocities[0],
        velocities[1],
        velocities[2],
        velocities[3],
        velocities[4],
        velocities[5],
        velocities[6],
        velocities[7],
        nexts[0],
        nexts[1],
        nexts[2],
        nexts[3],
        nexts[4],
        nexts[5],
        nexts[6],
        nexts[7],
    )


def solution(mesh):
    in_specs = (
        P("dp", "seq", None),
        P("dp", "seq", None),
        P("dp", "seq"),
        P("dp", "seq", None, None),
        P(),
        P(None, None, "seq"),
        P(None, None, "seq"),
        P(),
        P(None, None, "seq", None),
        P(None, "seq", None),
        P(None, "seq", None),
        P(None, "seq", None),
        P(None, "seq", None),
        P(None, "seq", None),
        P(None, None, "seq", None),
        P(None, "seq", None),
        P(None, None, "seq", None),
        P(None, "seq", None),
        P(None, "seq", None),
        P(None, "seq", None),
        P(None, "seq", None),
        P(None, "seq", None),
        P(None, None, "seq", None),
        P(None, "seq", None),
    )
    out_specs = (
        P("dp", "seq", None),
        P("dp", "seq", None),
        P(None, None, "seq", None),
        P(None, None, "seq", None),
        P(None, "seq", None),
        P(None, "seq", None),
        P(None, "seq", None),
        P(None, "seq", None),
        P(None, "seq", None),
        P(None, None, "seq", None),
        P(None, "seq", None),
        P(None, None, "seq", None),
        P(None, "seq", None),
        P(None, "seq", None),
        P(None, "seq", None),
        P(None, "seq", None),
        P(None, "seq", None),
        P(None, None, "seq", None),
        P(None, "seq", None),
    )
    return jax.shard_map(
        per_device, mesh=mesh, in_specs=in_specs, out_specs=out_specs, check_vma=False
    )
```

```python
import functools

import jax
import jax.numpy as jnp
from jax import lax
from jax.experimental import pallas as pl
from jax.experimental.pallas import tpu as pltpu
from jax.sharding import PartitionSpec as P

GROUPS = 2
LEVELS = 2
KERNEL = 7
STRIDE = 8
NS_STEPS = 5


highest = lax.Precision.HIGHEST
dilation_list = (1, 3, 9)
stacked_flags = (True, True, False, True, True, False, True, True)
coef_first = 3.4445
coef_second = -4.775
coef_third = 2.0315
commit_weight = 0.25
moment_decay = 0.5
update_rate = 0.5
code_rate = 0.5
norm_floor = 1e-07


def solve_mixing(gram):
    norm = jnp.sqrt(jnp.trace(gram, axis1=1, axis2=2)) + norm_floor
    scale = 1.0 / norm
    current = gram * (scale * scale)[:, None, None]
    eye = jnp.eye(gram.shape[-1], dtype=jnp.float32)[None]
    total = None
    for repeat in range(NS_STEPS):
        square = jnp.einsum("ncd,nde->nce", current, current, precision=highest)
        factor = coef_first * eye + coef_second * current + coef_third * square
        if total is None:
            total = factor
        else:
            total = jnp.einsum("ncd,nde->nce", total, factor, precision=highest)
        if repeat < NS_STEPS - 1:
            half = jnp.einsum("ncd,nde->nce", current, factor, precision=highest)
            current = jnp.einsum("ncd,nde->nce", half, factor, precision=highest)
    return total * scale[:, None, None]


def halves(array):
    width = array.shape[-1] // 2
    split = array.reshape(array.shape[:-1] + (2, width))
    return jnp.moveaxis(split, -2, 0)


def whole_rows(rows, high):
    unit = 32 * high
    return -(-rows // unit) * unit


def pack_side(dilated, pointwise, group, strided, high, lead):
    parts = [dilated, pointwise, group, strided]
    kept = dilated.shape[:lead]
    flat = [part.reshape(kept + (-1, part.shape[-1])) for part in parts]
    rows = sum(part.shape[lead] for part in flat)
    extra = whole_rows(rows, high) - rows
    if extra:
        flat.append(jnp.zeros(kept + (extra, flat[0].shape[-1]), flat[0].dtype))
    return jnp.concatenate(flat, axis=lead)


def take_side(rows, shapes):
    found = []
    start = 0
    for shape in shapes:
        size = 1
        for extent in shape[:-1]:
            size *= extent
        found.append(rows[..., start : start + size, :].reshape(rows.shape[:-2] + shape))
        start += size
    return found


MESH = pl.DeviceIdType.MESH


def line_sizes(seq, dp):
    across = 1
    while (2 * across) * (2 * across) <= seq:
        across *= 2
    return across, dp // 2, seq // across


def place(sizes):
    wide, high, _ = sizes
    row = lax.axis_index("dp")
    part = lax.axis_index("seq")
    return part % wide, row // 2, part // wide, row % 2


def greet(sizes):
    wide, high, deep = sizes
    x, y, z, c = place(sizes)
    barrier = pltpu.get_barrier_semaphore()
    others = [(y * 2 + 1 - c, z * wide + x)]
    others += [(y * 2 + c, z * wide + (x + k) % wide) for k in range(1, wide)]
    others += [((y + k) % high * 2 + c, z * wide + x) for k in range(1, high)]
    others += [(y * 2 + c, (z + k) % deep * wide + x) for k in range(1, deep)]
    count = deep * wide
    others += [(y * 2 + c, (z * wide + x + k) % count) for k in (1, count - 1)]
    for other in others:
        pl.semaphore_signal(barrier, inc=1, device_id=other, device_id_type=MESH)
    pl.semaphore_wait(barrier, len(others))


def gather_kernel(sizes, edges, *refs):
    in_ref, edge_in = refs[0], refs[1 : 1 + edges]
    out_ref, edge_out = refs[1 + edges], refs[2 + edges : 2 + 2 * edges]
    send_sem, recv_sem, local_sem, edge_sem = refs[2 + 2 * edges :]
    wide, high, deep = sizes
    x, y, z, c = place(sizes)
    greet(sizes)
    own = pltpu.make_async_copy(in_ref, out_ref.at[z, x], local_sem)
    own.start()
    sent = []
    count = deep * wide
    side_copies = []
    for number in range(edges):
        for way in range(2):
            other = (z * wide + x + (1 if way == 0 else count - 1)) % count
            copy = pltpu.make_async_remote_copy(
                src_ref=edge_in[number].at[way],
                dst_ref=edge_out[number].at[way],
                send_sem=edge_sem.at[0, number, way],
                recv_sem=edge_sem.at[1, number, way],
                device_id=(y * 2 + c, other),
                device_id_type=MESH,
            )
            copy.start()
            side_copies.append(copy)

    def send(zs, xs, ys, h, to, source=None):
        spot = out_ref.at[zs, xs, c, ys, h]
        copy = pltpu.make_async_remote_copy(
            src_ref=spot if source is None else source,
            dst_ref=spot,
            send_sem=send_sem.at[len(sent)],
            recv_sem=recv_sem.at[zs, xs, c, ys, h],
            device_id=to,
            device_id_type=MESH,
        )
        copy.start()
        sent.append(copy)

    def arrive(zs, xs, cs, ys, h):
        spot = out_ref.at[zs, xs, cs, ys, h]
        pltpu.make_async_remote_copy(
            src_ref=spot,
            dst_ref=spot,
            send_sem=send_sem.at[0],
            recv_sem=recv_sem.at[zs, xs, cs, ys, h],
            device_id=(y * 2 + 1 - c, z * wide + x),
            device_id_type=MESH,
        ).wait_recv()

    def to_x(zs, xs, ys, h, source=None):
        for k in range(1, wide):
            send(zs, xs, ys, h, (y * 2 + c, z * wide + (x + k) % wide), source)

    def to_y(zs, xs, ys, h):
        for k in range(1, high):
            send(zs, xs, ys, h, ((y + k) % high * 2 + c, z * wide + x))

    def to_core(zs, xs, ys, h):
        send(zs, xs, ys, h, (y * 2 + 1 - c, z * wide + x))

    for k in range(deep - 1, 0, -1):
        for h in range(2):
            send(z, x, y, h, (y * 2 + c, (z + k) % deep * wide + x), in_ref.at[c, y, h])
    to_x(z, x, y, 0, in_ref.at[c, y, 0])
    for j in range(high):
        ys = (y + j) % high
        to_x(z, x, ys, 1, in_ref.at[c, ys, 1])
    for k in range(1, deep):
        zs = (z + k) % deep
        arrive(zs, x, c, y, 0)
        to_x(zs, x, y, 0)
        to_y(zs, x, y, 0)
        to_core(zs, x, y, 0)
        arrive(zs, x, c, y, 1)
        to_y(zs, x, y, 1)
        to_x(zs, x, y, 1)
        to_core(zs, x, y, 1)
    for k in range(deep):
        zs = (z + k) % deep
        for i in range(1, wide):
            xs = (x + i) % wide
            arrive(zs, xs, c, y, 0)
            to_y(zs, xs, y, 0)
            to_core(zs, xs, y, 0)
        if k > 0:
            for j in range(1, high):
                ys = (y + j) % high
                arrive(zs, x, c, ys, 1)
                to_x(zs, x, ys, 1)
                to_core(zs, x, ys, 1)
    for k in range(deep):
        zs = (z + k) % deep
        for i in range(wide):
            xs = (x + i) % wide
            if k == 0 and i == 0:
                continue
            for j in range(1, high):
                ys = (y + j) % high
                arrive(zs, xs, c, ys, 0)
                to_core(zs, xs, ys, 0)
            if i > 0:
                for j in range(high):
                    ys = (y + j) % high
                    arrive(zs, xs, c, ys, 1)
                    to_core(zs, xs, ys, 1)
    for k in range(deep):
        zs = (z + k) % deep
        for i in range(wide):
            xs = (x + i) % wide
            if k == 0 and i == 0:
                continue
            for j in range(high):
                for h in range(2):
                    arrive(zs, xs, 1 - c, (y + j) % high, h)
    for copy in sent:
        copy.wait_send()
    for copy in side_copies:
        copy.wait()
    own.wait()


def gather_sends(sizes):
    wide, high, deep = sizes
    n = (deep - 1) * 2 + (wide - 1) * (1 + high)
    n += (deep - 1) * 2 * (wide - 1 + high - 1 + 1)
    n += deep * (wide - 1) * high + (deep - 1) * (high - 1) * wide
    n += (deep * wide - 1) * (high - 1) + deep * (wide - 1) * high
    return n


def gather_rows(shard, edges, sizes, collective_id):
    wide, high, deep = sizes
    total, width = shard.shape
    rows = total // (4 * high)
    block = shard.reshape(2, high, 2, rows, width)
    out = pl.pallas_call(
        functools.partial(gather_kernel, sizes, len(edges)),
        out_shape=[jax.ShapeDtypeStruct((deep, wide) + block.shape, block.dtype)]
        + [jax.ShapeDtypeStruct(edge.shape, edge.dtype) for edge in edges],
        in_specs=[pl.BlockSpec(memory_space=pl.ANY)] * (1 + len(edges)),
        out_specs=[pl.BlockSpec(memory_space=pl.ANY)] * (1 + len(edges)),
        scratch_shapes=[
            pltpu.SemaphoreType.DMA((gather_sends(sizes),)),
            pltpu.SemaphoreType.DMA((deep, wide, 2, high, 2)),
            pltpu.SemaphoreType.DMA,
            pltpu.SemaphoreType.DMA((2, len(edges), 2)),
        ],
        compiler_params=pltpu.CompilerParams(collective_id=collective_id, has_side_effects=True),
    )(block, *edges)
    return out[0].reshape(deep * wide, total, width), out[1:]


def reduce_kernel(
    sizes,
    in_ref,
    row_ref,
    out_ref,
    all_ref,
    held,
    from_core,
    from_x_a,
    from_y_b,
    from_y_a,
    from_x_b,
    from_z,
    final,
    send_sem,
    local_sem,
    core_sem,
    xa_sem,
    yb_sem,
    ya_sem,
    xb_sem,
    z_sem,
    done_sem,
    row_sem,
):
    wide, high, deep = sizes
    x, y, z, c = place(sizes)
    greet(sizes)
    partner = (y * 2 + 1 - c, z * wide + x)
    sent = []

    def send(src, dst, recv, to):
        copy = pltpu.make_async_remote_copy(
            src_ref=src,
            dst_ref=dst,
            send_sem=send_sem.at[len(sent)],
            recv_sem=recv,
            device_id=to,
            device_id_type=MESH,
        )
        copy.start()
        sent.append(copy)
        return copy

    def arrive(dst, recv):
        pltpu.make_async_remote_copy(
            src_ref=dst,
            dst_ref=dst,
            send_sem=send_sem.at[0],
            recv_sem=recv,
            device_id=partner,
            device_id_type=MESH,
        ).wait_recv()

    keep = pltpu.make_async_copy(row_ref, all_ref.at[z, x, y, c], local_sem.at[deep + 1])
    keep.start()

    def spread(stage):
        columns = [(z + k) % deep for k in range(deep)]
        lines = [(x + k) % wide for k in range(wide)]
        heights = [(y + k) % high for k in range(high)]

        def pass_on(zs, xs, ys, to, source=None):
            spot = all_ref.at[zs, xs, ys, c]
            send(spot if source is None else source, spot, row_sem.at[zs, xs, ys, c], to)

        def landed(zs, xs, ys, cs):
            arrive(all_ref.at[zs, xs, ys, cs], row_sem.at[zs, xs, ys, cs])

        if stage == 0:
            for zt in columns[1:]:
                pass_on(z, x, y, (y * 2 + c, zt * wide + x), row_ref)
        if stage == 1:
            for zs in columns[1:]:
                landed(zs, x, y, c)
            for zs in columns:
                for xt in lines[1:]:
                    pass_on(zs, x, y, (y * 2 + c, z * wide + xt), row_ref if zs is columns[0] else None)
        if stage == 2:
            for zs in columns:
                for xs in lines[1:]:
                    landed(zs, xs, y, c)
            for zs in columns:
                for xs in lines:
                    mine = zs is columns[0] and xs is lines[0]
                    for yt in heights[1:]:
                        pass_on(zs, xs, y, (yt * 2 + c, z * wide + x), row_ref if mine else None)
        if stage == 3:
            for zs in columns:
                for xs in lines:
                    for ys in heights[1:]:
                        landed(zs, xs, ys, c)
            for zs in columns:
                for xs in lines:
                    for ys in heights:
                        mine = zs is columns[0] and xs is lines[0] and ys is heights[0]
                        pass_on(zs, xs, ys, partner, row_ref if mine else None)
        if stage == 4:
            for zs in columns:
                for xs in lines:
                    for ys in heights:
                        landed(zs, xs, ys, 1 - c)

    def merge(target, extras):
        total = target[...].astype(jnp.float32)
        for extra in extras:
            total = total + extra[...].astype(jnp.float32)
        target[...] = total.astype(target.dtype)

    order = [(z + k) % deep for k in range(deep // 2, deep)] + [
        (z + k) % deep for k in range(deep // 2 - 1, 0, -1)
    ] + [z]
    local = []
    for step, zt in enumerate(order):
        copy = pltpu.make_async_copy(in_ref.at[zt, :, c], held.at[step], local_sem.at[step])
        copy.start()
        local.append(copy)
        send(in_ref.at[zt, :, 1 - c], from_core.at[step], core_sem.at[step], partner)

    def first(step):
        local[step].wait()
        arrive(from_core.at[step], core_sem.at[step])

        def body(i, carry):
            xi, yi, hi = i // (2 * high), i // 2 % high, i % 2
            merge(held.at[step, xi, yi, hi], [from_core.at[step, xi, yi, hi]])
            return carry

        lax.fori_loop(0, wide * high * 2, body, 0)
        for k in range(1, wide):
            xt = (x + k) % wide
            send(
                held.at[step, xt, :, 0],
                from_x_a.at[k - 1, step],
                xa_sem.at[k - 1, step],
                (y * 2 + c, z * wide + xt),
            )
        for k in range(1, high):
            yt = (y + k) % high
            send(
                held.at[step, :, yt, 1],
                from_y_b.at[k - 1, step],
                yb_sem.at[k - 1, step],
                (yt * 2 + c, z * wide + x),
            )

    def second(step):
        for k in range(1, wide):
            arrive(from_x_a.at[k - 1, step], xa_sem.at[k - 1, step])

        def body_a(i, carry):
            yt = (y + 1 + i) % high
            merge(held.at[step, x, yt, 0], [from_x_a.at[k, step, yt] for k in range(wide - 1)])
            return carry

        lax.fori_loop(0, high, body_a, 0)
        for k in range(1, high):
            yt = (y + k) % high
            send(
                held.at[step, x, yt, 0],
                from_y_a.at[k - 1, step],
                ya_sem.at[k - 1, step],
                (yt * 2 + c, z * wide + x),
            )
        for k in range(1, high):
            arrive(from_y_b.at[k - 1, step], yb_sem.at[k - 1, step])

        def body_b(i, carry):
            xt = (x + 1 + i) % wide
            merge(held.at[step, xt, y, 1], [from_y_b.at[k, step, xt] for k in range(high - 1)])
            return carry

        lax.fori_loop(0, wide, body_b, 0)
        for k in range(1, wide):
            xt = (x + k) % wide
            send(
                held.at[step, xt, y, 1],
                from_x_b.at[k - 1, step],
                xb_sem.at[k - 1, step],
                (y * 2 + c, z * wide + xt),
            )

    def third(step):
        for k in range(1, high):
            arrive(from_y_a.at[k - 1, step], ya_sem.at[k - 1, step])
        merge(held.at[step, x, y, 0], [from_y_a.at[k, step] for k in range(high - 1)])
        for k in range(1, wide):
            arrive(from_x_b.at[k - 1, step], xb_sem.at[k - 1, step])
        merge(held.at[step, x, y, 1], [from_x_b.at[k, step] for k in range(wide - 1)])
        if step < deep - 1:
            send(
                held.at[step, x, y],
                from_z.at[step],
                z_sem.at[step],
                (y * 2 + c, order[step] * wide + x),
            )

    spread(0)
    for turn in range(deep + 2):
        if turn < deep:
            first(turn)
        if turn in (1, 2, 3):
            spread(turn)
        if 0 <= turn - 1 < deep:
            second(turn - 1)
        if 0 <= turn - 2 < deep:
            third(turn - 2)
    spread(4)
    keep.wait()
    for step in range(deep - 1):
        arrive(from_z.at[step], z_sem.at[step])
    for h in range(2):
        total = held[deep - 1, x, y, h].astype(jnp.float32)
        for step in range(deep - 1):
            total = total + from_z[step, h].astype(jnp.float32)
        final[h] = total.astype(final.dtype)
    own = pltpu.make_async_copy(final, out_ref.at[c, y], local_sem.at[deep])
    own.start()
    for k in range(1, high):
        send(final, out_ref.at[c, y], done_sem.at[c, y], ((y + k) % high * 2 + c, z * wide + x))
    send(final, out_ref.at[c, y], done_sem.at[c, y], partner)
    for k in range(1, high):
        yt = (y + k) % high
        arrive(out_ref.at[c, yt], done_sem.at[c, yt])
        send(out_ref.at[c, yt], out_ref.at[c, yt], done_sem.at[c, yt], partner)
    for k in range(high):
        yt = (y + k) % high
        arrive(out_ref.at[1 - c, yt], done_sem.at[1 - c, yt])
    for copy in sent:
        copy.wait_send()
    own.wait()


def reduce_rows(partial, rows_own, sizes, collective_id):
    wide, high, deep = sizes
    _, total, width = partial.shape
    rows = total // (4 * high)
    kind = partial.dtype
    block = partial.reshape(deep, wide, 2, high, 2, rows, width)
    tail = (rows, width)
    dma = pltpu.SemaphoreType.DMA
    sends = deep + deep * 2 * (wide - 1 + high - 1) + deep - 1 + 2 * (high - 1) + 1
    sends += deep - 1 + deep * (wide - 1) + deep * wide * (high - 1) + deep * wide * high
    out = pl.pallas_call(
        functools.partial(reduce_kernel, sizes),
        out_shape=(
            jax.ShapeDtypeStruct((2, high, 2, rows, width), kind),
            jax.ShapeDtypeStruct((deep, wide, high, 2) + rows_own.shape, rows_own.dtype),
        ),
        in_specs=[pl.BlockSpec(memory_space=pl.ANY)] * 2,
        out_specs=(pl.BlockSpec(memory_space=pl.ANY),) * 2,
        scratch_shapes=[
            pltpu.VMEM((deep, wide, high, 2) + tail, kind),
            pltpu.VMEM((deep, wide, high, 2) + tail, kind),
            pltpu.VMEM((wide - 1, deep, high) + tail, kind),
            pltpu.VMEM((high - 1, deep, wide) + tail, kind),
            pltpu.VMEM((high - 1, deep) + tail, kind),
            pltpu.VMEM((wide - 1, deep) + tail, kind),
            pltpu.VMEM((deep - 1, 2) + tail, kind),
            pltpu.VMEM((2,) + tail, kind),
            dma((sends,)),
            dma((deep + 2,)),
            dma((deep,)),
            dma((wide - 1, deep)),
            dma((high - 1, deep)),
            dma((high - 1, deep)),
            dma((wide - 1, deep)),
            dma((deep - 1,)),
            dma((2, high)),
            dma((deep, wide, high, 2)),
        ],
        compiler_params=pltpu.CompilerParams(
            collective_id=collective_id, has_side_effects=True, vmem_limit_bytes=60 * 2**20
        ),
    )(block, rows_own)
    return out[0].reshape(total, width), out[1].reshape((-1,) + rows_own.shape)


margin = 32
lanes = 128


def elu_slope(values):
    return jnp.where(values > 0, 1.0, jnp.exp(jnp.minimum(values, 0.0)))


def elu(values):
    return jnp.where(values > 0, values, jnp.exp(jnp.minimum(values, 0.0)) - 1.0)


def dot(left, right):
    return jnp.dot(left, right, preferred_element_type=jnp.float32)


def dot_last(left, right):
    return lax.dot_general(
        left, right, (((1,), (1,)), ((), ())), preferred_element_type=jnp.float32
    )


def dot_rows(left, right):
    return lax.dot_general(
        left, right, (((0,), (0,)), ((), ())), preferred_element_type=jnp.float32
    )


def spread_taps(target, source, ids, width, sign, dilation, length):
    block = 64

    def body(step, carry):
        base = pl.multiple_of(step * block, block)
        window = ids[pl.ds(base, block + 2 * margin), :]
        own = window[margin : margin + block]
        for tap in range(KERNEL):
            start = margin + sign * (tap - KERNEL // 2) * dilation
            match = window[start : start + block] == own
            for piece in range(width // lanes):
                columns = slice(piece * lanes, (piece + 1) * lanes)
                values = source[pl.ds(base, block + 2 * margin), columns][start : start + block]
                spot = tap * width + piece * lanes
                target[pl.ds(base, block), spot : spot + lanes] = jnp.where(
                    match, values, 0.0
                ).astype(jnp.bfloat16)
        return carry

    lax.fori_loop(0, length // block, body, 0)


def forward_unit(unit, stream, follow, ids, weights, scratch, length):
    dilated, pointwise = weights
    padded, columns, hidden, excited, active = scratch
    channels = stream.shape[1]
    values = elu(stream[...])
    padded[margin : margin + length, :] = values
    active[unit] = values[length // 4 : 3 * length // 4].astype(jnp.bfloat16)
    spread_taps(columns, padded, ids, channels, 1, dilation_list[unit], length)
    kernel = dilated[unit * KERNEL : (unit + 1) * KERNEL].reshape(KERNEL * channels, -1)
    value = dot(columns[...], kernel)
    hidden[unit] = value
    lifted = elu(value).astype(jnp.bfloat16)
    excited[unit] = lifted
    follow[...] = stream[...] + dot_last(lifted, pointwise[unit])


def backward_unit(unit, grad, stream, ids, weights, scratch, length, store_dilated, store_point):
    dilated, pointwise = weights
    padded, columns, hidden, excited, active = scratch
    width = hidden.shape[2]
    first, last = length // 4, 3 * length // 4
    low = grad[...].astype(jnp.bfloat16)
    store_point(
        unit,
        dot(grad[first:last, :].T.astype(jnp.bfloat16), excited[unit, first:last, :]).astype(
            jnp.bfloat16
        ),
    )
    grad_hidden = dot(low, pointwise[unit]) * elu_slope(hidden[unit])
    padded[margin : margin + length, :width] = grad_hidden.astype(jnp.bfloat16).astype(jnp.float32)
    spread_taps(columns, padded, ids, width, -1, dilation_list[unit], length)
    turned = active[unit].astype(jnp.float32).T.astype(jnp.bfloat16)
    total = None
    for tap in range(KERNEL):
        piece = slice(tap * width, (tap + 1) * width)
        part = dot_last(columns[:, piece], dilated[unit * KERNEL + tap])
        total = part if total is None else total + part
        store_dilated(unit, tap, dot(turned, columns[first:last, piece]).astype(jnp.bfloat16))
    grad[...] = grad[...] + total * elu_slope(stream[...])


class Mover:
    def __init__(self, side, geometry, gathered, packed, weights, grads, sems):
        self.seq, self.share, self.blocks = geometry
        self.base = side * self.blocks
        self.gathered, self.packed = gathered, packed
        self.weights, self.grads = weights, grads
        self.sems = sems

    def block_start(self, kind):
        return self.base + (0, 3 * KERNEL, 3 * KERNEL + 3, 3 * KERNEL + 4)[kind]

    def load(self, kind, owner):
        rows = self.weights[kind]
        start = self.block_start(kind)
        source = self.gathered.at[owner, pl.ds(start, rows.shape[0])]
        target = rows.at[:, pl.ds(owner * self.share, self.share)]
        return pltpu.make_async_copy(source, target, self.sems.at[kind, owner])

    def start_loads(self, kind):
        for owner in range(self.seq):
            self.load(kind, owner).start()

    def wait_loads(self, kind):
        for owner in range(self.seq):
            self.load(kind, owner).wait()

    def store(self, kind, owner, first, size):
        rows = self.grads[kind]
        start = self.block_start(kind) + first
        source = rows.at[first : first + size, pl.ds(owner * self.share, self.share)]
        target = self.packed.at[owner, pl.ds(start, size)]
        return pltpu.make_async_copy(source, target, self.sems.at[4 + kind, owner])


def load_group(rows, seq, share):
    width = rows.shape[-1]
    part = width // seq
    value = rows.astype(jnp.float32).reshape(seq, GROUPS, part, width)
    return [value[:, g].reshape(width, width).astype(jnp.bfloat16) for g in range(GROUPS)]


def store_group(grads, seq, share):
    width = grads[0].shape[-1]
    part = width // seq
    value = jnp.stack([grad.reshape(seq, part, width) for grad in grads], axis=1)
    return value.reshape(seq, GROUPS * part, width).astype(jnp.bfloat16)


def put_tap(tiles, tap, value):
    latents = value.shape[0]
    for piece in range(tiles.shape[0]):
        tiles[piece, pl.ds(tap, latents, stride=STRIDE), :] = value[
            :, piece * lanes : (piece + 1) * lanes
        ]


def take_tap(tiles, tap, latents):
    return jnp.concatenate(
        [tiles[piece, pl.ds(tap, latents, stride=STRIDE), :] for piece in range(tiles.shape[0])],
        axis=1,
    )


def to_tiles(tiles, value):
    for piece in range(tiles.shape[0]):
        tiles[piece] = value[:, piece * lanes : (piece + 1) * lanes]


def from_tiles(tiles):
    return jnp.concatenate([tiles[piece] for piece in range(tiles.shape[0])], axis=1)


def set_edges(padded, length):
    zero = jnp.zeros((margin, padded.shape[1]), jnp.float32)
    padded[:margin, :] = zero
    padded[margin + length :, :] = zero


def decoder_kernel(
    geometry,
    length,
    code_ref,
    ids_ref,
    cot_ref,
    books_ref,
    gathered,
    decoded_ref,
    grad_quant_ref,
    picks_ref,
    packed,
    dilated,
    pointwise,
    group,
    strided,
    grad_dilated,
    grad_point,
    grad_group,
    grad_strided,
    streams,
    grad,
    padded,
    columns,
    hidden,
    excited,
    active,
    tiles,
    sems,
):
    seq, share, blocks = geometry
    weights = (dilated, pointwise, group, strided)
    grads = (grad_dilated, grad_point, grad_group, grad_strided)
    mover = Mover(1, geometry, gathered, packed, weights, grads, sems)
    for kind in (2, 3, 0, 1):
        mover.start_loads(kind)
    set_edges(padded, length)
    first, last = length // 4, 3 * length // 4
    latents = length // STRIDE
    codes = books_ref.shape[2]
    width = books_ref.shape[3]
    code_range = lax.broadcasted_iota(jnp.int32, (latents, codes), 1)
    quantized = []
    for g in range(GROUPS):
        picked = []
        for level in range(LEVELS):
            entry = g * LEVELS + level
            hot = (code_ref[:, entry : entry + 1] == code_range).astype(jnp.float32)
            pick = jnp.dot(hot, books_ref[g, level], precision=lax.Precision.HIGHEST)
            picks_ref[entry] = pick
            picked.append(pick)
        quantized.append((picked[0] + picked[1]).astype(jnp.bfloat16))
    mover.wait_loads(2)
    out_weights = load_group(group[0], seq, share)
    mixed = [dot(quantized[g], out_weights[g]) for g in range(GROUPS)]
    lifted = [elu(value).astype(jnp.bfloat16) for value in mixed]
    mover.wait_loads(3)
    for tap in range(STRIDE):
        value = dot_last(lifted[0], strided[tap]) + dot_last(lifted[1], strided[STRIDE + tap])
        put_tap(tiles, tap, value)
    streams[0] = from_tiles(tiles)
    mover.wait_loads(0)
    mover.wait_loads(1)
    scratch = (padded, columns, hidden, excited, active)
    for unit in range(3):
        forward_unit(
            unit, streams.at[unit], streams.at[unit + 1], ids_ref, (dilated, pointwise), scratch,
            length,
        )
    decoded_ref[...] = streams[3, first:last, :].astype(jnp.bfloat16)
    grad[...] = cot_ref[...]

    def store_dilated(unit, tap, value):
        grad_dilated[unit * KERNEL + tap] = value

    def store_point(unit, value):
        grad_point[unit] = value

    for unit in (2, 1, 0):
        backward_unit(
            unit, grad, streams.at[unit], ids_ref, (dilated, pointwise), scratch, length,
            store_dilated, store_point,
        )
        for owner in range(seq):
            mover.store(0, owner, unit * KERNEL, KERNEL).start()
    for owner in range(seq):
        mover.store(1, owner, 0, 3).start()
    own = slice(first // STRIDE, last // STRIDE)
    grad_lifted = [None, None]
    to_tiles(tiles, grad[...])
    for tap in range(STRIDE):
        part = take_tap(tiles, tap, latents)
        low = part.astype(jnp.bfloat16)
        turned = part[own].T.astype(jnp.bfloat16)
        for half in range(2):
            value = dot(low, strided[half * STRIDE + tap])
            grad_lifted[half] = value if tap == 0 else grad_lifted[half] + value
            grad_strided[half * STRIDE + tap] = dot(turned, lifted[half][own]).astype(jnp.bfloat16)
    for owner in range(seq):
        mover.store(3, owner, 0, 2 * STRIDE).start()
    group_grads = []
    for g in range(GROUPS):
        low = (grad_lifted[g] * elu_slope(mixed[g])).astype(jnp.bfloat16)
        group_grads.append(dot_rows(quantized[g][own], low[own]))
        grad_quant_ref[g] = dot_last(low, out_weights[g])
    grad_group[0] = store_group(group_grads, seq, share).reshape(grad_group.shape[1:])
    for owner in range(seq):
        mover.store(2, owner, 0, 1).start()
    finish_stores(mover, seq)


def finish_stores(mover, seq):
    for owner in range(seq):
        for unit in range(3):
            mover.store(0, owner, unit * KERNEL, KERNEL).wait()
        mover.store(1, owner, 0, 3).wait()
        mover.store(3, owner, 0, 2 * STRIDE).wait()
        mover.store(2, owner, 0, 1).wait()


def encoder_kernel(
    geometry,
    length,
    frames_ref,
    ids_ref,
    grad_quant_ref,
    picks_ref,
    gathered,
    unused,
    frames_grad_ref,
    rows_ref,
    packed,
    dilated,
    pointwise,
    group,
    strided,
    grad_dilated,
    grad_point,
    grad_group,
    grad_strided,
    streams,
    grad,
    padded,
    columns,
    hidden,
    excited,
    active,
    tiles,
    sems,
):
    seq, share, blocks = geometry
    weights = (dilated, pointwise, group, strided)
    grads = (grad_dilated, grad_point, grad_group, grad_strided)
    mover = Mover(0, geometry, gathered, packed, weights, grads, sems)
    for kind in (0, 1, 3, 2):
        mover.start_loads(kind)
    set_edges(padded, length)
    first, last = length // 4, 3 * length // 4
    latents = length // STRIDE
    own = slice(first // STRIDE, last // STRIDE)
    width = picks_ref.shape[2]
    streams[0] = frames_ref[...].astype(jnp.float32)
    mover.wait_loads(0)
    mover.wait_loads(1)
    scratch = (padded, columns, hidden, excited, active)
    for unit in range(3):
        forward_unit(
            unit, streams.at[unit], streams.at[unit + 1], ids_ref, (dilated, pointwise), scratch,
            length,
        )
    to_tiles(tiles, elu(streams[3]))
    mover.wait_loads(3)
    mover.wait_loads(2)
    in_weights = load_group(group[0], seq, share)
    latent = [None, None]
    for tap in range(STRIDE):
        low = take_tap(tiles, tap, latents).astype(jnp.bfloat16)
        for half in range(2):
            value = dot(low, strided[half * STRIDE + tap])
            latent[half] = value if tap == 0 else latent[half] + value
    group_grads = []
    grad_latent = []
    for g in range(GROUPS):
        low = latent[g].astype(jnp.bfloat16)
        first_part = dot(low, in_weights[g])
        pick = [picks_ref[g * LEVELS + level] for level in range(LEVELS)]
        second_part = first_part - pick[0]
        rows_ref[:, (g * LEVELS) * width : (g * LEVELS + 1) * width] = first_part[own].astype(jnp.bfloat16)
        rows_ref[:, (g * LEVELS + 1) * width : (g * LEVELS + 2) * width] = second_part[own].astype(jnp.bfloat16)
        grad_first = grad_quant_ref[g] + 2.0 * commit_weight * (
            second_part + (second_part - pick[1])
        )
        low_first = grad_first.astype(jnp.bfloat16)
        group_grads.append(dot_rows(low[own], low_first[own]))
        grad_latent.append(dot_last(low_first, in_weights[g]).astype(jnp.bfloat16))
    grad_group[0] = store_group(group_grads, seq, share).reshape(grad_group.shape[1:])
    for owner in range(seq):
        mover.store(2, owner, 0, 1).start()
    for tap in range(STRIDE):
        turned = take_tap(tiles, tap, latents)[own].T.astype(jnp.bfloat16)
        value = dot_last(grad_latent[0], strided[tap]) + dot_last(
            grad_latent[1], strided[STRIDE + tap]
        )
        put_tap(tiles, tap, value)
        for half in range(2):
            grad_strided[half * STRIDE + tap] = dot(turned, grad_latent[half][own]).astype(
                jnp.bfloat16
            )
    for owner in range(seq):
        mover.store(3, owner, 0, 2 * STRIDE).start()
    grad[...] = from_tiles(tiles) * elu_slope(streams[3])

    def store_dilated(unit, tap, value):
        grad_dilated[unit * KERNEL + tap] = value

    def store_point(unit, value):
        grad_point[unit] = value

    for unit in (2, 1, 0):
        backward_unit(
            unit, grad, streams.at[unit], ids_ref, (dilated, pointwise), scratch, length,
            store_dilated, store_point,
        )
        for owner in range(seq):
            mover.store(0, owner, unit * KERNEL, KERNEL).start()
    for owner in range(seq):
        mover.store(1, owner, 0, 3).start()
    frames_grad_ref[...] = grad[first:last, :]
    finish_stores(mover, seq)


def side_scratch(seq, share, length, channels, hidden):
    bf, f32 = jnp.bfloat16, jnp.float32
    group_rows = GROUPS * hidden // seq
    mats = [
        pltpu.VMEM((3 * KERNEL, channels, hidden), bf),
        pltpu.VMEM((3, channels, hidden), bf),
        pltpu.VMEM((1, seq * group_rows, hidden), bf),
        pltpu.VMEM((2 * STRIDE, channels, hidden), bf),
    ]
    return mats + list(mats) + [
        pltpu.VMEM((4, length, channels), f32),
        pltpu.VMEM((length, channels), f32),
        pltpu.VMEM((length + 2 * margin, channels), f32),
        pltpu.VMEM((length, KERNEL * channels), bf),
        pltpu.VMEM((3, length, hidden), f32),
        pltpu.VMEM((3, length, hidden), bf),
        pltpu.VMEM((3, length // 2, channels), bf),
        pltpu.VMEM((channels // lanes, length, lanes), f32),
        pltpu.SemaphoreType.DMA((8, seq)),
    ]


narrow = (0, 1, 3, 4, 6, 7)
wide_ones = (2, 5)


def per_device(
    frames,
    cotangent,
    segment_ids,
    code_index,
    codebooks,
    dead_codes,
    code_slots,
    buffered,
    encoder_dilated,
    encoder_pointwise,
    down_weight,
    group_in,
    group_out,
    up_weight,
    decoder_dilated,
    decoder_pointwise,
    encoder_dilated_moment,
    encoder_pointwise_moment,
    down_moment,
    group_in_moment,
    group_out_moment,
    up_moment,
    decoder_dilated_moment,
    decoder_pointwise_moment,
):
    masters = (
        encoder_dilated,
        encoder_pointwise,
        down_weight,
        group_in,
        group_out,
        up_weight,
        decoder_dilated,
        decoder_pointwise,
    )
    olds = (
        encoder_dilated_moment,
        encoder_pointwise_moment,
        down_moment,
        group_in_moment,
        group_out_moment,
        up_moment,
        decoder_dilated_moment,
        decoder_pointwise_moment,
    )
    lowered = [weight.astype(jnp.bfloat16) for weight in masters]
    count = lax.axis_size("seq")
    sizes = line_sizes(count, lax.axis_size("dp"))
    sides = ((0, 1, 3, 2), (6, 7, 4, 5))
    packed = []
    for side in sides:
        parts = [lowered[i] for i in side[:3]] + [halves(lowered[side[3]])]
        packed.append(pack_side(*parts, sizes[1], 0))
    side_rows = packed[0].shape[0]
    reach = frames.shape[1] // 2
    near = 80
    latent_reach = reach // STRIDE * GROUPS * LEVELS
    code_row = code_index.reshape(-1)
    number_edges = jnp.zeros((2, 8, lanes), jnp.int32)
    number_edges = number_edges.at[0, 0, :reach].set(segment_ids[0, reach:])
    number_edges = number_edges.at[1, 0, :reach].set(segment_ids[0, :reach])
    number_edges = number_edges.at[0, 1, :latent_reach].set(code_row[latent_reach:])
    number_edges = number_edges.at[1, 1, :latent_reach].set(code_row[:latent_reach])
    gathered, (frame_edges, cot_edges, numbers) = gather_rows(
        jnp.concatenate(packed),
        (
            jnp.stack([frames[0, reach:], frames[0, :reach]]),
            jnp.stack([cotangent[0, -near:], cotangent[0, :near]]),
            number_edges,
        ),
        sizes,
        0,
    )
    part_shapes = []
    for side in sides:
        shapes = [masters[i].shape for i in side[:3]]
        taps, share, width = masters[side[3]].shape
        shapes.append((2, taps, share, width // 2))
        part_shapes.append(shapes)
    row_count, length, channels = frames.shape
    long = 2 * length
    latent_len = long // STRIDE
    reach = length // 2
    near = 80
    place_seq = lax.axis_index("seq")
    hidden = encoder_dilated.shape[-1]
    share = masters[0].shape[2]
    blocks = side_rows // share
    geometry = (count, share, blocks)
    gathered = gathered.reshape(count, 2 * blocks, share, hidden)
    no_match = jnp.full((margin,), -1, jnp.int32)
    ids_left = jnp.where(place_seq == 0, -1, numbers[0, 0])
    ids_right = jnp.where(place_seq == count - 1, -1, numbers[1, 0])
    ids = jnp.concatenate([no_match, ids_left, segment_ids[0], ids_right, no_match])
    ids = jnp.broadcast_to(ids[:, None], (long + 2 * margin, lanes))
    half_codes = reach // STRIDE
    codes = jnp.concatenate(
        [
            numbers[0, 1, : half_codes * 4].reshape(half_codes, 4),
            code_index[0].reshape(-1, 4),
            numbers[1, 1, : half_codes * 4].reshape(half_codes, 4),
        ]
    )
    frames_long = jnp.concatenate([frame_edges[0], frames[0], frame_edges[1]])
    blank = jnp.zeros((reach - near, channels), jnp.float32)
    cot_long = jnp.concatenate([blank, cot_edges[0], cotangent[0], cot_edges[1], blank])
    vmem = pl.BlockSpec(memory_space=pltpu.VMEM)
    anywhere = pl.BlockSpec(memory_space=pl.ANY)
    params = pltpu.CompilerParams(vmem_limit_bytes=60 * 2**20)
    packed_type = jax.ShapeDtypeStruct(gathered.shape, jnp.bfloat16)
    scratch = side_scratch(count, share, long, channels, hidden)
    decoded, grad_quant, picks, partial = pl.pallas_call(
        functools.partial(decoder_kernel, geometry, long),
        out_shape=(
            jax.ShapeDtypeStruct((length, channels), jnp.bfloat16),
            jax.ShapeDtypeStruct((GROUPS, latent_len, hidden), jnp.float32),
            jax.ShapeDtypeStruct((GROUPS * LEVELS, latent_len, hidden), jnp.float32),
            packed_type,
        ),
        in_specs=[vmem, vmem, vmem, vmem, anywhere],
        out_specs=(vmem, vmem, vmem, anywhere),
        scratch_shapes=scratch,
        compiler_params=params,
    )(codes, ids, cot_long, codebooks, gathered)
    grad, latent_rows, partial = pl.pallas_call(
        functools.partial(encoder_kernel, geometry, long),
        out_shape=(
            jax.ShapeDtypeStruct((length, channels), jnp.float32),
            jax.ShapeDtypeStruct((length // STRIDE, GROUPS * LEVELS * hidden), jnp.bfloat16),
            packed_type,
        ),
        in_specs=[vmem, vmem, vmem, vmem, anywhere, anywhere],
        out_specs=(vmem, vmem, anywhere),
        scratch_shapes=scratch,
        input_output_aliases={5: 2},
        compiler_params=params,
    )(frames_long, ids, grad_quant, picks, gathered, partial)
    decoded = decoded[None]
    grad = grad[None]
    own_codes_low = code_index[0].reshape(-1, GROUPS * LEVELS)
    digits = jnp.concatenate([own_codes_low // 32, own_codes_low % 32], axis=1)
    digits = jnp.pad(digits, ((0, 0), (0, lanes - digits.shape[1]))).astype(jnp.bfloat16)
    share_rows, all_rows = reduce_rows(
        partial.reshape(count, 2 * side_rows, hidden),
        jnp.concatenate([latent_rows, digits], axis=1),
        sizes,
        1,
    )
    all_rows = all_rows.reshape(-1, all_rows.shape[-1])
    group_width = hidden
    digits = all_rows[:, GROUPS * LEVELS * hidden :].astype(jnp.int32)
    all_codes = digits[:, :4] * 32 + digits[:, 4:8]
    code_share = dead_codes.shape[2]
    own_range = lax.broadcasted_iota(
        jnp.int32, (1, code_share), 1
    ) + code_share * place_seq
    sum_list = []
    count_list = []
    for entry in range(GROUPS * LEVELS):
        own_hot = (all_codes[:, entry : entry + 1] == own_range).astype(jnp.bfloat16)
        sum_list.append(
            lax.dot_general(
                own_hot,
                all_rows[:, entry * group_width : (entry + 1) * group_width],
                (((0,), (0,)), ((), ())),
                preferred_element_type=jnp.float32,
            )
        )
        count_list.append(jnp.sum(own_hot.astype(jnp.float32), axis=0))
    total_sums = jnp.stack(sum_list).reshape(GROUPS, LEVELS, code_share, group_width)
    total_counts = jnp.stack(count_list).reshape(GROUPS, LEVELS, code_share)
    reduced = [None] * 8
    for at, side in enumerate(sides):
        parts = take_side(share_rows[at * side_rows : (at + 1) * side_rows], part_shapes[at])
        for i, part in zip(side[:3], parts):
            reduced[i] = part.astype(jnp.float32)
        reduced[side[3]] = jnp.concatenate([parts[3][0], parts[3][1]], axis=-1).astype(jnp.float32)
    own_codes = lax.dynamic_slice_in_dim(
        codebooks, lax.axis_index("seq") * code_share, code_share, 2
    )
    code_means = total_sums / jnp.maximum(total_counts, 1.0)[..., None]
    code_used = jnp.minimum(total_counts, 1.0)[..., None]
    updated = own_codes + code_rate * code_used * (code_means - own_codes)
    slot_range = lax.broadcasted_iota(jnp.int32, (1, 1, 1, buffered.shape[1]), 3)
    slot_onehot = (code_slots[..., None] == slot_range).astype(jnp.float32)
    replaced = jnp.einsum("glsb,gbz->glsz", slot_onehot, buffered, precision=highest)
    new_codebooks = jnp.where(dead_codes[..., None] == 1, replaced, updated)
    velocities = tuple((moment_decay * olds[position] + reduced[position] for position in range(8)))
    views = tuple(
        (
            velocities[position].reshape(
                velocities[position].shape[0] if stacked_flags[position] else 1,
                -1,
                velocities[position].shape[-1],
            )
            for position in range(8)
        )
    )
    current = [None] * 8
    for members in (narrow, wide_ones):
        grams = lax.psum(
            jnp.concatenate(
                [
                    jnp.einsum("nrc,nrd->ncd", views[i], views[i], precision=highest)
                    for i in members
                ]
            ),
            "seq",
        )
        mixing = solve_mixing(grams)
        start = 0
        for i in members:
            stop = start + views[i].shape[0]
            current[i] = jnp.einsum(
                "nrc,ncd->nrd", views[i], mixing[start:stop], precision=highest
            )
            start = stop
    shaped = tuple((current[position].reshape(masters[position].shape) for position in range(8)))
    nexts = tuple((masters[position] - update_rate * shaped[position] for position in range(8)))
    return (
        decoded,
        grad,
        new_codebooks,
        velocities[0],
        velocities[1],
        velocities[2],
        velocities[3],
        velocities[4],
        velocities[5],
        velocities[6],
        velocities[7],
        nexts[0],
        nexts[1],
        nexts[2],
        nexts[3],
        nexts[4],
        nexts[5],
        nexts[6],
        nexts[7],
    )


def solution(mesh):
    in_specs = (
        P("dp", "seq", None),
        P("dp", "seq", None),
        P("dp", "seq"),
        P("dp", "seq", None, None),
        P(),
        P(None, None, "seq"),
        P(None, None, "seq"),
        P(),
        P(None, None, "seq", None),
        P(None, "seq", None),
        P(None, "seq", None),
        P(None, "seq", None),
        P(None, "seq", None),
        P(None, "seq", None),
        P(None, None, "seq", None),
        P(None, "seq", None),
        P(None, None, "seq", None),
        P(None, "seq", None),
        P(None, "seq", None),
        P(None, "seq", None),
        P(None, "seq", None),
        P(None, "seq", None),
        P(None, None, "seq", None),
        P(None, "seq", None),
    )
    out_specs = (
        P("dp", "seq", None),
        P("dp", "seq", None),
        P(None, None, "seq", None),
        P(None, None, "seq", None),
        P(None, "seq", None),
        P(None, "seq", None),
        P(None, "seq", None),
        P(None, "seq", None),
        P(None, "seq", None),
        P(None, None, "seq", None),
        P(None, "seq", None),
        P(None, None, "seq", None),
        P(None, "seq", None),
        P(None, "seq", None),
        P(None, "seq", None),
        P(None, "seq", None),
        P(None, "seq", None),
        P(None, None, "seq", None),
        P(None, "seq", None),
    )
    return jax.shard_map(
        per_device, mesh=mesh, in_specs=in_specs, out_specs=out_specs, check_vma=False
    )
```

```python
import functools

import jax
import jax.numpy as jnp
from jax import lax
from jax.experimental import pallas as pl
from jax.experimental.pallas import tpu as pltpu
from jax.sharding import PartitionSpec as P

GROUPS = 2
LEVELS = 2
KERNEL = 7
STRIDE = 8
NS_STEPS = 5


highest = lax.Precision.HIGHEST
dilation_list = (1, 3, 9)
coef_first = 3.4445
coef_second = -4.775
coef_third = 2.0315
commit_weight = 0.25
moment_decay = 0.5
update_rate = 0.5
code_rate = 0.5
norm_floor = 1e-07


def halves(array):
    width = array.shape[-1] // 2
    split = array.reshape(array.shape[:-1] + (2, width))
    return jnp.moveaxis(split, -2, 0)


def whole_rows(rows, high):
    unit = 32 * high
    return -(-rows // unit) * unit


def pack_side(dilated, pointwise, group, strided, high, lead):
    parts = [dilated, pointwise, group, strided]
    kept = dilated.shape[:lead]
    flat = [part.reshape(kept + (-1, part.shape[-1])) for part in parts]
    rows = sum(part.shape[lead] for part in flat)
    extra = whole_rows(rows, high) - rows
    if extra:
        flat.append(jnp.zeros(kept + (extra, flat[0].shape[-1]), flat[0].dtype))
    return jnp.concatenate(flat, axis=lead)


def take_side(rows, shapes):
    found = []
    start = 0
    for shape in shapes:
        size = 1
        for extent in shape[:-1]:
            size *= extent
        found.append(rows[..., start : start + size, :].reshape(rows.shape[:-2] + shape))
        start += size
    return found


MESH = pl.DeviceIdType.MESH


def line_sizes(seq, dp):
    across = 1
    while (2 * across) * (2 * across) <= seq:
        across *= 2
    return across, dp // 2, seq // across


def place(sizes):
    wide, high, _ = sizes
    row = lax.axis_index("dp")
    part = lax.axis_index("seq")
    return part % wide, row // 2, part // wide, row % 2


def greet(sizes):
    wide, high, deep = sizes
    x, y, z, c = place(sizes)
    barrier = pltpu.get_barrier_semaphore()
    others = [(y * 2 + 1 - c, z * wide + x)]
    others += [(y * 2 + c, z * wide + (x + k) % wide) for k in range(1, wide)]
    others += [((y + k) % high * 2 + c, z * wide + x) for k in range(1, high)]
    others += [(y * 2 + c, (z + k) % deep * wide + x) for k in range(1, deep)]
    count = deep * wide
    others += [(y * 2 + c, (z * wide + x + k) % count) for k in (1, count - 1)]
    for other in others:
        pl.semaphore_signal(barrier, inc=1, device_id=other, device_id_type=MESH)
    pl.semaphore_wait(barrier, len(others))


def gather_kernel(sizes, edges, *refs):
    in_ref, edge_in = refs[0], refs[1 : 1 + edges]
    out_ref, edge_out = refs[1 + edges], refs[2 + edges : 2 + 2 * edges]
    send_sem, recv_sem, local_sem, edge_sem = refs[2 + 2 * edges :]
    wide, high, deep = sizes
    x, y, z, c = place(sizes)
    greet(sizes)
    own = pltpu.make_async_copy(in_ref, out_ref.at[z, x], local_sem)
    own.start()
    sent = []
    count = deep * wide
    side_copies = []
    for number in range(edges):
        for way in range(2):
            other = (z * wide + x + (1 if way == 0 else count - 1)) % count
            copy = pltpu.make_async_remote_copy(
                src_ref=edge_in[number].at[way],
                dst_ref=edge_out[number].at[way],
                send_sem=edge_sem.at[0, number, way],
                recv_sem=edge_sem.at[1, number, way],
                device_id=(y * 2 + c, other),
                device_id_type=MESH,
            )
            copy.start()
            side_copies.append(copy)

    def send(zs, xs, ys, h, to, source=None):
        spot = out_ref.at[zs, xs, c, ys, h]
        copy = pltpu.make_async_remote_copy(
            src_ref=spot if source is None else source,
            dst_ref=spot,
            send_sem=send_sem.at[len(sent)],
            recv_sem=recv_sem.at[zs, xs, c, ys, h],
            device_id=to,
            device_id_type=MESH,
        )
        copy.start()
        sent.append(copy)

    def arrive(zs, xs, cs, ys, h):
        spot = out_ref.at[zs, xs, cs, ys, h]
        pltpu.make_async_remote_copy(
            src_ref=spot,
            dst_ref=spot,
            send_sem=send_sem.at[0],
            recv_sem=recv_sem.at[zs, xs, cs, ys, h],
            device_id=(y * 2 + 1 - c, z * wide + x),
            device_id_type=MESH,
        ).wait_recv()

    def to_x(zs, xs, ys, h, source=None):
        for k in range(1, wide):
            send(zs, xs, ys, h, (y * 2 + c, z * wide + (x + k) % wide), source)

    def to_y(zs, xs, ys, h):
        for k in range(1, high):
            send(zs, xs, ys, h, ((y + k) % high * 2 + c, z * wide + x))

    def to_core(zs, xs, ys, h):
        send(zs, xs, ys, h, (y * 2 + 1 - c, z * wide + x))

    for k in range(deep - 1, 0, -1):
        for h in range(2):
            send(z, x, y, h, (y * 2 + c, (z + k) % deep * wide + x), in_ref.at[c, y, h])
    to_x(z, x, y, 0, in_ref.at[c, y, 0])
    for j in range(high):
        ys = (y + j) % high
        to_x(z, x, ys, 1, in_ref.at[c, ys, 1])
    for k in range(1, deep):
        zs = (z + k) % deep
        arrive(zs, x, c, y, 0)
        to_x(zs, x, y, 0)
        to_y(zs, x, y, 0)
        to_core(zs, x, y, 0)
        arrive(zs, x, c, y, 1)
        to_y(zs, x, y, 1)
        to_x(zs, x, y, 1)
        to_core(zs, x, y, 1)
    for k in range(deep):
        zs = (z + k) % deep
        for i in range(1, wide):
            xs = (x + i) % wide
            arrive(zs, xs, c, y, 0)
            to_y(zs, xs, y, 0)
            to_core(zs, xs, y, 0)
        if k > 0:
            for j in range(1, high):
                ys = (y + j) % high
                arrive(zs, x, c, ys, 1)
                to_x(zs, x, ys, 1)
                to_core(zs, x, ys, 1)
    for k in range(deep):
        zs = (z + k) % deep
        for i in range(wide):
            xs = (x + i) % wide
            if k == 0 and i == 0:
                continue
            for j in range(1, high):
                ys = (y + j) % high
                arrive(zs, xs, c, ys, 0)
                to_core(zs, xs, ys, 0)
            if i > 0:
                for j in range(high):
                    ys = (y + j) % high
                    arrive(zs, xs, c, ys, 1)
                    to_core(zs, xs, ys, 1)
    for k in range(deep):
        zs = (z + k) % deep
        for i in range(wide):
            xs = (x + i) % wide
            if k == 0 and i == 0:
                continue
            for j in range(high):
                for h in range(2):
                    arrive(zs, xs, 1 - c, (y + j) % high, h)
    for copy in sent:
        copy.wait_send()
    for copy in side_copies:
        copy.wait()
    own.wait()


def gather_sends(sizes):
    wide, high, deep = sizes
    n = (deep - 1) * 2 + (wide - 1) * (1 + high)
    n += (deep - 1) * 2 * (wide - 1 + high - 1 + 1)
    n += deep * (wide - 1) * high + (deep - 1) * (high - 1) * wide
    n += (deep * wide - 1) * (high - 1) + deep * (wide - 1) * high
    return n


def gather_rows(shard, edges, sizes, collective_id):
    wide, high, deep = sizes
    total, width = shard.shape
    rows = total // (4 * high)
    block = shard.reshape(2, high, 2, rows, width)
    out = pl.pallas_call(
        functools.partial(gather_kernel, sizes, len(edges)),
        out_shape=[jax.ShapeDtypeStruct((deep, wide) + block.shape, block.dtype)]
        + [jax.ShapeDtypeStruct(edge.shape, edge.dtype) for edge in edges],
        in_specs=[pl.BlockSpec(memory_space=pl.ANY)] * (1 + len(edges)),
        out_specs=[pl.BlockSpec(memory_space=pl.ANY)] * (1 + len(edges)),
        scratch_shapes=[
            pltpu.SemaphoreType.DMA((gather_sends(sizes),)),
            pltpu.SemaphoreType.DMA((deep, wide, 2, high, 2)),
            pltpu.SemaphoreType.DMA,
            pltpu.SemaphoreType.DMA((2, len(edges), 2)),
        ],
        compiler_params=pltpu.CompilerParams(collective_id=collective_id, has_side_effects=True),
    )(block, *edges)
    return out[0].reshape(deep * wide, total, width), out[1:]


def reduce_kernel(
    sizes,
    in_ref,
    row_ref,
    out_ref,
    all_ref,
    held,
    from_core,
    from_x_a,
    from_y_b,
    from_y_a,
    from_x_b,
    from_z,
    final,
    send_sem,
    local_sem,
    core_sem,
    xa_sem,
    yb_sem,
    ya_sem,
    xb_sem,
    z_sem,
    done_sem,
    row_sem,
):
    wide, high, deep = sizes
    x, y, z, c = place(sizes)
    greet(sizes)
    partner = (y * 2 + 1 - c, z * wide + x)
    sent = []

    def send(src, dst, recv, to):
        copy = pltpu.make_async_remote_copy(
            src_ref=src,
            dst_ref=dst,
            send_sem=send_sem.at[len(sent)],
            recv_sem=recv,
            device_id=to,
            device_id_type=MESH,
        )
        copy.start()
        sent.append(copy)
        return copy

    def arrive(dst, recv):
        pltpu.make_async_remote_copy(
            src_ref=dst,
            dst_ref=dst,
            send_sem=send_sem.at[0],
            recv_sem=recv,
            device_id=partner,
            device_id_type=MESH,
        ).wait_recv()

    keep = pltpu.make_async_copy(row_ref, all_ref.at[z, x, y, c], local_sem.at[deep + 1])
    keep.start()

    def spread(stage):
        columns = [(z + k) % deep for k in range(deep)]
        lines = [(x + k) % wide for k in range(wide)]
        heights = [(y + k) % high for k in range(high)]

        def pass_on(zs, xs, ys, to, source=None):
            spot = all_ref.at[zs, xs, ys, c]
            send(spot if source is None else source, spot, row_sem.at[zs, xs, ys, c], to)

        def landed(zs, xs, ys, cs):
            arrive(all_ref.at[zs, xs, ys, cs], row_sem.at[zs, xs, ys, cs])

        if stage == 0:
            for zt in columns[1:]:
                pass_on(z, x, y, (y * 2 + c, zt * wide + x), row_ref)
        if stage == 1:
            for zs in columns[1:]:
                landed(zs, x, y, c)
            for zs in columns:
                for xt in lines[1:]:
                    pass_on(zs, x, y, (y * 2 + c, z * wide + xt), row_ref if zs is columns[0] else None)
        if stage == 2:
            for zs in columns:
                for xs in lines[1:]:
                    landed(zs, xs, y, c)
            for zs in columns:
                for xs in lines:
                    mine = zs is columns[0] and xs is lines[0]
                    for yt in heights[1:]:
                        pass_on(zs, xs, y, (yt * 2 + c, z * wide + x), row_ref if mine else None)
        if stage == 3:
            for zs in columns:
                for xs in lines:
                    for ys in heights[1:]:
                        landed(zs, xs, ys, c)
            for zs in columns:
                for xs in lines:
                    for ys in heights:
                        mine = zs is columns[0] and xs is lines[0] and ys is heights[0]
                        pass_on(zs, xs, ys, partner, row_ref if mine else None)
        if stage == 4:
            for zs in columns:
                for xs in lines:
                    for ys in heights:
                        landed(zs, xs, ys, 1 - c)

    def merge(target, extras):
        total = target[...].astype(jnp.float32)
        for extra in extras:
            total = total + extra[...].astype(jnp.float32)
        target[...] = total.astype(target.dtype)

    order = [(z + k) % deep for k in range(deep // 2, deep)] + [
        (z + k) % deep for k in range(deep // 2 - 1, 0, -1)
    ] + [z]
    local = []
    for step, zt in enumerate(order):
        copy = pltpu.make_async_copy(in_ref.at[zt, :, c], held.at[step], local_sem.at[step])
        copy.start()
        local.append(copy)
        send(in_ref.at[zt, :, 1 - c], from_core.at[step], core_sem.at[step], partner)

    def first(step):
        local[step].wait()
        arrive(from_core.at[step], core_sem.at[step])

        def body(i, carry):
            xi, yi, hi = i // (2 * high), i // 2 % high, i % 2
            merge(held.at[step, xi, yi, hi], [from_core.at[step, xi, yi, hi]])
            return carry

        lax.fori_loop(0, wide * high * 2, body, 0)
        for k in range(1, wide):
            xt = (x + k) % wide
            send(
                held.at[step, xt, :, 0],
                from_x_a.at[k - 1, step],
                xa_sem.at[k - 1, step],
                (y * 2 + c, z * wide + xt),
            )
        for k in range(1, high):
            yt = (y + k) % high
            send(
                held.at[step, :, yt, 1],
                from_y_b.at[k - 1, step],
                yb_sem.at[k - 1, step],
                (yt * 2 + c, z * wide + x),
            )

    def second(step):
        for k in range(1, wide):
            arrive(from_x_a.at[k - 1, step], xa_sem.at[k - 1, step])

        def body_a(i, carry):
            yt = (y + 1 + i) % high
            merge(held.at[step, x, yt, 0], [from_x_a.at[k, step, yt] for k in range(wide - 1)])
            return carry

        lax.fori_loop(0, high, body_a, 0)
        for k in range(1, high):
            yt = (y + k) % high
            send(
                held.at[step, x, yt, 0],
                from_y_a.at[k - 1, step],
                ya_sem.at[k - 1, step],
                (yt * 2 + c, z * wide + x),
            )
        for k in range(1, high):
            arrive(from_y_b.at[k - 1, step], yb_sem.at[k - 1, step])

        def body_b(i, carry):
            xt = (x + 1 + i) % wide
            merge(held.at[step, xt, y, 1], [from_y_b.at[k, step, xt] for k in range(high - 1)])
            return carry

        lax.fori_loop(0, wide, body_b, 0)
        for k in range(1, wide):
            xt = (x + k) % wide
            send(
                held.at[step, xt, y, 1],
                from_x_b.at[k - 1, step],
                xb_sem.at[k - 1, step],
                (y * 2 + c, z * wide + xt),
            )

    def third(step):
        for k in range(1, high):
            arrive(from_y_a.at[k - 1, step], ya_sem.at[k - 1, step])
        merge(held.at[step, x, y, 0], [from_y_a.at[k, step] for k in range(high - 1)])
        for k in range(1, wide):
            arrive(from_x_b.at[k - 1, step], xb_sem.at[k - 1, step])
        merge(held.at[step, x, y, 1], [from_x_b.at[k, step] for k in range(wide - 1)])
        if step < deep - 1:
            send(
                held.at[step, x, y],
                from_z.at[step],
                z_sem.at[step],
                (y * 2 + c, order[step] * wide + x),
            )

    spread(0)
    for turn in range(deep + 2):
        if turn < deep:
            first(turn)
        if turn in (1, 2, 3):
            spread(turn)
        if 0 <= turn - 1 < deep:
            second(turn - 1)
        if 0 <= turn - 2 < deep:
            third(turn - 2)
    spread(4)
    keep.wait()
    for step in range(deep - 1):
        arrive(from_z.at[step], z_sem.at[step])
    for h in range(2):
        total = held[deep - 1, x, y, h].astype(jnp.float32)
        for step in range(deep - 1):
            total = total + from_z[step, h].astype(jnp.float32)
        final[h] = total.astype(final.dtype)
    own = pltpu.make_async_copy(final, out_ref.at[c, y], local_sem.at[deep])
    own.start()
    for k in range(1, high):
        send(final, out_ref.at[c, y], done_sem.at[c, y], ((y + k) % high * 2 + c, z * wide + x))
    send(final, out_ref.at[c, y], done_sem.at[c, y], partner)
    for k in range(1, high):
        yt = (y + k) % high
        arrive(out_ref.at[c, yt], done_sem.at[c, yt])
        send(out_ref.at[c, yt], out_ref.at[c, yt], done_sem.at[c, yt], partner)
    for k in range(high):
        yt = (y + k) % high
        arrive(out_ref.at[1 - c, yt], done_sem.at[1 - c, yt])
    for copy in sent:
        copy.wait_send()
    own.wait()


def reduce_rows(partial, rows_own, sizes, collective_id):
    wide, high, deep = sizes
    _, total, width = partial.shape
    rows = total // (4 * high)
    kind = partial.dtype
    block = partial.reshape(deep, wide, 2, high, 2, rows, width)
    tail = (rows, width)
    dma = pltpu.SemaphoreType.DMA
    sends = deep + deep * 2 * (wide - 1 + high - 1) + deep - 1 + 2 * (high - 1) + 1
    sends += deep - 1 + deep * (wide - 1) + deep * wide * (high - 1) + deep * wide * high
    out = pl.pallas_call(
        functools.partial(reduce_kernel, sizes),
        out_shape=(
            jax.ShapeDtypeStruct((2, high, 2, rows, width), kind),
            jax.ShapeDtypeStruct((deep, wide, high, 2) + rows_own.shape, rows_own.dtype),
        ),
        in_specs=[pl.BlockSpec(memory_space=pl.ANY)] * 2,
        out_specs=(pl.BlockSpec(memory_space=pl.ANY),) * 2,
        scratch_shapes=[
            pltpu.VMEM((deep, wide, high, 2) + tail, kind),
            pltpu.VMEM((deep, wide, high, 2) + tail, kind),
            pltpu.VMEM((wide - 1, deep, high) + tail, kind),
            pltpu.VMEM((high - 1, deep, wide) + tail, kind),
            pltpu.VMEM((high - 1, deep) + tail, kind),
            pltpu.VMEM((wide - 1, deep) + tail, kind),
            pltpu.VMEM((deep - 1, 2) + tail, kind),
            pltpu.VMEM((2,) + tail, kind),
            dma((sends,)),
            dma((deep + 2,)),
            dma((deep,)),
            dma((wide - 1, deep)),
            dma((high - 1, deep)),
            dma((high - 1, deep)),
            dma((wide - 1, deep)),
            dma((deep - 1,)),
            dma((2, high)),
            dma((deep, wide, high, 2)),
        ],
        compiler_params=pltpu.CompilerParams(
            collective_id=collective_id, has_side_effects=True, vmem_limit_bytes=60 * 2**20
        ),
    )(block, rows_own)
    return out[0].reshape(total, width), out[1].reshape((-1,) + rows_own.shape)


margin = 32
lanes = 128


def elu_slope(values):
    return jnp.where(values > 0, 1.0, jnp.exp(jnp.minimum(values, 0.0)))


def elu(values):
    return jnp.where(values > 0, values, jnp.exp(jnp.minimum(values, 0.0)) - 1.0)


def dot(left, right):
    return jnp.dot(left, right, preferred_element_type=jnp.float32)


def dot_last(left, right):
    return lax.dot_general(
        left, right, (((1,), (1,)), ((), ())), preferred_element_type=jnp.float32
    )


def dot_rows(left, right):
    return lax.dot_general(
        left, right, (((0,), (0,)), ((), ())), preferred_element_type=jnp.float32
    )


def spread_taps(target, source, ids, width, sign, dilation, length):
    block = 64

    def body(step, carry):
        base = pl.multiple_of(step * block, block)
        window = ids[pl.ds(base, block + 2 * margin), :]
        own = window[margin : margin + block]
        for tap in range(KERNEL):
            start = margin + sign * (tap - KERNEL // 2) * dilation
            match = window[start : start + block] == own
            for piece in range(width // lanes):
                columns = slice(piece * lanes, (piece + 1) * lanes)
                values = source[pl.ds(base, block + 2 * margin), columns][start : start + block]
                spot = tap * width + piece * lanes
                target[pl.ds(base, block), spot : spot + lanes] = jnp.where(
                    match, values, 0.0
                ).astype(jnp.bfloat16)
        return carry

    lax.fori_loop(0, length // block, body, 0)


def forward_unit(unit, stream, follow, ids, weights, scratch, length):
    dilated, pointwise = weights
    padded, columns, hidden, excited, active = scratch
    channels = stream.shape[1]
    values = elu(stream[...])
    padded[margin : margin + length, :] = values
    active[unit] = values[length // 4 : 3 * length // 4].astype(jnp.bfloat16)
    spread_taps(columns, padded, ids, channels, 1, dilation_list[unit], length)
    kernel = dilated[unit * KERNEL : (unit + 1) * KERNEL].reshape(KERNEL * channels, -1)
    value = dot(columns[...], kernel)
    hidden[unit] = value
    lifted = elu(value).astype(jnp.bfloat16)
    excited[unit] = lifted
    follow[...] = stream[...] + dot_last(lifted, pointwise[unit])


def backward_unit(unit, grad, stream, ids, weights, scratch, length, store_dilated, store_point):
    dilated, pointwise = weights
    padded, columns, hidden, excited, active = scratch
    width = hidden.shape[2]
    first, last = length // 4, 3 * length // 4
    low = grad[...].astype(jnp.bfloat16)
    store_point(
        unit,
        dot(grad[first:last, :].T.astype(jnp.bfloat16), excited[unit, first:last, :]).astype(
            jnp.bfloat16
        ),
    )
    grad_hidden = dot(low, pointwise[unit]) * elu_slope(hidden[unit])
    padded[margin : margin + length, :width] = grad_hidden.astype(jnp.bfloat16).astype(jnp.float32)
    spread_taps(columns, padded, ids, width, -1, dilation_list[unit], length)
    turned = active[unit].astype(jnp.float32).T.astype(jnp.bfloat16)
    total = None
    for tap in range(KERNEL):
        piece = slice(tap * width, (tap + 1) * width)
        part = dot_last(columns[:, piece], dilated[unit * KERNEL + tap])
        total = part if total is None else total + part
        store_dilated(unit, tap, dot(turned, columns[first:last, piece]).astype(jnp.bfloat16))
    grad[...] = grad[...] + total * elu_slope(stream[...])


class Mover:
    def __init__(self, side, geometry, gathered, packed, weights, grads, sems):
        self.seq, self.share, self.blocks = geometry
        self.base = side * self.blocks
        self.gathered, self.packed = gathered, packed
        self.weights, self.grads = weights, grads
        self.sems = sems

    def block_start(self, kind):
        return self.base + (0, 3 * KERNEL, 3 * KERNEL + 3, 3 * KERNEL + 4)[kind]

    def load(self, kind, owner):
        rows = self.weights[kind]
        start = self.block_start(kind)
        source = self.gathered.at[owner, pl.ds(start, rows.shape[0])]
        target = rows.at[:, pl.ds(owner * self.share, self.share)]
        return pltpu.make_async_copy(source, target, self.sems.at[kind, owner])

    def start_loads(self, kind):
        for owner in range(self.seq):
            self.load(kind, owner).start()

    def wait_loads(self, kind):
        for owner in range(self.seq):
            self.load(kind, owner).wait()

    def store(self, kind, owner, first, size):
        rows = self.grads[kind]
        start = self.block_start(kind) + first
        source = rows.at[first : first + size, pl.ds(owner * self.share, self.share)]
        target = self.packed.at[owner, pl.ds(start, size)]
        return pltpu.make_async_copy(source, target, self.sems.at[4 + kind, owner])


def load_group(rows, seq, share):
    width = rows.shape[-1]
    part = width // seq
    value = rows.astype(jnp.float32).reshape(seq, GROUPS, part, width)
    return [value[:, g].reshape(width, width).astype(jnp.bfloat16) for g in range(GROUPS)]


def store_group(grads, seq, share):
    width = grads[0].shape[-1]
    part = width // seq
    value = jnp.stack([grad.reshape(seq, part, width) for grad in grads], axis=1)
    return value.reshape(seq, GROUPS * part, width).astype(jnp.bfloat16)


def put_tap(tiles, tap, value):
    latents = value.shape[0]
    for piece in range(tiles.shape[0]):
        tiles[piece, pl.ds(tap, latents, stride=STRIDE), :] = value[
            :, piece * lanes : (piece + 1) * lanes
        ]


def take_tap(tiles, tap, latents):
    return jnp.concatenate(
        [tiles[piece, pl.ds(tap, latents, stride=STRIDE), :] for piece in range(tiles.shape[0])],
        axis=1,
    )


def to_tiles(tiles, value):
    for piece in range(tiles.shape[0]):
        tiles[piece] = value[:, piece * lanes : (piece + 1) * lanes]


def from_tiles(tiles):
    return jnp.concatenate([tiles[piece] for piece in range(tiles.shape[0])], axis=1)


def set_edges(padded, length):
    zero = jnp.zeros((margin, padded.shape[1]), jnp.float32)
    padded[:margin, :] = zero
    padded[margin + length :, :] = zero


def decoder_kernel(
    geometry,
    length,
    code_ref,
    ids_ref,
    cot_ref,
    books_ref,
    gathered,
    decoded_ref,
    grad_quant_ref,
    picks_ref,
    packed,
    dilated,
    pointwise,
    group,
    strided,
    grad_dilated,
    grad_point,
    grad_group,
    grad_strided,
    streams,
    grad,
    padded,
    columns,
    hidden,
    excited,
    active,
    tiles,
    sems,
):
    seq, share, blocks = geometry
    weights = (dilated, pointwise, group, strided)
    grads = (grad_dilated, grad_point, grad_group, grad_strided)
    mover = Mover(1, geometry, gathered, packed, weights, grads, sems)
    for kind in (2, 3, 0, 1):
        mover.start_loads(kind)
    set_edges(padded, length)
    first, last = length // 4, 3 * length // 4
    latents = length // STRIDE
    codes = books_ref.shape[2]
    width = books_ref.shape[3]
    code_range = lax.broadcasted_iota(jnp.int32, (latents, codes), 1)
    quantized = []
    for g in range(GROUPS):
        picked = []
        for level in range(LEVELS):
            entry = g * LEVELS + level
            hot = (code_ref[:, entry : entry + 1] == code_range).astype(jnp.float32)
            pick = jnp.dot(hot, books_ref[g, level], precision=lax.Precision.HIGHEST)
            picks_ref[entry] = pick
            picked.append(pick)
        quantized.append((picked[0] + picked[1]).astype(jnp.bfloat16))
    mover.wait_loads(2)
    out_weights = load_group(group[0], seq, share)
    mixed = [dot(quantized[g], out_weights[g]) for g in range(GROUPS)]
    lifted = [elu(value).astype(jnp.bfloat16) for value in mixed]
    mover.wait_loads(3)
    for tap in range(STRIDE):
        value = dot_last(lifted[0], strided[tap]) + dot_last(lifted[1], strided[STRIDE + tap])
        put_tap(tiles, tap, value)
    streams[0] = from_tiles(tiles)
    mover.wait_loads(0)
    mover.wait_loads(1)
    scratch = (padded, columns, hidden, excited, active)
    for unit in range(3):
        forward_unit(
            unit, streams.at[unit], streams.at[unit + 1], ids_ref, (dilated, pointwise), scratch,
            length,
        )
    decoded_ref[...] = streams[3, first:last, :].astype(jnp.bfloat16)
    grad[...] = cot_ref[...]

    def store_dilated(unit, tap, value):
        grad_dilated[unit * KERNEL + tap] = value

    def store_point(unit, value):
        grad_point[unit] = value

    for unit in (2, 1, 0):
        backward_unit(
            unit, grad, streams.at[unit], ids_ref, (dilated, pointwise), scratch, length,
            store_dilated, store_point,
        )
        for owner in range(seq):
            mover.store(0, owner, unit * KERNEL, KERNEL).start()
    for owner in range(seq):
        mover.store(1, owner, 0, 3).start()
    own = slice(first // STRIDE, last // STRIDE)
    grad_lifted = [None, None]
    to_tiles(tiles, grad[...])
    for tap in range(STRIDE):
        part = take_tap(tiles, tap, latents)
        low = part.astype(jnp.bfloat16)
        turned = part[own].T.astype(jnp.bfloat16)
        for half in range(2):
            value = dot(low, strided[half * STRIDE + tap])
            grad_lifted[half] = value if tap == 0 else grad_lifted[half] + value
            grad_strided[half * STRIDE + tap] = dot(turned, lifted[half][own]).astype(jnp.bfloat16)
    for owner in range(seq):
        mover.store(3, owner, 0, 2 * STRIDE).start()
    group_grads = []
    for g in range(GROUPS):
        low = (grad_lifted[g] * elu_slope(mixed[g])).astype(jnp.bfloat16)
        group_grads.append(dot_rows(quantized[g][own], low[own]))
        grad_quant_ref[g] = dot_last(low, out_weights[g])
    grad_group[0] = store_group(group_grads, seq, share).reshape(grad_group.shape[1:])
    for owner in range(seq):
        mover.store(2, owner, 0, 1).start()
    finish_stores(mover, seq)


def finish_stores(mover, seq):
    for owner in range(seq):
        for unit in range(3):
            mover.store(0, owner, unit * KERNEL, KERNEL).wait()
        mover.store(1, owner, 0, 3).wait()
        mover.store(3, owner, 0, 2 * STRIDE).wait()
        mover.store(2, owner, 0, 1).wait()


def encoder_kernel(
    geometry,
    length,
    frames_ref,
    ids_ref,
    grad_quant_ref,
    picks_ref,
    gathered,
    unused,
    frames_grad_ref,
    rows_ref,
    packed,
    dilated,
    pointwise,
    group,
    strided,
    grad_dilated,
    grad_point,
    grad_group,
    grad_strided,
    streams,
    grad,
    padded,
    columns,
    hidden,
    excited,
    active,
    tiles,
    sems,
):
    seq, share, blocks = geometry
    weights = (dilated, pointwise, group, strided)
    grads = (grad_dilated, grad_point, grad_group, grad_strided)
    mover = Mover(0, geometry, gathered, packed, weights, grads, sems)
    for kind in (0, 1, 3, 2):
        mover.start_loads(kind)
    set_edges(padded, length)
    first, last = length // 4, 3 * length // 4
    latents = length // STRIDE
    own = slice(first // STRIDE, last // STRIDE)
    width = picks_ref.shape[2]
    streams[0] = frames_ref[...].astype(jnp.float32)
    mover.wait_loads(0)
    mover.wait_loads(1)
    scratch = (padded, columns, hidden, excited, active)
    for unit in range(3):
        forward_unit(
            unit, streams.at[unit], streams.at[unit + 1], ids_ref, (dilated, pointwise), scratch,
            length,
        )
    to_tiles(tiles, elu(streams[3]))
    mover.wait_loads(3)
    mover.wait_loads(2)
    in_weights = load_group(group[0], seq, share)
    latent = [None, None]
    for tap in range(STRIDE):
        low = take_tap(tiles, tap, latents).astype(jnp.bfloat16)
        for half in range(2):
            value = dot(low, strided[half * STRIDE + tap])
            latent[half] = value if tap == 0 else latent[half] + value
    group_grads = []
    grad_latent = []
    for g in range(GROUPS):
        low = latent[g].astype(jnp.bfloat16)
        first_part = dot(low, in_weights[g])
        pick = [picks_ref[g * LEVELS + level] for level in range(LEVELS)]
        second_part = first_part - pick[0]
        rows_ref[:, (g * LEVELS) * width : (g * LEVELS + 1) * width] = first_part[own].astype(jnp.bfloat16)
        rows_ref[:, (g * LEVELS + 1) * width : (g * LEVELS + 2) * width] = second_part[own].astype(jnp.bfloat16)
        grad_first = grad_quant_ref[g] + 2.0 * commit_weight * (
            second_part + (second_part - pick[1])
        )
        low_first = grad_first.astype(jnp.bfloat16)
        group_grads.append(dot_rows(low[own], low_first[own]))
        grad_latent.append(dot_last(low_first, in_weights[g]).astype(jnp.bfloat16))
    grad_group[0] = store_group(group_grads, seq, share).reshape(grad_group.shape[1:])
    for owner in range(seq):
        mover.store(2, owner, 0, 1).start()
    for tap in range(STRIDE):
        turned = take_tap(tiles, tap, latents)[own].T.astype(jnp.bfloat16)
        value = dot_last(grad_latent[0], strided[tap]) + dot_last(
            grad_latent[1], strided[STRIDE + tap]
        )
        put_tap(tiles, tap, value)
        for half in range(2):
            grad_strided[half * STRIDE + tap] = dot(turned, grad_latent[half][own]).astype(
                jnp.bfloat16
            )
    for owner in range(seq):
        mover.store(3, owner, 0, 2 * STRIDE).start()
    grad[...] = from_tiles(tiles) * elu_slope(streams[3])

    def store_dilated(unit, tap, value):
        grad_dilated[unit * KERNEL + tap] = value

    def store_point(unit, value):
        grad_point[unit] = value

    for unit in (2, 1, 0):
        backward_unit(
            unit, grad, streams.at[unit], ids_ref, (dilated, pointwise), scratch, length,
            store_dilated, store_point,
        )
        for owner in range(seq):
            mover.store(0, owner, unit * KERNEL, KERNEL).start()
    for owner in range(seq):
        mover.store(1, owner, 0, 3).start()
    frames_grad_ref[...] = grad[first:last, :]
    finish_stores(mover, seq)


def side_scratch(seq, share, length, channels, hidden):
    bf, f32 = jnp.bfloat16, jnp.float32
    group_rows = GROUPS * hidden // seq
    mats = [
        pltpu.VMEM((3 * KERNEL, channels, hidden), bf),
        pltpu.VMEM((3, channels, hidden), bf),
        pltpu.VMEM((1, seq * group_rows, hidden), bf),
        pltpu.VMEM((2 * STRIDE, channels, hidden), bf),
    ]
    return mats + list(mats) + [
        pltpu.VMEM((4, length, channels), f32),
        pltpu.VMEM((length, channels), f32),
        pltpu.VMEM((length + 2 * margin, channels), f32),
        pltpu.VMEM((length, KERNEL * channels), bf),
        pltpu.VMEM((3, length, hidden), f32),
        pltpu.VMEM((3, length, hidden), bf),
        pltpu.VMEM((3, length // 2, channels), bf),
        pltpu.VMEM((channels // lanes, length, lanes), f32),
        pltpu.SemaphoreType.DMA((8, seq)),
    ]


def split_terms(value, count):
    terms = []
    for number in range(count):
        term = value.astype(jnp.bfloat16)
        terms.append(term)
        if number < count - 1:
            value = value - term.astype(jnp.float32)
    return terms


def product(left, right):
    def pair(i, j):
        return jnp.dot(left[i], right[j], preferred_element_type=jnp.float32)

    low = pair(0, 1) + pair(1, 0)
    if len(left) > 2:
        low = low + (pair(1, 1) + pair(0, 2) + pair(2, 0))
    return pair(0, 0) + low


def gram_of(left, right):
    return product(split_terms(left.T, 3), split_terms(right, 3))


def solve_mixing(gram):
    size = gram.shape[0]
    eye = (
        lax.broadcasted_iota(jnp.int32, (size, size), 0)
        == lax.broadcasted_iota(jnp.int32, (size, size), 1)
    ).astype(jnp.float32)
    scale = 1.0 / (jnp.sqrt(jnp.sum(gram * eye)) + norm_floor)
    current = gram * (scale * scale)
    total = None
    for repeat in range(NS_STEPS):
        terms = 3 if repeat < 2 else 2
        parts = split_terms(current, terms)
        factor = coef_first * eye + coef_second * current + coef_third * product(parts, parts)
        factors = split_terms(factor, terms)
        if total is None:
            total = factor
        else:
            total = product(split_terms(total, 2), factors[:2])
        if repeat < NS_STEPS - 1:
            half = split_terms(product(parts, factors), terms)
            current = product(half, factors)
    return total * scale


def mixing_kernel(
    sizes,
    share,
    enc_dilated,
    enc_point,
    enc_group,
    enc_strided,
    dec_dilated,
    dec_point,
    dec_group,
    dec_strided,
    mix_ref,
    small_ref,
    dilated,
    point,
    group,
    strided,
    blocks,
    slots,
    point_all,
    group_all,
    work,
    point_done,
    group_done,
    load_sem,
    send_sem,
    slot_sem,
    rows_sem,
    mix_sem,
    small_sem,
):
    wide, high, deep = sizes
    x, y, z, c = place(sizes)
    count = wide * deep
    me = z * wide + x
    row = y * 2 + c
    middle = count // 2
    partner = (y * 2 + 1 - c, me)
    others = [(row, (me + k) % count) for k in range(1, count)]
    others += [((y + k) % high * 2 + c, me) for k in range(1, high)] + [partner]
    barrier = pltpu.get_barrier_semaphore()
    for other in others:
        pl.semaphore_signal(barrier, inc=1, device_id=other, device_id_type=MESH)
    pl.semaphore_wait(barrier, len(others))

    pending = []

    def remote(src, dst, number, recv, to):
        return pltpu.make_async_remote_copy(
            src_ref=src,
            dst_ref=dst,
            send_sem=send_sem.at[number],
            recv_sem=recv,
            device_id=to,
            device_id_type=MESH,
        )

    def send(when, src, dst, recv, to):
        number = len(pending)
        pending.append((when, src, dst, recv, to))

        @pl.when(when)
        def _():
            remote(src, dst, number, recv, to).start()

    def arrive(dst, recv):
        remote(dst, dst, 0, recv, partner).wait_recv()

    first_set = y == 0
    second_set = y == 1
    for core, sources in (
        (0, (enc_dilated, enc_point, enc_group, enc_strided)),
        (1, (dec_dilated, dec_point, dec_group, dec_strided)),
    ):
        copies = [
            pltpu.make_async_copy(source, target, load_sem.at[number])
            for number, (source, target) in enumerate(
                zip(sources, (dilated, point, group, strided))
            )
        ]

        @pl.when(first_set & (c == core))
        def _():
            copies[0].start()
            copies[0].wait()

        @pl.when(second_set & (c == core))
        def _():
            for copy in copies[1:]:
                copy.start()
            for copy in copies[1:]:
                copy.wait()

    dilated_at = [middle - 2 + unit + c for unit in range(3)]
    strided_at = middle - 1 + c
    point_at = [middle - 2, middle - c, middle + 1]
    group_at = [middle - 3, middle + 2]
    part = share // GROUPS

    for unit in range(3):
        at = point_at[unit]
        rows = pl.ds(pl.multiple_of(me * share, 8), share)
        send(
            second_set & (me != at),
            point.at[unit],
            point_all.at[rows],
            rows_sem.at[me],
            (row, at),
        )

        @pl.when(second_set & (me == at))
        def _():
            point_all[rows, :] = point[unit]

    for g in range(GROUPS):
        at = group_at[g]
        rows = pl.ds(pl.multiple_of(me * part, 8), part)
        send(
            second_set & (me != at),
            group.at[g],
            group_all.at[rows],
            rows_sem.at[me],
            (row, at),
        )

        @pl.when(second_set & (me == at))
        def _():
            group_all[rows, :] = group[g]

    block = blocks.shape[1]

    @pl.when(first_set)
    def _():
        for unit in range(3):
            value = dilated[unit * KERNEL : (unit + 1) * KERNEL].reshape(KERNEL * share, block)
            blocks[unit] = gram_of(value, value)

    @pl.when(second_set)
    def _():
        value = strided[...].reshape(-1, 2 * block)
        left, right = value[:, :block], value[:, block:]
        blocks[0] = gram_of(left, left)
        blocks[1] = gram_of(left, right)
        blocks[2] = gram_of(right, right)

    for number in range(3):
        at = jnp.where(first_set, dilated_at[number], strided_at)
        send(
            (first_set | second_set) & (me != at),
            blocks.at[number],
            slots.at[number, me],
            slot_sem.at[number, me],
            (row, at),
        )

    def summed(number):
        total = blocks[number]
        for k in range(1, count):
            source = (me + k) % count
            arrive(slots.at[number, source], slot_sem.at[number, source])
            total = total + slots[number, source]
        return total

    for unit in range(3):

        @pl.when(first_set & (me == dilated_at[unit]))
        def _():
            work[...] = summed(unit)

    is_point = second_set & (
        (me == point_at[0]) | (me == point_at[1]) | (me == point_at[2])
    )
    is_group = second_set & ((me == group_at[0]) | (me == group_at[1]))
    is_dilated = first_set & (
        (me == dilated_at[0]) | (me == dilated_at[1]) | (me == dilated_at[2])
    )

    @pl.when(is_point)
    def _():
        for k in range(1, count):
            source = (me + k) % count
            rows = pl.ds(pl.multiple_of(source * share, 8), share)
            arrive(point_all.at[rows], rows_sem.at[source])
        work[...] = gram_of(point_all[...], point_all[...])

    @pl.when(is_group)
    def _():
        for k in range(1, count):
            source = (me + k) % count
            rows = pl.ds(pl.multiple_of(source * part, 8), part)
            arrive(group_all.at[rows], rows_sem.at[source])
        work[...] = gram_of(group_all[...], group_all[...])

    @pl.when(is_dilated | is_point | is_group)
    def _():
        work[...] = solve_mixing(work[...])

    for unit in range(3):

        @pl.when(first_set & (me == dilated_at[unit]))
        def _():
            mix_ref[0, c, unit] = work[...]

    @pl.when(is_point)
    def _():
        point_done[...] = product(split_terms(point_all[...], 3), split_terms(work[...], 3))

    @pl.when(is_group)
    def _():
        group_done[...] = product(split_terms(group_all[...], 3), split_terms(work[...], 3))

    for unit in range(3):
        at = point_at[unit]
        for k in range(1, count):
            target = (me + k) % count
            rows = pl.ds(pl.multiple_of(target * share, 8), share)
            send(
                second_set & (me == at),
                point_done.at[rows],
                small_ref.at[c, unit],
                small_sem.at[unit],
                (row, target),
            )

        @pl.when(second_set & (me == at))
        def _():
            small_ref[c, unit] = point_done[pl.ds(pl.multiple_of(me * share, 8), share), :]

        @pl.when(second_set & (me != at))
        def _():
            arrive(small_ref.at[c, unit], small_sem.at[unit])

    for g in range(GROUPS):
        at = group_at[g]
        spot = small_ref.at[c, 3, g * part : (g + 1) * part]
        for k in range(1, count):
            target = (me + k) % count
            rows = pl.ds(pl.multiple_of(target * part, 8), part)
            send(
                second_set & (me == at),
                group_done.at[rows],
                spot,
                small_sem.at[3 + g],
                (row, target),
            )

        @pl.when(second_set & (me == at))
        def _():
            spot[...] = group_done[pl.ds(pl.multiple_of(me * part, 8), part), :]

        @pl.when(second_set & (me != at))
        def _():
            arrive(spot, small_sem.at[3 + g])

    for k in range(1, high):
        send(
            second_set,
            small_ref.at[c],
            small_ref.at[c],
            small_sem.at[5],
            ((y + k) % high * 2 + c, me),
        )

    @pl.when(jnp.logical_not(second_set))
    def _():
        arrive(small_ref.at[c], small_sem.at[5])

    always = y >= 0
    send(always, small_ref.at[c], small_ref.at[c], small_sem.at[6], partner)

    def hand_out(which, number, at):
        spot = mix_ref.at[which, c, number]
        recv = mix_sem.at[which, c, number]
        mine = y == which
        at_x = at % wide
        owner = mine & (me == at)
        for k in range(1, deep):
            send(owner, spot, spot, recv, (row, (z + k) % deep * wide + x))

        @pl.when(jnp.logical_not(owner))
        def _():
            arrive(spot, recv)

        for k in range(1, wide):
            send(mine & (x == at_x), spot, spot, recv, (row, z * wide + (x + k) % wide))
        for k in range(1, high):
            send(mine, spot, spot, recv, ((y + k) % high * 2 + c, me))
        send(always, spot, spot, recv, partner)

    for unit in range(3):
        hand_out(0, unit, dilated_at[unit])

    @pl.when(second_set & (me == strided_at))
    def _():
        corner = [summed(number) for number in range(3)]
        gram = jnp.concatenate(
            [
                jnp.concatenate([corner[0], corner[1]], axis=1),
                jnp.concatenate([corner[1].T, corner[2]], axis=1),
            ],
            axis=0,
        )
        mixing = solve_mixing(gram)
        mix_ref[1, c, 0] = mixing[:block, :block]
        mix_ref[1, c, 1] = mixing[:block, block:]
        mix_ref[1, c, 2] = mixing[block:, block:]

    for number in range(3):
        hand_out(1, number, strided_at)

    arrive(small_ref.at[1 - c], small_sem.at[6])
    for which in range(2):
        for number in range(3):
            arrive(mix_ref.at[which, 1 - c, number], mix_sem.at[which, 1 - c, number])

    for number, (when, src, dst, recv, to) in enumerate(pending):

        @pl.when(when)
        def _():
            remote(src, dst, number, recv, to).wait_send()


def solve_all(views, sizes, collective_id):
    wide, high, deep = sizes
    count = wide * deep
    share, block = views[0].shape[1:]
    part = share // GROUPS
    f32 = jnp.float32
    dma = pltpu.SemaphoreType.DMA
    sends = 5 + 3 + 5 * (count - 1) + (high - 1) + 1 + 6 * (deep - 1 + wide - 1 + high - 1 + 1)
    vmem = pl.BlockSpec(memory_space=pltpu.VMEM)
    return pl.pallas_call(
        functools.partial(mixing_kernel, sizes, share),
        out_shape=(
            jax.ShapeDtypeStruct((2, 2, 3, block, block), f32),
            jax.ShapeDtypeStruct((2, 4, share, block), f32),
        ),
        in_specs=[pl.BlockSpec(memory_space=pl.ANY)] * 8,
        out_specs=(vmem, vmem),
        scratch_shapes=[
            pltpu.VMEM(views[0].shape, f32),
            pltpu.VMEM(views[1].shape, f32),
            pltpu.VMEM(views[2].shape, f32),
            pltpu.VMEM(views[3].shape, f32),
            pltpu.VMEM((3, block, block), f32),
            pltpu.VMEM((3, count, block, block), f32),
            pltpu.VMEM((count * share, block), f32),
            pltpu.VMEM((count * part, block), f32),
            pltpu.VMEM((block, block), f32),
            pltpu.VMEM((count * share, block), f32),
            pltpu.VMEM((count * part, block), f32),
            dma((4,)),
            dma((sends,)),
            dma((3, count)),
            dma((count,)),
            dma((2, 2, 3)),
            dma((7,)),
        ],
        compiler_params=pltpu.CompilerParams(
            collective_id=collective_id, has_side_effects=True, vmem_limit_bytes=60 * 2**20
        ),
    )(*views)


def apply_kernel(
    dilated_v, strided_v, dilated_w, strided_w, mix_ref, dilated_out, strided_out, update_rate
):
    block = mix_ref.shape[-1]
    share = dilated_v.shape[2]
    for unit in range(3):
        rows = dilated_v[unit].reshape(KERNEL * share, block)
        moved = product(split_terms(rows, 2), split_terms(mix_ref[0, 0, unit], 2))
        dilated_out[unit] = dilated_w[unit] - update_rate * moved.reshape(KERNEL, share, block)
    corner = [split_terms(mix_ref[1, 0, number], 2) for number in range(3)]
    turned = split_terms(mix_ref[1, 0, 1].T, 2)
    rows = strided_v[...].reshape(-1, 2 * block)
    left, right = split_terms(rows[:, :block], 2), split_terms(rows[:, block:], 2)
    low = product(left, corner[0]) + product(right, turned)
    top = product(left, corner[1]) + product(right, corner[2])
    shape = (strided_w.shape[0], share, block)
    strided_out[:, :, :block] = strided_w[:, :, :block] - update_rate * low.reshape(shape)
    strided_out[:, :, block:] = strided_w[:, :, block:] - update_rate * top.reshape(shape)


def apply_side(side, dilated_v, strided_v, dilated_w, strided_w, mixing, update_rate):
    vmem = pl.BlockSpec(memory_space=pltpu.VMEM)
    pick = pl.BlockSpec(
        (2, 1, 3) + mixing.shape[3:], lambda i: (0, side, 0, 0, 0), memory_space=pltpu.VMEM
    )
    whole = [
        pl.BlockSpec(array.shape, lambda i, n=array.ndim: (0,) * n, memory_space=pltpu.VMEM)
        for array in (dilated_v, strided_v, dilated_w, strided_w)
    ]
    return pl.pallas_call(
        functools.partial(apply_kernel, update_rate=update_rate),
        grid=(1,),
        out_shape=(
            jax.ShapeDtypeStruct(dilated_w.shape, jnp.float32),
            jax.ShapeDtypeStruct(strided_w.shape, jnp.float32),
        ),
        in_specs=whole + [pick],
        out_specs=tuple(whole[2:]),
        compiler_params=pltpu.CompilerParams(vmem_limit_bytes=60 * 2**20),
    )(dilated_v, strided_v, dilated_w, strided_w, mixing)


def per_device(
    frames,
    cotangent,
    segment_ids,
    code_index,
    codebooks,
    dead_codes,
    code_slots,
    buffered,
    encoder_dilated,
    encoder_pointwise,
    down_weight,
    group_in,
    group_out,
    up_weight,
    decoder_dilated,
    decoder_pointwise,
    encoder_dilated_moment,
    encoder_pointwise_moment,
    down_moment,
    group_in_moment,
    group_out_moment,
    up_moment,
    decoder_dilated_moment,
    decoder_pointwise_moment,
):
    masters = (
        encoder_dilated,
        encoder_pointwise,
        down_weight,
        group_in,
        group_out,
        up_weight,
        decoder_dilated,
        decoder_pointwise,
    )
    olds = (
        encoder_dilated_moment,
        encoder_pointwise_moment,
        down_moment,
        group_in_moment,
        group_out_moment,
        up_moment,
        decoder_dilated_moment,
        decoder_pointwise_moment,
    )
    lowered = [weight.astype(jnp.bfloat16) for weight in masters]
    count = lax.axis_size("seq")
    sizes = line_sizes(count, lax.axis_size("dp"))
    sides = ((0, 1, 3, 2), (6, 7, 4, 5))
    packed = []
    for side in sides:
        parts = [lowered[i] for i in side[:3]] + [halves(lowered[side[3]])]
        packed.append(pack_side(*parts, sizes[1], 0))
    side_rows = packed[0].shape[0]
    reach = frames.shape[1] // 2
    near = 80
    latent_reach = reach // STRIDE * GROUPS * LEVELS
    code_row = code_index.reshape(-1)
    number_edges = jnp.zeros((2, 8, lanes), jnp.int32)
    number_edges = number_edges.at[0, 0, :reach].set(segment_ids[0, reach:])
    number_edges = number_edges.at[1, 0, :reach].set(segment_ids[0, :reach])
    number_edges = number_edges.at[0, 1, :latent_reach].set(code_row[latent_reach:])
    number_edges = number_edges.at[1, 1, :latent_reach].set(code_row[:latent_reach])
    gathered, (frame_edges, cot_edges, numbers) = gather_rows(
        jnp.concatenate(packed),
        (
            jnp.stack([frames[0, reach:], frames[0, :reach]]),
            jnp.stack([cotangent[0, -near:], cotangent[0, :near]]),
            number_edges,
        ),
        sizes,
        0,
    )
    part_shapes = []
    for side in sides:
        shapes = [masters[i].shape for i in side[:3]]
        taps, share, width = masters[side[3]].shape
        shapes.append((2, taps, share, width // 2))
        part_shapes.append(shapes)
    row_count, length, channels = frames.shape
    long = 2 * length
    latent_len = long // STRIDE
    reach = length // 2
    near = 80
    place_seq = lax.axis_index("seq")
    hidden = encoder_dilated.shape[-1]
    share = masters[0].shape[2]
    blocks = side_rows // share
    geometry = (count, share, blocks)
    gathered = gathered.reshape(count, 2 * blocks, share, hidden)
    no_match = jnp.full((margin,), -1, jnp.int32)
    ids_left = jnp.where(place_seq == 0, -1, numbers[0, 0])
    ids_right = jnp.where(place_seq == count - 1, -1, numbers[1, 0])
    ids = jnp.concatenate([no_match, ids_left, segment_ids[0], ids_right, no_match])
    ids = jnp.broadcast_to(ids[:, None], (long + 2 * margin, lanes))
    half_codes = reach // STRIDE
    codes = jnp.concatenate(
        [
            numbers[0, 1, : half_codes * 4].reshape(half_codes, 4),
            code_index[0].reshape(-1, 4),
            numbers[1, 1, : half_codes * 4].reshape(half_codes, 4),
        ]
    )
    frames_long = jnp.concatenate([frame_edges[0], frames[0], frame_edges[1]])
    blank = jnp.zeros((reach - near, channels), jnp.float32)
    cot_long = jnp.concatenate([blank, cot_edges[0], cotangent[0], cot_edges[1], blank])
    vmem = pl.BlockSpec(memory_space=pltpu.VMEM)
    anywhere = pl.BlockSpec(memory_space=pl.ANY)
    params = pltpu.CompilerParams(vmem_limit_bytes=60 * 2**20)
    packed_type = jax.ShapeDtypeStruct(gathered.shape, jnp.bfloat16)
    scratch = side_scratch(count, share, long, channels, hidden)
    decoded, grad_quant, picks, partial = pl.pallas_call(
        functools.partial(decoder_kernel, geometry, long),
        out_shape=(
            jax.ShapeDtypeStruct((length, channels), jnp.bfloat16),
            jax.ShapeDtypeStruct((GROUPS, latent_len, hidden), jnp.float32),
            jax.ShapeDtypeStruct((GROUPS * LEVELS, latent_len, hidden), jnp.float32),
            packed_type,
        ),
        in_specs=[vmem, vmem, vmem, vmem, anywhere],
        out_specs=(vmem, vmem, vmem, anywhere),
        scratch_shapes=scratch,
        compiler_params=params,
    )(codes, ids, cot_long, codebooks, gathered)
    grad, latent_rows, partial = pl.pallas_call(
        functools.partial(encoder_kernel, geometry, long),
        out_shape=(
            jax.ShapeDtypeStruct((length, channels), jnp.float32),
            jax.ShapeDtypeStruct((length // STRIDE, GROUPS * LEVELS * hidden), jnp.bfloat16),
            packed_type,
        ),
        in_specs=[vmem, vmem, vmem, vmem, anywhere, anywhere],
        out_specs=(vmem, vmem, anywhere),
        scratch_shapes=scratch,
        input_output_aliases={5: 2},
        compiler_params=params,
    )(frames_long, ids, grad_quant, picks, gathered, partial)
    decoded = decoded[None]
    grad = grad[None]
    own_codes_low = code_index[0].reshape(-1, GROUPS * LEVELS)
    digits = jnp.concatenate([own_codes_low // 32, own_codes_low % 32], axis=1)
    digits = jnp.pad(digits, ((0, 0), (0, lanes - digits.shape[1]))).astype(jnp.bfloat16)
    share_rows, all_rows = reduce_rows(
        partial.reshape(count, 2 * side_rows, hidden),
        jnp.concatenate([latent_rows, digits], axis=1),
        sizes,
        1,
    )
    all_rows = all_rows.reshape(-1, all_rows.shape[-1])
    group_width = hidden
    digits = all_rows[:, GROUPS * LEVELS * hidden :].astype(jnp.int32)
    all_codes = digits[:, :4] * 32 + digits[:, 4:8]
    code_share = dead_codes.shape[2]
    own_range = lax.broadcasted_iota(
        jnp.int32, (1, code_share), 1
    ) + code_share * place_seq
    sum_list = []
    count_list = []
    for entry in range(GROUPS * LEVELS):
        own_hot = (all_codes[:, entry : entry + 1] == own_range).astype(jnp.bfloat16)
        sum_list.append(
            lax.dot_general(
                own_hot,
                all_rows[:, entry * group_width : (entry + 1) * group_width],
                (((0,), (0,)), ((), ())),
                preferred_element_type=jnp.float32,
            )
        )
        count_list.append(jnp.sum(own_hot.astype(jnp.float32), axis=0))
    total_sums = jnp.stack(sum_list).reshape(GROUPS, LEVELS, code_share, group_width)
    total_counts = jnp.stack(count_list).reshape(GROUPS, LEVELS, code_share)
    reduced = [None] * 8
    for at, side in enumerate(sides):
        parts = take_side(share_rows[at * side_rows : (at + 1) * side_rows], part_shapes[at])
        for i, part in zip(side[:3], parts):
            reduced[i] = part.astype(jnp.float32)
        reduced[side[3]] = jnp.concatenate([parts[3][0], parts[3][1]], axis=-1).astype(jnp.float32)
    own_codes = lax.dynamic_slice_in_dim(
        codebooks, lax.axis_index("seq") * code_share, code_share, 2
    )
    code_means = total_sums / jnp.maximum(total_counts, 1.0)[..., None]
    code_used = jnp.minimum(total_counts, 1.0)[..., None]
    updated = own_codes + code_rate * code_used * (code_means - own_codes)
    slot_range = lax.broadcasted_iota(jnp.int32, (1, 1, 1, buffered.shape[1]), 3)
    slot_onehot = (code_slots[..., None] == slot_range).astype(jnp.float32)
    replaced = jnp.einsum("glsb,gbz->glsz", slot_onehot, buffered, precision=highest)
    new_codebooks = jnp.where(dead_codes[..., None] == 1, replaced, updated)
    velocities = tuple((moment_decay * olds[position] + reduced[position] for position in range(8)))
    views = []
    for side in sides:
        dilated_v, point_v, group_v, strided_v = [velocities[i] for i in side]
        views += [dilated_v.reshape((-1,) + dilated_v.shape[2:]), point_v, group_v, strided_v]
    mixing, small = solve_all(views, sizes, 2)
    nexts = [None] * 8
    for at, side in enumerate(sides):
        dil, point, group, strided = side
        nexts[dil], nexts[strided] = apply_side(
            at, velocities[dil], velocities[strided], masters[dil], masters[strided], mixing,
            update_rate,
        )
        nexts[point] = masters[point] - update_rate * small[at, :3]
        nexts[group] = masters[group] - update_rate * small[at, 3].reshape(masters[group].shape)
    return (
        decoded,
        grad,
        new_codebooks,
        velocities[0],
        velocities[1],
        velocities[2],
        velocities[3],
        velocities[4],
        velocities[5],
        velocities[6],
        velocities[7],
        nexts[0],
        nexts[1],
        nexts[2],
        nexts[3],
        nexts[4],
        nexts[5],
        nexts[6],
        nexts[7],
    )


def solution(mesh):
    in_specs = (
        P("dp", "seq", None),
        P("dp", "seq", None),
        P("dp", "seq"),
        P("dp", "seq", None, None),
        P(),
        P(None, None, "seq"),
        P(None, None, "seq"),
        P(),
        P(None, None, "seq", None),
        P(None, "seq", None),
        P(None, "seq", None),
        P(None, "seq", None),
        P(None, "seq", None),
        P(None, "seq", None),
        P(None, None, "seq", None),
        P(None, "seq", None),
        P(None, None, "seq", None),
        P(None, "seq", None),
        P(None, "seq", None),
        P(None, "seq", None),
        P(None, "seq", None),
        P(None, "seq", None),
        P(None, None, "seq", None),
        P(None, "seq", None),
    )
    out_specs = (
        P("dp", "seq", None),
        P("dp", "seq", None),
        P(None, None, "seq", None),
        P(None, None, "seq", None),
        P(None, "seq", None),
        P(None, "seq", None),
        P(None, "seq", None),
        P(None, "seq", None),
        P(None, "seq", None),
        P(None, None, "seq", None),
        P(None, "seq", None),
        P(None, None, "seq", None),
        P(None, "seq", None),
        P(None, "seq", None),
        P(None, "seq", None),
        P(None, "seq", None),
        P(None, "seq", None),
        P(None, None, "seq", None),
        P(None, "seq", None),
    )
    return jax.shard_map(
        per_device, mesh=mesh, in_specs=in_specs, out_specs=out_specs, check_vma=False
    )
```

```python
import functools

import jax
import jax.numpy as jnp
from jax import lax
from jax.experimental import pallas as pl
from jax.experimental.pallas import tpu as pltpu
from jax.sharding import PartitionSpec as P

GROUPS = 2
LEVELS = 2
KERNEL = 7
STRIDE = 8
NS_STEPS = 5


highest = lax.Precision.HIGHEST
dilation_list = (1, 3, 9)
coef_first = 3.4445
coef_second = -4.775
coef_third = 2.0315
commit_weight = 0.25
moment_decay = 0.5
update_rate = 0.5
code_rate = 0.5
norm_floor = 1e-07


def halves(array):
    width = array.shape[-1] // 2
    split = array.reshape(array.shape[:-1] + (2, width))
    return jnp.moveaxis(split, -2, 0)


def whole_rows(rows, high, share):
    unit = 64 * high
    while unit % share:
        unit += 64 * high
    return -(-rows // unit) * unit


def pack_side(dilated, pointwise, group, strided, high, share, lead):
    parts = [dilated, pointwise, group, strided]
    kept = dilated.shape[:lead]
    flat = [part.reshape(kept + (-1, part.shape[-1])) for part in parts]
    rows = sum(part.shape[lead] for part in flat)
    extra = whole_rows(rows, high, share) - rows
    if extra:
        flat.append(jnp.zeros(kept + (extra, flat[0].shape[-1]), flat[0].dtype))
    return jnp.concatenate(flat, axis=lead)


def take_side(rows, shapes):
    found = []
    start = 0
    for shape in shapes:
        size = 1
        for extent in shape[:-1]:
            size *= extent
        found.append(rows[..., start : start + size, :].reshape(rows.shape[:-2] + shape))
        start += size
    return found


MESH = pl.DeviceIdType.MESH


def line_sizes(seq, dp):
    across = 1
    while (2 * across) * (2 * across) <= seq:
        across *= 2
    return across, dp // 2, seq // across


def place(sizes):
    wide, high, _ = sizes
    row = lax.axis_index("dp")
    part = lax.axis_index("seq")
    return part % wide, row // 2, part // wide, row % 2


def greet(sizes):
    wide, high, deep = sizes
    x, y, z, c = place(sizes)
    barrier = pltpu.get_barrier_semaphore()
    others = [(y * 2 + 1 - c, z * wide + x)]
    others += [(y * 2 + c, z * wide + (x + k) % wide) for k in range(1, wide)]
    others += [((y + k) % high * 2 + c, z * wide + x) for k in range(1, high)]
    others += [(y * 2 + c, (z + k) % deep * wide + x) for k in range(1, deep)]
    count = deep * wide
    others += [(y * 2 + c, (z * wide + x + k) % count) for k in (1, count - 1)]
    for other in others:
        pl.semaphore_signal(barrier, inc=1, device_id=other, device_id_type=MESH)
    pl.semaphore_wait(barrier, len(others))


class Sender:
    def __init__(self, send_sem, partner):
        self.send_sem = send_sem
        self.partner = partner
        self.sent = []

    def send(self, src, dst, recv, to):
        copy = pltpu.make_async_remote_copy(
            src_ref=src,
            dst_ref=dst,
            send_sem=self.send_sem.at[len(self.sent)],
            recv_sem=recv,
            device_id=to,
            device_id_type=MESH,
        )
        copy.start()
        self.sent.append(copy)

    def arrive(self, dst, recv):
        pltpu.make_async_remote_copy(
            src_ref=dst,
            dst_ref=dst,
            send_sem=self.send_sem.at[0],
            recv_sem=recv,
            device_id=self.partner,
            device_id_type=MESH,
        ).wait_recv()

    def finish(self):
        for copy in self.sent:
            copy.wait_send()


class Gather:
    def __init__(self, sizes, sender, in_ref, out_ref, recv_sem):
        self.sizes = sizes
        self.place = place(sizes)
        self.sender = sender
        self.in_ref, self.out_ref, self.recv_sem = in_ref, out_ref, recv_sem

    def send(self, zs, xs, ys, h, to, source=None):
        c = self.place[3]
        spot = self.out_ref.at[zs, xs, c, ys, h]
        src = spot if source is None else source
        self.sender.send(src, spot, self.recv_sem.at[zs, xs, c, ys, h], to)

    def arrive(self, zs, xs, cs, ys, h):
        self.sender.arrive(self.out_ref.at[zs, xs, cs, ys, h], self.recv_sem.at[zs, xs, cs, ys, h])

    def to_x(self, zs, xs, ys, h, source=None):
        wide, high, deep = self.sizes
        x, y, z, c = self.place
        for k in range(1, wide):
            self.send(zs, xs, ys, h, (y * 2 + c, z * wide + (x + k) % wide), source)

    def to_y(self, zs, xs, ys, h):
        wide, high, deep = self.sizes
        x, y, z, c = self.place
        for k in range(1, high):
            self.send(zs, xs, ys, h, ((y + k) % high * 2 + c, z * wide + x))

    def to_core(self, zs, xs, ys, h):
        wide, high, deep = self.sizes
        x, y, z, c = self.place
        self.send(zs, xs, ys, h, (y * 2 + 1 - c, z * wide + x))

    def own_z(self):
        wide, high, deep = self.sizes
        x, y, z, c = self.place
        for k in range(deep - 1, 0, -1):
            for h in range(2):
                to = (y * 2 + c, (z + k) % deep * wide + x)
                self.send(z, x, y, h, to, self.in_ref.at[c, y, h])

    def own_x(self):
        wide, high, deep = self.sizes
        x, y, z, c = self.place
        self.to_x(z, x, y, 0, self.in_ref.at[c, y, 0])
        for j in range(high):
            ys = (y + j) % high
            self.to_x(z, x, ys, 1, self.in_ref.at[c, ys, 1])

    def from_z(self, k):
        x, y, z, c = self.place
        zs = (z + k) % self.sizes[2]
        self.arrive(zs, x, c, y, 0)
        self.to_x(zs, x, y, 0)
        self.to_y(zs, x, y, 0)
        self.to_core(zs, x, y, 0)
        self.arrive(zs, x, c, y, 1)
        self.to_y(zs, x, y, 1)
        self.to_x(zs, x, y, 1)
        self.to_core(zs, x, y, 1)

    def second(self, k):
        wide, high, deep = self.sizes
        x, y, z, c = self.place
        zs = (z + k) % deep
        for i in range(1, wide):
            xs = (x + i) % wide
            self.arrive(zs, xs, c, y, 0)
            self.to_y(zs, xs, y, 0)
            self.to_core(zs, xs, y, 0)
        if k > 0:
            for j in range(1, high):
                ys = (y + j) % high
                self.arrive(zs, x, c, ys, 1)
                self.to_x(zs, x, ys, 1)
                self.to_core(zs, x, ys, 1)

    def third(self, k):
        wide, high, deep = self.sizes
        x, y, z, c = self.place
        zs = (z + k) % deep
        for i in range(wide):
            xs = (x + i) % wide
            if k == 0 and i == 0:
                continue
            for j in range(1, high):
                ys = (y + j) % high
                self.arrive(zs, xs, c, ys, 0)
                self.to_core(zs, xs, ys, 0)
            if i > 0:
                for j in range(high):
                    ys = (y + j) % high
                    self.arrive(zs, xs, c, ys, 1)
                    self.to_core(zs, xs, ys, 1)

    def last(self):
        wide, high, deep = self.sizes
        x, y, z, c = self.place
        for k in range(deep):
            zs = (z + k) % deep
            for i in range(wide):
                xs = (x + i) % wide
                if k == 0 and i == 0:
                    continue
                for j in range(high):
                    for h in range(2):
                        self.arrive(zs, xs, 1 - c, (y + j) % high, h)


def gather_sends(sizes):
    wide, high, deep = sizes
    n = (deep - 1) * 2 + (wide - 1) * (1 + high)
    n += (deep - 1) * 2 * (wide - 1 + high - 1 + 1)
    n += deep * (wide - 1) * high + (deep - 1) * (high - 1) * wide
    n += (deep * wide - 1) * (high - 1) + deep * (wide - 1) * high
    return n


class Spread:
    def __init__(self, sizes, sender, row_ref, all_ref, row_sem, keep_sem):
        self.sizes = sizes
        self.place = place(sizes)
        self.sender = sender
        self.row_ref, self.all_ref, self.row_sem = row_ref, all_ref, row_sem
        x, y, z, c = self.place
        self.keep = pltpu.make_async_copy(row_ref, all_ref.at[z, x, y, c], keep_sem)

    def pass_on(self, zs, xs, ys, to, own):
        c = self.place[3]
        spot = self.all_ref.at[zs, xs, ys, c]
        self.sender.send(self.row_ref if own else spot, spot, self.row_sem.at[zs, xs, ys, c], to)

    def landed(self, zs, xs, ys, cs):
        self.sender.arrive(self.all_ref.at[zs, xs, ys, cs], self.row_sem.at[zs, xs, ys, cs])

    def stage(self, number):
        wide, high, deep = self.sizes
        x, y, z, c = self.place
        columns = [(z + k) % deep for k in range(deep)]
        lines = [(x + k) % wide for k in range(wide)]
        heights = [(y + k) % high for k in range(high)]
        if number == 0:
            self.keep.start()
            for zt in columns[1:]:
                self.pass_on(z, x, y, (y * 2 + c, zt * wide + x), True)
        if number == 1:
            for zs in columns[1:]:
                self.landed(zs, x, y, c)
            for zs in columns:
                for xt in lines[1:]:
                    self.pass_on(zs, x, y, (y * 2 + c, z * wide + xt), zs is columns[0])
        if number == 2:
            for zs in columns:
                for xs in lines[1:]:
                    self.landed(zs, xs, y, c)
            for zs in columns:
                for xs in lines:
                    own = zs is columns[0] and xs is lines[0]
                    for yt in heights[1:]:
                        self.pass_on(zs, xs, y, (yt * 2 + c, z * wide + x), own)
        if number == 3:
            for zs in columns:
                for xs in lines:
                    for ys in heights[1:]:
                        self.landed(zs, xs, ys, c)
            for zs in columns:
                for xs in lines:
                    for ys in heights:
                        own = zs is columns[0] and xs is lines[0] and ys is heights[0]
                        self.pass_on(zs, xs, ys, (y * 2 + 1 - c, z * wide + x), own)
        if number == 4:
            for zs in columns:
                for xs in lines:
                    for ys in heights:
                        self.landed(zs, xs, ys, 1 - c)
            self.keep.wait()


def spread_sends(sizes):
    wide, high, deep = sizes
    return deep - 1 + deep * (wide - 1) + deep * wide * (high - 1) + deep * wide * high


class Reduce:
    def __init__(self, sizes, sender, in_ref, out_ref, scratch):
        self.sizes = sizes
        self.place = place(sizes)
        self.sender = sender
        self.in_ref, self.out_ref = in_ref, out_ref
        (
            self.held,
            self.from_core,
            self.from_x_a,
            self.from_y_b,
            self.from_y_a,
            self.from_x_b,
            self.from_z,
            self.final,
            self.local_sem,
            self.core_sem,
            self.xa_sem,
            self.yb_sem,
            self.ya_sem,
            self.xb_sem,
            self.z_sem,
            self.done_sem,
        ) = scratch
        deep = sizes[2]
        z = self.place[2]
        far = list(range(deep // 2, deep)) + list(range(deep // 2 - 1, 0, -1))
        self.order = [(z + k) % deep for k in far] + [z]

    def local(self, step):
        c = self.place[3]
        source = self.in_ref.at[self.order[step], :, c]
        return pltpu.make_async_copy(source, self.held.at[step], self.local_sem.at[step])

    def start(self):
        wide, high, deep = self.sizes
        x, y, z, c = self.place
        for step in range(deep):
            self.local(step).start()
            self.sender.send(
                self.in_ref.at[self.order[step], :, 1 - c],
                self.from_core.at[step],
                self.core_sem.at[step],
                (y * 2 + 1 - c, z * wide + x),
            )

    def merge(self, target, extras):
        total = target[...].astype(jnp.float32)
        for extra in extras:
            total = total + extra[...].astype(jnp.float32)
        target[...] = total.astype(target.dtype)

    def first(self, step):
        wide, high, deep = self.sizes
        x, y, z, c = self.place
        self.local(step).wait()
        self.sender.arrive(self.from_core.at[step], self.core_sem.at[step])

        def body(i, carry):
            xi, yi, hi = i // (2 * high), i // 2 % high, i % 2
            self.merge(self.held.at[step, xi, yi, hi], [self.from_core.at[step, xi, yi, hi]])
            return carry

        lax.fori_loop(0, wide * high * 2, body, 0)
        for k in range(1, wide):
            xt = (x + k) % wide
            self.sender.send(
                self.held.at[step, xt, :, 0],
                self.from_x_a.at[k - 1, step],
                self.xa_sem.at[k - 1, step],
                (y * 2 + c, z * wide + xt),
            )
        for k in range(1, high):
            yt = (y + k) % high
            self.sender.send(
                self.held.at[step, :, yt, 1],
                self.from_y_b.at[k - 1, step],
                self.yb_sem.at[k - 1, step],
                (yt * 2 + c, z * wide + x),
            )

    def second(self, step):
        wide, high, deep = self.sizes
        x, y, z, c = self.place
        for k in range(1, wide):
            self.sender.arrive(self.from_x_a.at[k - 1, step], self.xa_sem.at[k - 1, step])

        def body_a(i, carry):
            yt = (y + 1 + i) % high
            extras = [self.from_x_a.at[k, step, yt] for k in range(wide - 1)]
            self.merge(self.held.at[step, x, yt, 0], extras)
            return carry

        lax.fori_loop(0, high, body_a, 0)
        for k in range(1, high):
            yt = (y + k) % high
            self.sender.send(
                self.held.at[step, x, yt, 0],
                self.from_y_a.at[k - 1, step],
                self.ya_sem.at[k - 1, step],
                (yt * 2 + c, z * wide + x),
            )
        for k in range(1, high):
            self.sender.arrive(self.from_y_b.at[k - 1, step], self.yb_sem.at[k - 1, step])

        def body_b(i, carry):
            xt = (x + 1 + i) % wide
            extras = [self.from_y_b.at[k, step, xt] for k in range(high - 1)]
            self.merge(self.held.at[step, xt, y, 1], extras)
            return carry

        lax.fori_loop(0, wide, body_b, 0)
        for k in range(1, wide):
            xt = (x + k) % wide
            self.sender.send(
                self.held.at[step, xt, y, 1],
                self.from_x_b.at[k - 1, step],
                self.xb_sem.at[k - 1, step],
                (y * 2 + c, z * wide + xt),
            )

    def third(self, step):
        wide, high, deep = self.sizes
        x, y, z, c = self.place
        for k in range(1, high):
            self.sender.arrive(self.from_y_a.at[k - 1, step], self.ya_sem.at[k - 1, step])
        self.merge(
            self.held.at[step, x, y, 0], [self.from_y_a.at[k, step] for k in range(high - 1)]
        )
        for k in range(1, wide):
            self.sender.arrive(self.from_x_b.at[k - 1, step], self.xb_sem.at[k - 1, step])
        self.merge(
            self.held.at[step, x, y, 1], [self.from_x_b.at[k, step] for k in range(wide - 1)]
        )
        if step < deep - 1:
            self.sender.send(
                self.held.at[step, x, y],
                self.from_z.at[step],
                self.z_sem.at[step],
                (y * 2 + c, self.order[step] * wide + x),
            )

    def turn(self, number):
        deep = self.sizes[2]
        if number < deep:
            self.first(number)
        if 0 <= number - 1 < deep:
            self.second(number - 1)
        if 0 <= number - 2 < deep:
            self.third(number - 2)

    def total(self):
        wide, high, deep = self.sizes
        x, y, z, c = self.place
        for step in range(deep - 1):
            self.sender.arrive(self.from_z.at[step], self.z_sem.at[step])
        for h in range(2):
            total = self.held[deep - 1, x, y, h].astype(jnp.float32)
            for step in range(deep - 1):
                total = total + self.from_z[step, h].astype(jnp.float32)
            self.final[h] = total.astype(self.final.dtype)
        spot, recv = self.out_ref.at[c, y], self.done_sem.at[c, y]
        pltpu.make_async_copy(self.final, spot, self.local_sem.at[deep]).start()
        for k in range(1, high):
            to = ((y + k) % high * 2 + c, z * wide + x)
            self.sender.send(self.final, spot, recv, to)
        self.sender.send(self.final, spot, recv, (y * 2 + 1 - c, z * wide + x))

    def last(self):
        wide, high, deep = self.sizes
        x, y, z, c = self.place
        for k in range(1, high):
            yt = (y + k) % high
            spot, recv = self.out_ref.at[c, yt], self.done_sem.at[c, yt]
            self.sender.arrive(spot, recv)
            self.sender.send(spot, spot, recv, (y * 2 + 1 - c, z * wide + x))
        for k in range(high):
            yt = (y + k) % high
            self.sender.arrive(self.out_ref.at[1 - c, yt], self.done_sem.at[1 - c, yt])
        own = self.out_ref.at[c, y]
        pltpu.make_async_copy(self.final, own, self.local_sem.at[deep]).wait()


def reduce_sends(sizes):
    wide, high, deep = sizes
    return deep + deep * 2 * (wide - 1 + high - 1) + deep - 1 + 2 * (high - 1) + 1


def reduce_scratch(sizes, rows, width, kind, final_kind):
    wide, high, deep = sizes
    tail = (rows, width)
    dma = pltpu.SemaphoreType.DMA
    return [
        pltpu.VMEM((deep, wide, high, 2) + tail, kind),
        pltpu.VMEM((deep, wide, high, 2) + tail, kind),
        pltpu.VMEM((wide - 1, deep, high) + tail, kind),
        pltpu.VMEM((high - 1, deep, wide) + tail, kind),
        pltpu.VMEM((high - 1, deep) + tail, kind),
        pltpu.VMEM((wide - 1, deep) + tail, kind),
        pltpu.VMEM((deep - 1, 2) + tail, kind),
        pltpu.VMEM((2,) + tail, final_kind),
        dma((deep + 1,)),
        dma((deep,)),
        dma((wide - 1, deep)),
        dma((high - 1, deep)),
        dma((high - 1, deep)),
        dma((wide - 1, deep)),
        dma((deep - 1,)),
        dma((2, high)),
    ]


reduce_parts = 16


def reduce_kernel(sizes, in_ref, row_ref, out_ref, all_ref, *refs):
    x, y, z, c = place(sizes)
    greet(sizes)
    sender = Sender(refs[-1], (y * 2 + 1 - c, z * sizes[0] + x))
    spread = Spread(sizes, sender, row_ref, all_ref, refs[-2], refs[-3])
    side = Reduce(sizes, sender, in_ref, out_ref, refs[:reduce_parts])
    side.start()
    spread.stage(0)
    for number in range(sizes[2] + 2):
        side.turn(number)
        if number in (1, 2, 3):
            spread.stage(number)
    side.total()
    spread.stage(4)
    side.last()
    sender.finish()


def reduce_rows(partial, rows_own, sizes, final_kind, collective_id):
    wide, high, deep = sizes
    _, total, width = partial.shape
    rows = total // (4 * high)
    block = partial.reshape(deep, wide, 2, high, 2, rows, width)
    dma = pltpu.SemaphoreType.DMA
    out = pl.pallas_call(
        functools.partial(reduce_kernel, sizes),
        out_shape=(
            jax.ShapeDtypeStruct((2, high, 2, rows, width), final_kind),
            jax.ShapeDtypeStruct((deep, wide, high, 2) + rows_own.shape, rows_own.dtype),
        ),
        in_specs=[pl.BlockSpec(memory_space=pl.ANY)] * 2,
        out_specs=(pl.BlockSpec(memory_space=pl.ANY),) * 2,
        scratch_shapes=reduce_scratch(sizes, rows, width, partial.dtype, final_kind)
        + [
            dma,
            dma((deep, wide, high, 2)),
            dma((reduce_sends(sizes) + spread_sends(sizes),)),
        ],
        compiler_params=pltpu.CompilerParams(
            collective_id=collective_id, has_side_effects=True, vmem_limit_bytes=60 * 2**20
        ),
    )(block, rows_own)
    return out[0].reshape(total, width), out[1].reshape((-1,) + rows_own.shape)


margin = 32
lanes = 128


def elu_slope(values):
    return jnp.where(values > 0, 1.0, jnp.exp(jnp.minimum(values, 0.0)))


def elu(values):
    return jnp.where(values > 0, values, jnp.exp(jnp.minimum(values, 0.0)) - 1.0)


def dot(left, right):
    return jnp.dot(left, right, preferred_element_type=jnp.float32)


def dot_last(left, right):
    return lax.dot_general(
        left, right, (((1,), (1,)), ((), ())), preferred_element_type=jnp.float32
    )


def dot_rows(left, right):
    return lax.dot_general(
        left, right, (((0,), (0,)), ((), ())), preferred_element_type=jnp.float32
    )


def spread_taps(target, source, ids, width, sign, dilation, length):
    block = 64

    def body(step, carry):
        base = pl.multiple_of(step * block, block)
        window = ids[pl.ds(base, block + 2 * margin), :]
        own = window[margin : margin + block]
        for tap in range(KERNEL):
            start = margin + sign * (tap - KERNEL // 2) * dilation
            match = window[start : start + block] == own
            for piece in range(width // lanes):
                columns = slice(piece * lanes, (piece + 1) * lanes)
                values = source[pl.ds(base, block + 2 * margin), columns][start : start + block]
                spot = tap * width + piece * lanes
                target[pl.ds(base, block), spot : spot + lanes] = jnp.where(
                    match, values, 0.0
                ).astype(jnp.bfloat16)
        return carry

    lax.fori_loop(0, length // block, body, 0)


def forward_unit(unit, stream, follow, ids, weights, scratch, length):
    dilated, pointwise = weights
    padded, columns, hidden, excited, active = scratch
    channels = stream.shape[1]
    values = elu(stream[...])
    padded[margin : margin + length, :] = values
    active[unit] = values[length // 4 : 3 * length // 4].astype(jnp.bfloat16)
    spread_taps(columns, padded, ids, channels, 1, dilation_list[unit], length)
    kernel = dilated[unit * KERNEL : (unit + 1) * KERNEL].reshape(KERNEL * channels, -1)
    value = dot(columns[...], kernel)
    hidden[unit] = value
    lifted = elu(value).astype(jnp.bfloat16)
    excited[unit] = lifted
    follow[...] = stream[...] + dot_last(lifted, pointwise[unit])


def backward_unit(unit, grad, stream, ids, weights, scratch, length, store_dilated, store_point):
    dilated, pointwise = weights
    padded, columns, hidden, excited, active = scratch
    width = hidden.shape[2]
    first, last = length // 4, 3 * length // 4
    low = grad[...].astype(jnp.bfloat16)
    store_point(
        unit,
        dot(grad[first:last, :].T.astype(jnp.bfloat16), excited[unit, first:last, :]).astype(
            jnp.bfloat16
        ),
    )
    grad_hidden = dot(low, pointwise[unit]) * elu_slope(hidden[unit])
    padded[margin : margin + length, :width] = grad_hidden.astype(jnp.bfloat16).astype(jnp.float32)
    spread_taps(columns, padded, ids, width, -1, dilation_list[unit], length)
    turned = active[unit].astype(jnp.float32).T.astype(jnp.bfloat16)
    total = None
    for tap in range(KERNEL):
        piece = slice(tap * width, (tap + 1) * width)
        part = dot_last(columns[:, piece], dilated[unit * KERNEL + tap])
        total = part if total is None else total + part
        store_dilated(unit, tap, dot(turned, columns[first:last, piece]).astype(jnp.bfloat16))
    grad[...] = grad[...] + total * elu_slope(stream[...])


class Mover:
    def __init__(self, side, geometry, me, own, gathered, packed, weights, grads, sems):
        self.seq, self.share, self.blocks = geometry
        self.base = side * self.blocks
        width = gathered.shape[-1]
        self.gathered = gathered.reshape(self.seq, -1, self.share, width)
        self.own = own.reshape(-1, self.share, width)
        self.me = me
        self.packed = packed
        self.weights, self.grads = weights, grads
        self.sems = sems

    def block_start(self, kind):
        return (0, 3 * KERNEL, 3 * KERNEL + 3, 3 * KERNEL + 4)[kind]

    def load(self, kind, owner):
        rows = self.weights[kind]
        start = self.base + self.block_start(kind)
        source = self.gathered.at[owner, pl.ds(start, rows.shape[0])]
        target = rows.at[:, pl.ds(pl.multiple_of(owner * self.share, 16), self.share)]
        return pltpu.make_async_copy(source, target, self.sems.at[kind, owner])

    def start_loads(self, kind):
        rows = self.weights[kind]
        blocks = pl.ds(self.base + self.block_start(kind), rows.shape[0])
        spot = rows.at[:, pl.ds(pl.multiple_of(self.me * self.share, 16), self.share)]
        pltpu.make_async_copy(self.own.at[blocks], spot, self.sems.at[kind, self.me]).start()
        for k in range(1, self.seq):
            self.load(kind, (self.me + k) % self.seq).start()

    def wait_loads(self, kind):
        for owner in range(self.seq):
            self.load(kind, owner).wait()

    def store(self, kind, owner, first, size):
        rows = self.grads[kind]
        start = self.block_start(kind) + first
        source = rows.at[first : first + size, pl.ds(owner * self.share, self.share)]
        target = self.packed.at[owner, pl.ds(start, size)]
        return pltpu.make_async_copy(source, target, self.sems.at[4 + kind, owner])


def load_group(rows, seq, share):
    width = rows.shape[-1]
    part = width // seq
    value = rows.astype(jnp.float32).reshape(seq, GROUPS, part, width)
    return [value[:, g].reshape(width, width).astype(jnp.bfloat16) for g in range(GROUPS)]


def store_group(grads, seq, share):
    width = grads[0].shape[-1]
    part = width // seq
    value = jnp.stack([grad.reshape(seq, part, width) for grad in grads], axis=1)
    return value.reshape(seq, GROUPS * part, width).astype(jnp.bfloat16)


def put_tap(tiles, tap, value):
    latents = value.shape[0]
    for piece in range(tiles.shape[0]):
        tiles[piece, pl.ds(tap, latents, stride=STRIDE), :] = value[
            :, piece * lanes : (piece + 1) * lanes
        ]


def take_tap(tiles, tap, latents):
    return jnp.concatenate(
        [tiles[piece, pl.ds(tap, latents, stride=STRIDE), :] for piece in range(tiles.shape[0])],
        axis=1,
    )


def to_tiles(tiles, value):
    for piece in range(tiles.shape[0]):
        tiles[piece] = value[:, piece * lanes : (piece + 1) * lanes]


def from_tiles(tiles):
    return jnp.concatenate([tiles[piece] for piece in range(tiles.shape[0])], axis=1)


def set_edges(padded, length):
    zero = jnp.zeros((margin, padded.shape[1]), jnp.float32)
    padded[:margin, :] = zero
    padded[margin + length :, :] = zero


def front_kernel(
    sizes,
    geometry,
    length,
    shard_ref,
    code_own,
    ids_own,
    frames_own,
    cot_own,
    books_ref,
    gathered,
    frames_long,
    ids_ref,
    decoded_ref,
    grad_quant_ref,
    picks_ref,
    packed,
    code_ref,
    cot_ref,
    dilated,
    pointwise,
    group,
    strided,
    grad_dilated,
    grad_point,
    grad_group,
    grad_strided,
    streams,
    grad,
    padded,
    columns,
    hidden,
    excited,
    active,
    tiles,
    sems,
    edge_sem,
    keep_sem,
    recv_sem,
    send_sem,
):
    seq, share, blocks = geometry
    wide, high, deep = sizes
    x, y, z, c = place(sizes)
    me = z * wide + x
    greet(sizes)
    sender = Sender(send_sem, (y * 2 + 1 - c, me))
    gathers = [
        Gather(sizes, sender, shard_ref.at[side], gathered.at[:, :, side], recv_sem.at[side])
        for side in range(2)
    ]
    encoder, decoder = gathers
    decoder.own_z()
    decoder.own_x()
    own = length // 2
    half = length // 4
    reach = half // STRIDE
    near = 80
    set_edges(padded, length)
    blank = jnp.zeros((half - near, cot_ref.shape[1]), jnp.float32)
    cot_ref[: half - near, :] = blank
    cot_ref[length - (half - near) :, :] = blank
    outside = jnp.full((margin, lanes), -1, jnp.int32)
    ids_ref[:margin, :] = outside
    ids_ref[margin + length :, :] = outside
    own_copies = [
        pltpu.make_async_copy(frames_own, frames_long.at[half : half + own], keep_sem.at[1]),
        pltpu.make_async_copy(cot_own, cot_ref.at[half : half + own], keep_sem.at[2]),
        pltpu.make_async_copy(
            ids_own, ids_ref.at[margin + half : margin + half + own], keep_sem.at[3]
        ),
        pltpu.make_async_copy(code_own, code_ref.at[:, reach : reach + own // STRIDE], keep_sem.at[4]),
    ]
    for copy in own_copies:
        copy.start()
    edges = [
        (frames_own.at[own - half :], frames_long.at[:half]),
        (cot_own.at[own - near :], cot_ref.at[half - near : half]),
        (ids_own.at[own - half :], ids_ref.at[margin : margin + half]),
        (code_own.at[:, own // STRIDE - reach :], code_ref.at[:, :reach]),
        (frames_own.at[:half], frames_long.at[half + own :]),
        (cot_own.at[:near], cot_ref.at[half + own : half + own + near]),
        (ids_own.at[:half], ids_ref.at[margin + half + own : margin + length]),
        (code_own.at[:, :reach], code_ref.at[:, reach + own // STRIDE :]),
    ]
    edge_copies = []
    for number, (src, dst) in enumerate(edges):
        other = (me + (1 if number < len(edges) // 2 else seq - 1)) % seq
        copy = pltpu.make_async_remote_copy(
            src_ref=src,
            dst_ref=dst,
            send_sem=edge_sem.at[0, number],
            recv_sem=edge_sem.at[1, number],
            device_id=(y * 2 + c, other),
            device_id_type=MESH,
        )
        copy.start()
        edge_copies.append(copy)
    encoder.own_z()
    for k in range(1, deep):
        decoder.from_z(k)
    for k in range(deep):
        decoder.second(k)
    encoder.own_x()
    for k in range(deep):
        decoder.third(k)
        if k > 0:
            encoder.from_z(k)
    for copy in edge_copies:
        copy.wait()
    for copy in own_copies:
        copy.wait()

    @pl.when(me == 0)
    def _():
        ids_ref[margin : margin + half, :] = jnp.full((half, lanes), -1, jnp.int32)

    @pl.when(me == seq - 1)
    def _():
        ids_ref[margin + half + own : margin + length, :] = jnp.full((half, lanes), -1, jnp.int32)

    decoder.last()
    weights = (dilated, pointwise, group, strided)
    grads = (grad_dilated, grad_point, grad_group, grad_strided)
    mover = Mover(1, geometry, me, shard_ref, gathered, packed, weights, grads, sems)
    for kind in (2, 3, 0, 1):
        mover.start_loads(kind)
    pump = [functools.partial(encoder.second, k) for k in range(deep)]
    pump += [functools.partial(encoder.third, k) for k in range(deep)]
    first, last = length // 4, 3 * length // 4
    latents = length // STRIDE
    codes = books_ref.shape[2]
    width = books_ref.shape[3]
    tile_range = lax.broadcasted_iota(jnp.int32, (latents, lanes), 1)
    quantized = []
    for g in range(GROUPS):
        picked = []
        for level in range(LEVELS):
            entry = g * LEVELS + level
            chosen = code_ref[entry]
            hot = jnp.concatenate(
                [
                    (chosen == tile_range + tile * lanes).astype(jnp.float32)
                    for tile in range(codes // lanes)
                ],
                axis=1,
            )
            pick = jnp.dot(hot, books_ref[g, level], precision=lax.Precision.HIGHEST)
            picks_ref[entry] = pick
            picked.append(pick)
        quantized.append((picked[0] + picked[1]).astype(jnp.bfloat16))
    mover.wait_loads(2)
    out_weights = load_group(group[0], seq, share)
    mixed = [dot(quantized[g], out_weights[g]) for g in range(GROUPS)]
    lifted = [elu(value).astype(jnp.bfloat16) for value in mixed]
    mover.wait_loads(3)
    for tap in range(STRIDE):
        value = dot_last(lifted[0], strided[tap]) + dot_last(lifted[1], strided[STRIDE + tap])
        put_tap(tiles, tap, value)
    streams[0] = from_tiles(tiles)
    mover.wait_loads(0)
    mover.wait_loads(1)
    scratch = (padded, columns, hidden, excited, active)
    pump.pop(0)()
    for unit in range(3):
        forward_unit(
            unit, streams.at[unit], streams.at[unit + 1], ids_ref, (dilated, pointwise), scratch,
            length,
        )
        pump.pop(0)()
    decoded_ref[...] = streams[3, first:last, :].astype(jnp.bfloat16)
    grad[...] = cot_ref[...]

    def store_dilated(unit, tap, value):
        grad_dilated[unit * KERNEL + tap] = value

    def store_point(unit, value):
        grad_point[unit] = value

    for unit in (2, 1, 0):
        backward_unit(
            unit, grad, streams.at[unit], ids_ref, (dilated, pointwise), scratch, length,
            store_dilated, store_point,
        )
        for owner in range(seq):
            mover.store(0, owner, unit * KERNEL, KERNEL).start()
        if pump:
            pump.pop(0)()
    for owner in range(seq):
        mover.store(1, owner, 0, 3).start()
    own = slice(first // STRIDE, last // STRIDE)
    grad_lifted = [None, None]
    to_tiles(tiles, grad[...])
    for tap in range(STRIDE):
        part = take_tap(tiles, tap, latents)
        low = part.astype(jnp.bfloat16)
        turned = part[own].T.astype(jnp.bfloat16)
        for half in range(2):
            value = dot(low, strided[half * STRIDE + tap])
            grad_lifted[half] = value if tap == 0 else grad_lifted[half] + value
            grad_strided[half * STRIDE + tap] = dot(turned, lifted[half][own]).astype(jnp.bfloat16)
    for owner in range(seq):
        mover.store(3, owner, 0, 2 * STRIDE).start()
    group_grads = []
    for g in range(GROUPS):
        low = (grad_lifted[g] * elu_slope(mixed[g])).astype(jnp.bfloat16)
        group_grads.append(dot_rows(quantized[g][own], low[own]))
        grad_quant_ref[g] = dot_last(low, out_weights[g])
    grad_group[0] = store_group(group_grads, seq, share).reshape(grad_group.shape[1:])
    for owner in range(seq):
        mover.store(2, owner, 0, 1).start()
    while pump:
        pump.pop(0)()
    finish_stores(mover, seq)
    encoder.last()
    sender.finish()


def finish_stores(mover, seq):
    for owner in range(seq):
        for unit in range(3):
            mover.store(0, owner, unit * KERNEL, KERNEL).wait()
        mover.store(1, owner, 0, 3).wait()
        mover.store(3, owner, 0, 2 * STRIDE).wait()
        mover.store(2, owner, 0, 1).wait()


def back_kernel(
    sizes,
    geometry,
    length,
    frames_ref,
    ids_ref,
    grad_quant_ref,
    picks_ref,
    shard_ref,
    gathered,
    partial_ref,
    frames_grad_ref,
    rows_ref,
    packed,
    share_ref,
    dilated,
    pointwise,
    group,
    strided,
    grad_dilated,
    grad_point,
    grad_group,
    grad_strided,
    streams,
    grad,
    padded,
    columns,
    hidden,
    excited,
    active,
    tiles,
    sems,
    *refs,
):
    seq, share, blocks = geometry
    x, y, z, c = place(sizes)
    me = z * sizes[0] + x
    greet(sizes)
    sender = Sender(refs[-1], (y * 2 + 1 - c, me))
    side = Reduce(sizes, sender, partial_ref, share_ref, refs[:reduce_parts])
    side.start()
    pump = [functools.partial(side.turn, number) for number in range(sizes[2] + 2)]
    pump += [side.total, side.last]
    weights = (dilated, pointwise, group, strided)
    grads = (grad_dilated, grad_point, grad_group, grad_strided)
    mover = Mover(0, geometry, me, shard_ref, gathered, packed, weights, grads, sems)
    for kind in (0, 1, 3, 2):
        mover.start_loads(kind)
    set_edges(padded, length)
    first, last = length // 4, 3 * length // 4
    latents = length // STRIDE
    own = slice(first // STRIDE, last // STRIDE)
    width = picks_ref.shape[2]
    streams[0] = frames_ref[...].astype(jnp.float32)
    mover.wait_loads(0)
    mover.wait_loads(1)
    scratch = (padded, columns, hidden, excited, active)
    for unit in range(3):
        forward_unit(
            unit, streams.at[unit], streams.at[unit + 1], ids_ref, (dilated, pointwise), scratch,
            length,
        )
        pump.pop(0)()
    to_tiles(tiles, elu(streams[3]))
    mover.wait_loads(3)
    mover.wait_loads(2)
    in_weights = load_group(group[0], seq, share)
    latent = [None, None]
    for tap in range(STRIDE):
        low = take_tap(tiles, tap, latents).astype(jnp.bfloat16)
        for half in range(2):
            value = dot(low, strided[half * STRIDE + tap])
            latent[half] = value if tap == 0 else latent[half] + value
    group_grads = []
    grad_latent = []
    for g in range(GROUPS):
        low = latent[g].astype(jnp.bfloat16)
        first_part = dot(low, in_weights[g])
        pick = [picks_ref[g * LEVELS + level] for level in range(LEVELS)]
        second_part = first_part - pick[0]
        rows_ref[:, (g * LEVELS) * width : (g * LEVELS + 1) * width] = first_part[own].astype(jnp.bfloat16)
        rows_ref[:, (g * LEVELS + 1) * width : (g * LEVELS + 2) * width] = second_part[own].astype(jnp.bfloat16)
        grad_first = grad_quant_ref[g] + 2.0 * commit_weight * (
            second_part + (second_part - pick[1])
        )
        low_first = grad_first.astype(jnp.bfloat16)
        group_grads.append(dot_rows(low[own], low_first[own]))
        grad_latent.append(dot_last(low_first, in_weights[g]).astype(jnp.bfloat16))
    grad_group[0] = store_group(group_grads, seq, share).reshape(grad_group.shape[1:])
    for owner in range(seq):
        mover.store(2, owner, 0, 1).start()
    for tap in range(STRIDE):
        turned = take_tap(tiles, tap, latents)[own].T.astype(jnp.bfloat16)
        value = dot_last(grad_latent[0], strided[tap]) + dot_last(
            grad_latent[1], strided[STRIDE + tap]
        )
        put_tap(tiles, tap, value)
        for half in range(2):
            grad_strided[half * STRIDE + tap] = dot(turned, grad_latent[half][own]).astype(
                jnp.bfloat16
            )
    for owner in range(seq):
        mover.store(3, owner, 0, 2 * STRIDE).start()
    grad[...] = from_tiles(tiles) * elu_slope(streams[3])
    pump.pop(0)()

    def store_dilated(unit, tap, value):
        grad_dilated[unit * KERNEL + tap] = value

    def store_point(unit, value):
        grad_point[unit] = value

    for unit in (2, 1, 0):
        backward_unit(
            unit, grad, streams.at[unit], ids_ref, (dilated, pointwise), scratch, length,
            store_dilated, store_point,
        )
        for owner in range(seq):
            mover.store(0, owner, unit * KERNEL, KERNEL).start()
        if pump:
            pump.pop(0)()
    for owner in range(seq):
        mover.store(1, owner, 0, 3).start()
    frames_grad_ref[...] = grad[first:last, :]
    finish_stores(mover, seq)
    while pump:
        pump.pop(0)()
    sender.finish()


def side_scratch(seq, share, length, channels, hidden):
    bf, f32 = jnp.bfloat16, jnp.float32
    group_rows = GROUPS * hidden // seq
    mats = [
        pltpu.VMEM((3 * KERNEL, channels, hidden), bf),
        pltpu.VMEM((3, channels, hidden), bf),
        pltpu.VMEM((1, seq * group_rows, hidden), bf),
        pltpu.VMEM((2 * STRIDE, channels, hidden), bf),
    ]
    return mats + list(mats) + [
        pltpu.VMEM((4, length, channels), f32),
        pltpu.VMEM((length, channels), f32),
        pltpu.VMEM((length + 2 * margin, channels), f32),
        pltpu.VMEM((length, KERNEL * channels), bf),
        pltpu.VMEM((3, length, hidden), f32),
        pltpu.VMEM((3, length, hidden), bf),
        pltpu.VMEM((3, length // 2, channels), bf),
        pltpu.VMEM((channels // lanes, length, lanes), f32),
        pltpu.SemaphoreType.DMA((8, seq)),
    ]


def split_terms(value, count):
    terms = []
    for number in range(count):
        term = value.astype(jnp.bfloat16)
        terms.append(term)
        if number < count - 1:
            value = value - term.astype(jnp.float32)
    return terms


def product(left, right):
    def pair(i, j):
        return jnp.dot(left[i], right[j], preferred_element_type=jnp.float32)

    low = pair(0, 1) + pair(1, 0)
    if len(left) > 2:
        low = low + (pair(1, 1) + pair(0, 2) + pair(2, 0))
    return pair(0, 0) + low


def gram_of(left, right):
    return product(split_terms(left.T, 3), split_terms(right, 3))


def solve_mixing(gram):
    size = gram.shape[0]
    eye = (
        lax.broadcasted_iota(jnp.int32, (size, size), 0)
        == lax.broadcasted_iota(jnp.int32, (size, size), 1)
    ).astype(jnp.float32)
    scale = 1.0 / (jnp.sqrt(jnp.sum(gram * eye)) + norm_floor)
    current = gram * (scale * scale)
    total = None
    for repeat in range(NS_STEPS):
        terms = 3 if repeat < 2 else 2
        parts = split_terms(current, terms)
        factor = coef_first * eye + coef_second * current + coef_third * product(parts, parts)
        factors = split_terms(factor, terms)
        if total is None:
            total = factor
        else:
            total = product(split_terms(total, 2), factors[:2])
        if repeat < NS_STEPS - 1:
            half = split_terms(product(parts, factors), terms)
            current = product(half, factors)
    return total * scale


def mixing_kernel(
    sizes,
    share,
    enc_dilated,
    enc_point,
    enc_group,
    enc_strided,
    dec_dilated,
    dec_point,
    dec_group,
    dec_strided,
    enc_dilated_w,
    enc_strided_w,
    dec_dilated_w,
    dec_strided_w,
    small_ref,
    enc_dilated_next,
    enc_strided_next,
    dec_dilated_next,
    dec_strided_next,
    mix_ref,
    dilated,
    point,
    group,
    strided,
    dilated_w,
    strided_w,
    blocks,
    corner,
    slots,
    point_all,
    group_all,
    work,
    point_done,
    group_done,
    load_sem,
    send_sem,
    slot_sem,
    rows_sem,
    mix_sem,
    small_sem,
    corner_sem,
):
    wide, high, deep = sizes
    x, y, z, c = place(sizes)
    count = wide * deep
    me = z * wide + x
    row = y * 2 + c
    middle = count // 2
    partner = (y * 2 + 1 - c, me)
    others = [(row, (me + k) % count) for k in range(1, count)]
    others += [((y + k) % high * 2 + c, me) for k in range(1, high)] + [partner]
    barrier = pltpu.get_barrier_semaphore()
    for other in others:
        pl.semaphore_signal(barrier, inc=1, device_id=other, device_id_type=MESH)
    pl.semaphore_wait(barrier, len(others))

    pending = []

    def remote(src, dst, number, recv, to):
        return pltpu.make_async_remote_copy(
            src_ref=src,
            dst_ref=dst,
            send_sem=send_sem.at[number],
            recv_sem=recv,
            device_id=to,
            device_id_type=MESH,
        )

    def send(when, src, dst, recv, to):
        number = len(pending)
        pending.append((when, src, dst, recv, to))

        @pl.when(when)
        def _():
            remote(src, dst, number, recv, to).start()

    def arrive(dst, recv):
        remote(dst, dst, 0, recv, partner).wait_recv()

    first_set = y == 0
    second_set = y == 1

    def load(number, source, target):
        return pltpu.make_async_copy(source, target, load_sem.at[number])

    own_loads = [
        (enc_dilated, dilated.at[0]),
        (dec_dilated, dilated.at[1]),
        (enc_strided, strided.at[0]),
        (dec_strided, strided.at[1]),
        (enc_point, point.at[0]),
        (dec_point, point.at[1]),
        (enc_group, group.at[0]),
        (dec_group, group.at[1]),
        (enc_dilated_w, dilated_w.at[0]),
        (dec_dilated_w, dilated_w.at[1]),
        (enc_strided_w, strided_w.at[0]),
        (dec_strided_w, strided_w.at[1]),
    ]
    for number, (source, target) in enumerate(own_loads):
        load(number, source, target).start()
    for number in (4, 5, 6, 7, 2, 3, 0, 1):
        load(number, *own_loads[number]).wait()

    block_at = [middle - 2 + number + c for number in range(3)]
    strided_at = block_at[1]
    small_at = [(middle + c + offset + count) % count for offset in (1, 2, 3, -3, -4)]
    point_at, group_at = small_at[:3], small_at[3:]
    part = share // GROUPS

    for unit in range(3):
        at = point_at[unit]
        rows = pl.ds(pl.multiple_of(me * share, 8), share)
        send(
            second_set & (me != at),
            point.at[c, unit],
            point_all.at[rows],
            rows_sem.at[me],
            (row, at),
        )

        @pl.when(second_set & (me == at))
        def _():
            point_all[rows, :] = point[c, unit]

    for g in range(GROUPS):
        at = group_at[g]
        rows = pl.ds(pl.multiple_of(me * part, 8), part)
        send(
            second_set & (me != at),
            group.at[c, g],
            group_all.at[rows],
            rows_sem.at[me],
            (row, at),
        )

        @pl.when(second_set & (me == at))
        def _():
            group_all[rows, :] = group[c, g]

    block = blocks.shape[1]

    @pl.when(first_set)
    def _():
        for unit in range(3):
            value = dilated[c, unit * KERNEL : (unit + 1) * KERNEL].reshape(KERNEL * share, block)
            blocks[unit] = gram_of(value, value)

    @pl.when(second_set)
    def _():
        value = strided[c].reshape(-1, 2 * block)
        left, right = value[:, :block], value[:, block:]
        blocks[0] = gram_of(left, left)
        blocks[1] = gram_of(left, right)
        blocks[2] = gram_of(right, right)

    for number in range(3):
        at = block_at[number]
        send(
            (first_set | second_set) & (me != at),
            blocks.at[number],
            slots.at[number, me],
            slot_sem.at[number, me],
            (row, at),
        )

    def summed(number):
        total = blocks[number]
        for k in range(1, count):
            source = (me + k) % count
            arrive(slots.at[number, source], slot_sem.at[number, source])
            total = total + slots[number, source]
        return total

    for number in range(3):

        @pl.when((first_set | second_set) & (me == block_at[number]))
        def _():
            work[...] = summed(number)

    for number in (0, 2):
        send(
            second_set & (me == block_at[number]),
            work,
            corner.at[number // 2],
            corner_sem.at[number // 2],
            (row, strided_at),
        )

    @pl.when(second_set & (me == strided_at))
    def _():
        for number in range(2):
            arrive(corner.at[number], corner_sem.at[number])
        side = work[...]
        gram = jnp.concatenate(
            [
                jnp.concatenate([corner[0], side], axis=1),
                jnp.concatenate([side.T, corner[1]], axis=1),
            ],
            axis=0,
        )
        mixing = solve_mixing(gram)
        mix_ref[1, c, 0] = mixing[:block, :block]
        mix_ref[1, c, 1] = mixing[:block, block:]
        mix_ref[1, c, 2] = mixing[block:, block:]

    def hand_first(which, number, at):
        spot = mix_ref.at[which, c, number]
        owner = (y == which) & (me == at)
        for k in range(1, deep):
            to = (row, (z + k) % deep * wide + x)
            send(owner, spot, spot, mix_sem.at[which, c, number], to)

    for number in range(3):
        hand_first(1, number, strided_at)

    is_point = second_set & (
        (me == point_at[0]) | (me == point_at[1]) | (me == point_at[2])
    )
    is_group = second_set & ((me == group_at[0]) | (me == group_at[1]))
    is_dilated = first_set & (
        (me == block_at[0]) | (me == block_at[1]) | (me == block_at[2])
    )

    @pl.when(is_point)
    def _():
        for k in range(1, count):
            source = (me + k) % count
            rows = pl.ds(pl.multiple_of(source * share, 8), share)
            arrive(point_all.at[rows], rows_sem.at[source])
        work[...] = gram_of(point_all[...], point_all[...])

    @pl.when(is_group)
    def _():
        for k in range(1, count):
            source = (me + k) % count
            rows = pl.ds(pl.multiple_of(source * part, 8), part)
            arrive(group_all.at[rows], rows_sem.at[source])
        work[...] = gram_of(group_all[...], group_all[...])

    @pl.when(is_dilated | is_point | is_group)
    def _():
        work[...] = solve_mixing(work[...])

    for unit in range(3):

        @pl.when(first_set & (me == block_at[unit]))
        def _():
            mix_ref[0, c, unit] = work[...]

        hand_first(0, unit, block_at[unit])

    @pl.when(is_point)
    def _():
        point_done[...] = product(split_terms(point_all[...], 3), split_terms(work[...], 3))

    @pl.when(is_group)
    def _():
        group_done[...] = product(split_terms(group_all[...], 3), split_terms(work[...], 3))

    for unit in range(3):
        at = point_at[unit]
        for k in range(1, count):
            target = (me + k) % count
            rows = pl.ds(pl.multiple_of(target * share, 8), share)
            send(
                second_set & (me == at),
                point_done.at[rows],
                small_ref.at[c, unit],
                small_sem.at[unit],
                (row, target),
            )

        @pl.when(second_set & (me == at))
        def _():
            small_ref[c, unit] = point_done[pl.ds(pl.multiple_of(me * share, 8), share), :]

        @pl.when(second_set & (me != at))
        def _():
            arrive(small_ref.at[c, unit], small_sem.at[unit])

    for g in range(GROUPS):
        at = group_at[g]
        spot = small_ref.at[c, 3, g * part : (g + 1) * part]
        for k in range(1, count):
            target = (me + k) % count
            rows = pl.ds(pl.multiple_of(target * part, 8), part)
            send(
                second_set & (me == at),
                group_done.at[rows],
                spot,
                small_sem.at[3 + g],
                (row, target),
            )

        @pl.when(second_set & (me == at))
        def _():
            spot[...] = group_done[pl.ds(pl.multiple_of(me * part, 8), part), :]

        @pl.when(second_set & (me != at))
        def _():
            arrive(spot, small_sem.at[3 + g])

    for k in range(1, high):
        send(
            second_set,
            small_ref.at[c],
            small_ref.at[c],
            small_sem.at[5],
            ((y + k) % high * 2 + c, me),
        )

    @pl.when(jnp.logical_not(second_set))
    def _():
        arrive(small_ref.at[c], small_sem.at[5])

    always = y >= 0
    send(always, small_ref.at[c], small_ref.at[c], small_sem.at[6], partner)

    def hand_out(which, number, at):
        spot = mix_ref.at[which, c, number]
        recv = mix_sem.at[which, c, number]
        mine = y == which
        at_x = at % wide
        owner = mine & (me == at)

        @pl.when(jnp.logical_not(owner))
        def _():
            arrive(spot, recv)

        for k in range(1, wide):
            send(mine & (x == at_x), spot, spot, recv, (row, z * wide + (x + k) % wide))
        for k in range(1, high):
            send(mine, spot, spot, recv, ((y + k) % high * 2 + c, me))
        send(always, spot, spot, recv, partner)

    for unit in range(3):
        hand_out(0, unit, block_at[unit])
    arrive(small_ref.at[1 - c], small_sem.at[6])
    for unit in range(3):
        arrive(mix_ref.at[0, 1 - c, unit], mix_sem.at[0, 1 - c, unit])
    for number in range(8, 12):
        load(number, *own_loads[number]).wait()
    for side, target in enumerate((enc_dilated_next, dec_dilated_next)):
        for unit in range(3):
            taps = slice(unit * KERNEL, (unit + 1) * KERNEL)
            rows = dilated[side, taps].reshape(KERNEL * share, block)
            moved = product(split_terms(rows, 2), split_terms(mix_ref[0, side, unit], 2))
            target[taps] = dilated_w[side, taps] - update_rate * moved.reshape(
                KERNEL, share, block
            )
    for number in range(3):
        hand_out(1, number, strided_at)
    for number in range(3):
        arrive(mix_ref.at[1, 1 - c, number], mix_sem.at[1, 1 - c, number])
    for side, target in enumerate((enc_strided_next, dec_strided_next)):
        corners = [split_terms(mix_ref[1, side, number], 2) for number in range(3)]
        turned = split_terms(mix_ref[1, side, 1].T, 2)
        rows = strided[side].reshape(-1, 2 * block)
        left, right = split_terms(rows[:, :block], 2), split_terms(rows[:, block:], 2)
        low = product(left, corners[0]) + product(right, turned)
        top = product(left, corners[1]) + product(right, corners[2])
        shape = (strided.shape[1], share, block)
        target[:, :, :block] = strided_w[side, :, :, :block] - update_rate * low.reshape(shape)
        target[:, :, block:] = strided_w[side, :, :, block:] - update_rate * top.reshape(shape)

    for number, (when, src, dst, recv, to) in enumerate(pending):

        @pl.when(when)
        def _():
            remote(src, dst, number, recv, to).wait_send()


def solve_all(views, weights, sizes, collective_id):
    wide, high, deep = sizes
    count = wide * deep
    share, block = views[0].shape[1:]
    part = share // GROUPS
    f32 = jnp.float32
    dma = pltpu.SemaphoreType.DMA
    sends = 5 + 3 + 2 + 5 * (count - 1) + (high - 1) + 1 + 6 * (deep - 1 + wide - 1 + high)
    vmem = pl.BlockSpec(memory_space=pltpu.VMEM)
    return pl.pallas_call(
        functools.partial(mixing_kernel, sizes, share),
        out_shape=(jax.ShapeDtypeStruct((2, 4, share, block), f32),)
        + tuple(jax.ShapeDtypeStruct(weight.shape, f32) for weight in weights),
        in_specs=[pl.BlockSpec(memory_space=pl.ANY)] * 12,
        out_specs=(vmem,) * 5,
        scratch_shapes=[
            pltpu.VMEM((2, 2, 3, block, block), f32),
            pltpu.VMEM((2,) + views[0].shape, f32),
            pltpu.VMEM((2,) + views[1].shape, f32),
            pltpu.VMEM((2,) + views[2].shape, f32),
            pltpu.VMEM((2,) + views[3].shape, f32),
            pltpu.VMEM((2,) + views[0].shape, f32),
            pltpu.VMEM((2,) + views[3].shape, f32),
            pltpu.VMEM((3, block, block), f32),
            pltpu.VMEM((2, block, block), f32),
            pltpu.VMEM((3, count, block, block), f32),
            pltpu.VMEM((count * share, block), f32),
            pltpu.VMEM((count * part, block), f32),
            pltpu.VMEM((block, block), f32),
            pltpu.VMEM((count * share, block), f32),
            pltpu.VMEM((count * part, block), f32),
            dma((12,)),
            dma((sends,)),
            dma((3, count)),
            dma((count,)),
            dma((2, 2, 3)),
            dma((7,)),
            dma((2,)),
        ],
        compiler_params=pltpu.CompilerParams(
            collective_id=collective_id, has_side_effects=True, vmem_limit_bytes=60 * 2**20
        ),
    )(*views, *weights)


def per_device(
    frames,
    cotangent,
    segment_ids,
    code_index,
    codebooks,
    dead_codes,
    code_slots,
    buffered,
    encoder_dilated,
    encoder_pointwise,
    down_weight,
    group_in,
    group_out,
    up_weight,
    decoder_dilated,
    decoder_pointwise,
    encoder_dilated_moment,
    encoder_pointwise_moment,
    down_moment,
    group_in_moment,
    group_out_moment,
    up_moment,
    decoder_dilated_moment,
    decoder_pointwise_moment,
):
    masters = (
        encoder_dilated,
        encoder_pointwise,
        down_weight,
        group_in,
        group_out,
        up_weight,
        decoder_dilated,
        decoder_pointwise,
    )
    olds = (
        encoder_dilated_moment,
        encoder_pointwise_moment,
        down_moment,
        group_in_moment,
        group_out_moment,
        up_moment,
        decoder_dilated_moment,
        decoder_pointwise_moment,
    )
    lowered = [weight.astype(jnp.bfloat16) for weight in masters]
    count = lax.axis_size("seq")
    sizes = line_sizes(count, lax.axis_size("dp"))
    sides = ((0, 1, 3, 2), (6, 7, 4, 5))
    packed = []
    for side in sides:
        parts = [lowered[i] for i in side[:3]] + [halves(lowered[side[3]])]
        packed.append(pack_side(*parts, sizes[1], masters[0].shape[2], 0))
    side_rows = packed[0].shape[0]
    wide, high, deep = sizes
    _, length, channels = frames.shape
    long = 2 * length
    latent_len = long // STRIDE
    place_seq = lax.axis_index("seq")
    hidden = encoder_dilated.shape[-1]
    share = masters[0].shape[2]
    blocks = side_rows // share
    geometry = (count, share, blocks)
    rows = side_rows // (4 * high)
    part_shapes = []
    for side in sides:
        shapes = [masters[i].shape for i in side[:3]]
        taps, _, width = masters[side[3]].shape
        shapes.append((2, taps, share, width // 2))
        part_shapes.append(shapes)
    low, f32 = jnp.bfloat16, jnp.float32
    dma = pltpu.SemaphoreType.DMA
    ids_own = jnp.broadcast_to(segment_ids[0][:, None], (length, lanes))
    entries = GROUPS * LEVELS
    code_own = code_index[0].reshape(-1, entries).T
    code_own = jnp.broadcast_to(code_own[:, :, None], code_own.shape + (lanes,))
    vmem = pl.BlockSpec(memory_space=pltpu.VMEM)
    anywhere = pl.BlockSpec(memory_space=pl.ANY)
    partial_type = jax.ShapeDtypeStruct((count, blocks, share, hidden), low)
    scratch = side_scratch(count, share, long, channels, hidden)
    shard = jnp.stack(packed).reshape(2, 2, high, 2, rows, hidden)
    gathered, frames_long, ids, decoded, grad_quant, picks, partial = pl.pallas_call(
        functools.partial(front_kernel, sizes, geometry, long),
        out_shape=(
            jax.ShapeDtypeStruct((deep, wide) + shard.shape, low),
            jax.ShapeDtypeStruct((long, channels), frames.dtype),
            jax.ShapeDtypeStruct((long + 2 * margin, lanes), jnp.int32),
            jax.ShapeDtypeStruct((length, channels), low),
            jax.ShapeDtypeStruct((GROUPS, latent_len, hidden), f32),
            jax.ShapeDtypeStruct((entries, latent_len, hidden), f32),
            partial_type,
        ),
        in_specs=[anywhere] * 5 + [vmem],
        out_specs=(anywhere, vmem, vmem, vmem, vmem, vmem, anywhere),
        scratch_shapes=[
            pltpu.VMEM((entries, latent_len, lanes), jnp.int32),
            pltpu.VMEM((long, channels), f32),
        ]
        + scratch
        + [
            dma((2, 8)),
            dma((5,)),
            dma((2, deep, wide, 2, high, 2)),
            dma((2 * gather_sends(sizes),)),
        ],
        compiler_params=pltpu.CompilerParams(
            collective_id=0, has_side_effects=True, vmem_limit_bytes=60 * 2**20
        ),
    )(shard, code_own, ids_own, frames[0], cotangent[0], codebooks)
    grad, latent_rows, partial_encoder, share_decoder = pl.pallas_call(
        functools.partial(back_kernel, sizes, geometry, long),
        out_shape=(
            jax.ShapeDtypeStruct((length, channels), f32),
            jax.ShapeDtypeStruct((length // STRIDE, entries * hidden), low),
            partial_type,
            jax.ShapeDtypeStruct((2, high, 2, rows, hidden), low),
        ),
        in_specs=[vmem, vmem, vmem, vmem, anywhere, anywhere, anywhere],
        out_specs=(vmem, vmem, anywhere, anywhere),
        scratch_shapes=scratch
        + reduce_scratch(sizes, rows, hidden, low, low)
        + [dma((reduce_sends(sizes),))],
        compiler_params=pltpu.CompilerParams(
            collective_id=1, has_side_effects=True, vmem_limit_bytes=60 * 2**20
        ),
    )(
        frames_long, ids, grad_quant, picks, shard, gathered,
        partial.reshape(deep, wide, 2, high, 2, rows, hidden),
    )
    decoded = decoded[None]
    grad = grad[None]
    own_codes_low = code_index[0].reshape(-1, entries)
    digits = jnp.concatenate([own_codes_low // 32, own_codes_low % 32], axis=1)
    digits = jnp.pad(digits, ((0, 0), (0, lanes - digits.shape[1]))).astype(low)
    share_encoder, all_rows = reduce_rows(
        partial_encoder.reshape(count, side_rows, hidden),
        jnp.concatenate([latent_rows, digits], axis=1),
        sizes,
        f32,
        3,
    )
    side_shares = (share_encoder, share_decoder.reshape(side_rows, hidden))
    all_rows = all_rows.reshape(-1, all_rows.shape[-1])
    digits = all_rows[:, entries * hidden :].astype(jnp.int32)
    all_codes = digits[:, :4] * 32 + digits[:, 4:8]
    group_width = hidden
    digits = all_rows[:, GROUPS * LEVELS * hidden :].astype(jnp.int32)
    all_codes = digits[:, :4] * 32 + digits[:, 4:8]
    code_share = dead_codes.shape[2]
    own_range = lax.broadcasted_iota(
        jnp.int32, (1, code_share), 1
    ) + code_share * place_seq
    sum_list = []
    count_list = []
    for entry in range(GROUPS * LEVELS):
        own_hot = (all_codes[:, entry : entry + 1] == own_range).astype(jnp.bfloat16)
        sum_list.append(
            lax.dot_general(
                own_hot,
                all_rows[:, entry * group_width : (entry + 1) * group_width],
                (((0,), (0,)), ((), ())),
                preferred_element_type=jnp.float32,
            )
        )
        count_list.append(jnp.sum(own_hot.astype(jnp.float32), axis=0))
    total_sums = jnp.stack(sum_list).reshape(GROUPS, LEVELS, code_share, group_width)
    total_counts = jnp.stack(count_list).reshape(GROUPS, LEVELS, code_share)
    reduced = [None] * 8
    for at, side in enumerate(sides):
        parts = take_side(side_shares[at], part_shapes[at])
        for i, part in zip(side[:3], parts):
            reduced[i] = part.astype(jnp.float32)
        reduced[side[3]] = jnp.concatenate([parts[3][0], parts[3][1]], axis=-1).astype(jnp.float32)
    own_codes = lax.dynamic_slice_in_dim(
        codebooks, lax.axis_index("seq") * code_share, code_share, 2
    )
    code_means = total_sums / jnp.maximum(total_counts, 1.0)[..., None]
    code_used = jnp.minimum(total_counts, 1.0)[..., None]
    updated = own_codes + code_rate * code_used * (code_means - own_codes)
    slot_range = lax.broadcasted_iota(jnp.int32, (1, 1, 1, buffered.shape[1]), 3)
    slot_onehot = (code_slots[..., None] == slot_range).astype(jnp.float32)
    replaced = jnp.einsum("glsb,gbz->glsz", slot_onehot, buffered, precision=highest)
    new_codebooks = jnp.where(dead_codes[..., None] == 1, replaced, updated)
    velocities = tuple((moment_decay * olds[position] + reduced[position] for position in range(8)))
    views = []
    for side in sides:
        dilated_v, point_v, group_v, strided_v = [velocities[i] for i in side]
        views += [dilated_v.reshape((-1,) + dilated_v.shape[2:]), point_v, group_v, strided_v]
    flat = [masters[i].reshape((-1,) + masters[i].shape[-2:]) for i in (0, 2, 6, 5)]
    small, *moved = solve_all(views, flat, sizes, 2)
    nexts = [None] * 8
    for i, value in zip((0, 2, 6, 5), moved):
        nexts[i] = value.reshape(masters[i].shape)
    for at, side in enumerate(sides):
        _, point, group, _ = side
        nexts[point] = masters[point] - update_rate * small[at, :3]
        nexts[group] = masters[group] - update_rate * small[at, 3].reshape(masters[group].shape)
    return (
        decoded,
        grad,
        new_codebooks,
        velocities[0],
        velocities[1],
        velocities[2],
        velocities[3],
        velocities[4],
        velocities[5],
        velocities[6],
        velocities[7],
        nexts[0],
        nexts[1],
        nexts[2],
        nexts[3],
        nexts[4],
        nexts[5],
        nexts[6],
        nexts[7],
    )


def solution(mesh):
    in_specs = (
        P("dp", "seq", None),
        P("dp", "seq", None),
        P("dp", "seq"),
        P("dp", "seq", None, None),
        P(),
        P(None, None, "seq"),
        P(None, None, "seq"),
        P(),
        P(None, None, "seq", None),
        P(None, "seq", None),
        P(None, "seq", None),
        P(None, "seq", None),
        P(None, "seq", None),
        P(None, "seq", None),
        P(None, None, "seq", None),
        P(None, "seq", None),
        P(None, None, "seq", None),
        P(None, "seq", None),
        P(None, "seq", None),
        P(None, "seq", None),
        P(None, "seq", None),
        P(None, "seq", None),
        P(None, None, "seq", None),
        P(None, "seq", None),
    )
    out_specs = (
        P("dp", "seq", None),
        P("dp", "seq", None),
        P(None, None, "seq", None),
        P(None, None, "seq", None),
        P(None, "seq", None),
        P(None, "seq", None),
        P(None, "seq", None),
        P(None, "seq", None),
        P(None, "seq", None),
        P(None, None, "seq", None),
        P(None, "seq", None),
        P(None, None, "seq", None),
        P(None, "seq", None),
        P(None, "seq", None),
        P(None, "seq", None),
        P(None, "seq", None),
        P(None, "seq", None),
        P(None, None, "seq", None),
        P(None, "seq", None),
    )
    return jax.shard_map(
        per_device, mesh=mesh, in_specs=in_specs, out_specs=out_specs, check_vma=False
    )
```

```python
import functools

import jax
import jax.numpy as jnp
from jax import lax
from jax.experimental import pallas as pl
from jax.experimental.pallas import tpu as pltpu
from jax.sharding import PartitionSpec as P

GROUPS = 2
LEVELS = 2
KERNEL = 7
STRIDE = 8
NS_STEPS = 5


highest = lax.Precision.HIGHEST
dilation_list = (1, 3, 9)
coef_first = 3.4445
coef_second = -4.775
coef_third = 2.0315
commit_weight = 0.25
moment_decay = 0.5
update_rate = 0.5
code_rate = 0.5
norm_floor = 1e-07


def whole_rows(masters, high):
    dilated, pointwise, strided, group = masters[:4]
    share, width = dilated.shape[2:]
    rows = (dilated.size + pointwise.size + strided.size + group.size) // width
    unit = 192 * high
    while unit % share:
        unit += 192 * high
    return -(-rows // unit) * unit


MESH = pl.DeviceIdType.MESH


def line_sizes(seq, dp):
    across = 1
    while (2 * across) * (2 * across) <= seq:
        across *= 2
    return across, dp // 2, seq // across


def place(sizes):
    wide, high, _ = sizes
    row = lax.axis_index("dp")
    part = lax.axis_index("seq")
    return part % wide, row // 2, part // wide, row % 2


def greet(sizes):
    wide, high, deep = sizes
    x, y, z, c = place(sizes)
    barrier = pltpu.get_barrier_semaphore()
    others = [(y * 2 + 1 - c, z * wide + x)]
    others += [(y * 2 + c, z * wide + (x + k) % wide) for k in range(1, wide)]
    others += [((y + k) % high * 2 + c, z * wide + x) for k in range(1, high)]
    others += [(y * 2 + c, (z + k) % deep * wide + x) for k in range(1, deep)]
    count = deep * wide
    others += [(y * 2 + c, (z * wide + x + k) % count) for k in (1, count - 1)]
    for other in others:
        pl.semaphore_signal(barrier, inc=1, device_id=other, device_id_type=MESH)
    pl.semaphore_wait(barrier, len(others))


class Sender:
    def __init__(self, send_sem, partner):
        self.send_sem = send_sem
        self.partner = partner
        self.sent = []

    def send(self, src, dst, recv, to):
        copy = pltpu.make_async_remote_copy(
            src_ref=src,
            dst_ref=dst,
            send_sem=self.send_sem.at[len(self.sent)],
            recv_sem=recv,
            device_id=to,
            device_id_type=MESH,
        )
        copy.start()
        self.sent.append(copy)

    def arrive(self, dst, recv):
        pltpu.make_async_remote_copy(
            src_ref=dst,
            dst_ref=dst,
            send_sem=self.send_sem.at[0],
            recv_sem=recv,
            device_id=self.partner,
            device_id_type=MESH,
        ).wait_recv()

    def finish(self):
        for copy in self.sent:
            copy.wait_send()


class Gather:
    def __init__(self, sizes, sender, in_ref, out_ref, recv_sem):
        self.sizes = sizes
        self.place = place(sizes)
        self.sender = sender
        self.in_ref, self.out_ref, self.recv_sem = in_ref, out_ref, recv_sem

    def send(self, zs, xs, ys, h, to, source=None):
        c = self.place[3]
        spot = self.out_ref.at[zs, xs, c, ys, h]
        src = spot if source is None else source
        self.sender.send(src, spot, self.recv_sem.at[zs, xs, c, ys, h], to)

    def arrive(self, zs, xs, cs, ys, h):
        self.sender.arrive(self.out_ref.at[zs, xs, cs, ys, h], self.recv_sem.at[zs, xs, cs, ys, h])

    def to_x(self, zs, xs, ys, h, source=None):
        wide, high, deep = self.sizes
        x, y, z, c = self.place
        for k in range(1, wide):
            self.send(zs, xs, ys, h, (y * 2 + c, z * wide + (x + k) % wide), source)

    def to_y(self, zs, xs, ys, h):
        wide, high, deep = self.sizes
        x, y, z, c = self.place
        for k in range(1, high):
            self.send(zs, xs, ys, h, ((y + k) % high * 2 + c, z * wide + x))

    def to_core(self, zs, xs, ys, h):
        wide, high, deep = self.sizes
        x, y, z, c = self.place
        self.send(zs, xs, ys, h, (y * 2 + 1 - c, z * wide + x))

    def own_z(self):
        wide, high, deep = self.sizes
        x, y, z, c = self.place
        for k in range(deep - 1, 0, -1):
            for h in range(2):
                to = (y * 2 + c, (z + k) % deep * wide + x)
                self.send(z, x, y, h, to, self.in_ref.at[c, y, h])

    def own_x(self):
        wide, high, deep = self.sizes
        x, y, z, c = self.place
        self.to_x(z, x, y, 0, self.in_ref.at[c, y, 0])
        for j in range(high):
            ys = (y + j) % high
            self.to_x(z, x, ys, 1, self.in_ref.at[c, ys, 1])

    def from_z(self, k):
        x, y, z, c = self.place
        zs = (z + k) % self.sizes[2]
        self.arrive(zs, x, c, y, 0)
        self.to_x(zs, x, y, 0)
        self.to_y(zs, x, y, 0)
        self.to_core(zs, x, y, 0)
        self.arrive(zs, x, c, y, 1)
        self.to_y(zs, x, y, 1)
        self.to_x(zs, x, y, 1)
        self.to_core(zs, x, y, 1)

    def second(self, k):
        wide, high, deep = self.sizes
        x, y, z, c = self.place
        zs = (z + k) % deep
        for i in range(1, wide):
            xs = (x + i) % wide
            self.arrive(zs, xs, c, y, 0)
            self.to_y(zs, xs, y, 0)
            self.to_core(zs, xs, y, 0)
        if k > 0:
            for j in range(1, high):
                ys = (y + j) % high
                self.arrive(zs, x, c, ys, 1)
                self.to_x(zs, x, ys, 1)
                self.to_core(zs, x, ys, 1)

    def third(self, k):
        wide, high, deep = self.sizes
        x, y, z, c = self.place
        zs = (z + k) % deep
        for i in range(wide):
            xs = (x + i) % wide
            if k == 0 and i == 0:
                continue
            for j in range(1, high):
                ys = (y + j) % high
                self.arrive(zs, xs, c, ys, 0)
                self.to_core(zs, xs, ys, 0)
            if i > 0:
                for j in range(high):
                    ys = (y + j) % high
                    self.arrive(zs, xs, c, ys, 1)
                    self.to_core(zs, xs, ys, 1)

    def last(self):
        wide, high, deep = self.sizes
        x, y, z, c = self.place
        for k in range(deep):
            zs = (z + k) % deep
            for i in range(wide):
                xs = (x + i) % wide
                if k == 0 and i == 0:
                    continue
                for j in range(high):
                    for h in range(2):
                        self.arrive(zs, xs, 1 - c, (y + j) % high, h)


def gather_sends(sizes):
    wide, high, deep = sizes
    n = (deep - 1) * 2 + (wide - 1) * (1 + high)
    n += (deep - 1) * 2 * (wide - 1 + high - 1 + 1)
    n += deep * (wide - 1) * high + (deep - 1) * (high - 1) * wide
    n += (deep * wide - 1) * (high - 1) + deep * (wide - 1) * high
    return n


class Spread:
    def __init__(self, sizes, sender, row_ref, all_ref, row_sem, keep_sem):
        self.sizes = sizes
        self.place = place(sizes)
        self.sender = sender
        self.row_ref, self.all_ref, self.row_sem = row_ref, all_ref, row_sem
        x, y, z, c = self.place
        self.keep = pltpu.make_async_copy(row_ref, all_ref.at[z, x, y, c], keep_sem)

    def pass_on(self, zs, xs, ys, to, own):
        c = self.place[3]
        spot = self.all_ref.at[zs, xs, ys, c]
        self.sender.send(self.row_ref if own else spot, spot, self.row_sem.at[zs, xs, ys, c], to)

    def landed(self, zs, xs, ys, cs):
        self.sender.arrive(self.all_ref.at[zs, xs, ys, cs], self.row_sem.at[zs, xs, ys, cs])

    def stage(self, number):
        wide, high, deep = self.sizes
        x, y, z, c = self.place
        columns = [(z + k) % deep for k in range(deep)]
        lines = [(x + k) % wide for k in range(wide)]
        heights = [(y + k) % high for k in range(high)]
        if number == 0:
            self.keep.start()
            for zt in columns[1:]:
                self.pass_on(z, x, y, (y * 2 + c, zt * wide + x), True)
        if number == 1:
            for zs in columns[1:]:
                self.landed(zs, x, y, c)
            for zs in columns:
                for yt in heights[1:]:
                    self.pass_on(zs, x, y, (yt * 2 + c, z * wide + x), zs is columns[0])
        if number == 2:
            for zs in columns:
                for ys in heights[1:]:
                    self.landed(zs, x, ys, c)
            for zs in columns:
                for ys in heights:
                    own = zs is columns[0] and ys is heights[0]
                    for xt in lines[1:]:
                        self.pass_on(zs, x, ys, (y * 2 + c, z * wide + xt), own)
        if number == 3:
            for zs in columns:
                for xs in lines[1:]:
                    for ys in heights:
                        self.landed(zs, xs, ys, c)
            for zs in columns:
                for xs in lines:
                    for ys in heights:
                        own = zs is columns[0] and xs is lines[0] and ys is heights[0]
                        self.pass_on(zs, xs, ys, (y * 2 + 1 - c, z * wide + x), own)
        if number == 4:
            for zs in columns:
                for xs in lines:
                    for ys in heights:
                        self.landed(zs, xs, ys, 1 - c)
            self.keep.wait()


def spread_sends(sizes):
    wide, high, deep = sizes
    return deep - 1 + deep * (high - 1) + deep * high * (wide - 1) + deep * wide * high


x_first, y_first = 2, 1
pieces = x_first + y_first


class Reduce:
    def __init__(self, sizes, sender, in_ref, out_ref, scratch):
        self.sizes = sizes
        self.place = place(sizes)
        self.sender = sender
        self.in_ref, self.out_ref = in_ref, out_ref
        (
            self.held,
            self.from_core,
            self.from_x_a,
            self.from_y_b,
            self.from_y_a,
            self.from_x_b,
            self.from_z,
            self.final,
            self.local_sem,
            self.core_sem,
            self.xa_sem,
            self.yb_sem,
            self.ya_sem,
            self.xb_sem,
            self.z_sem,
            self.done_sem,
        ) = scratch
        deep = sizes[2]
        z = self.place[2]
        far = list(range(deep // 2, deep)) + list(range(deep // 2 - 1, 0, -1))
        self.order = [(z + k) % deep for k in far] + [z]

    def local(self, step):
        c = self.place[3]
        source = self.in_ref.at[self.order[step], :, c]
        return pltpu.make_async_copy(source, self.held.at[step], self.local_sem.at[step])

    def start(self):
        wide, high, deep = self.sizes
        x, y, z, c = self.place
        for step in range(deep):
            self.local(step).start()
            self.sender.send(
                self.in_ref.at[self.order[step], :, 1 - c],
                self.from_core.at[step],
                self.core_sem.at[step],
                (y * 2 + 1 - c, z * wide + x),
            )

    def merge(self, target, extras):
        total = target[...].astype(jnp.float32)
        for extra in extras:
            total = total + extra[...].astype(jnp.float32)
        target[...] = total.astype(target.dtype)

    def first(self, step):
        wide, high, deep = self.sizes
        x, y, z, c = self.place
        self.local(step).wait()
        self.sender.arrive(self.from_core.at[step], self.core_sem.at[step])

        def body(i, carry):
            xi, yi, hi = i // (pieces * high), i // pieces % high, i % pieces
            self.merge(self.held.at[step, xi, yi, hi], [self.from_core.at[step, xi, yi, hi]])
            return carry

        lax.fori_loop(0, wide * high * pieces, body, 0)
        for k in range(1, wide):
            xt = (x + k) % wide
            self.sender.send(
                self.held.at[step, xt, :, :x_first],
                self.from_x_a.at[k - 1, step],
                self.xa_sem.at[k - 1, step],
                (y * 2 + c, z * wide + xt),
            )
        for k in range(1, high):
            yt = (y + k) % high
            self.sender.send(
                self.held.at[step, :, yt, x_first:],
                self.from_y_b.at[k - 1, step],
                self.yb_sem.at[k - 1, step],
                (yt * 2 + c, z * wide + x),
            )

    def second(self, step):
        wide, high, deep = self.sizes
        x, y, z, c = self.place
        for k in range(1, wide):
            self.sender.arrive(self.from_x_a.at[k - 1, step], self.xa_sem.at[k - 1, step])

        def body_a(i, carry):
            yt, h = (y + 1 + i // x_first) % high, i % x_first
            extras = [self.from_x_a.at[k, step, yt, h] for k in range(wide - 1)]
            self.merge(self.held.at[step, x, yt, h], extras)
            return carry

        lax.fori_loop(0, high * x_first, body_a, 0)
        for k in range(1, high):
            yt = (y + k) % high
            self.sender.send(
                self.held.at[step, x, yt, :x_first],
                self.from_y_a.at[k - 1, step],
                self.ya_sem.at[k - 1, step],
                (yt * 2 + c, z * wide + x),
            )
        for k in range(1, high):
            self.sender.arrive(self.from_y_b.at[k - 1, step], self.yb_sem.at[k - 1, step])

        def body_b(i, carry):
            xt, h = (x + 1 + i // y_first) % wide, i % y_first
            extras = [self.from_y_b.at[k, step, xt, h] for k in range(high - 1)]
            self.merge(self.held.at[step, xt, y, x_first + h], extras)
            return carry

        lax.fori_loop(0, wide * y_first, body_b, 0)
        for k in range(1, wide):
            xt = (x + k) % wide
            self.sender.send(
                self.held.at[step, xt, y, x_first:],
                self.from_x_b.at[k - 1, step],
                self.xb_sem.at[k - 1, step],
                (y * 2 + c, z * wide + xt),
            )

    def third(self, step):
        wide, high, deep = self.sizes
        x, y, z, c = self.place
        for k in range(1, high):
            self.sender.arrive(self.from_y_a.at[k - 1, step], self.ya_sem.at[k - 1, step])
        for h in range(x_first):
            extras = [self.from_y_a.at[k, step, h] for k in range(high - 1)]
            self.merge(self.held.at[step, x, y, h], extras)
        for k in range(1, wide):
            self.sender.arrive(self.from_x_b.at[k - 1, step], self.xb_sem.at[k - 1, step])
        for h in range(y_first):
            extras = [self.from_x_b.at[k, step, h] for k in range(wide - 1)]
            self.merge(self.held.at[step, x, y, x_first + h], extras)
        if step < deep - 1:
            self.sender.send(
                self.held.at[step, x, y],
                self.from_z.at[step],
                self.z_sem.at[step],
                (y * 2 + c, self.order[step] * wide + x),
            )

    def turn(self, number):
        deep = self.sizes[2]
        if number < deep:
            self.first(number)
        if 0 <= number - 1 < deep:
            self.second(number - 1)
        if 0 <= number - 2 < deep:
            self.third(number - 2)

    def total(self):
        wide, high, deep = self.sizes
        x, y, z, c = self.place
        for step in range(deep - 1):
            self.sender.arrive(self.from_z.at[step], self.z_sem.at[step])
        for h in range(pieces):
            total = self.held[deep - 1, x, y, h].astype(jnp.float32)
            for step in range(deep - 1):
                total = total + self.from_z[step, h].astype(jnp.float32)
            self.final[h] = total.astype(self.final.dtype)
        spot, recv = self.out_ref.at[c, y], self.done_sem.at[c, y]
        pltpu.make_async_copy(self.final, spot, self.local_sem.at[deep]).start()
        for k in range(1, high):
            to = ((y + k) % high * 2 + c, z * wide + x)
            self.sender.send(self.final, spot, recv, to)
        self.sender.send(self.final, spot, recv, (y * 2 + 1 - c, z * wide + x))

    def last(self):
        wide, high, deep = self.sizes
        x, y, z, c = self.place
        for k in range(1, high):
            yt = (y + k) % high
            spot, recv = self.out_ref.at[c, yt], self.done_sem.at[c, yt]
            self.sender.arrive(spot, recv)
            self.sender.send(spot, spot, recv, (y * 2 + 1 - c, z * wide + x))
        for k in range(high):
            yt = (y + k) % high
            self.sender.arrive(self.out_ref.at[1 - c, yt], self.done_sem.at[1 - c, yt])
        own = self.out_ref.at[c, y]
        pltpu.make_async_copy(self.final, own, self.local_sem.at[deep]).wait()


def reduce_sends(sizes):
    wide, high, deep = sizes
    return deep + deep * 2 * (wide - 1 + high - 1) + deep - 1 + 2 * (high - 1) + 1


def reduce_scratch(sizes, rows, width, kind, final_kind):
    wide, high, deep = sizes
    tail = (rows, width)
    dma = pltpu.SemaphoreType.DMA
    return [
        pltpu.VMEM((deep, wide, high, pieces) + tail, kind),
        pltpu.VMEM((deep, wide, high, pieces) + tail, kind),
        pltpu.VMEM((wide - 1, deep, high, x_first) + tail, kind),
        pltpu.VMEM((high - 1, deep, wide, y_first) + tail, kind),
        pltpu.VMEM((high - 1, deep, x_first) + tail, kind),
        pltpu.VMEM((wide - 1, deep, y_first) + tail, kind),
        pltpu.VMEM((deep - 1, pieces) + tail, kind),
        pltpu.VMEM((pieces,) + tail, final_kind),
        dma((deep + 1,)),
        dma((deep,)),
        dma((wide - 1, deep)),
        dma((high - 1, deep)),
        dma((high - 1, deep)),
        dma((wide - 1, deep)),
        dma((deep - 1,)),
        dma((2, high)),
    ]


reduce_parts = 16


margin = 32
lanes = 128


def elu_slope(values):
    return jnp.where(values > 0, 1.0, jnp.exp(jnp.minimum(values, 0.0)))


def elu(values):
    return jnp.where(values > 0, values, jnp.exp(jnp.minimum(values, 0.0)) - 1.0)


def dot(left, right):
    return jnp.dot(left, right, preferred_element_type=jnp.float32)


def dot_last(left, right):
    return lax.dot_general(
        left, right, (((1,), (1,)), ((), ())), preferred_element_type=jnp.float32
    )


def dot_rows(left, right):
    return lax.dot_general(
        left, right, (((0,), (0,)), ((), ())), preferred_element_type=jnp.float32
    )


def spread_taps(target, source, ids, width, sign, dilation, length):
    block = 64

    def body(step, carry):
        base = pl.multiple_of(step * block, block)
        window = ids[pl.ds(base, block + 2 * margin), :]
        own = window[margin : margin + block]
        for tap in range(KERNEL):
            start = margin + sign * (tap - KERNEL // 2) * dilation
            match = window[start : start + block] == own
            for piece in range(width // lanes):
                columns = slice(piece * lanes, (piece + 1) * lanes)
                values = source[pl.ds(base, block + 2 * margin), columns][start : start + block]
                spot = tap * width + piece * lanes
                target[pl.ds(base, block), spot : spot + lanes] = jnp.where(
                    match, values, 0.0
                ).astype(jnp.bfloat16)
        return carry

    lax.fori_loop(0, length // block, body, 0)


def forward_unit(unit, stream, follow, ids, weights, scratch, length):
    dilated, pointwise = weights
    padded, columns, hidden, excited, active = scratch
    channels = stream.shape[1]
    values = elu(stream[...])
    padded[margin : margin + length, :] = values
    active[unit] = values[length // 4 : 3 * length // 4].astype(jnp.bfloat16)
    spread_taps(columns, padded, ids, channels, 1, dilation_list[unit], length)
    kernel = dilated[unit * KERNEL : (unit + 1) * KERNEL].reshape(KERNEL * channels, -1)
    value = dot(columns[...], kernel)
    hidden[unit] = value
    lifted = elu(value).astype(jnp.bfloat16)
    excited[unit] = lifted
    follow[...] = stream[...] + dot_last(lifted, pointwise[unit])


def backward_unit(unit, grad, stream, ids, weights, scratch, length):
    dilated, pointwise = weights
    padded, columns, hidden, excited, active = scratch
    width = hidden.shape[2]
    first, last = length // 4, 3 * length // 4
    low = grad[...].astype(jnp.bfloat16)
    grad_hidden = dot(low, pointwise[unit]) * elu_slope(hidden[unit])
    pointwise[unit] = dot(
        grad[first:last, :].T.astype(jnp.bfloat16), excited[unit, first:last, :]
    ).astype(jnp.bfloat16)
    padded[margin : margin + length, :width] = grad_hidden.astype(jnp.bfloat16).astype(jnp.float32)
    spread_taps(columns, padded, ids, width, -1, dilation_list[unit], length)
    turned = active[unit].astype(jnp.float32).T.astype(jnp.bfloat16)
    total = None
    for tap in range(KERNEL):
        piece = slice(tap * width, (tap + 1) * width)
        part = dot_last(columns[:, piece], dilated[unit * KERNEL + tap])
        total = part if total is None else total + part
        dilated[unit * KERNEL + tap] = dot(turned, columns[first:last, piece]).astype(jnp.bfloat16)
    grad[...] = grad[...] + total * elu_slope(stream[...])


class Mover:
    def __init__(self, side, geometry, gathered, packed, weights, sems):
        self.seq, self.share, self.blocks = geometry
        self.base = side * self.blocks
        width = gathered.shape[-1]
        self.gathered = gathered.reshape(self.seq, -1, self.share, width)
        self.packed = packed
        self.weights = weights
        self.sems = sems

    def block_start(self, kind):
        return (0, 3 * KERNEL, 3 * KERNEL + 3, 3 * KERNEL + 4)[kind]

    def load(self, kind, owner):
        rows = self.weights[kind]
        start = self.base + self.block_start(kind)
        source = self.gathered.at[owner, pl.ds(start, rows.shape[0])]
        target = rows.at[:, pl.ds(pl.multiple_of(owner * self.share, 16), self.share)]
        return pltpu.make_async_copy(source, target, self.sems.at[kind, owner])

    def start_loads(self, kind):
        for owner in range(self.seq):
            self.load(kind, owner).start()

    def wait_loads(self, kind):
        for owner in range(self.seq):
            self.load(kind, owner).wait()

    def store(self, kind, owner, first, size):
        rows = self.weights[kind]
        start = self.block_start(kind) + first
        source = rows.at[first : first + size, pl.ds(owner * self.share, self.share)]
        target = self.packed.at[owner, pl.ds(start, size)]
        return pltpu.make_async_copy(source, target, self.sems.at[4 + kind, owner])


def load_group(rows, seq, share):
    width = rows.shape[-1]
    part = width // seq
    value = rows.astype(jnp.float32).reshape(seq, GROUPS, part, width)
    return [value[:, g].reshape(width, width).astype(jnp.bfloat16) for g in range(GROUPS)]


def store_group(grads, seq, share):
    width = grads[0].shape[-1]
    part = width // seq
    value = jnp.stack([grad.reshape(seq, part, width) for grad in grads], axis=1)
    return value.reshape(seq, GROUPS * part, width).astype(jnp.bfloat16)


def put_tap(tiles, tap, value):
    latents = value.shape[0]
    for piece in range(tiles.shape[0]):
        tiles[piece, pl.ds(tap, latents, stride=STRIDE), :] = value[
            :, piece * lanes : (piece + 1) * lanes
        ]


def take_tap(tiles, tap, latents):
    return jnp.concatenate(
        [tiles[piece, pl.ds(tap, latents, stride=STRIDE), :] for piece in range(tiles.shape[0])],
        axis=1,
    )


def to_tiles(tiles, value):
    for piece in range(tiles.shape[0]):
        tiles[piece] = value[:, piece * lanes : (piece + 1) * lanes]


def from_tiles(tiles):
    return jnp.concatenate([tiles[piece] for piece in range(tiles.shape[0])], axis=1)


def set_edges(padded, length):
    zero = jnp.zeros((margin, padded.shape[1]), jnp.float32)
    padded[:margin, :] = zero
    padded[margin + length :, :] = zero


def front_kernel(
    sizes,
    geometry,
    length,
    enc_dilated,
    enc_point,
    enc_group,
    enc_strided,
    dec_dilated,
    dec_point,
    dec_group,
    dec_strided,
    code_own,
    ids_own,
    frames_own,
    cot_own,
    books_ref,
    gathered,
    frames_long,
    ids_ref,
    decoded_ref,
    grad_quant_ref,
    picks_ref,
    packed,
    shard_ref,
    wide_dilated,
    wide_point,
    wide_group,
    wide_strided,
    code_ref,
    cot_ref,
    dilated,
    pointwise,
    group,
    strided,
    streams,
    padded,
    columns,
    hidden,
    excited,
    active,
    tiles,
    sems,
    edge_sem,
    keep_sem,
    recv_sem,
    send_sem,
):
    seq, share, blocks = geometry
    wide, high, deep = sizes
    x, y, z, c = place(sizes)
    me = z * wide + x
    greet(sizes)
    sender = Sender(send_sem, (y * 2 + 1 - c, me))
    gathers = [
        Gather(
            sizes,
            sender,
            shard_ref.at[side].reshape(2, high, 2, -1, shard_ref.shape[-1]),
            gathered.at[:, :, side],
            recv_sem.at[side],
        )
        for side in range(2)
    ]
    encoder, decoder = gathers

    def pack(side):
        dil, point, both = wide_dilated[side], wide_point[side], wide_group[side]
        width = shard_ref.shape[-1]
        low = jnp.bfloat16
        at = 0
        for value in (dil, point, both.reshape(1, share, width)):
            shard_ref[side, at : at + value.shape[0]] = value.astype(low)
            at += value.shape[0]
        for part in range(2):
            value = wide_strided[side, :, :, part * width : (part + 1) * width]
            shard_ref[side, at : at + value.shape[0]] = value.astype(low)
            at += value.shape[0]
        if at < blocks:
            shard_ref[side, at:] = jnp.zeros((blocks - at, share, width), low)

    masters = ((enc_dilated, enc_point, enc_group, enc_strided),) + (
        (dec_dilated, dec_point, dec_group, dec_strided),
    )
    wides = (wide_dilated, wide_point, wide_group, wide_strided)
    reads = [
        [
            pltpu.make_async_copy(source, target.at[side], keep_sem.at[5 + 4 * side + number])
            for number, (source, target) in enumerate(zip(masters[side], wides))
        ]
        for side in range(2)
    ]
    for side in (1, 0):
        for copy in reads[side]:
            copy.start()
    for copy in reads[1]:
        copy.wait()
    pack(1)
    decoder.own_z()
    decoder.own_x()
    keeps = [
        pltpu.make_async_copy(
            gathers[side].in_ref, gathered.at[z, x, side], keep_sem.at[13 + side]
        )
        for side in range(2)
    ]
    keeps[1].start()
    for copy in reads[0]:
        copy.wait()
    pack(0)
    keeps[0].start()
    own = length // 2
    half = length // 4
    reach = half // STRIDE
    near = 80
    set_edges(padded, length)
    blank = jnp.zeros((half - near, cot_ref.shape[1]), jnp.float32)
    cot_ref[: half - near, :] = blank
    cot_ref[length - (half - near) :, :] = blank
    outside = jnp.full((margin, lanes), -1, jnp.int32)
    ids_ref[:margin, :] = outside
    ids_ref[margin + length :, :] = outside
    own_copies = [
        pltpu.make_async_copy(frames_own, frames_long.at[half : half + own], keep_sem.at[1]),
        pltpu.make_async_copy(cot_own, cot_ref.at[half : half + own], keep_sem.at[2]),
        pltpu.make_async_copy(
            ids_own, ids_ref.at[margin + half : margin + half + own], keep_sem.at[3]
        ),
        pltpu.make_async_copy(code_own, code_ref.at[:, reach : reach + own // STRIDE], keep_sem.at[4]),
    ]
    for copy in own_copies:
        copy.start()
    edges = [
        (frames_own.at[own - half :], frames_long.at[:half]),
        (cot_own.at[own - near :], cot_ref.at[half - near : half]),
        (ids_own.at[own - half :], ids_ref.at[margin : margin + half]),
        (code_own.at[:, own // STRIDE - reach :], code_ref.at[:, :reach]),
        (frames_own.at[:half], frames_long.at[half + own :]),
        (cot_own.at[:near], cot_ref.at[half + own : half + own + near]),
        (ids_own.at[:half], ids_ref.at[margin + half + own : margin + length]),
        (code_own.at[:, :reach], code_ref.at[:, reach + own // STRIDE :]),
    ]
    edge_copies = []
    for number, (src, dst) in enumerate(edges):
        other = (me + (1 if number < len(edges) // 2 else seq - 1)) % seq
        copy = pltpu.make_async_remote_copy(
            src_ref=src,
            dst_ref=dst,
            send_sem=edge_sem.at[0, number],
            recv_sem=edge_sem.at[1, number],
            device_id=(y * 2 + c, other),
            device_id_type=MESH,
        )
        copy.start()
        edge_copies.append(copy)
    for number in (3, 7):
        edge_copies[number].wait()
    own_copies[3].wait()
    latents = length // STRIDE
    codes = books_ref.shape[2]
    width = books_ref.shape[3]
    tile_range = lax.broadcasted_iota(jnp.int32, (latents, lanes), 1)
    quantized = []
    for g in range(GROUPS):
        picked = []
        for level in range(LEVELS):
            entry = g * LEVELS + level
            chosen = code_ref[entry]
            hot = jnp.concatenate(
                [
                    (chosen == tile_range + tile * lanes).astype(jnp.float32)
                    for tile in range(codes // lanes)
                ],
                axis=1,
            )
            pick = jnp.dot(hot, books_ref[g, level], precision=lax.Precision.HIGHEST)
            picks_ref[entry] = pick
            picked.append(pick)
        quantized.append((picked[0] + picked[1]).astype(jnp.bfloat16))
    for k in range(1, deep):
        decoder.from_z(k)
    encoder.own_z()
    for k in range(deep):
        decoder.second(k)
    encoder.own_x()
    for k in range(deep):
        decoder.third(k)
        if k > 0:
            encoder.from_z(k)
    for number, copy in enumerate(edge_copies):
        if number not in (3, 7):
            copy.wait()
    for copy in own_copies[:3]:
        copy.wait()

    @pl.when(me == 0)
    def _():
        ids_ref[margin : margin + half, :] = jnp.full((half, lanes), -1, jnp.int32)

    @pl.when(me == seq - 1)
    def _():
        ids_ref[margin + half + own : margin + length, :] = jnp.full((half, lanes), -1, jnp.int32)

    for copy in keeps:
        copy.wait()
    decoder.last()
    weights = (dilated, pointwise, group, strided)
    mover = Mover(1, geometry, gathered, packed, weights, sems)
    for kind in (2, 3, 0, 1):
        mover.start_loads(kind)
    pump = [functools.partial(encoder.second, k) for k in range(deep)]
    pump += [functools.partial(encoder.third, k) for k in range(deep)]
    first, last = length // 4, 3 * length // 4
    mover.wait_loads(2)
    out_weights = load_group(group[0], seq, share)
    mixed = [dot(quantized[g], out_weights[g]) for g in range(GROUPS)]
    lifted = [elu(value).astype(jnp.bfloat16) for value in mixed]
    mover.wait_loads(3)
    for tap in range(STRIDE):
        value = dot_last(lifted[0], strided[tap]) + dot_last(lifted[1], strided[STRIDE + tap])
        put_tap(tiles, tap, value)
    streams[0] = from_tiles(tiles)
    mover.wait_loads(0)
    mover.wait_loads(1)
    scratch = (padded, columns, hidden, excited, active)
    pump.pop(0)()
    for unit in range(3):
        forward_unit(
            unit, streams.at[unit], streams.at[unit + 1], ids_ref, (dilated, pointwise), scratch,
            length,
        )
        pump.pop(0)()
    decoded_ref[...] = streams[3, first:last, :].astype(jnp.bfloat16)
    grad = streams.at[3]
    grad[...] = cot_ref[...]

    for unit in (2, 1, 0):
        backward_unit(
            unit, grad, streams.at[unit], ids_ref, (dilated, pointwise), scratch, length,
        )
        for owner in range(seq):
            mover.store(0, owner, unit * KERNEL, KERNEL).start()
        if pump:
            pump.pop(0)()
    for owner in range(seq):
        mover.store(1, owner, 0, 3).start()
    own = slice(first // STRIDE, last // STRIDE)
    grad_lifted = [None, None]
    to_tiles(tiles, grad[...])
    for tap in range(STRIDE):
        part = take_tap(tiles, tap, latents)
        low = part.astype(jnp.bfloat16)
        turned = part[own].T.astype(jnp.bfloat16)
        for half in range(2):
            value = dot(low, strided[half * STRIDE + tap])
            grad_lifted[half] = value if tap == 0 else grad_lifted[half] + value
            strided[half * STRIDE + tap] = dot(turned, lifted[half][own]).astype(jnp.bfloat16)
    for owner in range(seq):
        mover.store(3, owner, 0, 2 * STRIDE).start()
    group_grads = []
    for g in range(GROUPS):
        low = (grad_lifted[g] * elu_slope(mixed[g])).astype(jnp.bfloat16)
        group_grads.append(dot_rows(quantized[g][own], low[own]))
        grad_quant_ref[g] = dot_last(low, out_weights[g])
    group[0] = store_group(group_grads, seq, share).reshape(group.shape[1:])
    for owner in range(seq):
        mover.store(2, owner, 0, 1).start()
    while pump:
        pump.pop(0)()
    finish_stores(mover, seq)
    encoder.last()
    sender.finish()


def finish_stores(mover, seq):
    for owner in range(seq):
        for unit in range(3):
            mover.store(0, owner, unit * KERNEL, KERNEL).wait()
        mover.store(1, owner, 0, 3).wait()
        mover.store(3, owner, 0, 2 * STRIDE).wait()
        mover.store(2, owner, 0, 1).wait()


def back_kernel(
    sizes,
    geometry,
    length,
    frames_ref,
    ids_ref,
    grad_quant_ref,
    picks_ref,
    digits_ref,
    gathered,
    partial_ref,
    frames_grad_ref,
    packed,
    share_decoder,
    share_encoder,
    all_ref,
    dilated,
    pointwise,
    group,
    strided,
    streams,
    padded,
    columns,
    hidden,
    excited,
    active,
    tiles,
    sems,
    *refs,
):
    seq, share, blocks = geometry
    x, y, z, c = place(sizes)
    me = z * sizes[0] + x
    greet(sizes)
    sender = Sender(refs[-1], (y * 2 + 1 - c, me))
    packed_view = packed.reshape(partial_ref.shape)
    other = Reduce(sizes, sender, partial_ref, share_decoder, refs[:reduce_parts])
    side = Reduce(sizes, sender, packed_view, share_encoder, refs[reduce_parts : 2 * reduce_parts])
    rows_ref, keep_sem, row_sem = refs[2 * reduce_parts : 2 * reduce_parts + 3]
    spread = Spread(sizes, sender, rows_ref, all_ref, row_sem, keep_sem)
    other.start()
    turns = sizes[2] + 2
    pump = [functools.partial(other.turn, number) for number in range(turns)]
    pump += [other.total, other.last]
    for spot in (2, 4, 6):
        pump.insert(spot, lambda: None)
    weights = (dilated, pointwise, group, strided)
    mover = Mover(0, geometry, gathered, packed, weights, sems)
    for kind in (0, 1, 3, 2):
        mover.start_loads(kind)
    set_edges(padded, length)
    first, last = length // 4, 3 * length // 4
    latents = length // STRIDE
    own = slice(first // STRIDE, last // STRIDE)
    width = picks_ref.shape[2]
    streams[0] = frames_ref[...].astype(jnp.float32)
    mover.wait_loads(0)
    mover.wait_loads(1)
    scratch = (padded, columns, hidden, excited, active)
    for unit in range(3):
        forward_unit(
            unit, streams.at[unit], streams.at[unit + 1], ids_ref, (dilated, pointwise), scratch,
            length,
        )
        pump.pop(0)()
    to_tiles(tiles, elu(streams[3]))
    mover.wait_loads(3)
    mover.wait_loads(2)
    in_weights = load_group(group[0], seq, share)
    latent = [None, None]
    for tap in range(STRIDE):
        low = take_tap(tiles, tap, latents).astype(jnp.bfloat16)
        for half in range(2):
            value = dot(low, strided[half * STRIDE + tap])
            latent[half] = value if tap == 0 else latent[half] + value
    group_grads = []
    grad_latent = []
    for g in range(GROUPS):
        low = latent[g].astype(jnp.bfloat16)
        first_part = dot(low, in_weights[g])
        pick = [picks_ref[g * LEVELS + level] for level in range(LEVELS)]
        second_part = first_part - pick[0]
        rows_ref[:, g * width : (g + 1) * width] = first_part[own].astype(jnp.bfloat16)
        grad_first = grad_quant_ref[g] + 2.0 * commit_weight * (
            second_part + (second_part - pick[1])
        )
        low_first = grad_first.astype(jnp.bfloat16)
        group_grads.append(dot_rows(low[own], low_first[own]))
        grad_latent.append(dot_last(low_first, in_weights[g]).astype(jnp.bfloat16))
    group[0] = store_group(group_grads, seq, share).reshape(group.shape[1:])
    rows_ref[:, GROUPS * width :] = digits_ref[...]
    spread.stage(0)
    for owner in range(seq):
        mover.store(2, owner, 0, 1).start()
    for tap in range(STRIDE):
        turned = take_tap(tiles, tap, latents)[own].T.astype(jnp.bfloat16)
        value = dot_last(grad_latent[0], strided[tap]) + dot_last(
            grad_latent[1], strided[STRIDE + tap]
        )
        put_tap(tiles, tap, value)
        for half in range(2):
            strided[half * STRIDE + tap] = dot(turned, grad_latent[half][own]).astype(
                jnp.bfloat16
            )
    for owner in range(seq):
        mover.store(3, owner, 0, 2 * STRIDE).start()
    grad = streams.at[3]
    grad[...] = from_tiles(tiles) * elu_slope(grad[...])
    pump.pop(0)()

    for unit in (2, 1, 0):
        backward_unit(
            unit, grad, streams.at[unit], ids_ref, (dilated, pointwise), scratch, length,
        )
        for owner in range(seq):
            mover.store(0, owner, unit * KERNEL, KERNEL).start()
        if pump:
            pump.pop(0)()
        if unit == 0:
            spread.stage(1)
    for owner in range(seq):
        mover.store(1, owner, 0, 3).start()
    frames_grad_ref[...] = grad[first:last, :]
    finish_stores(mover, seq)
    side.start()
    for number in range(turns):
        if pump:
            pump.pop(0)()
        side.turn(number)
        if number in (1, 4):
            spread.stage(2 + number // 3)
    while pump:
        pump.pop(0)()
    side.total()
    spread.stage(4)
    side.last()
    sender.finish()


def side_scratch(seq, share, length, channels, hidden):
    bf, f32 = jnp.bfloat16, jnp.float32
    group_rows = GROUPS * hidden // seq
    mats = [
        pltpu.VMEM((3 * KERNEL, channels, hidden), bf),
        pltpu.VMEM((3, channels, hidden), bf),
        pltpu.VMEM((1, seq * group_rows, hidden), bf),
        pltpu.VMEM((2 * STRIDE, channels, hidden), bf),
    ]
    return mats + [
        pltpu.VMEM((4, length, channels), f32),
        pltpu.VMEM((length + 2 * margin, channels), f32),
        pltpu.VMEM((length, KERNEL * channels), bf),
        pltpu.VMEM((3, length, hidden), f32),
        pltpu.VMEM((3, length, hidden), bf),
        pltpu.VMEM((3, length // 2, channels), bf),
        pltpu.VMEM((channels // lanes, length, lanes), f32),
        pltpu.SemaphoreType.DMA((8, seq)),
    ]


def split_terms(value, count):
    terms = []
    for number in range(count):
        term = value.astype(jnp.bfloat16)
        terms.append(term)
        if number < count - 1:
            value = value - term.astype(jnp.float32)
    return terms


def product(left, right):
    def pair(i, j):
        return jnp.dot(left[i], right[j], preferred_element_type=jnp.float32)

    low = pair(0, 1) + pair(1, 0)
    if len(left) > 2:
        low = low + (pair(1, 1) + pair(0, 2) + pair(2, 0))
    return pair(0, 0) + low


def gram_of(left, right):
    return product(split_terms(left.T, 3), split_terms(right, 3))


def solve_mixing(gram):
    size = gram.shape[0]
    eye = (
        lax.broadcasted_iota(jnp.int32, (size, size), 0)
        == lax.broadcasted_iota(jnp.int32, (size, size), 1)
    ).astype(jnp.float32)
    scale = 1.0 / (jnp.sqrt(jnp.sum(gram * eye)) + norm_floor)
    current = gram * (scale * scale)
    total = None
    for repeat in range(NS_STEPS):
        terms = 3 if repeat < 2 else 2
        parts = split_terms(current, terms)
        factor = coef_first * eye + coef_second * current + coef_third * product(parts, parts)
        factors = split_terms(factor, terms)
        if total is None:
            total = factor
        else:
            total = product(split_terms(total, 2), factors[:2])
        if repeat < NS_STEPS - 1:
            half = split_terms(product(parts, factors), terms)
            current = product(half, factors)
    return total * scale


def mixing_kernel(
    sizes,
    share,
    enc_dilated,
    enc_point,
    enc_group,
    enc_strided,
    dec_dilated,
    dec_point,
    dec_group,
    dec_strided,
    enc_dilated_w,
    enc_strided_w,
    dec_dilated_w,
    dec_strided_w,
    row_ref,
    books_ref,
    buffered_ref,
    marks_ref,
    small_ref,
    enc_dilated_next,
    enc_strided_next,
    dec_dilated_next,
    dec_strided_next,
    books_next,
    mix_ref,
    dilated,
    point,
    group,
    strided,
    dilated_w,
    strided_w,
    blocks,
    corner,
    slots,
    point_all,
    group_all,
    work,
    point_done,
    group_done,
    load_sem,
    send_sem,
    slot_sem,
    rows_sem,
    mix_sem,
    small_sem,
    corner_sem,
    all_ref,
    books,
    first_books,
    buffered,
    code_sem,
):
    wide, high, deep = sizes
    x, y, z, c = place(sizes)
    count = wide * deep
    me = z * wide + x
    row = y * 2 + c
    middle = count // 2
    partner = (y * 2 + 1 - c, me)
    others = [(row, (me + k) % count) for k in range(1, count)]
    others += [((y + k) % high * 2 + c, me) for k in range(1, high)] + [partner]
    barrier = pltpu.get_barrier_semaphore()
    for other in others:
        pl.semaphore_signal(barrier, inc=1, device_id=other, device_id_type=MESH)
    pl.semaphore_wait(barrier, len(others))

    pending = []

    def remote(src, dst, number, recv, to):
        return pltpu.make_async_remote_copy(
            src_ref=src,
            dst_ref=dst,
            send_sem=send_sem.at[number],
            recv_sem=recv,
            device_id=to,
            device_id_type=MESH,
        )

    def send(when, src, dst, recv, to):
        number = len(pending)
        pending.append((when, src, dst, recv, to))

        @pl.when(when)
        def _():
            remote(src, dst, number, recv, to).start()

    def arrive(dst, recv):
        remote(dst, dst, 0, recv, partner).wait_recv()

    first_set = y == 0
    second_set = y == 1

    def load(number, source, target):
        return pltpu.make_async_copy(source, target, load_sem.at[number])

    own_loads = [
        (enc_dilated, dilated.at[0]),
        (dec_dilated, dilated.at[1]),
        (enc_strided, strided.at[0]),
        (dec_strided, strided.at[1]),
        (enc_point, point.at[0]),
        (dec_point, point.at[1]),
        (enc_group, group.at[0]),
        (dec_group, group.at[1]),
        (enc_dilated_w, dilated_w.at[0]),
        (dec_dilated_w, dilated_w.at[1]),
        (enc_strided_w, strided_w.at[0]),
        (dec_strided_w, strided_w.at[1]),
    ]
    for number, (source, target) in enumerate(own_loads):
        load(number, source, target).start()
    code_share = books.shape[2]
    own_books = books_ref.at[:, :, pl.ds(pl.multiple_of(me * code_share, 8), code_share)]
    code_loads = [
        pltpu.make_async_copy(row_ref, all_ref, code_sem.at[0]),
        pltpu.make_async_copy(own_books, books, code_sem.at[1]),
        pltpu.make_async_copy(buffered_ref, buffered, code_sem.at[2]),
        pltpu.make_async_copy(books_ref.at[:, 0], first_books, code_sem.at[3]),
    ]
    for copy in code_loads:
        copy.start()
    for number in (4, 5, 6, 7, 2, 3, 0, 1):
        load(number, *own_loads[number]).wait()

    block_at = [middle - 2 + number + c for number in range(3)]
    strided_at = block_at[1]
    small_at = [(middle + c + offset + count) % count for offset in (1, 2, 3, -3, -4)]
    point_at, group_at = small_at[:3], small_at[3:]
    part = share // GROUPS

    for unit in range(3):
        at = point_at[unit]
        rows = pl.ds(pl.multiple_of(me * share, 8), share)
        send(
            second_set & (me != at),
            point.at[c, unit],
            point_all.at[rows],
            rows_sem.at[me],
            (row, at),
        )

        @pl.when(second_set & (me == at))
        def _():
            point_all[rows, :] = point[c, unit]

    for g in range(GROUPS):
        at = group_at[g]
        rows = pl.ds(pl.multiple_of(me * part, 8), part)
        send(
            second_set & (me != at),
            group.at[c, g],
            group_all.at[rows],
            rows_sem.at[me],
            (row, at),
        )

        @pl.when(second_set & (me == at))
        def _():
            group_all[rows, :] = group[c, g]

    block = blocks.shape[1]

    @pl.when(first_set)
    def _():
        for unit in range(3):
            value = dilated[c, unit * KERNEL : (unit + 1) * KERNEL].reshape(KERNEL * share, block)
            blocks[unit] = gram_of(value, value)

    @pl.when(second_set)
    def _():
        value = strided[c].reshape(-1, 2 * block)
        left, right = value[:, :block], value[:, block:]
        blocks[0] = gram_of(left, left)
        blocks[1] = gram_of(left, right)
        blocks[2] = gram_of(right, right)

    for number in range(3):
        at = block_at[number]
        send(
            (first_set | second_set) & (me != at),
            blocks.at[number],
            slots.at[number, me],
            slot_sem.at[number, me],
            (row, at),
        )

    for copy in code_loads:
        copy.wait()
    renew_codes(me, all_ref, books, first_books, buffered, marks_ref, books_next)

    def summed(number):
        total = blocks[number]
        for k in range(1, count):
            source = (me + k) % count
            arrive(slots.at[number, source], slot_sem.at[number, source])
            total = total + slots[number, source]
        return total

    for number in range(3):

        @pl.when((first_set | second_set) & (me == block_at[number]))
        def _():
            work[...] = summed(number)

    for number in (0, 2):
        send(
            second_set & (me == block_at[number]),
            work,
            corner.at[number // 2],
            corner_sem.at[number // 2],
            (row, strided_at),
        )

    @pl.when(second_set & (me == strided_at))
    def _():
        for number in range(2):
            arrive(corner.at[number], corner_sem.at[number])
        side = work[...]
        gram = jnp.concatenate(
            [
                jnp.concatenate([corner[0], side], axis=1),
                jnp.concatenate([side.T, corner[1]], axis=1),
            ],
            axis=0,
        )
        mixing = solve_mixing(gram)
        mix_ref[1, c, 0] = mixing[:block, :block]
        mix_ref[1, c, 1] = mixing[:block, block:]
        mix_ref[1, c, 2] = mixing[block:, block:]

    def hand_first(which, number, at):
        spot = mix_ref.at[which, c, number]
        owner = (y == which) & (me == at)
        targets = [(row, (z + k) % deep * wide + x) for k in range(1, deep)]
        targets += [(row, z * wide + (x + k) % wide) for k in range(1, wide)]
        targets += [((y + k) % high * 2 + c, me) for k in range(1, high)] + [partner]
        for to in targets:
            send(owner, spot, spot, mix_sem.at[which, c, number], to)

    for number in range(3):
        hand_first(1, number, strided_at)

    is_point = second_set & (
        (me == point_at[0]) | (me == point_at[1]) | (me == point_at[2])
    )
    is_group = second_set & ((me == group_at[0]) | (me == group_at[1]))
    is_dilated = first_set & (
        (me == block_at[0]) | (me == block_at[1]) | (me == block_at[2])
    )

    @pl.when(is_point)
    def _():
        for k in range(1, count):
            source = (me + k) % count
            rows = pl.ds(pl.multiple_of(source * share, 8), share)
            arrive(point_all.at[rows], rows_sem.at[source])
        work[...] = gram_of(point_all[...], point_all[...])

    @pl.when(is_group)
    def _():
        for k in range(1, count):
            source = (me + k) % count
            rows = pl.ds(pl.multiple_of(source * part, 8), part)
            arrive(group_all.at[rows], rows_sem.at[source])
        work[...] = gram_of(group_all[...], group_all[...])

    @pl.when(is_dilated | is_point | is_group)
    def _():
        work[...] = solve_mixing(work[...])

    for unit in range(3):

        @pl.when(first_set & (me == block_at[unit]))
        def _():
            mix_ref[0, c, unit] = work[...]

        hand_first(0, unit, block_at[unit])

    @pl.when(is_point)
    def _():
        point_done[...] = product(split_terms(point_all[...], 3), split_terms(work[...], 3))

    @pl.when(is_group)
    def _():
        group_done[...] = product(split_terms(group_all[...], 3), split_terms(work[...], 3))

    for unit in range(3):
        at = point_at[unit]
        for k in range(1, count):
            target = (me + k) % count
            rows = pl.ds(pl.multiple_of(target * share, 8), share)
            send(
                second_set & (me == at),
                point_done.at[rows],
                small_ref.at[c, unit],
                small_sem.at[unit],
                (row, target),
            )

        @pl.when(second_set & (me == at))
        def _():
            small_ref[c, unit] = point_done[pl.ds(pl.multiple_of(me * share, 8), share), :]

        @pl.when(second_set & (me != at))
        def _():
            arrive(small_ref.at[c, unit], small_sem.at[unit])

    for g in range(GROUPS):
        at = group_at[g]
        spot = small_ref.at[c, 3, g * part : (g + 1) * part]
        for k in range(1, count):
            target = (me + k) % count
            rows = pl.ds(pl.multiple_of(target * part, 8), part)
            send(
                second_set & (me == at),
                group_done.at[rows],
                spot,
                small_sem.at[3 + g],
                (row, target),
            )

        @pl.when(second_set & (me == at))
        def _():
            spot[...] = group_done[pl.ds(pl.multiple_of(me * part, 8), part), :]

        @pl.when(second_set & (me != at))
        def _():
            arrive(spot, small_sem.at[3 + g])

    for k in range(1, high):
        send(
            second_set,
            small_ref.at[c],
            small_ref.at[c],
            small_sem.at[5],
            ((y + k) % high * 2 + c, me),
        )

    @pl.when(jnp.logical_not(second_set))
    def _():
        arrive(small_ref.at[c], small_sem.at[5])

    always = y >= 0
    send(always, small_ref.at[c], small_ref.at[c], small_sem.at[6], partner)

    def hand_out(which, number, at):
        spot = mix_ref.at[which, c, number]
        recv = mix_sem.at[which, c, number]
        mine = y == which
        at_x = at % wide
        owner = mine & (me == at)

        @pl.when(jnp.logical_not(owner))
        def _():
            arrive(spot, recv)

        passing = jnp.logical_not(owner)
        for k in range(1, wide):
            to = (row, z * wide + (x + k) % wide)
            send(mine & (x == at_x) & passing, spot, spot, recv, to)
        for k in range(1, high):
            send(mine & passing, spot, spot, recv, ((y + k) % high * 2 + c, me))
        send(passing, spot, spot, recv, partner)

    for unit in range(3):
        hand_out(0, unit, block_at[unit])
    arrive(small_ref.at[1 - c], small_sem.at[6])
    for unit in range(3):
        arrive(mix_ref.at[0, 1 - c, unit], mix_sem.at[0, 1 - c, unit])
    for number in range(8, 12):
        load(number, *own_loads[number]).wait()
    for side, target in enumerate((enc_dilated_next, dec_dilated_next)):
        for unit in range(3):
            taps = slice(unit * KERNEL, (unit + 1) * KERNEL)
            rows = dilated[side, taps].reshape(KERNEL * share, block)
            moved = product(split_terms(rows, 2), split_terms(mix_ref[0, side, unit], 2))
            target[taps] = dilated_w[side, taps] - update_rate * moved.reshape(
                KERNEL, share, block
            )
    for number in range(3):
        hand_out(1, number, strided_at)
    for number in range(3):
        arrive(mix_ref.at[1, 1 - c, number], mix_sem.at[1, 1 - c, number])
    for side, target in enumerate((enc_strided_next, dec_strided_next)):
        corners = [split_terms(mix_ref[1, side, number], 2) for number in range(3)]
        turned = split_terms(mix_ref[1, side, 1].T, 2)
        rows = strided[side].reshape(-1, 2 * block)
        left, right = split_terms(rows[:, :block], 2), split_terms(rows[:, block:], 2)
        low = product(left, corners[0]) + product(right, turned)
        top = product(left, corners[1]) + product(right, corners[2])
        shape = (strided.shape[1], share, block)
        target[:, :, :block] = strided_w[side, :, :, :block] - update_rate * low.reshape(shape)
        target[:, :, block:] = strided_w[side, :, :, block:] - update_rate * top.reshape(shape)

    for number, (when, src, dst, recv, to) in enumerate(pending):

        @pl.when(when)
        def _():
            remote(src, dst, number, recv, to).wait_send()


def renew_codes(me, all_ref, books, first_books, buffered, marks_ref, books_next):
    groups, levels, share, width = books.shape
    entries = groups * levels
    codes = first_books.shape[1]
    slot_range = lax.broadcasted_iota(jnp.int32, (share, buffered.shape[1]), 1)
    deep, wide, high, _, length, _ = all_ref.shape
    size = wide * high * 2 * length
    every = lax.broadcasted_iota(jnp.int32, (codes, size), 0).astype(jnp.float32)
    own_range = lax.broadcasted_iota(jnp.int32, (share, size), 0) + me * share
    own_range = own_range.astype(jnp.float32)
    ones = jnp.ones((size, lanes), jnp.bfloat16)
    sums = [None] * entries
    counts = [None] * entries
    pairs = [None] * groups

    def add(target, number, value):
        target[number] = value if target[number] is None else target[number] + value

    def chosen(digits, entry, choices):
        code = digits[entry : entry + 1] * 32.0 + digits[entries + entry : entries + entry + 1]
        return (code == choices).astype(jnp.float32).astype(jnp.bfloat16)

    for zs in range(deep):
        rows = all_ref[zs].reshape(size, -1)
        digits = rows[:, groups * width :].astype(jnp.float32).T
        for g in range(groups):
            values = rows[:, g * width : (g + 1) * width]
            for level in range(levels):
                entry = g * levels + level
                hot = chosen(digits, entry, own_range)
                add(sums, entry, dot(hot, values))
                add(counts, entry, dot(hot, ones))
            add(pairs, g, dot_last(hot, chosen(digits, g * levels, every)))
    for entry in range(entries):
        g, level = entry // levels, entry % levels
        if level == 1:
            both = split_terms(pairs[g], 2)
            taken = product(both, split_terms(first_books[g], 2))
            sums[entry] = sums[entry] - taken
        count = jnp.concatenate([counts[entry]] * (width // lanes), axis=1)
        own = books[g, level]
        mean = sums[entry] / jnp.maximum(count, 1.0)
        updated = own + code_rate * jnp.minimum(count, 1.0) * (mean - own)
        hot = (marks_ref[:, entry : entry + 1] == slot_range).astype(jnp.bfloat16)
        replaced = None
        for term in split_terms(buffered[g], 3):
            part = dot(hot, term)
            replaced = part if replaced is None else replaced + part
        dead = marks_ref[:, entries + entry : entries + entry + 1] == 1
        books_next[g, level] = jnp.where(dead, replaced, updated)


def solve_all(views, weights, codes, sizes, collective_id):
    wide, high, deep = sizes
    count = wide * deep
    share, block = views[0].shape[1:]
    part = share // GROUPS
    f32 = jnp.float32
    dma = pltpu.SemaphoreType.DMA
    sends = 5 + 3 + 2 + 5 * (count - 1) + (high - 1) + 1 + 12 * (deep - 1 + wide - 1 + high)
    all_rows, books, buffered, marks = codes
    own_books = books.shape[:2] + (books.shape[2] // count,) + books.shape[3:]
    vmem = pl.BlockSpec(memory_space=pltpu.VMEM)
    return pl.pallas_call(
        functools.partial(mixing_kernel, sizes, share),
        out_shape=(jax.ShapeDtypeStruct((2, 4, share, block), f32),)
        + tuple(jax.ShapeDtypeStruct(weight.shape, f32) for weight in weights)
        + (jax.ShapeDtypeStruct(own_books, f32),),
        in_specs=[pl.BlockSpec(memory_space=pl.ANY)] * 15 + [vmem],
        out_specs=(vmem,) * 6,
        scratch_shapes=[
            pltpu.VMEM((2, 2, 3, block, block), f32),
            pltpu.VMEM((2,) + views[0].shape, f32),
            pltpu.VMEM((2,) + views[1].shape, f32),
            pltpu.VMEM((2,) + views[2].shape, f32),
            pltpu.VMEM((2,) + views[3].shape, f32),
            pltpu.VMEM((2,) + views[0].shape, f32),
            pltpu.VMEM((2,) + views[3].shape, f32),
            pltpu.VMEM((3, block, block), f32),
            pltpu.VMEM((2, block, block), f32),
            pltpu.VMEM((3, count, block, block), f32),
            pltpu.VMEM((count * share, block), f32),
            pltpu.VMEM((count * part, block), f32),
            pltpu.VMEM((block, block), f32),
            pltpu.VMEM((count * share, block), f32),
            pltpu.VMEM((count * part, block), f32),
            dma((12,)),
            dma((sends,)),
            dma((3, count)),
            dma((count,)),
            dma((2, 2, 3)),
            dma((7,)),
            dma((2,)),
            pltpu.VMEM(all_rows.shape, all_rows.dtype),
            pltpu.VMEM(own_books, f32),
            pltpu.VMEM(books.shape[:1] + books.shape[2:], f32),
            pltpu.VMEM(buffered.shape, f32),
            dma((4,)),
        ],
        compiler_params=pltpu.CompilerParams(
            collective_id=collective_id, has_side_effects=True, vmem_limit_bytes=60 * 2**20
        ),
    )(*views, *weights, *codes)


def velocity_kernel(share_encoder, share_decoder, *refs):
    moments, outs = refs[:8], refs[8:]
    for side, rows in enumerate((share_encoder, share_decoder)):
        dilated, point, group, strided = range(4 * side, 4 * side + 4)
        at = 0
        for number in (dilated, point):
            size = moments[number].shape[0]
            step = rows[at : at + size].astype(jnp.float32)
            outs[number][...] = moment_decay * moments[number][...] + step
            at += size
        step = rows[at].astype(jnp.float32).reshape(moments[group].shape)
        outs[group][...] = moment_decay * moments[group][...] + step
        at += 1
        taps, _, width = moments[strided].shape
        for part in range(2):
            columns = slice(part * width // 2, (part + 1) * width // 2)
            step = rows[at : at + taps].astype(jnp.float32)
            outs[strided][:, :, columns] = moment_decay * moments[strided][:, :, columns] + step
            at += taps


def new_velocities(side_shares, moments):
    vmem = pl.BlockSpec(memory_space=pltpu.VMEM)
    return pl.pallas_call(
        velocity_kernel,
        out_shape=tuple(jax.ShapeDtypeStruct(moment.shape, jnp.float32) for moment in moments),
        in_specs=[vmem] * (2 + len(moments)),
        out_specs=(vmem,) * len(moments),
        compiler_params=pltpu.CompilerParams(vmem_limit_bytes=60 * 2**20),
    )(*side_shares, *moments)


def per_device(
    frames,
    cotangent,
    segment_ids,
    code_index,
    codebooks,
    dead_codes,
    code_slots,
    buffered,
    encoder_dilated,
    encoder_pointwise,
    down_weight,
    group_in,
    group_out,
    up_weight,
    decoder_dilated,
    decoder_pointwise,
    encoder_dilated_moment,
    encoder_pointwise_moment,
    down_moment,
    group_in_moment,
    group_out_moment,
    up_moment,
    decoder_dilated_moment,
    decoder_pointwise_moment,
):
    masters = (
        encoder_dilated,
        encoder_pointwise,
        down_weight,
        group_in,
        group_out,
        up_weight,
        decoder_dilated,
        decoder_pointwise,
    )
    olds = (
        encoder_dilated_moment,
        encoder_pointwise_moment,
        down_moment,
        group_in_moment,
        group_out_moment,
        up_moment,
        decoder_dilated_moment,
        decoder_pointwise_moment,
    )
    count = lax.axis_size("seq")
    sizes = line_sizes(count, lax.axis_size("dp"))
    sides = ((0, 1, 3, 2), (6, 7, 4, 5))
    side_rows = whole_rows(masters, sizes[1])
    wide, high, deep = sizes
    _, length, channels = frames.shape
    long = 2 * length
    latent_len = long // STRIDE
    place_seq = lax.axis_index("seq")
    hidden = encoder_dilated.shape[-1]
    share = masters[0].shape[2]
    blocks = side_rows // share
    geometry = (count, share, blocks)
    rows = side_rows // (4 * high)
    low, f32 = jnp.bfloat16, jnp.float32
    dma = pltpu.SemaphoreType.DMA
    ids_own = jnp.broadcast_to(segment_ids[0][:, None], (length, lanes))
    entries = GROUPS * LEVELS
    code_own = code_index[0].reshape(-1, entries).T
    code_own = jnp.broadcast_to(code_own[:, :, None], code_own.shape + (lanes,))
    vmem = pl.BlockSpec(memory_space=pltpu.VMEM)
    anywhere = pl.BlockSpec(memory_space=pl.ANY)
    partial_type = jax.ShapeDtypeStruct((count, blocks, share, hidden), low)
    scratch = side_scratch(count, share, long, channels, hidden)
    flat = [masters[i].reshape((-1,) + masters[i].shape[-2:]) for side in sides for i in side]
    packed_shape = (2, high, 2, rows, hidden)
    reduce_rows = side_rows // (2 * high * pieces)
    reduce_shape = (2, high, pieces, reduce_rows, hidden)
    both = [pltpu.VMEM((2,) + array.shape, f32) for array in flat[:4]]
    gathered, frames_long, ids, decoded, grad_quant, picks, partial = pl.pallas_call(
        functools.partial(front_kernel, sizes, geometry, long),
        out_shape=(
            jax.ShapeDtypeStruct((deep, wide, 2) + packed_shape, low),
            jax.ShapeDtypeStruct((long, channels), frames.dtype),
            jax.ShapeDtypeStruct((long + 2 * margin, lanes), jnp.int32),
            jax.ShapeDtypeStruct((length, channels), low),
            jax.ShapeDtypeStruct((GROUPS, latent_len, hidden), f32),
            jax.ShapeDtypeStruct((entries, latent_len, hidden), f32),
            partial_type,
        ),
        in_specs=[anywhere] * 12 + [vmem],
        out_specs=(anywhere, vmem, vmem, vmem, vmem, vmem, anywhere),
        scratch_shapes=[pltpu.VMEM((2, blocks, share, hidden), low)]
        + both
        + [
            pltpu.VMEM((entries, latent_len, lanes), jnp.int32),
            pltpu.VMEM((long, channels), f32),
        ]
        + scratch
        + [
            dma((2, 8)),
            dma((15,)),
            dma((2, deep, wide, 2, high, 2)),
            dma((2 * gather_sends(sizes),)),
        ],
        compiler_params=pltpu.CompilerParams(
            collective_id=0, has_side_effects=True, vmem_limit_bytes=60 * 2**20
        ),
    )(*flat, code_own, ids_own, frames[0], cotangent[0], codebooks)
    own_codes_low = code_index[0].reshape(-1, entries)
    digits = jnp.concatenate([own_codes_low // 32, own_codes_low % 32], axis=1)
    digits = jnp.pad(digits, ((0, 0), (0, lanes - digits.shape[1]))).astype(low)
    rows_own = (length // STRIDE, GROUPS * hidden + lanes)
    grad, _, share_decoder, share_encoder, all_rows = pl.pallas_call(
        functools.partial(back_kernel, sizes, geometry, long),
        out_shape=(
            jax.ShapeDtypeStruct((length, channels), f32),
            partial_type,
            jax.ShapeDtypeStruct(reduce_shape, low),
            jax.ShapeDtypeStruct(reduce_shape, f32),
            jax.ShapeDtypeStruct((deep, wide, high, 2) + rows_own, low),
        ),
        in_specs=[vmem, vmem, vmem, vmem, vmem, anywhere, anywhere],
        out_specs=(vmem, anywhere, anywhere, anywhere, anywhere),
        scratch_shapes=scratch
        + reduce_scratch(sizes, reduce_rows, hidden, low, low)
        + reduce_scratch(sizes, reduce_rows, hidden, low, f32)
        + [
            pltpu.VMEM(rows_own, low),
            dma,
            dma((deep, wide, high, 2)),
            dma((2 * reduce_sends(sizes) + spread_sends(sizes),)),
        ],
        compiler_params=pltpu.CompilerParams(
            collective_id=1, has_side_effects=True, vmem_limit_bytes=63 * 2**20
        ),
    )(
        frames_long, ids, grad_quant, picks, digits, gathered,
        partial.reshape((deep, wide) + reduce_shape),
    )
    decoded = decoded[None]
    grad = grad[None]
    side_shares = (
        share_encoder.reshape(blocks, share, hidden),
        share_decoder.reshape(blocks, share, hidden),
    )
    order = [i for side in sides for i in side]
    moments = [olds[i].reshape((-1,) + olds[i].shape[-2:]) for i in order]
    views = new_velocities(side_shares, moments)
    velocities = [None] * 8
    for i, view in zip(order, views):
        velocities[i] = view.reshape(olds[i].shape)
    flat = [masters[i].reshape((-1,) + masters[i].shape[-2:]) for i in (0, 2, 6, 5)]
    marks = jnp.concatenate(
        [code_slots.reshape(entries, -1).T, dead_codes.reshape(entries, -1).T], axis=1
    )
    small, *moved, new_codebooks = solve_all(
        views, flat, (all_rows, codebooks, buffered, marks), sizes, 2
    )
    nexts = [None] * 8
    for i, value in zip((0, 2, 6, 5), moved):
        nexts[i] = value.reshape(masters[i].shape)
    for at, side in enumerate(sides):
        _, point, group, _ = side
        nexts[point] = masters[point] - update_rate * small[at, :3]
        nexts[group] = masters[group] - update_rate * small[at, 3].reshape(masters[group].shape)
    return (
        decoded,
        grad,
        new_codebooks,
        velocities[0],
        velocities[1],
        velocities[2],
        velocities[3],
        velocities[4],
        velocities[5],
        velocities[6],
        velocities[7],
        nexts[0],
        nexts[1],
        nexts[2],
        nexts[3],
        nexts[4],
        nexts[5],
        nexts[6],
        nexts[7],
    )


def solution(mesh):
    in_specs = (
        P("dp", "seq", None),
        P("dp", "seq", None),
        P("dp", "seq"),
        P("dp", "seq", None, None),
        P(),
        P(None, None, "seq"),
        P(None, None, "seq"),
        P(),
        P(None, None, "seq", None),
        P(None, "seq", None),
        P(None, "seq", None),
        P(None, "seq", None),
        P(None, "seq", None),
        P(None, "seq", None),
        P(None, None, "seq", None),
        P(None, "seq", None),
        P(None, None, "seq", None),
        P(None, "seq", None),
        P(None, "seq", None),
        P(None, "seq", None),
        P(None, "seq", None),
        P(None, "seq", None),
        P(None, None, "seq", None),
        P(None, "seq", None),
    )
    out_specs = (
        P("dp", "seq", None),
        P("dp", "seq", None),
        P(None, None, "seq", None),
        P(None, None, "seq", None),
        P(None, "seq", None),
        P(None, "seq", None),
        P(None, "seq", None),
        P(None, "seq", None),
        P(None, "seq", None),
        P(None, None, "seq", None),
        P(None, "seq", None),
        P(None, None, "seq", None),
        P(None, "seq", None),
        P(None, "seq", None),
        P(None, "seq", None),
        P(None, "seq", None),
        P(None, "seq", None),
        P(None, None, "seq", None),
        P(None, "seq", None),
    )
    return jax.shard_map(
        per_device, mesh=mesh, in_specs=in_specs, out_specs=out_specs, check_vma=False
    )
```

```python
import functools

import jax
import jax.numpy as jnp
from jax import lax
from jax.experimental import pallas as pl
from jax.experimental.pallas import tpu as pltpu
from jax.sharding import PartitionSpec as P

GROUPS = 2
LEVELS = 2
KERNEL = 7
STRIDE = 8
NS_STEPS = 5


highest = lax.Precision.HIGHEST
dilation_list = (1, 3, 9)
coef_first = 3.4445
coef_second = -4.775
coef_third = 2.0315
commit_weight = 0.25
moment_decay = 0.5
update_rate = 0.5
code_rate = 0.5
norm_floor = 1e-07


def whole_rows(masters, high):
    dilated, pointwise, strided, group = masters[:4]
    share, width = dilated.shape[2:]
    rows = (dilated.size + pointwise.size + strided.size + group.size) // width
    return whole_units(rows, 64 * high, share)


def whole_units(rows, unit, share):
    step = unit
    while unit % share:
        unit += step
    return -(-rows // unit) * unit


def reduce_rows(masters, high):
    dilated, pointwise, _, group = masters[:4]
    share, width = dilated.shape[2:]
    rows = (dilated.size + pointwise.size + group.size) // width
    for split in ((2, 1), (1, 1)):
        whole = whole_units(rows, 32 * sum(split) * high, share)
        if 8 * (whole - rows) <= rows:
            break
    return whole, split


MESH = pl.DeviceIdType.MESH


def line_sizes(seq, dp):
    across = 1
    while (2 * across) * (2 * across) <= seq:
        across *= 2
    return across, dp // 2, seq // across


def place(sizes):
    wide, high, _ = sizes
    row = lax.axis_index("dp")
    part = lax.axis_index("seq")
    return part % wide, row // 2, part // wide, row % 2


def greet(sizes, row=False):
    wide, high, deep = sizes
    x, y, z, c = place(sizes)
    me, count = z * wide + x, deep * wide
    others = [(y * 2 + 1 - c, me)]
    others += [((y + k) % high * 2 + c, me) for k in range(1, high)]
    if row:
        others += [(y * 2 + c, (me + k) % count) for k in range(1, count)]
    else:
        others += [(y * 2 + c, z * wide + (x + k) % wide) for k in range(1, wide)]
        others += [(y * 2 + c, (z + k) % deep * wide + x) for k in range(1, deep)]
        others += [(y * 2 + c, (me + k) % count) for k in (1, count - 1)]
    barrier = pltpu.get_barrier_semaphore()
    for other in others:
        pl.semaphore_signal(barrier, inc=1, device_id=other, device_id_type=MESH)
    pl.semaphore_wait(barrier, len(others))


class Sender:
    def __init__(self, send_sem, partner):
        self.send_sem = send_sem
        self.partner = partner
        self.sent = []

    def send(self, src, dst, recv, to):
        copy = pltpu.make_async_remote_copy(
            src_ref=src,
            dst_ref=dst,
            send_sem=self.send_sem.at[len(self.sent)],
            recv_sem=recv,
            device_id=to,
            device_id_type=MESH,
        )
        copy.start()
        self.sent.append(copy)

    def arrive(self, dst, recv):
        pltpu.make_async_remote_copy(
            src_ref=dst,
            dst_ref=dst,
            send_sem=self.send_sem.at[0],
            recv_sem=recv,
            device_id=self.partner,
            device_id_type=MESH,
        ).wait_recv()

    def finish(self):
        for copy in self.sent:
            copy.wait_send()


class Gather:
    def __init__(self, sizes, sender, in_ref, out_ref, recv_sem):
        self.sizes = sizes
        self.place = place(sizes)
        self.sender = sender
        self.in_ref, self.out_ref, self.recv_sem = in_ref, out_ref, recv_sem

    def send(self, zs, xs, ys, h, to, source=None):
        c = self.place[3]
        spot = self.out_ref.at[zs, xs, c, ys, h]
        src = spot if source is None else source
        self.sender.send(src, spot, self.recv_sem.at[zs, xs, c, ys, h], to)

    def arrive(self, zs, xs, cs, ys, h):
        self.sender.arrive(self.out_ref.at[zs, xs, cs, ys, h], self.recv_sem.at[zs, xs, cs, ys, h])

    def to_x(self, zs, xs, ys, h, source=None):
        wide, high, deep = self.sizes
        x, y, z, c = self.place
        for k in range(1, wide):
            self.send(zs, xs, ys, h, (y * 2 + c, z * wide + (x + k) % wide), source)

    def to_y(self, zs, xs, ys, h):
        wide, high, deep = self.sizes
        x, y, z, c = self.place
        for k in range(1, high):
            self.send(zs, xs, ys, h, ((y + k) % high * 2 + c, z * wide + x))

    def to_core(self, zs, xs, ys, h):
        wide, high, deep = self.sizes
        x, y, z, c = self.place
        self.send(zs, xs, ys, h, (y * 2 + 1 - c, z * wide + x))

    def own_z(self):
        wide, high, deep = self.sizes
        x, y, z, c = self.place
        for k in range(deep - 1, 0, -1):
            for h in range(2):
                to = (y * 2 + c, (z + k) % deep * wide + x)
                self.send(z, x, y, h, to, self.in_ref.at[c, y, h])

    def own_x(self):
        wide, high, deep = self.sizes
        x, y, z, c = self.place
        self.to_x(z, x, y, 0, self.in_ref.at[c, y, 0])
        for j in range(high):
            ys = (y + j) % high
            self.to_x(z, x, ys, 1, self.in_ref.at[c, ys, 1])

    def from_z(self, k):
        x, y, z, c = self.place
        zs = (z + k) % self.sizes[2]
        self.arrive(zs, x, c, y, 0)
        self.to_x(zs, x, y, 0)
        self.to_y(zs, x, y, 0)
        self.to_core(zs, x, y, 0)
        self.arrive(zs, x, c, y, 1)
        self.to_y(zs, x, y, 1)
        self.to_x(zs, x, y, 1)
        self.to_core(zs, x, y, 1)

    def second(self, k):
        wide, high, deep = self.sizes
        x, y, z, c = self.place
        zs = (z + k) % deep
        for i in range(1, wide):
            xs = (x + i) % wide
            self.arrive(zs, xs, c, y, 0)
            self.to_y(zs, xs, y, 0)
            self.to_core(zs, xs, y, 0)
        if k > 0:
            for j in range(1, high):
                ys = (y + j) % high
                self.arrive(zs, x, c, ys, 1)
                self.to_x(zs, x, ys, 1)
                self.to_core(zs, x, ys, 1)

    def third(self, k):
        wide, high, deep = self.sizes
        x, y, z, c = self.place
        zs = (z + k) % deep
        for i in range(wide):
            xs = (x + i) % wide
            if k == 0 and i == 0:
                continue
            for j in range(1, high):
                ys = (y + j) % high
                self.arrive(zs, xs, c, ys, 0)
                self.to_core(zs, xs, ys, 0)
            if i > 0:
                for j in range(high):
                    ys = (y + j) % high
                    self.arrive(zs, xs, c, ys, 1)
                    self.to_core(zs, xs, ys, 1)

    def last(self):
        wide, high, deep = self.sizes
        x, y, z, c = self.place
        for k in range(deep):
            zs = (z + k) % deep
            for i in range(wide):
                xs = (x + i) % wide
                if k == 0 and i == 0:
                    continue
                for j in range(high):
                    for h in range(2):
                        self.arrive(zs, xs, 1 - c, (y + j) % high, h)


def gather_sends(sizes):
    wide, high, deep = sizes
    n = (deep - 1) * 2 + (wide - 1) * (1 + high)
    n += (deep - 1) * 2 * (wide - 1 + high - 1 + 1)
    n += deep * (wide - 1) * high + (deep - 1) * (high - 1) * wide
    n += (deep * wide - 1) * (high - 1) + deep * (wide - 1) * high
    return n


class Spread:
    def __init__(self, sizes, sender, row_ref, all_ref, row_sem, keep_sem):
        self.sizes = sizes
        self.place = place(sizes)
        self.sender = sender
        self.row_ref, self.all_ref, self.row_sem = row_ref, all_ref, row_sem
        x, y, z, c = self.place
        self.keep = pltpu.make_async_copy(row_ref, all_ref.at[z, x, y, c], keep_sem)

    def pass_on(self, zs, xs, ys, to, own):
        c = self.place[3]
        spot = self.all_ref.at[zs, xs, ys, c]
        self.sender.send(self.row_ref if own else spot, spot, self.row_sem.at[zs, xs, ys, c], to)

    def landed(self, zs, xs, ys, cs):
        self.sender.arrive(self.all_ref.at[zs, xs, ys, cs], self.row_sem.at[zs, xs, ys, cs])

    def stage(self, number):
        wide, high, deep = self.sizes
        x, y, z, c = self.place
        columns = [(z + k) % deep for k in range(deep)]
        lines = [(x + k) % wide for k in range(wide)]
        heights = [(y + k) % high for k in range(high)]
        if number == 0:
            self.keep.start()
            for zt in columns[1:]:
                self.pass_on(z, x, y, (y * 2 + c, zt * wide + x), True)
        if number == 1:
            for zs in columns[1:]:
                self.landed(zs, x, y, c)
            for zs in columns:
                for yt in heights[1:]:
                    self.pass_on(zs, x, y, (yt * 2 + c, z * wide + x), zs is columns[0])
        if number == 2:
            for zs in columns:
                for ys in heights[1:]:
                    self.landed(zs, x, ys, c)
            for zs in columns:
                for ys in heights:
                    own = zs is columns[0] and ys is heights[0]
                    for xt in lines[1:]:
                        self.pass_on(zs, x, ys, (y * 2 + c, z * wide + xt), own)
        if number == 3:
            for zs in columns:
                for xs in lines[1:]:
                    for ys in heights:
                        self.landed(zs, xs, ys, c)
            for zs in columns:
                for xs in lines:
                    for ys in heights:
                        own = zs is columns[0] and xs is lines[0] and ys is heights[0]
                        self.pass_on(zs, xs, ys, (y * 2 + 1 - c, z * wide + x), own)
        if number == 4:
            for zs in columns:
                for xs in lines:
                    for ys in heights:
                        self.landed(zs, xs, ys, 1 - c)
            self.keep.wait()


def spread_sends(sizes):
    wide, high, deep = sizes
    return deep - 1 + deep * (high - 1) + deep * high * (wide - 1) + deep * wide * high


class Reduce:
    def __init__(self, sizes, split, sender, in_ref, out_ref, scratch):
        self.sizes = sizes
        self.split = split
        self.place = place(sizes)
        self.sender = sender
        self.in_ref, self.out_ref = in_ref, out_ref
        (
            self.held,
            self.from_core,
            self.from_x_a,
            self.from_y_b,
            self.from_y_a,
            self.from_x_b,
            self.from_z,
            self.final,
            self.local_sem,
            self.core_sem,
            self.xa_sem,
            self.yb_sem,
            self.ya_sem,
            self.xb_sem,
            self.z_sem,
            self.done_sem,
        ) = scratch
        deep = sizes[2]
        z = self.place[2]
        far = list(range(deep // 2, deep)) + list(range(deep // 2 - 1, 0, -1))
        self.order = [(z + k) % deep for k in far] + [z]

    def local(self, step):
        c = self.place[3]
        source = self.in_ref.at[self.order[step], :, c]
        return pltpu.make_async_copy(source, self.held.at[step], self.local_sem.at[step])

    def start(self):
        wide, high, deep = self.sizes
        x, y, z, c = self.place
        x_first, y_first = self.split
        pieces = x_first + y_first
        for step in range(deep):
            self.local(step).start()
            self.sender.send(
                self.in_ref.at[self.order[step], :, 1 - c],
                self.from_core.at[step],
                self.core_sem.at[step],
                (y * 2 + 1 - c, z * wide + x),
            )

    def merge(self, target, extras):
        total = target[...].astype(jnp.float32)
        for extra in extras:
            total = total + extra[...].astype(jnp.float32)
        target[...] = total.astype(target.dtype)

    def first(self, step):
        wide, high, deep = self.sizes
        x, y, z, c = self.place
        x_first, y_first = self.split
        pieces = x_first + y_first
        self.local(step).wait()
        self.sender.arrive(self.from_core.at[step], self.core_sem.at[step])

        def body(i, carry):
            xi, yi, hi = i // (pieces * high), i // pieces % high, i % pieces
            self.merge(self.held.at[step, xi, yi, hi], [self.from_core.at[step, xi, yi, hi]])
            return carry

        lax.fori_loop(0, wide * high * pieces, body, 0)
        for k in range(1, wide):
            xt = (x + k) % wide
            self.sender.send(
                self.held.at[step, xt, :, :x_first],
                self.from_x_a.at[k - 1, step],
                self.xa_sem.at[k - 1, step],
                (y * 2 + c, z * wide + xt),
            )
        for k in range(1, high):
            yt = (y + k) % high
            self.sender.send(
                self.held.at[step, :, yt, x_first:],
                self.from_y_b.at[k - 1, step],
                self.yb_sem.at[k - 1, step],
                (yt * 2 + c, z * wide + x),
            )

    def second(self, step):
        wide, high, deep = self.sizes
        x, y, z, c = self.place
        x_first, y_first = self.split
        pieces = x_first + y_first
        for k in range(1, wide):
            self.sender.arrive(self.from_x_a.at[k - 1, step], self.xa_sem.at[k - 1, step])

        def body_a(i, carry):
            yt, h = (y + 1 + i // x_first) % high, i % x_first
            extras = [self.from_x_a.at[k, step, yt, h] for k in range(wide - 1)]
            self.merge(self.held.at[step, x, yt, h], extras)
            return carry

        lax.fori_loop(0, high * x_first, body_a, 0)
        for k in range(1, high):
            yt = (y + k) % high
            self.sender.send(
                self.held.at[step, x, yt, :x_first],
                self.from_y_a.at[k - 1, step],
                self.ya_sem.at[k - 1, step],
                (yt * 2 + c, z * wide + x),
            )
        for k in range(1, high):
            self.sender.arrive(self.from_y_b.at[k - 1, step], self.yb_sem.at[k - 1, step])

        def body_b(i, carry):
            xt, h = (x + 1 + i // y_first) % wide, i % y_first
            extras = [self.from_y_b.at[k, step, xt, h] for k in range(high - 1)]
            self.merge(self.held.at[step, xt, y, x_first + h], extras)
            return carry

        lax.fori_loop(0, wide * y_first, body_b, 0)
        for k in range(1, wide):
            xt = (x + k) % wide
            self.sender.send(
                self.held.at[step, xt, y, x_first:],
                self.from_x_b.at[k - 1, step],
                self.xb_sem.at[k - 1, step],
                (y * 2 + c, z * wide + xt),
            )

    def third(self, step):
        wide, high, deep = self.sizes
        x, y, z, c = self.place
        x_first, y_first = self.split
        pieces = x_first + y_first
        for k in range(1, high):
            self.sender.arrive(self.from_y_a.at[k - 1, step], self.ya_sem.at[k - 1, step])
        for h in range(x_first):
            extras = [self.from_y_a.at[k, step, h] for k in range(high - 1)]
            self.merge(self.held.at[step, x, y, h], extras)
        for k in range(1, wide):
            self.sender.arrive(self.from_x_b.at[k - 1, step], self.xb_sem.at[k - 1, step])
        for h in range(y_first):
            extras = [self.from_x_b.at[k, step, h] for k in range(wide - 1)]
            self.merge(self.held.at[step, x, y, x_first + h], extras)
        if step < deep - 1:
            self.sender.send(
                self.held.at[step, x, y],
                self.from_z.at[step],
                self.z_sem.at[step],
                (y * 2 + c, self.order[step] * wide + x),
            )

    def turn(self, number):
        deep = self.sizes[2]
        if number < deep:
            self.first(number)
        if 0 <= number - 1 < deep:
            self.second(number - 1)
        if 0 <= number - 2 < deep:
            self.third(number - 2)

    def total(self):
        wide, high, deep = self.sizes
        x, y, z, c = self.place
        x_first, y_first = self.split
        pieces = x_first + y_first
        for step in range(deep - 1):
            self.sender.arrive(self.from_z.at[step], self.z_sem.at[step])
        for h in range(pieces):
            total = self.held[deep - 1, x, y, h].astype(jnp.float32)
            for step in range(deep - 1):
                total = total + self.from_z[step, h].astype(jnp.float32)
            self.final[h] = total.astype(self.final.dtype)
        spot, recv = self.out_ref.at[c, y], self.done_sem.at[c, y]
        pltpu.make_async_copy(self.final, spot, self.local_sem.at[deep]).start()
        for k in range(1, high):
            to = ((y + k) % high * 2 + c, z * wide + x)
            self.sender.send(self.final, spot, recv, to)
        self.sender.send(self.final, spot, recv, (y * 2 + 1 - c, z * wide + x))

    def last(self):
        wide, high, deep = self.sizes
        x, y, z, c = self.place
        x_first, y_first = self.split
        pieces = x_first + y_first
        for k in range(1, high):
            yt = (y + k) % high
            spot, recv = self.out_ref.at[c, yt], self.done_sem.at[c, yt]
            self.sender.arrive(spot, recv)
            self.sender.send(spot, spot, recv, (y * 2 + 1 - c, z * wide + x))
        for k in range(high):
            yt = (y + k) % high
            self.sender.arrive(self.out_ref.at[1 - c, yt], self.done_sem.at[1 - c, yt])
        own = self.out_ref.at[c, y]
        pltpu.make_async_copy(self.final, own, self.local_sem.at[deep]).wait()


def reduce_sends(sizes):
    wide, high, deep = sizes
    return deep + deep * 2 * (wide - 1 + high - 1) + deep - 1 + 2 * (high - 1) + 1


def reduce_scratch(sizes, split, rows, width, kind):
    wide, high, deep = sizes
    x_first, y_first = split
    pieces = x_first + y_first
    tail = (rows, width)
    dma = pltpu.SemaphoreType.DMA
    return [
        pltpu.VMEM((deep, wide, high, pieces) + tail, kind),
        pltpu.VMEM((deep, wide, high, pieces) + tail, kind),
        pltpu.VMEM((wide - 1, deep, high, x_first) + tail, kind),
        pltpu.VMEM((high - 1, deep, wide, y_first) + tail, kind),
        pltpu.VMEM((high - 1, deep, x_first) + tail, kind),
        pltpu.VMEM((wide - 1, deep, y_first) + tail, kind),
        pltpu.VMEM((deep - 1, pieces) + tail, kind),
        pltpu.VMEM((pieces,) + tail, kind),
        dma((deep + 1,)),
        dma((deep,)),
        dma((wide - 1, deep)),
        dma((high - 1, deep)),
        dma((high - 1, deep)),
        dma((wide - 1, deep)),
        dma((deep - 1,)),
        dma((2, high)),
    ]


reduce_parts = 16


class Outer:
    def __init__(self, sizes, sender, left, right, lefts, rights, left_sem, right_sem):
        self.sizes = sizes
        self.place = place(sizes)
        self.sender = sender
        self.left, self.right = left, right
        self.lefts, self.rights = lefts, rights
        self.left_sem, self.right_sem = left_sem, right_sem
        x, y, z, c = self.place
        self.count = sizes[0] * sizes[2]
        self.me = z * sizes[0] + x

    def own(self, part):
        share = self.lefts.shape[2]
        return self.left.at[:, pl.ds(pl.multiple_of(part * share, 16), share)]

    def start(self):
        x, y, z, c = self.place
        me = self.me
        for k in range(1, self.count):
            to = (me + k) % self.count
            self.sender.send(self.own(to), self.lefts.at[me], self.left_sem.at[me], (y * 2 + c, to))
            self.sender.send(self.right, self.rights.at[me], self.right_sem.at[me], (y * 2 + c, to))
        self.lefts[me] = self.own(me)[...]
        self.rights[me] = self.right[...]

    def multiply(self, target):
        for k in range(1, self.count):
            source = (self.me + k) % self.count
            self.sender.arrive(self.lefts.at[source], self.left_sem.at[source])
            self.sender.arrive(self.rights.at[source], self.right_sem.at[source])
        share = self.lefts.shape[2]
        latents = self.right.shape[0]
        taps = lanes // latents
        lane = lax.broadcasted_iota(jnp.int32, (share, lanes), 1) // latents
        rights = jnp.concatenate(
            [self.rights[source] for source in range(self.count) for _ in range(taps)], axis=0
        )
        for group in range(self.left.shape[0]):
            pieces = []
            for source in range(self.count):
                block = self.lefts[source, group].astype(jnp.float32)
                pieces.append(
                    jnp.concatenate(
                        [jnp.where(lane == tap, block, 0.0) for tap in range(taps)], axis=0
                    ).astype(jnp.bfloat16)
                )
            value = dot(jnp.concatenate(pieces, axis=1), rights)
            target[group * taps : (group + 1) * taps] = value.reshape(taps, share, -1)


class OuterSum:
    def __init__(self, sizes, sender, partials, out_ref, scratch):
        self.sizes = sizes
        self.place = place(sizes)
        self.sender = sender
        self.partials, self.out_ref = partials, out_ref
        self.peer, self.low, self.peers, self.core_sem, self.y_sem, self.out_sem, self.last_sem = scratch
        self.taps = partials.shape[1] // sizes[1]

    def to_core(self):
        wide, high, deep = self.sizes
        x, y, z, c = self.place
        to = (y * 2 + 1 - c, z * wide + x)
        self.sender.send(self.partials.at[1 - c], self.peer, self.core_sem, to)

    def to_y(self):
        wide, high, deep = self.sizes
        x, y, z, c = self.place
        self.sender.arrive(self.peer, self.core_sem)
        total = self.partials[c] + self.peer[...]
        self.partials[c] = total
        self.low[...] = total.astype(self.low.dtype)
        for k in range(1, high):
            yt = (y + k) % high
            self.sender.send(
                self.low.at[pl.ds(yt * self.taps, self.taps)],
                self.peers.at[k - 1],
                self.y_sem.at[k - 1],
                (yt * 2 + c, z * wide + x),
            )

    def back_y(self):
        wide, high, deep = self.sizes
        x, y, z, c = self.place
        mine = pl.ds(y * self.taps, self.taps)
        total = self.partials[c, mine]
        for k in range(1, high):
            self.sender.arrive(self.peers.at[k - 1], self.y_sem.at[k - 1])
            total = total + self.peers[k - 1].astype(jnp.float32)
        spot = self.out_ref.at[c, mine]
        spot[...] = total
        for k in range(1, high):
            to = ((y + k) % high * 2 + c, z * wide + x)
            self.sender.send(spot, spot, self.out_sem.at[y], to)

    def back_core(self):
        wide, high, deep = self.sizes
        x, y, z, c = self.place
        for k in range(1, high):
            yt = (y + k) % high
            spot = self.out_ref.at[c, pl.ds(yt * self.taps, self.taps)]
            self.sender.arrive(spot, self.out_sem.at[yt])
        to = (y * 2 + 1 - c, z * wide + x)
        self.sender.send(self.out_ref.at[c], self.out_ref.at[c], self.last_sem, to)

    def last(self):
        c = self.place[3]
        self.sender.arrive(self.out_ref.at[1 - c], self.last_sem)


def outer_sends(sizes):
    wide, high, deep = sizes
    return 4 * (wide * deep - 1) + 2 * high


def outer_left(taps):
    per = lanes // taps[0].shape[0]
    turned = [tap.T for tap in taps]
    return [
        jnp.concatenate(turned[start : start + per], axis=1).astype(jnp.bfloat16)
        for start in range(0, len(taps), per)
    ]


margin = 32
lanes = 128


def elu_slope(values):
    return jnp.where(values > 0, 1.0, jnp.exp(jnp.minimum(values, 0.0)))


def elu(values):
    return jnp.where(values > 0, values, jnp.exp(jnp.minimum(values, 0.0)) - 1.0)


def dot(left, right):
    return jnp.dot(left, right, preferred_element_type=jnp.float32)


def dot_last(left, right):
    return lax.dot_general(
        left, right, (((1,), (1,)), ((), ())), preferred_element_type=jnp.float32
    )


def dot_rows(left, right):
    return lax.dot_general(
        left, right, (((0,), (0,)), ((), ())), preferred_element_type=jnp.float32
    )


def spread_taps(target, source, ids, width, sign, dilation, length):
    block = 64

    def body(step, carry):
        base = pl.multiple_of(step * block, block)
        window = ids[pl.ds(base, block + 2 * margin), :]
        own = window[margin : margin + block]
        for tap in range(KERNEL):
            start = margin + sign * (tap - KERNEL // 2) * dilation
            match = window[start : start + block] == own
            for piece in range(width // lanes):
                columns = slice(piece * lanes, (piece + 1) * lanes)
                values = source[pl.ds(base, block + 2 * margin), columns][start : start + block]
                spot = tap * width + piece * lanes
                target[pl.ds(base, block), spot : spot + lanes] = jnp.where(
                    match, values, 0.0
                ).astype(jnp.bfloat16)
        return carry

    lax.fori_loop(0, length // block, body, 0)


def forward_unit(unit, stream, follow, ids, weights, scratch, length):
    dilated, pointwise = weights
    padded, columns, hidden, excited, active = scratch
    channels = stream.shape[1]
    values = elu(stream[...])
    padded[margin : margin + length, :] = values
    active[unit] = values[length // 4 : 3 * length // 4].astype(jnp.bfloat16)
    spread_taps(columns, padded, ids, channels, 1, dilation_list[unit], length)
    kernel = dilated[unit * KERNEL : (unit + 1) * KERNEL].reshape(KERNEL * channels, -1)
    value = dot(columns[...], kernel)
    hidden[unit] = value
    lifted = elu(value).astype(jnp.bfloat16)
    excited[unit] = lifted
    follow[...] = stream[...] + dot_last(lifted, pointwise[unit])


def backward_unit(unit, grad, stream, ids, weights, scratch, length):
    dilated, pointwise = weights
    padded, columns, hidden, excited, active = scratch
    width = hidden.shape[2]
    first, last = length // 4, 3 * length // 4
    low = grad[...].astype(jnp.bfloat16)
    grad_hidden = dot(low, pointwise[unit]) * elu_slope(hidden[unit])
    pointwise[unit] = dot(
        grad[first:last, :].T.astype(jnp.bfloat16), excited[unit, first:last, :]
    ).astype(jnp.bfloat16)
    padded[margin : margin + length, :width] = grad_hidden.astype(jnp.bfloat16).astype(jnp.float32)
    spread_taps(columns, padded, ids, width, -1, dilation_list[unit], length)
    turned = active[unit].astype(jnp.float32).T.astype(jnp.bfloat16)
    total = None
    for tap in range(KERNEL):
        piece = slice(tap * width, (tap + 1) * width)
        part = dot_last(columns[:, piece], dilated[unit * KERNEL + tap])
        total = part if total is None else total + part
        dilated[unit * KERNEL + tap] = dot(turned, columns[first:last, piece]).astype(jnp.bfloat16)
    grad[...] = grad[...] + total * elu_slope(stream[...])


class Mover:
    def __init__(self, side, geometry, gathered, packed, weights, sems):
        self.seq, self.share, self.blocks = geometry
        self.base = side * self.blocks
        width = gathered.shape[-1]
        self.gathered = gathered.reshape(self.seq, -1, self.share, width)
        self.packed = packed
        self.weights = weights
        self.sems = sems

    def block_start(self, kind):
        return (0, 3 * KERNEL, 3 * KERNEL + 3, 3 * KERNEL + 4)[kind]

    def load(self, kind, owner):
        rows = self.weights[kind]
        start = self.base + self.block_start(kind)
        source = self.gathered.at[owner, pl.ds(start, rows.shape[0])]
        target = rows.at[:, pl.ds(pl.multiple_of(owner * self.share, 16), self.share)]
        return pltpu.make_async_copy(source, target, self.sems.at[kind, owner])

    def start_loads(self, kind):
        for owner in range(self.seq):
            self.load(kind, owner).start()

    def wait_loads(self, kind):
        for owner in range(self.seq):
            self.load(kind, owner).wait()

    def store(self, kind, owner, first, size):
        rows = self.weights[kind]
        start = self.block_start(kind) + first
        source = rows.at[first : first + size, pl.ds(owner * self.share, self.share)]
        target = self.packed.at[owner, pl.ds(start, size)]
        return pltpu.make_async_copy(source, target, self.sems.at[4 + kind, owner])


def load_group(rows, seq, share):
    width = rows.shape[-1]
    part = width // seq
    value = rows.astype(jnp.float32).reshape(seq, GROUPS, part, width)
    return [value[:, g].reshape(width, width).astype(jnp.bfloat16) for g in range(GROUPS)]


def store_group(grads, seq, share):
    width = grads[0].shape[-1]
    part = width // seq
    value = jnp.stack([grad.reshape(seq, part, width) for grad in grads], axis=1)
    return value.reshape(seq, GROUPS * part, width).astype(jnp.bfloat16)


def put_tap(tiles, tap, value):
    latents = value.shape[0]
    for piece in range(tiles.shape[0]):
        tiles[piece, pl.ds(tap, latents, stride=STRIDE), :] = value[
            :, piece * lanes : (piece + 1) * lanes
        ]


def take_tap(tiles, tap, latents):
    return jnp.concatenate(
        [tiles[piece, pl.ds(tap, latents, stride=STRIDE), :] for piece in range(tiles.shape[0])],
        axis=1,
    )


def to_tiles(tiles, value):
    for piece in range(tiles.shape[0]):
        tiles[piece] = value[:, piece * lanes : (piece + 1) * lanes]


def from_tiles(tiles):
    return jnp.concatenate([tiles[piece] for piece in range(tiles.shape[0])], axis=1)


def set_edges(padded, length):
    zero = jnp.zeros((margin, padded.shape[1]), jnp.float32)
    padded[:margin, :] = zero
    padded[margin + length :, :] = zero


def front_kernel(
    sizes,
    geometry,
    length,
    enc_dilated,
    enc_point,
    enc_group,
    enc_strided,
    dec_dilated,
    dec_point,
    dec_group,
    dec_strided,
    code_own,
    ids_own,
    frames_own,
    cot_own,
    books_ref,
    gathered,
    frames_long,
    ids_ref,
    decoded_ref,
    grad_quant_ref,
    picks_ref,
    packed,
    left_ref,
    right_ref,
    shard_ref,
    wide_dilated,
    wide_point,
    wide_group,
    wide_strided,
    code_ref,
    cot_ref,
    dilated,
    pointwise,
    group,
    strided,
    streams,
    padded,
    columns,
    hidden,
    excited,
    active,
    tiles,
    sems,
    edge_sem,
    keep_sem,
    recv_sem,
    send_sem,
):
    seq, share, blocks = geometry
    wide, high, deep = sizes
    x, y, z, c = place(sizes)
    me = z * wide + x
    greet(sizes)
    sender = Sender(send_sem, (y * 2 + 1 - c, me))
    gathers = [
        Gather(
            sizes,
            sender,
            shard_ref.at[side].reshape(2, high, 2, -1, shard_ref.shape[-1]),
            gathered.at[:, :, side],
            recv_sem.at[side],
        )
        for side in range(2)
    ]
    encoder, decoder = gathers

    def pack(side):
        dil, point, both = wide_dilated[side], wide_point[side], wide_group[side]
        width = shard_ref.shape[-1]
        low = jnp.bfloat16
        at = 0
        for value in (dil, point, both.reshape(1, share, width)):
            shard_ref[side, at : at + value.shape[0]] = value.astype(low)
            at += value.shape[0]
        for part in range(2):
            value = wide_strided[side, :, :, part * width : (part + 1) * width]
            shard_ref[side, at : at + value.shape[0]] = value.astype(low)
            at += value.shape[0]
        if at < blocks:
            shard_ref[side, at:] = jnp.zeros((blocks - at, share, width), low)

    masters = ((enc_dilated, enc_point, enc_group, enc_strided),) + (
        (dec_dilated, dec_point, dec_group, dec_strided),
    )
    wides = (wide_dilated, wide_point, wide_group, wide_strided)
    reads = [
        [
            pltpu.make_async_copy(source, target.at[side], keep_sem.at[5 + 4 * side + number])
            for number, (source, target) in enumerate(zip(masters[side], wides))
        ]
        for side in range(2)
    ]
    for side in (1, 0):
        for copy in reads[side]:
            copy.start()
    for copy in reads[1]:
        copy.wait()
    pack(1)
    decoder.own_z()
    decoder.own_x()
    keeps = [
        pltpu.make_async_copy(
            gathers[side].in_ref, gathered.at[z, x, side], keep_sem.at[13 + side]
        )
        for side in range(2)
    ]
    keeps[1].start()
    for copy in reads[0]:
        copy.wait()
    pack(0)
    keeps[0].start()
    own = length // 2
    half = length // 4
    reach = half // STRIDE
    near = 80
    set_edges(padded, length)
    blank = jnp.zeros((half - near, cot_ref.shape[1]), jnp.float32)
    cot_ref[: half - near, :] = blank
    cot_ref[length - (half - near) :, :] = blank
    outside = jnp.full((margin, lanes), -1, jnp.int32)
    ids_ref[:margin, :] = outside
    ids_ref[margin + length :, :] = outside
    own_copies = [
        pltpu.make_async_copy(frames_own, frames_long.at[half : half + own], keep_sem.at[1]),
        pltpu.make_async_copy(cot_own, cot_ref.at[half : half + own], keep_sem.at[2]),
        pltpu.make_async_copy(
            ids_own, ids_ref.at[margin + half : margin + half + own], keep_sem.at[3]
        ),
        pltpu.make_async_copy(code_own, code_ref.at[:, reach : reach + own // STRIDE], keep_sem.at[4]),
    ]
    for copy in own_copies:
        copy.start()
    edges = [
        (frames_own.at[own - half :], frames_long.at[:half]),
        (cot_own.at[own - near :], cot_ref.at[half - near : half]),
        (ids_own.at[own - half :], ids_ref.at[margin : margin + half]),
        (code_own.at[:, own // STRIDE - reach :], code_ref.at[:, :reach]),
        (frames_own.at[:half], frames_long.at[half + own :]),
        (cot_own.at[:near], cot_ref.at[half + own : half + own + near]),
        (ids_own.at[:half], ids_ref.at[margin + half + own : margin + length]),
        (code_own.at[:, :reach], code_ref.at[:, reach + own // STRIDE :]),
    ]
    edge_copies = []
    for number, (src, dst) in enumerate(edges):
        other = (me + (1 if number < len(edges) // 2 else seq - 1)) % seq
        copy = pltpu.make_async_remote_copy(
            src_ref=src,
            dst_ref=dst,
            send_sem=edge_sem.at[0, number],
            recv_sem=edge_sem.at[1, number],
            device_id=(y * 2 + c, other),
            device_id_type=MESH,
        )
        copy.start()
        edge_copies.append(copy)
    for number in (3, 7):
        edge_copies[number].wait()
    own_copies[3].wait()
    latents = length // STRIDE
    codes = books_ref.shape[2]
    width = books_ref.shape[3]
    tile_range = lax.broadcasted_iota(jnp.int32, (latents, lanes), 1)
    quantized = []
    for g in range(GROUPS):
        picked = []
        for level in range(LEVELS):
            entry = g * LEVELS + level
            chosen = code_ref[entry]
            hot = jnp.concatenate(
                [
                    (chosen == tile_range + tile * lanes).astype(jnp.float32)
                    for tile in range(codes // lanes)
                ],
                axis=1,
            )
            pick = jnp.dot(hot, books_ref[g, level], precision=lax.Precision.HIGHEST)
            picks_ref[entry] = pick
            picked.append(pick)
        quantized.append((picked[0] + picked[1]).astype(jnp.bfloat16))
    for k in range(1, deep):
        decoder.from_z(k)
    encoder.own_z()
    for k in range(deep):
        decoder.second(k)
    encoder.own_x()
    for k in range(deep):
        decoder.third(k)
        if k > 0:
            encoder.from_z(k)
    for number, copy in enumerate(edge_copies):
        if number not in (3, 7):
            copy.wait()
    for copy in own_copies[:3]:
        copy.wait()

    @pl.when(me == 0)
    def _():
        ids_ref[margin : margin + half, :] = jnp.full((half, lanes), -1, jnp.int32)

    @pl.when(me == seq - 1)
    def _():
        ids_ref[margin + half + own : margin + length, :] = jnp.full((half, lanes), -1, jnp.int32)

    for copy in keeps:
        copy.wait()
    decoder.last()
    weights = (dilated, pointwise, group, strided)
    mover = Mover(1, geometry, gathered, packed, weights, sems)
    for kind in (2, 3, 0, 1):
        mover.start_loads(kind)
    pump = [functools.partial(encoder.second, k) for k in range(deep)]
    pump += [functools.partial(encoder.third, k) for k in range(deep)]
    first, last = length // 4, 3 * length // 4
    mover.wait_loads(2)
    out_weights = load_group(group[0], seq, share)
    mixed = [dot(quantized[g], out_weights[g]) for g in range(GROUPS)]
    lifted = [elu(value).astype(jnp.bfloat16) for value in mixed]
    mover.wait_loads(3)
    for tap in range(STRIDE):
        value = dot_last(lifted[0], strided[tap]) + dot_last(lifted[1], strided[STRIDE + tap])
        put_tap(tiles, tap, value)
    streams[0] = from_tiles(tiles)
    mover.wait_loads(0)
    mover.wait_loads(1)
    scratch = (padded, columns, hidden, excited, active)
    pump.pop(0)()
    for unit in range(3):
        forward_unit(
            unit, streams.at[unit], streams.at[unit + 1], ids_ref, (dilated, pointwise), scratch,
            length,
        )
        pump.pop(0)()
    decoded_ref[...] = streams[3, first:last, :].astype(jnp.bfloat16)
    grad = streams.at[3]
    grad[...] = cot_ref[...]

    for unit in (2, 1, 0):
        backward_unit(
            unit, grad, streams.at[unit], ids_ref, (dilated, pointwise), scratch, length,
        )
        for owner in range(seq):
            mover.store(0, owner, unit * KERNEL, KERNEL).start()
        if pump:
            pump.pop(0)()
    for owner in range(seq):
        mover.store(1, owner, 0, 3).start()
    own = slice(first // STRIDE, last // STRIDE)
    grad_lifted = [None, None]
    own_taps = []
    to_tiles(tiles, grad[...])
    for tap in range(STRIDE):
        part = take_tap(tiles, tap, latents)
        low = part.astype(jnp.bfloat16)
        own_taps.append(part[own])
        for half in range(2):
            value = dot(low, strided[half * STRIDE + tap])
            grad_lifted[half] = value if tap == 0 else grad_lifted[half] + value
    for number, value in enumerate(outer_left(own_taps)):
        left_ref[number] = value
    right_ref[...] = jnp.concatenate([lifted[0][own], lifted[1][own]], axis=1)
    group_grads = []
    for g in range(GROUPS):
        low = (grad_lifted[g] * elu_slope(mixed[g])).astype(jnp.bfloat16)
        group_grads.append(dot_rows(quantized[g][own], low[own]))
        grad_quant_ref[g] = dot_last(low, out_weights[g])
    group[0] = store_group(group_grads, seq, share).reshape(group.shape[1:])
    for owner in range(seq):
        mover.store(2, owner, 0, 1).start()
    while pump:
        pump.pop(0)()
    finish_stores(mover, seq)
    encoder.last()
    sender.finish()


def finish_stores(mover, seq):
    for owner in range(seq):
        for unit in range(3):
            mover.store(0, owner, unit * KERNEL, KERNEL).wait()
        mover.store(1, owner, 0, 3).wait()
        mover.store(2, owner, 0, 1).wait()


def back_kernel(
    sizes,
    split,
    geometry,
    length,
    frames_ref,
    ids_ref,
    grad_quant_ref,
    picks_ref,
    digits_ref,
    left_ref,
    right_ref,
    gathered,
    partial_ref,
    frames_grad_ref,
    packed,
    share_decoder,
    share_encoder,
    all_ref,
    strided_out,
    dilated,
    pointwise,
    group,
    strided,
    streams,
    padded,
    columns,
    hidden,
    excited,
    active,
    tiles,
    sems,
    *refs,
):
    seq, share, blocks = geometry
    x, y, z, c = place(sizes)
    me = z * sizes[0] + x
    greet(sizes, row=True)
    sender = Sender(refs[-1], (y * 2 + 1 - c, me))
    packed_view = packed.reshape(partial_ref.shape)
    other = Reduce(sizes, split, sender, partial_ref, share_decoder, refs[:reduce_parts])
    side = Reduce(sizes, split, sender, packed_view, share_encoder, refs[reduce_parts : 2 * reduce_parts])
    rows_ref, keep_sem, row_sem = refs[2 * reduce_parts : 2 * reduce_parts + 3]
    spread = Spread(sizes, sender, rows_ref, all_ref, row_sem, keep_sem)
    extra = refs[2 * reduce_parts + 3 : -1]
    left_own, right_own, lefts, rights, partials = extra[:5]
    left_sem, right_sem = extra[5:7]
    down, up = [
        Outer(
            sizes, sender, left, right, lefts.at[side], rights.at[side], left_sem.at[side],
            right_sem.at[side],
        )
        for side, (left, right) in enumerate(((left_own, right_own), (left_ref, right_ref)))
    ]
    both = OuterSum(sizes, sender, partials, strided_out, extra[7:])
    other.start()
    up.start()
    turns = sizes[2] + 2
    pump = [functools.partial(other.turn, number) for number in range(turns)]
    pump += [other.total, other.last]
    for spot in (2, 4, 6):
        pump.insert(spot, lambda: None)
    weights = (dilated, pointwise, group, strided)
    mover = Mover(0, geometry, gathered, packed, weights, sems)
    for kind in (0, 1, 3, 2):
        mover.start_loads(kind)
    set_edges(padded, length)
    first, last = length // 4, 3 * length // 4
    latents = length // STRIDE
    own = slice(first // STRIDE, last // STRIDE)
    width = picks_ref.shape[2]
    streams[0] = frames_ref[...].astype(jnp.float32)
    mover.wait_loads(0)
    mover.wait_loads(1)
    scratch = (padded, columns, hidden, excited, active)
    for unit in range(3):
        forward_unit(
            unit, streams.at[unit], streams.at[unit + 1], ids_ref, (dilated, pointwise), scratch,
            length,
        )
        pump.pop(0)()
    to_tiles(tiles, elu(streams[3]))
    mover.wait_loads(3)
    mover.wait_loads(2)
    in_weights = load_group(group[0], seq, share)
    latent = [None, None]
    for tap in range(STRIDE):
        low = take_tap(tiles, tap, latents).astype(jnp.bfloat16)
        for half in range(2):
            value = dot(low, strided[half * STRIDE + tap])
            latent[half] = value if tap == 0 else latent[half] + value
    group_grads = []
    grad_latent = []
    for g in range(GROUPS):
        low = latent[g].astype(jnp.bfloat16)
        first_part = dot(low, in_weights[g])
        pick = [picks_ref[g * LEVELS + level] for level in range(LEVELS)]
        second_part = first_part - pick[0]
        rows_ref[:, g * width : (g + 1) * width] = first_part[own].astype(jnp.bfloat16)
        grad_first = grad_quant_ref[g] + 2.0 * commit_weight * (
            second_part + (second_part - pick[1])
        )
        low_first = grad_first.astype(jnp.bfloat16)
        group_grads.append(dot_rows(low[own], low_first[own]))
        grad_latent.append(dot_last(low_first, in_weights[g]).astype(jnp.bfloat16))
    group[0] = store_group(group_grads, seq, share).reshape(group.shape[1:])
    rows_ref[:, GROUPS * width :] = digits_ref[...]
    spread.stage(0)
    for owner in range(seq):
        mover.store(2, owner, 0, 1).start()
    own_taps = []
    for tap in range(STRIDE):
        own_taps.append(take_tap(tiles, tap, latents)[own])
        value = dot_last(grad_latent[0], strided[tap]) + dot_last(
            grad_latent[1], strided[STRIDE + tap]
        )
        put_tap(tiles, tap, value)
    for number, value in enumerate(outer_left(own_taps)):
        left_own[number] = value
    right_own[...] = jnp.concatenate([grad_latent[0][own], grad_latent[1][own]], axis=1)
    down.start()
    grad = streams.at[3]
    grad[...] = from_tiles(tiles) * elu_slope(grad[...])
    pump.pop(0)()

    for unit in (2, 1, 0):
        backward_unit(
            unit, grad, streams.at[unit], ids_ref, (dilated, pointwise), scratch, length,
        )
        for owner in range(seq):
            mover.store(0, owner, unit * KERNEL, KERNEL).start()
        if pump:
            pump.pop(0)()
    for owner in range(seq):
        mover.store(1, owner, 0, 3).start()
    frames_grad_ref[...] = grad[first:last, :]
    finish_stores(mover, seq)
    side.start()
    outer = [both.to_core, both.to_y, both.back_y, both.back_core, both.last]
    up.multiply(partials.at[1])
    for number in range(turns):
        if pump:
            pump.pop(0)()
        side.turn(number)
        if number == 0:
            down.multiply(partials.at[0])
        outer.pop(0)() if outer else None
        if number >= turns - 2:
            spread.stage(number - turns + 3)
    side.total()
    spread.stage(3)
    side.last()
    spread.stage(4)
    sender.finish()


def side_scratch(seq, share, length, channels, hidden):
    bf, f32 = jnp.bfloat16, jnp.float32
    group_rows = GROUPS * hidden // seq
    mats = [
        pltpu.VMEM((3 * KERNEL, channels, hidden), bf),
        pltpu.VMEM((3, channels, hidden), bf),
        pltpu.VMEM((1, seq * group_rows, hidden), bf),
        pltpu.VMEM((2 * STRIDE, channels, hidden), bf),
    ]
    return mats + [
        pltpu.VMEM((4, length, channels), f32),
        pltpu.VMEM((length + 2 * margin, channels), f32),
        pltpu.VMEM((length, KERNEL * channels), bf),
        pltpu.VMEM((3, length, hidden), f32),
        pltpu.VMEM((3, length, hidden), bf),
        pltpu.VMEM((3, length // 2, channels), bf),
        pltpu.VMEM((channels // lanes, length, lanes), f32),
        pltpu.SemaphoreType.DMA((8, seq)),
    ]


def split_terms(value, count):
    terms = []
    for number in range(count):
        term = value.astype(jnp.bfloat16)
        terms.append(term)
        if number < count - 1:
            value = value - term.astype(jnp.float32)
    return terms


def product(left, right):
    def pair(i, j):
        return jnp.dot(left[i], right[j], preferred_element_type=jnp.float32)

    low = pair(0, 1) + pair(1, 0)
    if len(left) > 2:
        low = low + (pair(1, 1) + pair(0, 2) + pair(2, 0))
    return pair(0, 0) + low


def gram_of(left, right):
    return product(split_terms(left.T, 3), split_terms(right, 3))


def solve_mixing(gram):
    size = gram.shape[0]
    eye = (
        lax.broadcasted_iota(jnp.int32, (size, size), 0)
        == lax.broadcasted_iota(jnp.int32, (size, size), 1)
    ).astype(jnp.float32)
    scale = 1.0 / (jnp.sqrt(jnp.sum(gram * eye)) + norm_floor)
    current = gram * (scale * scale)
    total = None
    for repeat in range(NS_STEPS):
        terms = 3 if repeat < 2 else 2
        parts = split_terms(current, terms)
        factor = coef_first * eye + coef_second * current + coef_third * product(parts, parts)
        factors = split_terms(factor, terms)
        if total is None:
            total = factor
        else:
            total = product(split_terms(total, 2), factors[:2])
        if repeat < NS_STEPS - 1:
            half = split_terms(product(parts, factors), terms)
            current = product(half, factors)
    return total * scale


def solve_pair(corner, side, other):
    size = corner.shape[0]
    eye = (
        lax.broadcasted_iota(jnp.int32, (size, size), 0)
        == lax.broadcasted_iota(jnp.int32, (size, size), 1)
    ).astype(jnp.float32)
    scale = 1.0 / (jnp.sqrt(jnp.sum((corner + other) * eye)) + norm_floor)
    current = [value * (scale * scale) for value in (corner, side, other)]

    def whole(blocks, terms):
        parts = [split_terms(value, terms) for value in blocks]
        turned = split_terms(blocks[1].T, terms)
        top = [jnp.concatenate([p, q], axis=1) for p, q in zip(parts[0], parts[1])]
        low = [jnp.concatenate([p, q], axis=1) for p, q in zip(turned, parts[2])]
        return top, low

    def times(left, right):
        rows = [jnp.concatenate([p, q], axis=0) for p, q in zip(*right)]
        top = product(left[0], rows)
        low = product(left[1], [value[:, size:] for value in rows])
        return [top[:, :size], top[:, size:], low]

    total = None
    for repeat in range(NS_STEPS):
        terms = 3 if repeat < 2 else 2
        parts = whole(current, terms)
        square = times(parts, parts)
        factor = [
            coef_second * value + coef_third * double for value, double in zip(current, square)
        ]
        factor = [factor[0] + coef_first * eye, factor[1], factor[2] + coef_first * eye]
        factors = whole(factor, terms)
        if total is None:
            total = factor
        else:
            total = times(whole(total, 2), [values[:2] for values in factors])
        if repeat < NS_STEPS - 1:
            half = whole(times(parts, factors), terms)
            current = times(half, factors)
    return [value * scale for value in total]


def mixing_kernel(
    sizes,
    share,
    enc_dilated,
    enc_point,
    enc_group,
    enc_strided,
    dec_dilated,
    dec_point,
    dec_group,
    dec_strided,
    enc_dilated_w,
    enc_strided_w,
    dec_dilated_w,
    dec_strided_w,
    row_ref,
    books_ref,
    buffered_ref,
    marks_ref,
    small_ref,
    enc_dilated_next,
    enc_strided_next,
    dec_dilated_next,
    dec_strided_next,
    books_next,
    mix_ref,
    dilated,
    point,
    group,
    strided,
    dilated_w,
    strided_w,
    blocks,
    corner,
    slots,
    point_all,
    group_all,
    work,
    point_done,
    group_done,
    load_sem,
    send_sem,
    slot_sem,
    rows_sem,
    mix_sem,
    core_sem,
    small_sem,
    corner_sem,
    all_ref,
    books,
    first_books,
    buffered,
    code_sem,
):
    wide, high, deep = sizes
    x, y, z, c = place(sizes)
    count = wide * deep
    me = z * wide + x
    row = y * 2 + c
    middle = count // 2
    partner = (y * 2 + 1 - c, me)
    others = [(row, (me + k) % count) for k in range(1, count)]
    others += [
        ((y + j) % high * 2 + c, z * wide + (x + i) % wide)
        for i in range(wide)
        for j in range(1, high)
    ] + [partner]
    barrier = pltpu.get_barrier_semaphore()
    for other in others:
        pl.semaphore_signal(barrier, inc=1, device_id=other, device_id_type=MESH)
    pl.semaphore_wait(barrier, len(others))

    pending = []

    def remote(src, dst, number, recv, to):
        return pltpu.make_async_remote_copy(
            src_ref=src,
            dst_ref=dst,
            send_sem=send_sem.at[number],
            recv_sem=recv,
            device_id=to,
            device_id_type=MESH,
        )

    def send(when, src, dst, recv, to):
        number = len(pending)
        pending.append((when, src, dst, recv, to))

        @pl.when(when)
        def _():
            remote(src, dst, number, recv, to).start()

    def arrive(dst, recv):
        remote(dst, dst, 0, recv, partner).wait_recv()

    first_set = y == 0
    second_set = y == 1

    def load(number, source, target):
        return pltpu.make_async_copy(source, target, load_sem.at[number])

    own_loads = [
        (enc_dilated, dilated.at[0]),
        (dec_dilated, dilated.at[1]),
        (enc_strided, strided.at[0]),
        (dec_strided, strided.at[1]),
        (enc_point, point.at[0]),
        (dec_point, point.at[1]),
        (enc_group, group.at[0]),
        (dec_group, group.at[1]),
        (enc_dilated_w, dilated_w.at[0]),
        (dec_dilated_w, dilated_w.at[1]),
        (enc_strided_w, strided_w.at[0]),
        (dec_strided_w, strided_w.at[1]),
    ]
    for number, (source, target) in enumerate(own_loads):
        load(number, source, target).start()
    code_share = books.shape[2]
    own_books = books_ref.at[:, :, pl.ds(pl.multiple_of(me * code_share, 8), code_share)]
    code_loads = [
        pltpu.make_async_copy(row_ref, all_ref, code_sem.at[0]),
        pltpu.make_async_copy(own_books, books, code_sem.at[1]),
        pltpu.make_async_copy(buffered_ref, buffered, code_sem.at[2]),
        pltpu.make_async_copy(books_ref.at[:, 0], first_books, code_sem.at[3]),
    ]
    for copy in code_loads:
        copy.start()
    for number in (4, 5, 6, 7, 2, 3, 0, 1):
        load(number, *own_loads[number]).wait()

    block_at = [middle - 2 + number + c for number in range(3)]
    strided_at = block_at[1]
    small_at = [(middle + c + offset + count) % count for offset in (1, 2, 3, -3, -4)]
    point_at, group_at = small_at[:3], small_at[3:]
    part = share // GROUPS
    piece = blocks.shape[1] // (wide * high)

    for unit in range(3):
        at = point_at[unit]
        rows = pl.ds(pl.multiple_of(me * share, 8), share)
        send(
            second_set & (me != at),
            point.at[c, unit],
            point_all.at[rows],
            rows_sem.at[me],
            (row, at),
        )

        @pl.when(second_set & (me == at))
        def _():
            point_all[rows, :] = point[c, unit]

    for g in range(GROUPS):
        at = group_at[g]
        rows = pl.ds(pl.multiple_of(me * part, 8), part)
        send(
            second_set & (me != at),
            group.at[c, g],
            group_all.at[rows],
            rows_sem.at[me],
            (row, at),
        )

        @pl.when(second_set & (me == at))
        def _():
            group_all[rows, :] = group[c, g]

    block = blocks.shape[1]

    @pl.when(first_set)
    def _():
        for unit in range(3):
            value = dilated[c, unit * KERNEL : (unit + 1) * KERNEL].reshape(KERNEL * share, block)
            blocks[unit] = gram_of(value, value)

    @pl.when(second_set)
    def _():
        value = strided[c].reshape(-1, 2 * block)
        left, right = value[:, :block], value[:, block:]
        blocks[0] = gram_of(left, left)
        blocks[1] = gram_of(left, right)
        blocks[2] = gram_of(right, right)

    for number in range(3):
        at = block_at[number]
        send(
            (first_set | second_set) & (me != at),
            blocks.at[number],
            slots.at[number, me],
            slot_sem.at[number, me],
            (row, at),
        )

    for copy in code_loads:
        copy.wait()
    renew_codes(me, all_ref, books, first_books, buffered, marks_ref, books_next)

    def summed(number):
        total = blocks[number]
        for k in range(1, count):
            source = (me + k) % count
            arrive(slots.at[number, source], slot_sem.at[number, source])
            total = total + slots[number, source]
        return total

    for number in range(3):

        @pl.when((first_set | second_set) & (me == block_at[number]))
        def _():
            work[...] = summed(number)

    for number in (0, 2):
        send(
            second_set & (me == block_at[number]),
            work,
            corner.at[number // 2],
            corner_sem.at[number // 2],
            (row, strided_at),
        )

    @pl.when(second_set & (me == strided_at))
    def _():
        for number in range(2):
            arrive(corner.at[number], corner_sem.at[number])
        solved = solve_pair(corner[0], work[...], corner[1])
        for number in range(3):
            mix_ref[1, c, number] = solved[number]

    def piece_of(which, number, xs, ys):
        rows = pl.ds(pl.multiple_of((xs * high + ys) * piece, 8), piece)
        return (
            mix_ref.at[which, c, number, rows],
            mix_sem.at[which, c, number, xs * high + ys],
        )

    def hand_first(which, number, at):
        owner = (y == which) & (me == at)
        for i in range(wide):
            for j in range(high):
                if i == 0 and j == 0:
                    continue
                xt, yt = (x + i) % wide, (y + j) % high
                spot, recv = piece_of(which, number, xt, yt)
                send(owner, spot, spot, recv, (yt * 2 + c, z * wide + xt))

    for number in range(3):
        hand_first(1, number, strided_at)

    is_point = second_set & (
        (me == point_at[0]) | (me == point_at[1]) | (me == point_at[2])
    )
    is_group = second_set & ((me == group_at[0]) | (me == group_at[1]))
    is_dilated = first_set & (
        (me == block_at[0]) | (me == block_at[1]) | (me == block_at[2])
    )

    @pl.when(is_point)
    def _():
        for k in range(1, count):
            source = (me + k) % count
            rows = pl.ds(pl.multiple_of(source * share, 8), share)
            arrive(point_all.at[rows], rows_sem.at[source])
        work[...] = gram_of(point_all[...], point_all[...])

    @pl.when(is_group)
    def _():
        for k in range(1, count):
            source = (me + k) % count
            rows = pl.ds(pl.multiple_of(source * part, 8), part)
            arrive(group_all.at[rows], rows_sem.at[source])
        work[...] = gram_of(group_all[...], group_all[...])

    @pl.when(is_dilated | is_point | is_group)
    def _():
        work[...] = solve_mixing(work[...])

    for unit in range(3):

        @pl.when(first_set & (me == block_at[unit]))
        def _():
            mix_ref[0, c, unit] = work[...]

        hand_first(0, unit, block_at[unit])

    @pl.when(is_point)
    def _():
        point_done[...] = product(split_terms(point_all[...], 3), split_terms(work[...], 3))

    @pl.when(is_group)
    def _():
        group_done[...] = product(split_terms(group_all[...], 3), split_terms(work[...], 3))

    for unit in range(3):
        at = point_at[unit]
        for k in range(1, count):
            target = (me + k) % count
            rows = pl.ds(pl.multiple_of(target * share, 8), share)
            send(
                second_set & (me == at),
                point_done.at[rows],
                small_ref.at[c, unit],
                small_sem.at[unit],
                (row, target),
            )

        @pl.when(second_set & (me == at))
        def _():
            small_ref[c, unit] = point_done[pl.ds(pl.multiple_of(me * share, 8), share), :]

    for g in range(GROUPS):
        at = group_at[g]
        spot = small_ref.at[c, 3, g * part : (g + 1) * part]
        for k in range(1, count):
            target = (me + k) % count
            rows = pl.ds(pl.multiple_of(target * part, 8), part)
            send(
                second_set & (me == at),
                group_done.at[rows],
                spot,
                small_sem.at[3 + g],
                (row, target),
            )

        @pl.when(second_set & (me == at))
        def _():
            spot[...] = group_done[pl.ds(pl.multiple_of(me * part, 8), part), :]

    always = y >= 0

    def hand_down(which, number, at):
        owner = (y == which) & (me == at)
        in_plane = z == at // wide
        spot, recv = piece_of(which, number, x, y)

        @pl.when(jnp.logical_not(owner))
        def _():
            arrive(spot, recv)

        for k in range(1, deep):
            send(in_plane, spot, spot, recv, (row, (z + k) % deep * wide + x))

    def hand_across(which, number, at):
        spot, recv = piece_of(which, number, x, y)
        for i in range(wide):
            for j in range(high):
                if i == 0 and j == 0:
                    continue
                xt, yt = (x + i) % wide, (y + j) % high
                target = z * wide + xt
                wants = jnp.logical_not((yt == which) & (target == at))
                send(wants, spot, spot, recv, (yt * 2 + c, target))

    def hand_over(which, number, at):
        owner = (y == which) & (me == at)

        @pl.when(jnp.logical_not(owner))
        def _():
            for i in range(wide):
                for j in range(high):
                    if i == 0 and j == 0:
                        continue
                    arrive(*piece_of(which, number, (x + i) % wide, (y + j) % high))

        spot = mix_ref.at[which, c, number]
        send(always, spot, spot, core_sem.at[which, c, number], partner)

    strided_ats = [strided_at] * 3
    for which, ats in ((0, block_at), (1, strided_ats)):
        for step in (hand_down, hand_across):
            for number in range(3):
                step(which, number, ats[number])
    for unit in range(3):

        @pl.when(second_set & (me != point_at[unit]))
        def _():
            arrive(small_ref.at[c, unit], small_sem.at[unit])

    for g in range(GROUPS):

        @pl.when(second_set & (me != group_at[g]))
        def _():
            arrive(small_ref.at[c, 3, g * part : (g + 1) * part], small_sem.at[3 + g])

    for k in range(1, high):
        send(
            second_set,
            small_ref.at[c],
            small_ref.at[c],
            small_sem.at[5],
            ((y + k) % high * 2 + c, me),
        )

    @pl.when(jnp.logical_not(second_set))
    def _():
        arrive(small_ref.at[c], small_sem.at[5])

    send(always, small_ref.at[c], small_ref.at[c], small_sem.at[6], partner)
    for which, ats in ((0, block_at), (1, strided_ats)):
        for number in range(3):
            hand_over(which, number, ats[number])
    for unit in range(3):
        arrive(mix_ref.at[0, 1 - c, unit], core_sem.at[0, 1 - c, unit])
    for number in range(8, 12):
        load(number, *own_loads[number]).wait()
    for side, target in enumerate((enc_dilated_next, dec_dilated_next)):
        for unit in range(3):
            taps = slice(unit * KERNEL, (unit + 1) * KERNEL)
            rows = dilated[side, taps].reshape(KERNEL * share, block)
            moved = product(split_terms(rows, 2), split_terms(mix_ref[0, side, unit], 2))
            target[taps] = dilated_w[side, taps] - update_rate * moved.reshape(
                KERNEL, share, block
            )
    arrive(small_ref.at[1 - c], small_sem.at[6])
    for number in range(3):
        arrive(mix_ref.at[1, 1 - c, number], core_sem.at[1, 1 - c, number])
    for side, target in enumerate((enc_strided_next, dec_strided_next)):
        corners = [split_terms(mix_ref[1, side, number], 2) for number in range(3)]
        turned = split_terms(mix_ref[1, side, 1].T, 2)
        rows = strided[side].reshape(-1, 2 * block)
        left, right = split_terms(rows[:, :block], 2), split_terms(rows[:, block:], 2)
        low = product(left, corners[0]) + product(right, turned)
        top = product(left, corners[1]) + product(right, corners[2])
        shape = (strided.shape[1], share, block)
        target[:, :, :block] = strided_w[side, :, :, :block] - update_rate * low.reshape(shape)
        target[:, :, block:] = strided_w[side, :, :, block:] - update_rate * top.reshape(shape)

    for number, (when, src, dst, recv, to) in enumerate(pending):

        @pl.when(when)
        def _():
            remote(src, dst, number, recv, to).wait_send()


def renew_codes(me, all_ref, books, first_books, buffered, marks_ref, books_next):
    groups, levels, share, width = books.shape
    entries = groups * levels
    codes = first_books.shape[1]
    slot_range = lax.broadcasted_iota(jnp.int32, (share, buffered.shape[1]), 1)
    deep, wide, high, _, length, _ = all_ref.shape
    size = wide * high * 2 * length
    every = lax.broadcasted_iota(jnp.int32, (codes, size), 0).astype(jnp.float32)
    own_range = lax.broadcasted_iota(jnp.int32, (share, size), 0) + me * share
    own_range = own_range.astype(jnp.float32)
    ones = jnp.ones((size, lanes), jnp.bfloat16)
    sums = [None] * entries
    counts = [None] * entries
    pairs = [None] * groups

    def add(target, number, value):
        target[number] = value if target[number] is None else target[number] + value

    def chosen(digits, entry, choices):
        code = digits[entry : entry + 1] * 32.0 + digits[entries + entry : entries + entry + 1]
        return (code == choices).astype(jnp.float32).astype(jnp.bfloat16)

    for zs in range(deep):
        rows = all_ref[zs].reshape(size, -1)
        digits = rows[:, groups * width :].astype(jnp.float32).T
        for g in range(groups):
            values = rows[:, g * width : (g + 1) * width]
            for level in range(levels):
                entry = g * levels + level
                hot = chosen(digits, entry, own_range)
                add(sums, entry, dot(hot, values))
                add(counts, entry, dot(hot, ones))
            add(pairs, g, dot_last(hot, chosen(digits, g * levels, every)))
    for entry in range(entries):
        g, level = entry // levels, entry % levels
        if level == 1:
            both = split_terms(pairs[g], 2)
            taken = product(both, split_terms(first_books[g], 2))
            sums[entry] = sums[entry] - taken
        count = jnp.concatenate([counts[entry]] * (width // lanes), axis=1)
        own = books[g, level]
        mean = sums[entry] / jnp.maximum(count, 1.0)
        updated = own + code_rate * jnp.minimum(count, 1.0) * (mean - own)
        hot = (marks_ref[:, entry : entry + 1] == slot_range).astype(jnp.bfloat16)
        replaced = None
        for term in split_terms(buffered[g], 3):
            part = dot(hot, term)
            replaced = part if replaced is None else replaced + part
        dead = marks_ref[:, entries + entry : entries + entry + 1] == 1
        books_next[g, level] = jnp.where(dead, replaced, updated)


def solve_all(views, weights, codes, sizes, collective_id):
    wide, high, deep = sizes
    count = wide * deep
    share, block = views[0].shape[1:]
    part = share // GROUPS
    f32 = jnp.float32
    dma = pltpu.SemaphoreType.DMA
    sends = 5 + 3 + 2 + 5 * (count - 1) + (high - 1) + 1 + 6 * (deep + 2 * (wide * high - 1))
    all_rows, books, buffered, marks = codes
    own_books = books.shape[:2] + (books.shape[2] // count,) + books.shape[3:]
    vmem = pl.BlockSpec(memory_space=pltpu.VMEM)
    return pl.pallas_call(
        functools.partial(mixing_kernel, sizes, share),
        out_shape=(jax.ShapeDtypeStruct((2, 4, share, block), f32),)
        + tuple(jax.ShapeDtypeStruct(weight.shape, f32) for weight in weights)
        + (jax.ShapeDtypeStruct(own_books, f32),),
        in_specs=[pl.BlockSpec(memory_space=pl.ANY)] * 15 + [vmem],
        out_specs=(vmem,) * 6,
        scratch_shapes=[
            pltpu.VMEM((2, 2, 3, block, block), f32),
            pltpu.VMEM((2,) + views[0].shape, f32),
            pltpu.VMEM((2,) + views[1].shape, f32),
            pltpu.VMEM((2,) + views[2].shape, f32),
            pltpu.VMEM((2,) + views[3].shape, f32),
            pltpu.VMEM((2,) + views[0].shape, f32),
            pltpu.VMEM((2,) + views[3].shape, f32),
            pltpu.VMEM((3, block, block), f32),
            pltpu.VMEM((2, block, block), f32),
            pltpu.VMEM((3, count, block, block), f32),
            pltpu.VMEM((count * share, block), f32),
            pltpu.VMEM((count * part, block), f32),
            pltpu.VMEM((block, block), f32),
            pltpu.VMEM((count * share, block), f32),
            pltpu.VMEM((count * part, block), f32),
            dma((12,)),
            dma((sends,)),
            dma((3, count)),
            dma((count,)),
            dma((2, 2, 3, wide * high)),
            dma((2, 2, 3)),
            dma((7,)),
            dma((2,)),
            pltpu.VMEM(all_rows.shape, all_rows.dtype),
            pltpu.VMEM(own_books, f32),
            pltpu.VMEM(books.shape[:1] + books.shape[2:], f32),
            pltpu.VMEM(buffered.shape, f32),
            dma((4,)),
        ],
        compiler_params=pltpu.CompilerParams(
            collective_id=collective_id, has_side_effects=True, vmem_limit_bytes=60 * 2**20
        ),
    )(*views, *weights, *codes)


def velocity_kernel(share_encoder, share_decoder, strided_sums, *refs):
    moments, outs = refs[:8], refs[8:]
    for side, rows in enumerate((share_encoder, share_decoder)):
        dilated, point, group, strided = range(4 * side, 4 * side + 4)
        at = 0
        for number in (dilated, point):
            size = moments[number].shape[0]
            step = rows[at : at + size].astype(jnp.float32)
            outs[number][...] = moment_decay * moments[number][...] + step
            at += size
        step = rows[at].astype(jnp.float32).reshape(moments[group].shape)
        outs[group][...] = moment_decay * moments[group][...] + step
        outs[strided][...] = moment_decay * moments[strided][...] + strided_sums[side]


def new_velocities(side_shares, moments):
    vmem = pl.BlockSpec(memory_space=pltpu.VMEM)
    return pl.pallas_call(
        velocity_kernel,
        out_shape=tuple(jax.ShapeDtypeStruct(moment.shape, jnp.float32) for moment in moments),
        in_specs=[vmem] * (len(side_shares) + len(moments)),
        out_specs=(vmem,) * len(moments),
        compiler_params=pltpu.CompilerParams(vmem_limit_bytes=60 * 2**20),
    )(*side_shares, *moments)


def per_device(
    frames,
    cotangent,
    segment_ids,
    code_index,
    codebooks,
    dead_codes,
    code_slots,
    buffered,
    encoder_dilated,
    encoder_pointwise,
    down_weight,
    group_in,
    group_out,
    up_weight,
    decoder_dilated,
    decoder_pointwise,
    encoder_dilated_moment,
    encoder_pointwise_moment,
    down_moment,
    group_in_moment,
    group_out_moment,
    up_moment,
    decoder_dilated_moment,
    decoder_pointwise_moment,
):
    masters = (
        encoder_dilated,
        encoder_pointwise,
        down_weight,
        group_in,
        group_out,
        up_weight,
        decoder_dilated,
        decoder_pointwise,
    )
    olds = (
        encoder_dilated_moment,
        encoder_pointwise_moment,
        down_moment,
        group_in_moment,
        group_out_moment,
        up_moment,
        decoder_dilated_moment,
        decoder_pointwise_moment,
    )
    count = lax.axis_size("seq")
    sizes = line_sizes(count, lax.axis_size("dp"))
    sides = ((0, 1, 3, 2), (6, 7, 4, 5))
    side_rows = whole_rows(masters, sizes[1])
    wide, high, deep = sizes
    _, length, channels = frames.shape
    long = 2 * length
    latent_len = long // STRIDE
    place_seq = lax.axis_index("seq")
    hidden = encoder_dilated.shape[-1]
    share = masters[0].shape[2]
    blocks = side_rows // share
    geometry = (count, share, blocks)
    rows = side_rows // (4 * high)
    low, f32 = jnp.bfloat16, jnp.float32
    dma = pltpu.SemaphoreType.DMA
    ids_own = jnp.broadcast_to(segment_ids[0][:, None], (length, lanes))
    entries = GROUPS * LEVELS
    code_own = code_index[0].reshape(-1, entries).T
    code_own = jnp.broadcast_to(code_own[:, :, None], code_own.shape + (lanes,))
    vmem = pl.BlockSpec(memory_space=pltpu.VMEM)
    anywhere = pl.BlockSpec(memory_space=pl.ANY)
    grad_rows, split = reduce_rows(masters, high)
    pieces = sum(split)
    grad_blocks = grad_rows // share
    partial_type = jax.ShapeDtypeStruct((count, grad_blocks, share, hidden), low)
    latents = length // STRIDE
    taps = masters[2].shape[0]
    left_type = jax.ShapeDtypeStruct((taps * latents // lanes, channels, lanes), low)
    right_type = jax.ShapeDtypeStruct((latents, channels), low)
    scratch = side_scratch(count, share, long, channels, hidden)
    flat = [masters[i].reshape((-1,) + masters[i].shape[-2:]) for side in sides for i in side]
    packed_shape = (2, high, 2, rows, hidden)
    piece_rows = grad_rows // (2 * high * pieces)
    reduce_shape = (2, high, pieces, piece_rows, hidden)
    both = [pltpu.VMEM((2,) + array.shape, f32) for array in flat[:4]]
    gathered, frames_long, ids, decoded, grad_quant, picks, partial, left, right = pl.pallas_call(
        functools.partial(front_kernel, sizes, geometry, long),
        out_shape=(
            jax.ShapeDtypeStruct((deep, wide, 2) + packed_shape, low),
            jax.ShapeDtypeStruct((long, channels), frames.dtype),
            jax.ShapeDtypeStruct((long + 2 * margin, lanes), jnp.int32),
            jax.ShapeDtypeStruct((length, channels), low),
            jax.ShapeDtypeStruct((GROUPS, latent_len, hidden), f32),
            jax.ShapeDtypeStruct((entries, latent_len, hidden), f32),
            partial_type,
            left_type,
            right_type,
        ),
        in_specs=[anywhere] * 12 + [vmem],
        out_specs=(anywhere, vmem, vmem, vmem, vmem, vmem, anywhere, vmem, vmem),
        scratch_shapes=[pltpu.VMEM((2, blocks, share, hidden), low)]
        + both
        + [
            pltpu.VMEM((entries, latent_len, lanes), jnp.int32),
            pltpu.VMEM((long, channels), f32),
        ]
        + scratch
        + [
            dma((2, 8)),
            dma((15,)),
            dma((2, deep, wide, 2, high, 2)),
            dma((2 * gather_sends(sizes),)),
        ],
        compiler_params=pltpu.CompilerParams(
            collective_id=0, has_side_effects=True, vmem_limit_bytes=60 * 2**20
        ),
    )(*flat, code_own, ids_own, frames[0], cotangent[0], codebooks)
    own_codes_low = code_index[0].reshape(-1, entries)
    digits = jnp.concatenate([own_codes_low // 32, own_codes_low % 32], axis=1)
    digits = jnp.pad(digits, ((0, 0), (0, lanes - digits.shape[1]))).astype(low)
    rows_own = (length // STRIDE, GROUPS * hidden + lanes)
    grad, _, share_decoder, share_encoder, all_rows, strided_sums = pl.pallas_call(
        functools.partial(back_kernel, sizes, split, geometry, long),
        out_shape=(
            jax.ShapeDtypeStruct((length, channels), f32),
            partial_type,
            jax.ShapeDtypeStruct(reduce_shape, low),
            jax.ShapeDtypeStruct(reduce_shape, low),
            jax.ShapeDtypeStruct((deep, wide, high, 2) + rows_own, low),
            jax.ShapeDtypeStruct((2, taps, share, channels), f32),
        ),
        in_specs=[vmem] * 7 + [anywhere, anywhere],
        out_specs=(vmem, anywhere, anywhere, anywhere, anywhere, vmem),
        scratch_shapes=scratch
        + reduce_scratch(sizes, split, piece_rows, hidden, low)
        + reduce_scratch(sizes, split, piece_rows, hidden, low)
        + [
            pltpu.VMEM(rows_own, low),
            dma,
            dma((deep, wide, high, 2)),
            pltpu.VMEM(left_type.shape, low),
            pltpu.VMEM(right_type.shape, low),
            pltpu.VMEM((2, count, left_type.shape[0], share, lanes), low),
            pltpu.VMEM((2, count) + right_type.shape, low),
            pltpu.VMEM((2, taps, share, channels), f32),
            dma((2, count)),
            dma((2, count)),
            pltpu.VMEM((taps, share, channels), f32),
            pltpu.VMEM((taps, share, channels), low),
            pltpu.VMEM((high - 1, taps // high, share, channels), low),
            dma,
            dma((high - 1,)),
            dma((high,)),
            dma,
            dma((2 * reduce_sends(sizes) + spread_sends(sizes) + outer_sends(sizes),)),
        ],
        compiler_params=pltpu.CompilerParams(
            collective_id=1, has_side_effects=True, vmem_limit_bytes=63 * 2**20
        ),
    )(
        frames_long, ids, grad_quant, picks, digits, left, right, gathered,
        partial.reshape((deep, wide) + reduce_shape),
    )
    decoded = decoded[None]
    grad = grad[None]
    side_shares = (
        share_encoder.reshape(grad_blocks, share, hidden),
        share_decoder.reshape(grad_blocks, share, hidden),
        strided_sums,
    )
    order = [i for side in sides for i in side]
    moments = [olds[i].reshape((-1,) + olds[i].shape[-2:]) for i in order]
    views = new_velocities(side_shares, moments)
    velocities = [None] * 8
    for i, view in zip(order, views):
        velocities[i] = view.reshape(olds[i].shape)
    flat = [masters[i].reshape((-1,) + masters[i].shape[-2:]) for i in (0, 2, 6, 5)]
    marks = jnp.concatenate(
        [code_slots.reshape(entries, -1).T, dead_codes.reshape(entries, -1).T], axis=1
    )
    small, *moved, new_codebooks = solve_all(
        views, flat, (all_rows, codebooks, buffered, marks), sizes, 2
    )
    nexts = [None] * 8
    for i, value in zip((0, 2, 6, 5), moved):
        nexts[i] = value.reshape(masters[i].shape)
    for at, side in enumerate(sides):
        _, point, group, _ = side
        nexts[point] = masters[point] - update_rate * small[at, :3]
        nexts[group] = masters[group] - update_rate * small[at, 3].reshape(masters[group].shape)
    return (
        decoded,
        grad,
        new_codebooks,
        velocities[0],
        velocities[1],
        velocities[2],
        velocities[3],
        velocities[4],
        velocities[5],
        velocities[6],
        velocities[7],
        nexts[0],
        nexts[1],
        nexts[2],
        nexts[3],
        nexts[4],
        nexts[5],
        nexts[6],
        nexts[7],
    )


def solution(mesh):
    in_specs = (
        P("dp", "seq", None),
        P("dp", "seq", None),
        P("dp", "seq"),
        P("dp", "seq", None, None),
        P(),
        P(None, None, "seq"),
        P(None, None, "seq"),
        P(),
        P(None, None, "seq", None),
        P(None, "seq", None),
        P(None, "seq", None),
        P(None, "seq", None),
        P(None, "seq", None),
        P(None, "seq", None),
        P(None, None, "seq", None),
        P(None, "seq", None),
        P(None, None, "seq", None),
        P(None, "seq", None),
        P(None, "seq", None),
        P(None, "seq", None),
        P(None, "seq", None),
        P(None, "seq", None),
        P(None, None, "seq", None),
        P(None, "seq", None),
    )
    out_specs = (
        P("dp", "seq", None),
        P("dp", "seq", None),
        P(None, None, "seq", None),
        P(None, None, "seq", None),
        P(None, "seq", None),
        P(None, "seq", None),
        P(None, "seq", None),
        P(None, "seq", None),
        P(None, "seq", None),
        P(None, None, "seq", None),
        P(None, "seq", None),
        P(None, None, "seq", None),
        P(None, "seq", None),
        P(None, "seq", None),
        P(None, "seq", None),
        P(None, "seq", None),
        P(None, "seq", None),
        P(None, None, "seq", None),
        P(None, "seq", None),
    )
    return jax.shard_map(
        per_device, mesh=mesh, in_specs=in_specs, out_specs=out_specs, check_vma=False
    )
```

```python
import functools

import jax
import jax.numpy as jnp
from jax import lax
from jax.experimental import pallas as pl
from jax.experimental.pallas import tpu as pltpu
from jax.sharding import PartitionSpec as P

GROUPS = 2
LEVELS = 2
KERNEL = 7
STRIDE = 8
NS_STEPS = 5


highest = lax.Precision.HIGHEST
dilation_list = (1, 3, 9)
coef_first = 3.4445
coef_second = -4.775
coef_third = 2.0315
commit_weight = 0.25
moment_decay = 0.5
update_rate = 0.5
code_rate = 0.5
norm_floor = 1e-07


def whole_rows(masters, high):
    dilated, pointwise, strided, group = masters[:4]
    share, width = dilated.shape[2:]
    rows = (dilated.size + pointwise.size + strided.size + group.size) // width
    return whole_units(rows, 64 * high, share)


def whole_units(rows, unit, share):
    step = unit
    while unit % share:
        unit += step
    return -(-rows // unit) * unit


def reduce_rows(masters, high):
    dilated, pointwise, _, group = masters[:4]
    share, width = dilated.shape[2:]
    rows = (dilated.size + pointwise.size + group.size) // width
    for split in ((2, 1), (1, 1)):
        whole = whole_units(rows, 32 * sum(split) * high, share)
        if 8 * (whole - rows) <= rows:
            break
    return whole, split


MESH = pl.DeviceIdType.MESH


def line_sizes(seq, dp):
    across = 1
    while (2 * across) * (2 * across) <= seq:
        across *= 2
    return across, dp // 2, seq // across


def place(sizes):
    wide, high, _ = sizes
    row = lax.axis_index("dp")
    part = lax.axis_index("seq")
    return part % wide, row // 2, part // wide, row % 2


def greet(sizes, row=False):
    wide, high, deep = sizes
    x, y, z, c = place(sizes)
    me, count = z * wide + x, deep * wide
    others = [(y * 2 + 1 - c, me)]
    others += [((y + k) % high * 2 + c, me) for k in range(1, high)]
    if row:
        others += [(y * 2 + c, (me + k) % count) for k in range(1, count)]
    else:
        others += [(y * 2 + c, z * wide + (x + k) % wide) for k in range(1, wide)]
        others += [(y * 2 + c, (z + k) % deep * wide + x) for k in range(1, deep)]
        others += [(y * 2 + c, (me + k) % count) for k in (1, count - 1)]
    barrier = pltpu.get_barrier_semaphore()
    for other in others:
        pl.semaphore_signal(barrier, inc=1, device_id=other, device_id_type=MESH)
    pl.semaphore_wait(barrier, len(others))


class Sender:
    def __init__(self, send_sem, partner):
        self.send_sem = send_sem
        self.partner = partner
        self.sent = []

    def send(self, src, dst, recv, to):
        copy = pltpu.make_async_remote_copy(
            src_ref=src,
            dst_ref=dst,
            send_sem=self.send_sem.at[len(self.sent)],
            recv_sem=recv,
            device_id=to,
            device_id_type=MESH,
        )
        copy.start()
        self.sent.append(copy)

    def arrive(self, dst, recv):
        pltpu.make_async_remote_copy(
            src_ref=dst,
            dst_ref=dst,
            send_sem=self.send_sem.at[0],
            recv_sem=recv,
            device_id=self.partner,
            device_id_type=MESH,
        ).wait_recv()

    def finish(self):
        for copy in self.sent:
            copy.wait_send()


class Gather:
    def __init__(self, sizes, sender, in_ref, out_ref, recv_sem):
        self.sizes = sizes
        self.place = place(sizes)
        self.sender = sender
        self.in_ref, self.out_ref, self.recv_sem = in_ref, out_ref, recv_sem

    def send(self, zs, xs, ys, h, to, source=None):
        c = self.place[3]
        spot = self.out_ref.at[zs, xs, c, ys, h]
        src = spot if source is None else source
        self.sender.send(src, spot, self.recv_sem.at[zs, xs, c, ys, h], to)

    def arrive(self, zs, xs, cs, ys, h):
        self.sender.arrive(self.out_ref.at[zs, xs, cs, ys, h], self.recv_sem.at[zs, xs, cs, ys, h])

    def to_x(self, zs, xs, ys, h, source=None):
        wide, high, deep = self.sizes
        x, y, z, c = self.place
        for k in range(1, wide):
            self.send(zs, xs, ys, h, (y * 2 + c, z * wide + (x + k) % wide), source)

    def to_y(self, zs, xs, ys, h):
        wide, high, deep = self.sizes
        x, y, z, c = self.place
        for k in range(1, high):
            self.send(zs, xs, ys, h, ((y + k) % high * 2 + c, z * wide + x))

    def to_core(self, zs, xs, ys, h):
        wide, high, deep = self.sizes
        x, y, z, c = self.place
        self.send(zs, xs, ys, h, (y * 2 + 1 - c, z * wide + x))

    def own_z(self):
        wide, high, deep = self.sizes
        x, y, z, c = self.place
        for k in range(deep - 1, 0, -1):
            for h in range(2):
                to = (y * 2 + c, (z + k) % deep * wide + x)
                self.send(z, x, y, h, to, self.in_ref.at[c, y, h])

    def own_x(self):
        wide, high, deep = self.sizes
        x, y, z, c = self.place
        self.to_x(z, x, y, 0, self.in_ref.at[c, y, 0])
        for j in range(high):
            ys = (y + j) % high
            self.to_x(z, x, ys, 1, self.in_ref.at[c, ys, 1])

    def from_z(self, k):
        x, y, z, c = self.place
        zs = (z + k) % self.sizes[2]
        self.arrive(zs, x, c, y, 0)
        self.to_x(zs, x, y, 0)
        self.to_y(zs, x, y, 0)
        self.to_core(zs, x, y, 0)
        self.arrive(zs, x, c, y, 1)
        self.to_y(zs, x, y, 1)
        self.to_x(zs, x, y, 1)
        self.to_core(zs, x, y, 1)

    def second(self, k):
        wide, high, deep = self.sizes
        x, y, z, c = self.place
        zs = (z + k) % deep
        for i in range(1, wide):
            xs = (x + i) % wide
            self.arrive(zs, xs, c, y, 0)
            self.to_y(zs, xs, y, 0)
            self.to_core(zs, xs, y, 0)
        if k > 0:
            for j in range(1, high):
                ys = (y + j) % high
                self.arrive(zs, x, c, ys, 1)
                self.to_x(zs, x, ys, 1)
                self.to_core(zs, x, ys, 1)

    def third(self, k):
        wide, high, deep = self.sizes
        x, y, z, c = self.place
        zs = (z + k) % deep
        for i in range(wide):
            xs = (x + i) % wide
            if k == 0 and i == 0:
                continue
            for j in range(1, high):
                ys = (y + j) % high
                self.arrive(zs, xs, c, ys, 0)
                self.to_core(zs, xs, ys, 0)
            if i > 0:
                for j in range(high):
                    ys = (y + j) % high
                    self.arrive(zs, xs, c, ys, 1)
                    self.to_core(zs, xs, ys, 1)

    def last(self, ready=None):
        wide, high, deep = self.sizes
        x, y, z, c = self.place
        for k in range(deep):
            zs = (z + k) % deep
            for i in range(wide):
                xs = (x + i) % wide
                if k == 0 and i == 0:
                    continue
                for j in range(high):
                    for h in range(2):
                        self.arrive(zs, xs, 1 - c, (y + j) % high, h)
                if ready is not None:
                    ready(zs * wide + xs)


def gather_sends(sizes):
    wide, high, deep = sizes
    n = (deep - 1) * 2 + (wide - 1) * (1 + high)
    n += (deep - 1) * 2 * (wide - 1 + high - 1 + 1)
    n += deep * (wide - 1) * high + (deep - 1) * (high - 1) * wide
    n += (deep * wide - 1) * (high - 1) + deep * (wide - 1) * high
    return n


class Spread:
    def __init__(self, sizes, sender, row_ref, all_ref, row_sem, keep_sem):
        self.sizes = sizes
        self.place = place(sizes)
        self.sender = sender
        self.row_ref, self.all_ref, self.row_sem = row_ref, all_ref, row_sem
        x, y, z, c = self.place
        self.keep = pltpu.make_async_copy(row_ref, all_ref.at[z, x, y, c], keep_sem)

    def pass_on(self, zs, xs, ys, to, own):
        c = self.place[3]
        spot = self.all_ref.at[zs, xs, ys, c]
        self.sender.send(self.row_ref if own else spot, spot, self.row_sem.at[zs, xs, ys, c], to)

    def landed(self, zs, xs, ys, cs):
        self.sender.arrive(self.all_ref.at[zs, xs, ys, cs], self.row_sem.at[zs, xs, ys, cs])

    def stage(self, number):
        wide, high, deep = self.sizes
        x, y, z, c = self.place
        columns = [(z + k) % deep for k in range(deep)]
        lines = [(x + k) % wide for k in range(wide)]
        heights = [(y + k) % high for k in range(high)]
        if number == 0:
            self.keep.start()
            for zt in columns[1:]:
                self.pass_on(z, x, y, (y * 2 + c, zt * wide + x), True)
        if number == 1:
            for zs in columns[1:]:
                self.landed(zs, x, y, c)
            for zs in columns:
                for yt in heights[1:]:
                    self.pass_on(zs, x, y, (yt * 2 + c, z * wide + x), zs is columns[0])
        if number == 2:
            for zs in columns:
                for ys in heights[1:]:
                    self.landed(zs, x, ys, c)
            for zs in columns:
                for ys in heights:
                    own = zs is columns[0] and ys is heights[0]
                    for xt in lines[1:]:
                        self.pass_on(zs, x, ys, (y * 2 + c, z * wide + xt), own)
        if number == 3:
            for zs in columns:
                for xs in lines[1:]:
                    for ys in heights:
                        self.landed(zs, xs, ys, c)
            for zs in columns:
                for xs in lines:
                    for ys in heights:
                        own = zs is columns[0] and xs is lines[0] and ys is heights[0]
                        self.pass_on(zs, xs, ys, (y * 2 + 1 - c, z * wide + x), own)
        if number == 4:
            for zs in columns:
                for xs in lines:
                    for ys in heights:
                        self.landed(zs, xs, ys, 1 - c)
            self.keep.wait()


def spread_sends(sizes):
    wide, high, deep = sizes
    return deep - 1 + deep * (high - 1) + deep * high * (wide - 1) + deep * wide * high


class Reduce:
    def __init__(self, sizes, split, sender, in_ref, out_ref, scratch):
        self.sizes = sizes
        self.split = split
        self.place = place(sizes)
        self.sender = sender
        self.in_ref, self.out_ref = in_ref, out_ref
        (
            self.held,
            self.from_core,
            self.from_x_a,
            self.from_y_b,
            self.from_y_a,
            self.from_x_b,
            self.from_z,
            self.final,
            self.local_sem,
            self.core_sem,
            self.xa_sem,
            self.yb_sem,
            self.ya_sem,
            self.xb_sem,
            self.z_sem,
            self.done_sem,
        ) = scratch
        deep = sizes[2]
        z = self.place[2]
        far = list(range(deep // 2, deep)) + list(range(deep // 2 - 1, 0, -1))
        self.order = [(z + k) % deep for k in far] + [z]

    def local(self, step):
        c = self.place[3]
        source = self.in_ref.at[self.order[step], :, c]
        return pltpu.make_async_copy(source, self.held.at[step], self.local_sem.at[step])

    def start(self):
        wide, high, deep = self.sizes
        x, y, z, c = self.place
        x_first, y_first = self.split
        pieces = x_first + y_first
        for step in range(deep):
            self.local(step).start()
            self.sender.send(
                self.in_ref.at[self.order[step], :, 1 - c],
                self.from_core.at[step],
                self.core_sem.at[step],
                (y * 2 + 1 - c, z * wide + x),
            )

    def merge(self, target, extras):
        total = target[...].astype(jnp.float32)
        for extra in extras:
            total = total + extra[...].astype(jnp.float32)
        target[...] = total.astype(target.dtype)

    def first(self, step):
        wide, high, deep = self.sizes
        x, y, z, c = self.place
        x_first, y_first = self.split
        pieces = x_first + y_first
        self.local(step).wait()
        self.sender.arrive(self.from_core.at[step], self.core_sem.at[step])

        def body(i, carry):
            xi, yi, hi = i // (pieces * high), i // pieces % high, i % pieces
            self.merge(self.held.at[step, xi, yi, hi], [self.from_core.at[step, xi, yi, hi]])
            return carry

        lax.fori_loop(0, wide * high * pieces, body, 0)
        for k in range(1, wide):
            xt = (x + k) % wide
            self.sender.send(
                self.held.at[step, xt, :, :x_first],
                self.from_x_a.at[k - 1, step],
                self.xa_sem.at[k - 1, step],
                (y * 2 + c, z * wide + xt),
            )
        for k in range(1, high):
            yt = (y + k) % high
            self.sender.send(
                self.held.at[step, :, yt, x_first:],
                self.from_y_b.at[k - 1, step],
                self.yb_sem.at[k - 1, step],
                (yt * 2 + c, z * wide + x),
            )

    def second(self, step):
        wide, high, deep = self.sizes
        x, y, z, c = self.place
        x_first, y_first = self.split
        pieces = x_first + y_first
        for k in range(1, wide):
            self.sender.arrive(self.from_x_a.at[k - 1, step], self.xa_sem.at[k - 1, step])

        def body_a(i, carry):
            yt, h = (y + 1 + i // x_first) % high, i % x_first
            extras = [self.from_x_a.at[k, step, yt, h] for k in range(wide - 1)]
            self.merge(self.held.at[step, x, yt, h], extras)
            return carry

        lax.fori_loop(0, high * x_first, body_a, 0)
        for k in range(1, high):
            yt = (y + k) % high
            self.sender.send(
                self.held.at[step, x, yt, :x_first],
                self.from_y_a.at[k - 1, step],
                self.ya_sem.at[k - 1, step],
                (yt * 2 + c, z * wide + x),
            )
        for k in range(1, high):
            self.sender.arrive(self.from_y_b.at[k - 1, step], self.yb_sem.at[k - 1, step])

        def body_b(i, carry):
            xt, h = (x + 1 + i // y_first) % wide, i % y_first
            extras = [self.from_y_b.at[k, step, xt, h] for k in range(high - 1)]
            self.merge(self.held.at[step, xt, y, x_first + h], extras)
            return carry

        lax.fori_loop(0, wide * y_first, body_b, 0)
        for k in range(1, wide):
            xt = (x + k) % wide
            self.sender.send(
                self.held.at[step, xt, y, x_first:],
                self.from_x_b.at[k - 1, step],
                self.xb_sem.at[k - 1, step],
                (y * 2 + c, z * wide + xt),
            )

    def third(self, step):
        wide, high, deep = self.sizes
        x, y, z, c = self.place
        x_first, y_first = self.split
        pieces = x_first + y_first
        for k in range(1, high):
            self.sender.arrive(self.from_y_a.at[k - 1, step], self.ya_sem.at[k - 1, step])
        for h in range(x_first):
            extras = [self.from_y_a.at[k, step, h] for k in range(high - 1)]
            self.merge(self.held.at[step, x, y, h], extras)
        for k in range(1, wide):
            self.sender.arrive(self.from_x_b.at[k - 1, step], self.xb_sem.at[k - 1, step])
        for h in range(y_first):
            extras = [self.from_x_b.at[k, step, h] for k in range(wide - 1)]
            self.merge(self.held.at[step, x, y, x_first + h], extras)
        if step < deep - 1:
            self.sender.send(
                self.held.at[step, x, y],
                self.from_z.at[step],
                self.z_sem.at[step],
                (y * 2 + c, self.order[step] * wide + x),
            )

    def turn(self, number):
        deep = self.sizes[2]
        if number < deep:
            self.first(number)
        if 0 <= number - 1 < deep:
            self.second(number - 1)
        if 0 <= number - 2 < deep:
            self.third(number - 2)

    def total(self):
        wide, high, deep = self.sizes
        x, y, z, c = self.place
        x_first, y_first = self.split
        pieces = x_first + y_first
        for step in range(deep - 1):
            self.sender.arrive(self.from_z.at[step], self.z_sem.at[step])
        for h in range(pieces):
            total = self.held[deep - 1, x, y, h].astype(jnp.float32)
            for step in range(deep - 1):
                total = total + self.from_z[step, h].astype(jnp.float32)
            self.final[h] = total.astype(self.final.dtype)
        spot, recv = self.out_ref.at[c, y], self.done_sem.at[c, y]
        pltpu.make_async_copy(self.final, spot, self.local_sem.at[deep]).start()
        for k in range(1, high):
            to = ((y + k) % high * 2 + c, z * wide + x)
            self.sender.send(self.final, spot, recv, to)
        self.sender.send(self.final, spot, recv, (y * 2 + 1 - c, z * wide + x))

    def last(self):
        wide, high, deep = self.sizes
        x, y, z, c = self.place
        x_first, y_first = self.split
        pieces = x_first + y_first
        for k in range(1, high):
            yt = (y + k) % high
            spot, recv = self.out_ref.at[c, yt], self.done_sem.at[c, yt]
            self.sender.arrive(spot, recv)
            self.sender.send(spot, spot, recv, (y * 2 + 1 - c, z * wide + x))
        for k in range(high):
            yt = (y + k) % high
            self.sender.arrive(self.out_ref.at[1 - c, yt], self.done_sem.at[1 - c, yt])
        own = self.out_ref.at[c, y]
        pltpu.make_async_copy(self.final, own, self.local_sem.at[deep]).wait()


def reduce_sends(sizes):
    wide, high, deep = sizes
    return deep + deep * 2 * (wide - 1 + high - 1) + deep - 1 + 2 * (high - 1) + 1


def reduce_scratch(sizes, split, rows, width, kind):
    wide, high, deep = sizes
    x_first, y_first = split
    pieces = x_first + y_first
    tail = (rows, width)
    dma = pltpu.SemaphoreType.DMA
    return [
        pltpu.VMEM((deep, wide, high, pieces) + tail, kind),
        pltpu.VMEM((deep, wide, high, pieces) + tail, kind),
        pltpu.VMEM((wide - 1, deep, high, x_first) + tail, kind),
        pltpu.VMEM((high - 1, deep, wide, y_first) + tail, kind),
        pltpu.VMEM((high - 1, deep, x_first) + tail, kind),
        pltpu.VMEM((wide - 1, deep, y_first) + tail, kind),
        pltpu.VMEM((deep - 1, pieces) + tail, kind),
        pltpu.VMEM((pieces,) + tail, kind),
        dma((deep + 1,)),
        dma((deep,)),
        dma((wide - 1, deep)),
        dma((high - 1, deep)),
        dma((high - 1, deep)),
        dma((wide - 1, deep)),
        dma((deep - 1,)),
        dma((2, high)),
    ]


reduce_parts = 16


class Outer:
    def __init__(self, sizes, sender, left, right, lefts, rights, left_sem, right_sem):
        self.sizes = sizes
        self.place = place(sizes)
        self.sender = sender
        self.left, self.right = left, right
        self.lefts, self.rights = lefts, rights
        self.left_sem, self.right_sem = left_sem, right_sem
        x, y, z, c = self.place
        self.count = sizes[0] * sizes[2]
        self.me = z * sizes[0] + x

    def own(self, part):
        share = self.lefts.shape[2]
        return self.left.at[:, pl.ds(pl.multiple_of(part * share, 16), share)]

    def start(self):
        x, y, z, c = self.place
        me = self.me
        for k in range(1, self.count):
            to = (me + k) % self.count
            self.sender.send(self.own(to), self.lefts.at[me], self.left_sem.at[me], (y * 2 + c, to))
            self.sender.send(self.right, self.rights.at[me], self.right_sem.at[me], (y * 2 + c, to))
        self.lefts[me] = self.own(me)[...]
        self.rights[me] = self.right[...]

    def multiply(self, target):
        for k in range(1, self.count):
            source = (self.me + k) % self.count
            self.sender.arrive(self.lefts.at[source], self.left_sem.at[source])
            self.sender.arrive(self.rights.at[source], self.right_sem.at[source])
        share = self.lefts.shape[2]
        latents = self.right.shape[0]
        taps = lanes // latents
        lane = lax.broadcasted_iota(jnp.int32, (share, lanes), 1) // latents
        rights = jnp.concatenate(
            [self.rights[source] for source in range(self.count) for _ in range(taps)], axis=0
        )
        for group in range(self.left.shape[0]):
            pieces = []
            for source in range(self.count):
                block = self.lefts[source, group].astype(jnp.float32)
                pieces.append(
                    jnp.concatenate(
                        [jnp.where(lane == tap, block, 0.0) for tap in range(taps)], axis=0
                    ).astype(jnp.bfloat16)
                )
            value = dot(jnp.concatenate(pieces, axis=1), rights)
            target[group * taps : (group + 1) * taps] = value.reshape(taps, share, -1)


class OuterSum:
    def __init__(self, sizes, sender, partials, out_ref, scratch):
        self.sizes = sizes
        self.place = place(sizes)
        self.sender = sender
        self.partials, self.out_ref = partials, out_ref
        self.peer, self.low, self.peers, self.core_sem, self.y_sem, self.out_sem, self.last_sem = scratch
        self.taps = partials.shape[1] // sizes[1]

    def to_core(self):
        wide, high, deep = self.sizes
        x, y, z, c = self.place
        to = (y * 2 + 1 - c, z * wide + x)
        self.sender.send(self.partials.at[1 - c], self.peer, self.core_sem, to)

    def to_y(self):
        wide, high, deep = self.sizes
        x, y, z, c = self.place
        self.sender.arrive(self.peer, self.core_sem)
        total = self.partials[c] + self.peer[...]
        self.partials[c] = total
        self.low[...] = total.astype(self.low.dtype)
        for k in range(1, high):
            yt = (y + k) % high
            self.sender.send(
                self.low.at[pl.ds(yt * self.taps, self.taps)],
                self.peers.at[k - 1],
                self.y_sem.at[k - 1],
                (yt * 2 + c, z * wide + x),
            )

    def back_y(self):
        wide, high, deep = self.sizes
        x, y, z, c = self.place
        mine = pl.ds(y * self.taps, self.taps)
        total = self.partials[c, mine]
        for k in range(1, high):
            self.sender.arrive(self.peers.at[k - 1], self.y_sem.at[k - 1])
            total = total + self.peers[k - 1].astype(jnp.float32)
        spot = self.out_ref.at[c, mine]
        spot[...] = total
        for k in range(1, high):
            to = ((y + k) % high * 2 + c, z * wide + x)
            self.sender.send(spot, spot, self.out_sem.at[y], to)

    def back_core(self):
        wide, high, deep = self.sizes
        x, y, z, c = self.place
        for k in range(1, high):
            yt = (y + k) % high
            spot = self.out_ref.at[c, pl.ds(yt * self.taps, self.taps)]
            self.sender.arrive(spot, self.out_sem.at[yt])
        to = (y * 2 + 1 - c, z * wide + x)
        self.sender.send(self.out_ref.at[c], self.out_ref.at[c], self.last_sem, to)

    def last(self):
        c = self.place[3]
        self.sender.arrive(self.out_ref.at[1 - c], self.last_sem)


def outer_sends(sizes):
    wide, high, deep = sizes
    return 4 * (wide * deep - 1) + 2 * high


def outer_left(taps):
    per = lanes // taps[0].shape[0]
    turned = [tap.T for tap in taps]
    return [
        jnp.concatenate(turned[start : start + per], axis=1).astype(jnp.bfloat16)
        for start in range(0, len(taps), per)
    ]


margin = 32
lanes = 128


def elu_slope(values):
    return jnp.where(values > 0, 1.0, jnp.exp(jnp.minimum(values, 0.0)))


def elu(values):
    return jnp.where(values > 0, values, jnp.exp(jnp.minimum(values, 0.0)) - 1.0)


def dot(left, right):
    return jnp.dot(left, right, preferred_element_type=jnp.float32)


def dot_last(left, right):
    return lax.dot_general(
        left, right, (((1,), (1,)), ((), ())), preferred_element_type=jnp.float32
    )


def dot_rows(left, right):
    return lax.dot_general(
        left, right, (((0,), (0,)), ((), ())), preferred_element_type=jnp.float32
    )


def spread_taps(target, source, ids, width, sign, dilation, length):
    block = 64

    def body(step, carry):
        base = pl.multiple_of(step * block, block)
        window = ids[pl.ds(base, block + 2 * margin), :]
        own = window[margin : margin + block]
        for tap in range(KERNEL):
            start = margin + sign * (tap - KERNEL // 2) * dilation
            match = window[start : start + block] == own
            for piece in range(width // lanes):
                columns = slice(piece * lanes, (piece + 1) * lanes)
                values = source[pl.ds(base, block + 2 * margin), columns][start : start + block]
                spot = tap * width + piece * lanes
                target[pl.ds(base, block), spot : spot + lanes] = jnp.where(
                    match, values, 0.0
                ).astype(jnp.bfloat16)
        return carry

    lax.fori_loop(0, length // block, body, 0)


def forward_unit(unit, stream, follow, ids, weights, scratch, length, own):
    dilated, pointwise = weights
    padded, columns, hidden, excited, active = scratch
    channels = stream.shape[1]
    values = elu(stream[...])
    padded[margin : margin + length, :] = values
    active[unit] = values[own].astype(jnp.bfloat16)
    spread_taps(columns, padded, ids, channels, 1, dilation_list[unit], length)
    kernel = dilated[unit * KERNEL : (unit + 1) * KERNEL].reshape(KERNEL * channels, -1)
    value = dot(columns[...], kernel)
    hidden[unit] = value
    lifted = elu(value).astype(jnp.bfloat16)
    excited[unit] = lifted
    follow[...] = stream[...] + dot_last(lifted, pointwise[unit])


def backward_unit(unit, grad, stream, ids, weights, scratch, length, own):
    dilated, pointwise = weights
    padded, columns, hidden, excited, active = scratch
    width = hidden.shape[2]
    low = grad[...].astype(jnp.bfloat16)
    grad_hidden = dot(low, pointwise[unit]) * elu_slope(hidden[unit])
    pointwise[unit] = dot(
        grad[own, :].T.astype(jnp.bfloat16), excited[unit, own, :]
    ).astype(jnp.bfloat16)
    padded[margin : margin + length, :width] = grad_hidden.astype(jnp.bfloat16).astype(jnp.float32)
    spread_taps(columns, padded, ids, width, -1, dilation_list[unit], length)
    turned = active[unit].astype(jnp.float32).T.astype(jnp.bfloat16)
    total = None
    for tap in range(KERNEL):
        piece = slice(tap * width, (tap + 1) * width)
        part = dot_last(columns[:, piece], dilated[unit * KERNEL + tap])
        total = part if total is None else total + part
        dilated[unit * KERNEL + tap] = dot(turned, columns[own, piece]).astype(jnp.bfloat16)
    grad[...] = grad[...] + total * elu_slope(stream[...])


class Mover:
    def __init__(self, side, geometry, gathered, packed, weights, sems):
        self.seq, self.share, self.blocks = geometry
        self.base = side * self.blocks
        width = gathered.shape[-1]
        self.gathered = gathered.reshape(self.seq, -1, self.share, width)
        self.packed = packed
        self.weights = weights
        self.sems = sems

    def block_start(self, kind):
        return (0, 3 * KERNEL, 3 * KERNEL + 3, 3 * KERNEL + 4)[kind]

    def load(self, kind, owner):
        rows = self.weights[kind]
        start = self.base + self.block_start(kind)
        source = self.gathered.at[owner, pl.ds(start, rows.shape[0])]
        target = rows.at[:, pl.ds(pl.multiple_of(owner * self.share, 16), self.share)]
        return pltpu.make_async_copy(source, target, self.sems.at[kind, owner])

    def start_loads(self, kind):
        for owner in range(self.seq):
            self.load(kind, owner).start()

    def load_owner(self, owner):
        for kind in (2, 3, 0, 1):
            self.load(kind, owner).start()

    def wait_loads(self, kind):
        for owner in range(self.seq):
            self.load(kind, owner).wait()

    def store(self, kind, owner, first, size):
        rows = self.weights[kind]
        start = self.block_start(kind) + first
        source = rows.at[first : first + size, pl.ds(owner * self.share, self.share)]
        target = self.packed.at[owner, pl.ds(start, size)]
        return pltpu.make_async_copy(source, target, self.sems.at[4 + kind, owner])


def load_group(rows, seq, share):
    width = rows.shape[-1]
    part = width // seq
    value = rows.astype(jnp.float32).reshape(seq, GROUPS, part, width)
    return [value[:, g].reshape(width, width).astype(jnp.bfloat16) for g in range(GROUPS)]


def store_group(grads, seq, share):
    width = grads[0].shape[-1]
    part = width // seq
    value = jnp.stack([grad.reshape(seq, part, width) for grad in grads], axis=1)
    return value.reshape(seq, GROUPS * part, width).astype(jnp.bfloat16)


def put_tap(tiles, tap, value):
    latents = value.shape[0]
    for piece in range(tiles.shape[0]):
        tiles[piece, pl.ds(tap, latents, stride=STRIDE), :] = value[
            :, piece * lanes : (piece + 1) * lanes
        ]


def take_tap(tiles, tap, latents):
    return jnp.concatenate(
        [tiles[piece, pl.ds(tap, latents, stride=STRIDE), :] for piece in range(tiles.shape[0])],
        axis=1,
    )


def to_tiles(tiles, value):
    for piece in range(tiles.shape[0]):
        tiles[piece] = value[:, piece * lanes : (piece + 1) * lanes]


def from_tiles(tiles):
    return jnp.concatenate([tiles[piece] for piece in range(tiles.shape[0])], axis=1)


def set_edges(padded, length):
    zero = jnp.zeros((margin, padded.shape[1]), jnp.float32)
    padded[:margin, :] = zero
    padded[margin + length :, :] = zero


def front_kernel(
    sizes,
    geometry,
    length,
    enc_dilated,
    enc_point,
    enc_group,
    enc_strided,
    dec_dilated,
    dec_point,
    dec_group,
    dec_strided,
    code_own,
    ids_own,
    frames_own,
    cot_own,
    books_ref,
    gathered,
    frames_long,
    ids_ref,
    decoded_ref,
    grad_quant_ref,
    picks_ref,
    packed,
    left_ref,
    right_ref,
    shard_ref,
    wide_dilated,
    wide_point,
    wide_group,
    wide_strided,
    code_ref,
    cot_ref,
    dilated,
    pointwise,
    group,
    strided,
    streams,
    padded,
    columns,
    hidden,
    excited,
    active,
    tiles,
    sems,
    edge_sem,
    keep_sem,
    recv_sem,
    send_sem,
):
    seq, share, blocks = geometry
    wide, high, deep = sizes
    x, y, z, c = place(sizes)
    me = z * wide + x
    masters = ((enc_dilated, enc_point, enc_group, enc_strided),) + (
        (dec_dilated, dec_point, dec_group, dec_strided),
    )
    wides = (wide_dilated, wide_point, wide_group, wide_strided)
    reads = [
        [
            pltpu.make_async_copy(source, target.at[side], keep_sem.at[5 + 4 * side + number])
            for number, (source, target) in enumerate(zip(masters[side], wides))
        ]
        for side in range(2)
    ]
    for side in (1, 0):
        for copy in reads[side]:
            copy.start()
    greet(sizes)
    sender = Sender(send_sem, (y * 2 + 1 - c, me))
    gathers = [
        Gather(
            sizes,
            sender,
            shard_ref.at[side].reshape(2, high, 2, -1, shard_ref.shape[-1]),
            gathered.at[:, :, side],
            recv_sem.at[side],
        )
        for side in range(2)
    ]
    encoder, decoder = gathers

    def pack(side):
        dil, point, both = wide_dilated[side], wide_point[side], wide_group[side]
        width = shard_ref.shape[-1]
        low = jnp.bfloat16
        at = 0
        for value in (dil, point, both.reshape(1, share, width)):
            shard_ref[side, at : at + value.shape[0]] = value.astype(low)
            at += value.shape[0]
        for part in range(2):
            value = wide_strided[side, :, :, part * width : (part + 1) * width]
            shard_ref[side, at : at + value.shape[0]] = value.astype(low)
            at += value.shape[0]
        if at < blocks:
            shard_ref[side, at:] = jnp.zeros((blocks - at, share, width), low)

    for copy in reads[1]:
        copy.wait()
    pack(1)
    decoder.own_z()
    decoder.own_x()
    keeps = [
        pltpu.make_async_copy(
            gathers[side].in_ref, gathered.at[z, x, side], keep_sem.at[13 + side]
        )
        for side in range(2)
    ]
    keeps[1].start()
    for copy in reads[0]:
        copy.wait()
    pack(0)
    keeps[0].start()
    own = length // 2
    half = length // 4
    reach = half // STRIDE
    near = 80
    set_edges(padded, length)
    blank = jnp.zeros((half - near, cot_ref.shape[1]), jnp.float32)
    cot_ref[: half - near, :] = blank
    cot_ref[length - (half - near) :, :] = blank
    outside = jnp.full((margin, lanes), -1, jnp.int32)
    ids_ref[:margin, :] = outside
    ids_ref[margin + length :, :] = outside
    own_copies = [
        pltpu.make_async_copy(frames_own, frames_long.at[half : half + own], keep_sem.at[1]),
        pltpu.make_async_copy(cot_own, cot_ref.at[half : half + own], keep_sem.at[2]),
        pltpu.make_async_copy(
            ids_own, ids_ref.at[margin + half : margin + half + own], keep_sem.at[3]
        ),
        pltpu.make_async_copy(code_own, code_ref.at[:, reach : reach + own // STRIDE], keep_sem.at[4]),
    ]
    for copy in own_copies:
        copy.start()
    edges = [
        (frames_own.at[own - half :], frames_long.at[:half]),
        (cot_own.at[own - near :], cot_ref.at[half - near : half]),
        (ids_own.at[own - half :], ids_ref.at[margin : margin + half]),
        (code_own.at[:, own // STRIDE - reach :], code_ref.at[:, :reach]),
        (frames_own.at[:half], frames_long.at[half + own :]),
        (cot_own.at[:near], cot_ref.at[half + own : half + own + near]),
        (ids_own.at[:half], ids_ref.at[margin + half + own : margin + length]),
        (code_own.at[:, :reach], code_ref.at[:, reach + own // STRIDE :]),
    ]
    edge_copies = []
    for number, (src, dst) in enumerate(edges):
        other = (me + (1 if number < len(edges) // 2 else seq - 1)) % seq
        copy = pltpu.make_async_remote_copy(
            src_ref=src,
            dst_ref=dst,
            send_sem=edge_sem.at[0, number],
            recv_sem=edge_sem.at[1, number],
            device_id=(y * 2 + c, other),
            device_id_type=MESH,
        )
        copy.start()
        edge_copies.append(copy)
    for number in (3, 7):
        edge_copies[number].wait()
    own_copies[3].wait()
    latents = length // STRIDE
    codes = books_ref.shape[2]
    width = books_ref.shape[3]
    tile_range = lax.broadcasted_iota(jnp.int32, (latents, lanes), 1)
    quantized = []
    for g in range(GROUPS):
        picked = []
        for level in range(LEVELS):
            entry = g * LEVELS + level
            chosen = code_ref[entry]
            hot = jnp.concatenate(
                [
                    (chosen == tile_range + tile * lanes).astype(jnp.float32)
                    for tile in range(codes // lanes)
                ],
                axis=1,
            )
            pick = jnp.dot(hot, books_ref[g, level], precision=lax.Precision.HIGHEST)
            picks_ref[entry] = pick
            picked.append(pick)
        quantized.append((picked[0] + picked[1]).astype(jnp.bfloat16))
    for k in range(1, deep):
        decoder.from_z(k)
    encoder.own_z()
    for k in range(deep):
        decoder.second(k)
    encoder.own_x()
    for k in range(deep):
        decoder.third(k)
        if k > 0:
            encoder.from_z(k)
    for number, copy in enumerate(edge_copies):
        if number not in (3, 7):
            copy.wait()
    for copy in own_copies[:3]:
        copy.wait()

    @pl.when(me == 0)
    def _():
        ids_ref[margin : margin + half, :] = jnp.full((half, lanes), -1, jnp.int32)

    @pl.when(me == seq - 1)
    def _():
        ids_ref[margin + half + own : margin + length, :] = jnp.full((half, lanes), -1, jnp.int32)

    weights = (dilated, pointwise, group, strided)
    mover = Mover(1, geometry, gathered, packed, weights, sems)
    for copy in keeps:
        copy.wait()
    mover.load_owner(me)
    decoder.last(mover.load_owner)
    pump = [functools.partial(encoder.second, k) for k in range(deep)]
    pump += [functools.partial(encoder.third, k) for k in range(deep)]
    first, last = length // 4, 3 * length // 4
    mover.wait_loads(2)
    out_weights = load_group(group[0], seq, share)
    mixed = [dot(quantized[g], out_weights[g]) for g in range(GROUPS)]
    lifted = [elu(value).astype(jnp.bfloat16) for value in mixed]
    mover.wait_loads(3)
    for tap in range(STRIDE):
        value = dot_last(lifted[0], strided[tap]) + dot_last(lifted[1], strided[STRIDE + tap])
        put_tap(tiles, tap, value)
    streams[0] = from_tiles(tiles)
    mover.wait_loads(0)
    mover.wait_loads(1)
    scratch = (padded, columns, hidden, excited, active)
    pump.pop(0)()
    for unit in range(3):
        forward_unit(
            unit, streams.at[unit], streams.at[unit + 1], ids_ref, (dilated, pointwise), scratch,
            length, slice(first, last),
        )
        pump.pop(0)()
    decoded_ref[...] = streams[3, first:last, :].astype(jnp.bfloat16)
    grad = streams.at[3]
    grad[...] = cot_ref[...]

    for unit in (2, 1, 0):
        backward_unit(
            unit, grad, streams.at[unit], ids_ref, (dilated, pointwise), scratch, length,
            slice(first, last),
        )
        for owner in range(seq):
            mover.store(0, owner, unit * KERNEL, KERNEL).start()
        if pump:
            pump.pop(0)()
    for owner in range(seq):
        mover.store(1, owner, 0, 3).start()
    own = slice(first // STRIDE, last // STRIDE)
    grad_lifted = [None, None]
    own_taps = []
    to_tiles(tiles, grad[...])
    for tap in range(STRIDE):
        part = take_tap(tiles, tap, latents)
        low = part.astype(jnp.bfloat16)
        own_taps.append(part[own])
        for half in range(2):
            value = dot(low, strided[half * STRIDE + tap])
            grad_lifted[half] = value if tap == 0 else grad_lifted[half] + value
    for number, value in enumerate(outer_left(own_taps)):
        left_ref[number] = value
    right_ref[...] = jnp.concatenate([lifted[0][own], lifted[1][own]], axis=1)
    group_grads = []
    for g in range(GROUPS):
        low = (grad_lifted[g] * elu_slope(mixed[g])).astype(jnp.bfloat16)
        group_grads.append(dot_rows(quantized[g][own], low[own]))
        grad_quant_ref[g] = dot_last(low, out_weights[g])
    group[0] = store_group(group_grads, seq, share).reshape(group.shape[1:])
    for owner in range(seq):
        mover.store(2, owner, 0, 1).start()
    while pump:
        pump.pop(0)()
    finish_stores(mover, seq)
    encoder.last()
    sender.finish()


def finish_stores(mover, seq):
    for owner in range(seq):
        for unit in range(3):
            mover.store(0, owner, unit * KERNEL, KERNEL).wait()
        mover.store(1, owner, 0, 3).wait()
        mover.store(2, owner, 0, 1).wait()


def back_kernel(
    sizes,
    split,
    geometry,
    length,
    frames_ref,
    ids_ref,
    grad_quant_ref,
    picks_ref,
    digits_ref,
    left_ref,
    right_ref,
    gathered,
    partial_ref,
    frames_grad_ref,
    packed,
    share_decoder,
    share_encoder,
    all_ref,
    strided_out,
    dilated,
    pointwise,
    group,
    strided,
    streams,
    padded,
    columns,
    hidden,
    excited,
    active,
    tiles,
    sems,
    *refs,
):
    seq, share, blocks = geometry
    x, y, z, c = place(sizes)
    me = z * sizes[0] + x
    weights = (dilated, pointwise, group, strided)
    mover = Mover(0, geometry, gathered, packed, weights, sems)
    for kind in (0, 1, 3, 2):
        mover.start_loads(kind)
    greet(sizes, row=True)
    sender = Sender(refs[-1], (y * 2 + 1 - c, me))
    packed_view = packed.reshape(partial_ref.shape)
    other = Reduce(sizes, split, sender, partial_ref, share_decoder, refs[:reduce_parts])
    side = Reduce(sizes, split, sender, packed_view, share_encoder, refs[reduce_parts : 2 * reduce_parts])
    rows_ref, keep_sem, row_sem = refs[2 * reduce_parts : 2 * reduce_parts + 3]
    spread = Spread(sizes, sender, rows_ref, all_ref, row_sem, keep_sem)
    extra = refs[2 * reduce_parts + 3 : -1]
    left_own, right_own, lefts, rights, partials = extra[:5]
    left_sem, right_sem = extra[5:7]
    down, up = [
        Outer(
            sizes, sender, left, right, lefts.at[side], rights.at[side], left_sem.at[side],
            right_sem.at[side],
        )
        for side, (left, right) in enumerate(((left_own, right_own), (left_ref, right_ref)))
    ]
    both = OuterSum(sizes, sender, partials, strided_out, extra[7:])
    other.start()
    up.start()
    turns = sizes[2] + 2
    pump = [functools.partial(other.turn, number) for number in range(turns)]
    pump += [other.total, other.last]
    for spot in (1, 3, 5, 6):
        pump.insert(spot, lambda: None)
    set_edges(padded, length)
    own_frames = frames_grad_ref.shape[0]
    first = (length - own_frames) // 2
    last = first + own_frames
    skip = (frames_ref.shape[0] - length) // 2
    ids_ref = ids_ref.at[skip : skip + length + 2 * margin]
    latents = length // STRIDE
    own = slice(first // STRIDE, last // STRIDE)
    width = picks_ref.shape[2]
    streams[0] = frames_ref[skip : skip + length, :].astype(jnp.float32)
    mover.wait_loads(0)
    mover.wait_loads(1)
    scratch = (padded, columns, hidden, excited, active)
    for unit in range(3):
        forward_unit(
            unit, streams.at[unit], streams.at[unit + 1], ids_ref, (dilated, pointwise), scratch,
            length, slice(first, last),
        )
        pump.pop(0)()
    to_tiles(tiles, elu(streams[3]))
    mover.wait_loads(3)
    mover.wait_loads(2)
    in_weights = load_group(group[0], seq, share)
    latent = [None, None]
    for tap in range(STRIDE):
        low = take_tap(tiles, tap, latents).astype(jnp.bfloat16)
        for half in range(2):
            value = dot(low, strided[half * STRIDE + tap])
            latent[half] = value if tap == 0 else latent[half] + value
    group_grads = []
    grad_latent = []
    for g in range(GROUPS):
        low = latent[g].astype(jnp.bfloat16)
        first_part = dot(low, in_weights[g])
        wanted = slice(skip // STRIDE, skip // STRIDE + latents)
        pick = [picks_ref[g * LEVELS + level, wanted, :] for level in range(LEVELS)]
        second_part = first_part - pick[0]
        rows_ref[:, g * width : (g + 1) * width] = first_part[own].astype(jnp.bfloat16)
        grad_first = grad_quant_ref[g, wanted, :] + 2.0 * commit_weight * (
            second_part + (second_part - pick[1])
        )
        low_first = grad_first.astype(jnp.bfloat16)
        group_grads.append(dot_rows(low[own], low_first[own]))
        grad_latent.append(dot_last(low_first, in_weights[g]).astype(jnp.bfloat16))
    group[0] = store_group(group_grads, seq, share).reshape(group.shape[1:])
    rows_ref[:, GROUPS * width :] = digits_ref[...]
    spread.stage(0)
    for owner in range(seq):
        mover.store(2, owner, 0, 1).start()
    own_taps = []
    for tap in range(STRIDE):
        own_taps.append(take_tap(tiles, tap, latents)[own])
        value = dot_last(grad_latent[0], strided[tap]) + dot_last(
            grad_latent[1], strided[STRIDE + tap]
        )
        put_tap(tiles, tap, value)
    for number, value in enumerate(outer_left(own_taps)):
        left_own[number] = value
    right_own[...] = jnp.concatenate([grad_latent[0][own], grad_latent[1][own]], axis=1)
    down.start()
    grad = streams.at[3]
    grad[...] = from_tiles(tiles) * elu_slope(grad[...])
    pump.pop(0)()

    for unit in (2, 1, 0):
        backward_unit(
            unit, grad, streams.at[unit], ids_ref, (dilated, pointwise), scratch, length,
            slice(first, last),
        )
        for owner in range(seq):
            mover.store(0, owner, unit * KERNEL, KERNEL).start()
        if pump:
            pump.pop(0)()
    for owner in range(seq):
        mover.store(1, owner, 0, 3).start()
    frames_grad_ref[...] = grad[first:last, :]
    finish_stores(mover, seq)
    side.start()
    outer = [both.to_core, both.to_y, both.back_y, both.back_core, both.last]
    up.multiply(partials.at[1])
    for number in range(turns):
        if pump:
            pump.pop(0)()
        side.turn(number)
        if number == 0:
            down.multiply(partials.at[0])
        outer.pop(0)() if outer else None
        if number >= turns - 2:
            spread.stage(number - turns + 3)
    side.total()
    spread.stage(3)
    side.last()
    spread.stage(4)
    sender.finish()


def side_scratch(seq, share, length, own, channels, hidden):
    bf, f32 = jnp.bfloat16, jnp.float32
    group_rows = GROUPS * hidden // seq
    mats = [
        pltpu.VMEM((3 * KERNEL, channels, hidden), bf),
        pltpu.VMEM((3, channels, hidden), bf),
        pltpu.VMEM((1, seq * group_rows, hidden), bf),
        pltpu.VMEM((2 * STRIDE, channels, hidden), bf),
    ]
    return mats + [
        pltpu.VMEM((4, length, channels), f32),
        pltpu.VMEM((length + 2 * margin, channels), f32),
        pltpu.VMEM((length, KERNEL * channels), bf),
        pltpu.VMEM((3, length, hidden), f32),
        pltpu.VMEM((3, length, hidden), bf),
        pltpu.VMEM((3, own, channels), bf),
        pltpu.VMEM((channels // lanes, length, lanes), f32),
        pltpu.SemaphoreType.DMA((8, seq)),
    ]


def split_terms(value, count):
    terms = []
    for number in range(count):
        term = value.astype(jnp.bfloat16)
        terms.append(term)
        if number < count - 1:
            value = value - term.astype(jnp.float32)
    return terms


def product(left, right):
    def pair(i, j):
        return jnp.dot(left[i], right[j], preferred_element_type=jnp.float32)

    low = pair(0, 1) + pair(1, 0)
    if len(left) > 2:
        low = low + (pair(1, 1) + pair(0, 2) + pair(2, 0))
    return pair(0, 0) + low


def gram_of(left, right):
    return product(split_terms(left.T, 3), split_terms(right, 3))


def solve_mixing(gram):
    size = gram.shape[0]
    eye = (
        lax.broadcasted_iota(jnp.int32, (size, size), 0)
        == lax.broadcasted_iota(jnp.int32, (size, size), 1)
    ).astype(jnp.float32)
    scale = 1.0 / (jnp.sqrt(jnp.sum(gram * eye)) + norm_floor)
    current = gram * (scale * scale)
    total = None
    for repeat in range(NS_STEPS):
        terms = 3 if repeat < 2 else 2
        parts = split_terms(current, terms)
        factor = coef_first * eye + coef_second * current + coef_third * product(parts, parts)
        factors = split_terms(factor, terms)
        if total is None:
            total = factor
        else:
            total = product(split_terms(total, 2), factors[:2])
        if repeat < NS_STEPS - 1:
            half = split_terms(product(parts, factors), terms)
            current = product(half, factors)
    return total * scale


def solve_pair(corner, side, other):
    size = corner.shape[0]
    eye = (
        lax.broadcasted_iota(jnp.int32, (size, size), 0)
        == lax.broadcasted_iota(jnp.int32, (size, size), 1)
    ).astype(jnp.float32)
    scale = 1.0 / (jnp.sqrt(jnp.sum((corner + other) * eye)) + norm_floor)
    current = [value * (scale * scale) for value in (corner, side, other)]

    def whole(blocks, terms):
        parts = [split_terms(value, terms) for value in blocks]
        turned = split_terms(blocks[1].T, terms)
        top = [jnp.concatenate([p, q], axis=1) for p, q in zip(parts[0], parts[1])]
        low = [jnp.concatenate([p, q], axis=1) for p, q in zip(turned, parts[2])]
        return top, low

    def times(left, right):
        rows = [jnp.concatenate([p, q], axis=0) for p, q in zip(*right)]
        top = product(left[0], rows)
        low = product(left[1], [value[:, size:] for value in rows])
        return [top[:, :size], top[:, size:], low]

    total = None
    for repeat in range(NS_STEPS):
        terms = 3 if repeat < 2 else 2
        parts = whole(current, terms)
        square = times(parts, parts)
        factor = [
            coef_second * value + coef_third * double for value, double in zip(current, square)
        ]
        factor = [factor[0] + coef_first * eye, factor[1], factor[2] + coef_first * eye]
        factors = whole(factor, terms)
        if total is None:
            total = factor
        else:
            total = times(whole(total, 2), [values[:2] for values in factors])
        if repeat < NS_STEPS - 1:
            half = whole(times(parts, factors), terms)
            current = times(half, factors)
    return [value * scale for value in total]


def mixing_kernel(
    sizes,
    share,
    enc_dilated,
    enc_point,
    enc_group,
    enc_strided,
    dec_dilated,
    dec_point,
    dec_group,
    dec_strided,
    enc_dilated_w,
    enc_strided_w,
    dec_dilated_w,
    dec_strided_w,
    row_ref,
    books_ref,
    buffered_ref,
    marks_ref,
    small_ref,
    enc_dilated_next,
    enc_strided_next,
    dec_dilated_next,
    dec_strided_next,
    books_next,
    mix_ref,
    dilated,
    point,
    group,
    strided,
    dilated_w,
    strided_w,
    blocks,
    corner,
    slots,
    point_all,
    group_all,
    work,
    point_done,
    group_done,
    load_sem,
    send_sem,
    slot_sem,
    rows_sem,
    mix_sem,
    core_sem,
    small_sem,
    corner_sem,
    all_ref,
    books,
    first_books,
    buffered,
    code_sem,
):
    wide, high, deep = sizes
    x, y, z, c = place(sizes)
    count = wide * deep
    me = z * wide + x
    row = y * 2 + c
    middle = count // 2
    partner = (y * 2 + 1 - c, me)
    others = [(row, (me + k) % count) for k in range(1, count)]
    others += [
        ((y + j) % high * 2 + c, z * wide + (x + i) % wide)
        for i in range(wide)
        for j in range(1, high)
    ] + [partner]
    pending = []

    def remote(src, dst, number, recv, to):
        return pltpu.make_async_remote_copy(
            src_ref=src,
            dst_ref=dst,
            send_sem=send_sem.at[number],
            recv_sem=recv,
            device_id=to,
            device_id_type=MESH,
        )

    def send(when, src, dst, recv, to):
        number = len(pending)
        pending.append((when, src, dst, recv, to))

        @pl.when(when)
        def _():
            remote(src, dst, number, recv, to).start()

    def arrive(dst, recv):
        remote(dst, dst, 0, recv, partner).wait_recv()

    first_set = y == 0
    second_set = y == 1

    def load(number, source, target):
        return pltpu.make_async_copy(source, target, load_sem.at[number])

    own_loads = [
        (enc_dilated, dilated.at[0]),
        (dec_dilated, dilated.at[1]),
        (enc_strided, strided.at[0]),
        (dec_strided, strided.at[1]),
        (enc_point, point.at[0]),
        (dec_point, point.at[1]),
        (enc_group, group.at[0]),
        (dec_group, group.at[1]),
        (enc_dilated_w, dilated_w.at[0]),
        (dec_dilated_w, dilated_w.at[1]),
        (enc_strided_w, strided_w.at[0]),
        (dec_strided_w, strided_w.at[1]),
    ]
    for number, (source, target) in enumerate(own_loads):
        load(number, source, target).start()
    code_share = books.shape[2]
    own_books = books_ref.at[:, :, pl.ds(pl.multiple_of(me * code_share, 8), code_share)]
    code_loads = [
        pltpu.make_async_copy(row_ref, all_ref, code_sem.at[0]),
        pltpu.make_async_copy(own_books, books, code_sem.at[1]),
        pltpu.make_async_copy(buffered_ref, buffered, code_sem.at[2]),
        pltpu.make_async_copy(books_ref.at[:, 0], first_books, code_sem.at[3]),
    ]
    for copy in code_loads:
        copy.start()
    barrier = pltpu.get_barrier_semaphore()
    for other in others:
        pl.semaphore_signal(barrier, inc=1, device_id=other, device_id_type=MESH)
    pl.semaphore_wait(barrier, len(others))

    for number in (4, 5, 6, 7, 2, 3, 0, 1):
        load(number, *own_loads[number]).wait()

    block_at = [middle - 2 + number + c for number in range(3)]
    strided_at = block_at[1]
    small_at = [(middle + c + offset + count) % count for offset in (1, 2, 3, -3, -4)]
    point_at, group_at = small_at[:3], small_at[3:]
    part = share // GROUPS
    piece = blocks.shape[1] // (wide * high)

    for unit in range(3):
        at = point_at[unit]
        rows = pl.ds(pl.multiple_of(me * share, 8), share)
        send(
            second_set & (me != at),
            point.at[c, unit],
            point_all.at[rows],
            rows_sem.at[me],
            (row, at),
        )

        @pl.when(second_set & (me == at))
        def _():
            point_all[rows, :] = point[c, unit]

    for g in range(GROUPS):
        at = group_at[g]
        rows = pl.ds(pl.multiple_of(me * part, 8), part)
        send(
            second_set & (me != at),
            group.at[c, g],
            group_all.at[rows],
            rows_sem.at[me],
            (row, at),
        )

        @pl.when(second_set & (me == at))
        def _():
            group_all[rows, :] = group[c, g]

    block = blocks.shape[1]

    @pl.when(first_set)
    def _():
        for unit in range(3):
            value = dilated[c, unit * KERNEL : (unit + 1) * KERNEL].reshape(KERNEL * share, block)
            blocks[unit] = gram_of(value, value)

    @pl.when(second_set)
    def _():
        value = strided[c].reshape(-1, 2 * block)
        left, right = value[:, :block], value[:, block:]
        blocks[0] = gram_of(left, left)
        blocks[1] = gram_of(left, right)
        blocks[2] = gram_of(right, right)

    for number in range(3):
        at = block_at[number]
        send(
            (first_set | second_set) & (me != at),
            blocks.at[number],
            slots.at[number, me],
            slot_sem.at[number, me],
            (row, at),
        )

    for copy in code_loads:
        copy.wait()
    renew_codes(me, all_ref, books, first_books, buffered, marks_ref, books_next)

    def summed(number):
        total = blocks[number]
        for k in range(1, count):
            source = (me + k) % count
            arrive(slots.at[number, source], slot_sem.at[number, source])
            total = total + slots[number, source]
        return total

    for number in range(3):

        @pl.when((first_set | second_set) & (me == block_at[number]))
        def _():
            work[...] = summed(number)

    for number in (0, 2):
        send(
            second_set & (me == block_at[number]),
            work,
            corner.at[number // 2],
            corner_sem.at[number // 2],
            (row, strided_at),
        )

    @pl.when(second_set & (me == strided_at))
    def _():
        for number in range(2):
            arrive(corner.at[number], corner_sem.at[number])
        solved = solve_pair(corner[0], work[...], corner[1])
        for number in range(3):
            mix_ref[1, c, number] = solved[number]

    def piece_of(which, number, xs, ys):
        rows = pl.ds(pl.multiple_of((xs * high + ys) * piece, 8), piece)
        return (
            mix_ref.at[which, c, number, rows],
            mix_sem.at[which, c, number, xs * high + ys],
        )

    def hand_first(which, number, at):
        owner = (y == which) & (me == at)
        for i in range(wide):
            for j in range(high):
                if i == 0 and j == 0:
                    continue
                xt, yt = (x + i) % wide, (y + j) % high
                spot, recv = piece_of(which, number, xt, yt)
                send(owner, spot, spot, recv, (yt * 2 + c, z * wide + xt))

    for number in range(3):
        hand_first(1, number, strided_at)

    is_point = second_set & (
        (me == point_at[0]) | (me == point_at[1]) | (me == point_at[2])
    )
    is_group = second_set & ((me == group_at[0]) | (me == group_at[1]))
    is_dilated = first_set & (
        (me == block_at[0]) | (me == block_at[1]) | (me == block_at[2])
    )

    @pl.when(is_point)
    def _():
        for k in range(1, count):
            source = (me + k) % count
            rows = pl.ds(pl.multiple_of(source * share, 8), share)
            arrive(point_all.at[rows], rows_sem.at[source])
        work[...] = gram_of(point_all[...], point_all[...])

    @pl.when(is_group)
    def _():
        for k in range(1, count):
            source = (me + k) % count
            rows = pl.ds(pl.multiple_of(source * part, 8), part)
            arrive(group_all.at[rows], rows_sem.at[source])
        work[...] = gram_of(group_all[...], group_all[...])

    @pl.when(is_dilated | is_point | is_group)
    def _():
        work[...] = solve_mixing(work[...])

    for unit in range(3):

        @pl.when(first_set & (me == block_at[unit]))
        def _():
            mix_ref[0, c, unit] = work[...]

        hand_first(0, unit, block_at[unit])

    @pl.when(is_point)
    def _():
        point_done[...] = product(split_terms(point_all[...], 3), split_terms(work[...], 3))

    @pl.when(is_group)
    def _():
        group_done[...] = product(split_terms(group_all[...], 3), split_terms(work[...], 3))

    for unit in range(3):
        at = point_at[unit]
        for k in range(1, count):
            target = (me + k) % count
            rows = pl.ds(pl.multiple_of(target * share, 8), share)
            send(
                second_set & (me == at),
                point_done.at[rows],
                small_ref.at[c, unit],
                small_sem.at[unit],
                (row, target),
            )

        @pl.when(second_set & (me == at))
        def _():
            small_ref[c, unit] = point_done[pl.ds(pl.multiple_of(me * share, 8), share), :]

    for g in range(GROUPS):
        at = group_at[g]
        spot = small_ref.at[c, 3, g * part : (g + 1) * part]
        for k in range(1, count):
            target = (me + k) % count
            rows = pl.ds(pl.multiple_of(target * part, 8), part)
            send(
                second_set & (me == at),
                group_done.at[rows],
                spot,
                small_sem.at[3 + g],
                (row, target),
            )

        @pl.when(second_set & (me == at))
        def _():
            spot[...] = group_done[pl.ds(pl.multiple_of(me * part, 8), part), :]

    always = y >= 0

    def hand_down(which, number, at):
        owner = (y == which) & (me == at)
        in_plane = z == at // wide
        spot, recv = piece_of(which, number, x, y)

        @pl.when(jnp.logical_not(owner))
        def _():
            arrive(spot, recv)

        for k in range(1, deep):
            send(in_plane, spot, spot, recv, (row, (z + k) % deep * wide + x))

    def hand_across(which, number, at):
        spot, recv = piece_of(which, number, x, y)
        for i in range(wide):
            for j in range(high):
                if i == 0 and j == 0:
                    continue
                xt, yt = (x + i) % wide, (y + j) % high
                target = z * wide + xt
                wants = jnp.logical_not((yt == which) & (target == at))
                send(wants, spot, spot, recv, (yt * 2 + c, target))

    def hand_over(which, number, at):
        owner = (y == which) & (me == at)

        @pl.when(jnp.logical_not(owner))
        def _():
            for i in range(wide):
                for j in range(high):
                    if i == 0 and j == 0:
                        continue
                    arrive(*piece_of(which, number, (x + i) % wide, (y + j) % high))

        spot = mix_ref.at[which, c, number]
        send(always, spot, spot, core_sem.at[which, c, number], partner)

    strided_ats = [strided_at] * 3
    for which, ats in ((0, block_at), (1, strided_ats)):
        for step in (hand_down, hand_across):
            for number in range(3):
                step(which, number, ats[number])
    for unit in range(3):

        @pl.when(second_set & (me != point_at[unit]))
        def _():
            arrive(small_ref.at[c, unit], small_sem.at[unit])

    for g in range(GROUPS):

        @pl.when(second_set & (me != group_at[g]))
        def _():
            arrive(small_ref.at[c, 3, g * part : (g + 1) * part], small_sem.at[3 + g])

    for k in range(1, high):
        send(
            second_set,
            small_ref.at[c],
            small_ref.at[c],
            small_sem.at[5],
            ((y + k) % high * 2 + c, me),
        )

    @pl.when(jnp.logical_not(second_set))
    def _():
        arrive(small_ref.at[c], small_sem.at[5])

    send(always, small_ref.at[c], small_ref.at[c], small_sem.at[6], partner)
    for which, ats in ((0, block_at), (1, strided_ats)):
        for number in range(3):
            hand_over(which, number, ats[number])
    for unit in range(3):
        arrive(mix_ref.at[0, 1 - c, unit], core_sem.at[0, 1 - c, unit])
    for number in range(8, 12):
        load(number, *own_loads[number]).wait()
    for side, target in enumerate((enc_dilated_next, dec_dilated_next)):
        for unit in range(3):
            taps = slice(unit * KERNEL, (unit + 1) * KERNEL)
            rows = dilated[side, taps].reshape(KERNEL * share, block)
            moved = product(split_terms(rows, 2), split_terms(mix_ref[0, side, unit], 2))
            target[taps] = dilated_w[side, taps] - update_rate * moved.reshape(
                KERNEL, share, block
            )
    arrive(small_ref.at[1 - c], small_sem.at[6])
    for number in range(3):
        arrive(mix_ref.at[1, 1 - c, number], core_sem.at[1, 1 - c, number])
    for side, target in enumerate((enc_strided_next, dec_strided_next)):
        corners = [split_terms(mix_ref[1, side, number], 2) for number in range(3)]
        turned = split_terms(mix_ref[1, side, 1].T, 2)
        rows = strided[side].reshape(-1, 2 * block)
        left, right = split_terms(rows[:, :block], 2), split_terms(rows[:, block:], 2)
        low = product(left, corners[0]) + product(right, turned)
        top = product(left, corners[1]) + product(right, corners[2])
        shape = (strided.shape[1], share, block)
        target[:, :, :block] = strided_w[side, :, :, :block] - update_rate * low.reshape(shape)
        target[:, :, block:] = strided_w[side, :, :, block:] - update_rate * top.reshape(shape)

    for number, (when, src, dst, recv, to) in enumerate(pending):

        @pl.when(when)
        def _():
            remote(src, dst, number, recv, to).wait_send()


def renew_codes(me, all_ref, books, first_books, buffered, marks_ref, books_next):
    groups, levels, share, width = books.shape
    entries = groups * levels
    codes = first_books.shape[1]
    slot_range = lax.broadcasted_iota(jnp.int32, (share, buffered.shape[1]), 1)
    deep, wide, high, _, length, _ = all_ref.shape
    size = wide * high * 2 * length
    every = lax.broadcasted_iota(jnp.int32, (codes, size), 0).astype(jnp.float32)
    own_range = lax.broadcasted_iota(jnp.int32, (share, size), 0) + me * share
    own_range = own_range.astype(jnp.float32)
    ones = jnp.ones((size, lanes), jnp.bfloat16)
    sums = [None] * entries
    counts = [None] * entries
    pairs = [None] * groups

    def add(target, number, value):
        target[number] = value if target[number] is None else target[number] + value

    def chosen(digits, entry, choices):
        code = digits[entry : entry + 1] * 32.0 + digits[entries + entry : entries + entry + 1]
        return (code == choices).astype(jnp.float32).astype(jnp.bfloat16)

    for zs in range(deep):
        rows = all_ref[zs].reshape(size, -1)
        digits = rows[:, groups * width :].astype(jnp.float32).T
        for g in range(groups):
            values = rows[:, g * width : (g + 1) * width]
            for level in range(levels):
                entry = g * levels + level
                hot = chosen(digits, entry, own_range)
                add(sums, entry, dot(hot, values))
                add(counts, entry, dot(hot, ones))
            add(pairs, g, dot_last(hot, chosen(digits, g * levels, every)))
    for entry in range(entries):
        g, level = entry // levels, entry % levels
        if level == 1:
            both = split_terms(pairs[g], 2)
            taken = product(both, split_terms(first_books[g], 2))
            sums[entry] = sums[entry] - taken
        count = jnp.concatenate([counts[entry]] * (width // lanes), axis=1)
        own = books[g, level]
        mean = sums[entry] / jnp.maximum(count, 1.0)
        updated = own + code_rate * jnp.minimum(count, 1.0) * (mean - own)
        hot = (marks_ref[:, entry : entry + 1] == slot_range).astype(jnp.bfloat16)
        replaced = None
        for term in split_terms(buffered[g], 3):
            part = dot(hot, term)
            replaced = part if replaced is None else replaced + part
        dead = marks_ref[:, entries + entry : entries + entry + 1] == 1
        books_next[g, level] = jnp.where(dead, replaced, updated)


def solve_all(views, weights, codes, sizes, collective_id):
    wide, high, deep = sizes
    count = wide * deep
    share, block = views[0].shape[1:]
    part = share // GROUPS
    f32 = jnp.float32
    dma = pltpu.SemaphoreType.DMA
    sends = 5 + 3 + 2 + 5 * (count - 1) + (high - 1) + 1 + 6 * (deep + 2 * (wide * high - 1))
    all_rows, books, buffered, marks = codes
    own_books = books.shape[:2] + (books.shape[2] // count,) + books.shape[3:]
    vmem = pl.BlockSpec(memory_space=pltpu.VMEM)
    return pl.pallas_call(
        functools.partial(mixing_kernel, sizes, share),
        out_shape=(jax.ShapeDtypeStruct((2, 4, share, block), f32),)
        + tuple(jax.ShapeDtypeStruct(weight.shape, f32) for weight in weights)
        + (jax.ShapeDtypeStruct(own_books, f32),),
        in_specs=[pl.BlockSpec(memory_space=pl.ANY)] * 15 + [vmem],
        out_specs=(vmem,) * 6,
        scratch_shapes=[
            pltpu.VMEM((2, 2, 3, block, block), f32),
            pltpu.VMEM((2,) + views[0].shape, f32),
            pltpu.VMEM((2,) + views[1].shape, f32),
            pltpu.VMEM((2,) + views[2].shape, f32),
            pltpu.VMEM((2,) + views[3].shape, f32),
            pltpu.VMEM((2,) + views[0].shape, f32),
            pltpu.VMEM((2,) + views[3].shape, f32),
            pltpu.VMEM((3, block, block), f32),
            pltpu.VMEM((2, block, block), f32),
            pltpu.VMEM((3, count, block, block), f32),
            pltpu.VMEM((count * share, block), f32),
            pltpu.VMEM((count * part, block), f32),
            pltpu.VMEM((block, block), f32),
            pltpu.VMEM((count * share, block), f32),
            pltpu.VMEM((count * part, block), f32),
            dma((12,)),
            dma((sends,)),
            dma((3, count)),
            dma((count,)),
            dma((2, 2, 3, wide * high)),
            dma((2, 2, 3)),
            dma((7,)),
            dma((2,)),
            pltpu.VMEM(all_rows.shape, all_rows.dtype),
            pltpu.VMEM(own_books, f32),
            pltpu.VMEM(books.shape[:1] + books.shape[2:], f32),
            pltpu.VMEM(buffered.shape, f32),
            dma((4,)),
        ],
        compiler_params=pltpu.CompilerParams(
            collective_id=collective_id, has_side_effects=True, vmem_limit_bytes=60 * 2**20
        ),
    )(*views, *weights, *codes)


def velocity_kernel(share_encoder, share_decoder, strided_sums, *refs):
    moments, outs = refs[:8], refs[8:]
    for side, rows in enumerate((share_encoder, share_decoder)):
        dilated, point, group, strided = range(4 * side, 4 * side + 4)
        at = 0
        for number in (dilated, point):
            size = moments[number].shape[0]
            step = rows[at : at + size].astype(jnp.float32)
            outs[number][...] = moment_decay * moments[number][...] + step
            at += size
        step = rows[at].astype(jnp.float32).reshape(moments[group].shape)
        outs[group][...] = moment_decay * moments[group][...] + step
        outs[strided][...] = moment_decay * moments[strided][...] + strided_sums[side]


def new_velocities(side_shares, moments):
    vmem = pl.BlockSpec(memory_space=pltpu.VMEM)
    return pl.pallas_call(
        velocity_kernel,
        out_shape=tuple(jax.ShapeDtypeStruct(moment.shape, jnp.float32) for moment in moments),
        in_specs=[vmem] * (len(side_shares) + len(moments)),
        out_specs=(vmem,) * len(moments),
        compiler_params=pltpu.CompilerParams(vmem_limit_bytes=60 * 2**20),
    )(*side_shares, *moments)


def per_device(
    frames,
    cotangent,
    segment_ids,
    code_index,
    codebooks,
    dead_codes,
    code_slots,
    buffered,
    encoder_dilated,
    encoder_pointwise,
    down_weight,
    group_in,
    group_out,
    up_weight,
    decoder_dilated,
    decoder_pointwise,
    encoder_dilated_moment,
    encoder_pointwise_moment,
    down_moment,
    group_in_moment,
    group_out_moment,
    up_moment,
    decoder_dilated_moment,
    decoder_pointwise_moment,
):
    masters = (
        encoder_dilated,
        encoder_pointwise,
        down_weight,
        group_in,
        group_out,
        up_weight,
        decoder_dilated,
        decoder_pointwise,
    )
    olds = (
        encoder_dilated_moment,
        encoder_pointwise_moment,
        down_moment,
        group_in_moment,
        group_out_moment,
        up_moment,
        decoder_dilated_moment,
        decoder_pointwise_moment,
    )
    count = lax.axis_size("seq")
    sizes = line_sizes(count, lax.axis_size("dp"))
    sides = ((0, 1, 3, 2), (6, 7, 4, 5))
    side_rows = whole_rows(masters, sizes[1])
    wide, high, deep = sizes
    _, length, channels = frames.shape
    long = 2 * length
    latent_len = long // STRIDE
    place_seq = lax.axis_index("seq")
    hidden = encoder_dilated.shape[-1]
    share = masters[0].shape[2]
    blocks = side_rows // share
    geometry = (count, share, blocks)
    rows = side_rows // (4 * high)
    low, f32 = jnp.bfloat16, jnp.float32
    dma = pltpu.SemaphoreType.DMA
    ids_own = jnp.broadcast_to(segment_ids[0][:, None], (length, lanes))
    entries = GROUPS * LEVELS
    code_own = code_index[0].reshape(-1, entries).T
    code_own = jnp.broadcast_to(code_own[:, :, None], code_own.shape + (lanes,))
    vmem = pl.BlockSpec(memory_space=pltpu.VMEM)
    anywhere = pl.BlockSpec(memory_space=pl.ANY)
    grad_rows, split = reduce_rows(masters, high)
    pieces = sum(split)
    grad_blocks = grad_rows // share
    partial_type = jax.ShapeDtypeStruct((count, grad_blocks, share, hidden), low)
    latents = length // STRIDE
    taps = masters[2].shape[0]
    left_type = jax.ShapeDtypeStruct((taps * latents // lanes, channels, lanes), low)
    right_type = jax.ShapeDtypeStruct((latents, channels), low)
    scratch = side_scratch(count, share, long, length, channels, hidden)
    inner = length + 2 * 96
    inner_scratch = side_scratch(count, share, inner, length, channels, hidden)
    flat = [masters[i].reshape((-1,) + masters[i].shape[-2:]) for side in sides for i in side]
    packed_shape = (2, high, 2, rows, hidden)
    piece_rows = grad_rows // (2 * high * pieces)
    reduce_shape = (2, high, pieces, piece_rows, hidden)
    both = [pltpu.VMEM((2,) + array.shape, f32) for array in flat[:4]]
    gathered, frames_long, ids, decoded, grad_quant, picks, partial, left, right = pl.pallas_call(
        functools.partial(front_kernel, sizes, geometry, long),
        out_shape=(
            jax.ShapeDtypeStruct((deep, wide, 2) + packed_shape, low),
            jax.ShapeDtypeStruct((long, channels), frames.dtype),
            jax.ShapeDtypeStruct((long + 2 * margin, lanes), jnp.int32),
            jax.ShapeDtypeStruct((length, channels), low),
            jax.ShapeDtypeStruct((GROUPS, latent_len, hidden), f32),
            jax.ShapeDtypeStruct((entries, latent_len, hidden), f32),
            partial_type,
            left_type,
            right_type,
        ),
        in_specs=[anywhere] * 12 + [vmem],
        out_specs=(anywhere, vmem, vmem, vmem, vmem, vmem, anywhere, vmem, vmem),
        scratch_shapes=[pltpu.VMEM((2, blocks, share, hidden), low)]
        + both
        + [
            pltpu.VMEM((entries, latent_len, lanes), jnp.int32),
            pltpu.VMEM((long, channels), f32),
        ]
        + scratch
        + [
            dma((2, 8)),
            dma((15,)),
            dma((2, deep, wide, 2, high, 2)),
            dma((2 * gather_sends(sizes),)),
        ],
        compiler_params=pltpu.CompilerParams(
            collective_id=0, has_side_effects=True, vmem_limit_bytes=60 * 2**20
        ),
    )(*flat, code_own, ids_own, frames[0], cotangent[0], codebooks)
    own_codes_low = code_index[0].reshape(-1, entries)
    digits = jnp.concatenate([own_codes_low // 32, own_codes_low % 32], axis=1)
    digits = jnp.pad(digits, ((0, 0), (0, lanes - digits.shape[1]))).astype(low)
    rows_own = (length // STRIDE, GROUPS * hidden + lanes)
    grad, _, share_decoder, share_encoder, all_rows, strided_sums = pl.pallas_call(
        functools.partial(back_kernel, sizes, split, geometry, inner),
        out_shape=(
            jax.ShapeDtypeStruct((length, channels), f32),
            partial_type,
            jax.ShapeDtypeStruct(reduce_shape, low),
            jax.ShapeDtypeStruct(reduce_shape, low),
            jax.ShapeDtypeStruct((deep, wide, high, 2) + rows_own, low),
            jax.ShapeDtypeStruct((2, taps, share, channels), f32),
        ),
        in_specs=[vmem] * 7 + [anywhere, anywhere],
        out_specs=(vmem, anywhere, anywhere, anywhere, anywhere, vmem),
        scratch_shapes=inner_scratch
        + reduce_scratch(sizes, split, piece_rows, hidden, low)
        + reduce_scratch(sizes, split, piece_rows, hidden, low)
        + [
            pltpu.VMEM(rows_own, low),
            dma,
            dma((deep, wide, high, 2)),
            pltpu.VMEM(left_type.shape, low),
            pltpu.VMEM(right_type.shape, low),
            pltpu.VMEM((2, count, left_type.shape[0], share, lanes), low),
            pltpu.VMEM((2, count) + right_type.shape, low),
            pltpu.VMEM((2, taps, share, channels), f32),
            dma((2, count)),
            dma((2, count)),
            pltpu.VMEM((taps, share, channels), f32),
            pltpu.VMEM((taps, share, channels), low),
            pltpu.VMEM((high - 1, taps // high, share, channels), low),
            dma,
            dma((high - 1,)),
            dma((high,)),
            dma,
            dma((2 * reduce_sends(sizes) + spread_sends(sizes) + outer_sends(sizes),)),
        ],
        compiler_params=pltpu.CompilerParams(
            collective_id=1, has_side_effects=True, vmem_limit_bytes=63 * 2**20
        ),
    )(
        frames_long, ids, grad_quant, picks, digits, left, right, gathered,
        partial.reshape((deep, wide) + reduce_shape),
    )
    decoded = decoded[None]
    grad = grad[None]
    side_shares = (
        share_encoder.reshape(grad_blocks, share, hidden),
        share_decoder.reshape(grad_blocks, share, hidden),
        strided_sums,
    )
    order = [i for side in sides for i in side]
    moments = [olds[i].reshape((-1,) + olds[i].shape[-2:]) for i in order]
    views = new_velocities(side_shares, moments)
    velocities = [None] * 8
    for i, view in zip(order, views):
        velocities[i] = view.reshape(olds[i].shape)
    flat = [masters[i].reshape((-1,) + masters[i].shape[-2:]) for i in (0, 2, 6, 5)]
    marks = jnp.concatenate(
        [code_slots.reshape(entries, -1).T, dead_codes.reshape(entries, -1).T], axis=1
    )
    small, *moved, new_codebooks = solve_all(
        views, flat, (all_rows, codebooks, buffered, marks), sizes, 2
    )
    nexts = [None] * 8
    for i, value in zip((0, 2, 6, 5), moved):
        nexts[i] = value.reshape(masters[i].shape)
    for at, side in enumerate(sides):
        _, point, group, _ = side
        nexts[point] = masters[point] - update_rate * small[at, :3]
        nexts[group] = masters[group] - update_rate * small[at, 3].reshape(masters[group].shape)
    return (
        decoded,
        grad,
        new_codebooks,
        velocities[0],
        velocities[1],
        velocities[2],
        velocities[3],
        velocities[4],
        velocities[5],
        velocities[6],
        velocities[7],
        nexts[0],
        nexts[1],
        nexts[2],
        nexts[3],
        nexts[4],
        nexts[5],
        nexts[6],
        nexts[7],
    )


def solution(mesh):
    in_specs = (
        P("dp", "seq", None),
        P("dp", "seq", None),
        P("dp", "seq"),
        P("dp", "seq", None, None),
        P(),
        P(None, None, "seq"),
        P(None, None, "seq"),
        P(),
        P(None, None, "seq", None),
        P(None, "seq", None),
        P(None, "seq", None),
        P(None, "seq", None),
        P(None, "seq", None),
        P(None, "seq", None),
        P(None, None, "seq", None),
        P(None, "seq", None),
        P(None, None, "seq", None),
        P(None, "seq", None),
        P(None, "seq", None),
        P(None, "seq", None),
        P(None, "seq", None),
        P(None, "seq", None),
        P(None, None, "seq", None),
        P(None, "seq", None),
    )
    out_specs = (
        P("dp", "seq", None),
        P("dp", "seq", None),
        P(None, None, "seq", None),
        P(None, None, "seq", None),
        P(None, "seq", None),
        P(None, "seq", None),
        P(None, "seq", None),
        P(None, "seq", None),
        P(None, "seq", None),
        P(None, None, "seq", None),
        P(None, "seq", None),
        P(None, None, "seq", None),
        P(None, "seq", None),
        P(None, "seq", None),
        P(None, "seq", None),
        P(None, "seq", None),
        P(None, "seq", None),
        P(None, None, "seq", None),
        P(None, "seq", None),
    )
    return jax.shard_map(
        per_device, mesh=mesh, in_specs=in_specs, out_specs=out_specs, check_vma=False
    )
```

```python
import functools

import jax
import jax.numpy as jnp
from jax import lax
from jax.experimental import pallas as pl
from jax.experimental.pallas import tpu as pltpu
from jax.sharding import PartitionSpec as P

GROUPS = 2
LEVELS = 2
KERNEL = 7
STRIDE = 8
NS_STEPS = 5


highest = lax.Precision.HIGHEST
dilation_list = (1, 3, 9)
coef_first = 3.4445
coef_second = -4.775
coef_third = 2.0315
commit_weight = 0.25
moment_decay = 0.5
update_rate = 0.5
code_rate = 0.5
norm_floor = 1e-07


def whole_rows(masters, high):
    dilated, pointwise, strided, group = masters[:4]
    share, width = dilated.shape[2:]
    rows = (dilated.size + pointwise.size + strided.size + group.size) // width
    return whole_units(rows, 64 * high, share)


def whole_units(rows, unit, share):
    step = unit
    while unit % share:
        unit += step
    return -(-rows // unit) * unit


def reduce_rows(masters, high):
    dilated, pointwise, _, group = masters[:4]
    share, width = dilated.shape[2:]
    rows = (dilated.size + pointwise.size + group.size) // width
    for split in ((2, 1), (1, 1)):
        whole = whole_units(rows, 32 * sum(split) * high, share)
        if 8 * (whole - rows) <= rows:
            break
    return whole, split


MESH = pl.DeviceIdType.MESH


def line_sizes(seq, dp):
    across = 1
    while (2 * across) * (2 * across) <= seq:
        across *= 2
    return across, dp // 2, seq // across


def place(sizes):
    wide, high, _ = sizes
    row = lax.axis_index("dp")
    part = lax.axis_index("seq")
    return part % wide, row // 2, part // wide, row % 2


def greet(sizes, row=False):
    wide, high, deep = sizes
    x, y, z, c = place(sizes)
    me, count = z * wide + x, deep * wide
    others = [(y * 2 + 1 - c, me)]
    others += [((y + k) % high * 2 + c, me) for k in range(1, high)]
    if row:
        others += [(y * 2 + c, (me + k) % count) for k in range(1, count)]
    else:
        others += [(y * 2 + c, z * wide + (x + k) % wide) for k in range(1, wide)]
        others += [(y * 2 + c, (z + k) % deep * wide + x) for k in range(1, deep)]
        others += [(y * 2 + c, (me + k) % count) for k in (1, count - 1)]
    barrier = pltpu.get_barrier_semaphore()
    for other in others:
        pl.semaphore_signal(barrier, inc=1, device_id=other, device_id_type=MESH)
    pl.semaphore_wait(barrier, len(others))


class Sender:
    def __init__(self, send_sem, partner):
        self.send_sem = send_sem
        self.partner = partner
        self.sent = []

    def send(self, src, dst, recv, to):
        copy = pltpu.make_async_remote_copy(
            src_ref=src,
            dst_ref=dst,
            send_sem=self.send_sem.at[len(self.sent)],
            recv_sem=recv,
            device_id=to,
            device_id_type=MESH,
        )
        copy.start()
        self.sent.append(copy)

    def arrive(self, dst, recv):
        pltpu.make_async_remote_copy(
            src_ref=dst,
            dst_ref=dst,
            send_sem=self.send_sem.at[0],
            recv_sem=recv,
            device_id=self.partner,
            device_id_type=MESH,
        ).wait_recv()

    def finish(self):
        for copy in self.sent:
            copy.wait_send()


class Gather:
    def __init__(self, sizes, sender, in_ref, out_ref, recv_sem):
        self.sizes = sizes
        self.place = place(sizes)
        self.sender = sender
        self.in_ref, self.out_ref, self.recv_sem = in_ref, out_ref, recv_sem

    def send(self, zs, xs, ys, h, to, source=None):
        c = self.place[3]
        spot = self.out_ref.at[zs, xs, c, ys, h]
        src = spot if source is None else source
        self.sender.send(src, spot, self.recv_sem.at[zs, xs, c, ys, h], to)

    def arrive(self, zs, xs, cs, ys, h):
        self.sender.arrive(self.out_ref.at[zs, xs, cs, ys, h], self.recv_sem.at[zs, xs, cs, ys, h])

    def to_x(self, zs, xs, ys, h, source=None):
        wide, high, deep = self.sizes
        x, y, z, c = self.place
        for k in range(1, wide):
            self.send(zs, xs, ys, h, (y * 2 + c, z * wide + (x + k) % wide), source)

    def to_y(self, zs, xs, ys, h):
        wide, high, deep = self.sizes
        x, y, z, c = self.place
        for k in range(1, high):
            self.send(zs, xs, ys, h, ((y + k) % high * 2 + c, z * wide + x))

    def to_core(self, zs, xs, ys, h):
        wide, high, deep = self.sizes
        x, y, z, c = self.place
        self.send(zs, xs, ys, h, (y * 2 + 1 - c, z * wide + x))

    def own_z(self):
        wide, high, deep = self.sizes
        x, y, z, c = self.place
        for k in range(deep - 1, 0, -1):
            for h in range(2):
                to = (y * 2 + c, (z + k) % deep * wide + x)
                self.send(z, x, y, h, to, self.in_ref.at[c, y, h])

    def own_x(self):
        wide, high, deep = self.sizes
        x, y, z, c = self.place
        self.to_x(z, x, y, 0, self.in_ref.at[c, y, 0])
        for j in range(high):
            ys = (y + j) % high
            self.to_x(z, x, ys, 1, self.in_ref.at[c, ys, 1])

    def from_z(self, k):
        x, y, z, c = self.place
        zs = (z + k) % self.sizes[2]
        self.arrive(zs, x, c, y, 0)
        self.to_x(zs, x, y, 0)
        self.to_y(zs, x, y, 0)
        self.to_core(zs, x, y, 0)
        self.arrive(zs, x, c, y, 1)
        self.to_y(zs, x, y, 1)
        self.to_x(zs, x, y, 1)
        self.to_core(zs, x, y, 1)

    def second(self, k):
        wide, high, deep = self.sizes
        x, y, z, c = self.place
        zs = (z + k) % deep
        for i in range(1, wide):
            xs = (x + i) % wide
            self.arrive(zs, xs, c, y, 0)
            self.to_y(zs, xs, y, 0)
            self.to_core(zs, xs, y, 0)
        if k > 0:
            for j in range(1, high):
                ys = (y + j) % high
                self.arrive(zs, x, c, ys, 1)
                self.to_x(zs, x, ys, 1)
                self.to_core(zs, x, ys, 1)

    def third(self, k):
        wide, high, deep = self.sizes
        x, y, z, c = self.place
        zs = (z + k) % deep
        for i in range(wide):
            xs = (x + i) % wide
            if k == 0 and i == 0:
                continue
            for j in range(1, high):
                ys = (y + j) % high
                self.arrive(zs, xs, c, ys, 0)
                self.to_core(zs, xs, ys, 0)
            if i > 0:
                for j in range(high):
                    ys = (y + j) % high
                    self.arrive(zs, xs, c, ys, 1)
                    self.to_core(zs, xs, ys, 1)

    def last(self, ready=None):
        wide, high, deep = self.sizes
        x, y, z, c = self.place
        for k in range(deep):
            zs = (z + k) % deep
            for i in range(wide):
                xs = (x + i) % wide
                if k == 0 and i == 0:
                    continue
                for j in range(high):
                    for h in range(2):
                        self.arrive(zs, xs, 1 - c, (y + j) % high, h)
                if ready is not None:
                    ready(zs * wide + xs)


def gather_sends(sizes):
    wide, high, deep = sizes
    n = (deep - 1) * 2 + (wide - 1) * (1 + high)
    n += (deep - 1) * 2 * (wide - 1 + high - 1 + 1)
    n += deep * (wide - 1) * high + (deep - 1) * (high - 1) * wide
    n += (deep * wide - 1) * (high - 1) + deep * (wide - 1) * high
    return n


class Spread:
    def __init__(self, sizes, sender, row_ref, all_ref, row_sem, keep_sem):
        self.sizes = sizes
        self.place = place(sizes)
        self.sender = sender
        self.row_ref, self.all_ref, self.row_sem = row_ref, all_ref, row_sem
        x, y, z, c = self.place
        self.keep = pltpu.make_async_copy(row_ref, all_ref.at[z, x, y, c], keep_sem)

    def pass_on(self, zs, xs, ys, to, own):
        c = self.place[3]
        spot = self.all_ref.at[zs, xs, ys, c]
        self.sender.send(self.row_ref if own else spot, spot, self.row_sem.at[zs, xs, ys, c], to)

    def landed(self, zs, xs, ys, cs):
        self.sender.arrive(self.all_ref.at[zs, xs, ys, cs], self.row_sem.at[zs, xs, ys, cs])

    def stage(self, number):
        wide, high, deep = self.sizes
        x, y, z, c = self.place
        columns = [(z + k) % deep for k in range(deep)]
        lines = [(x + k) % wide for k in range(wide)]
        heights = [(y + k) % high for k in range(high)]
        if number == 0:
            self.keep.start()
            for zt in columns[1:]:
                self.pass_on(z, x, y, (y * 2 + c, zt * wide + x), True)
        if number == 1:
            for zs in columns[1:]:
                self.landed(zs, x, y, c)
            for zs in columns:
                for yt in heights[1:]:
                    self.pass_on(zs, x, y, (yt * 2 + c, z * wide + x), zs is columns[0])
        if number == 2:
            for zs in columns:
                for ys in heights[1:]:
                    self.landed(zs, x, ys, c)
            for zs in columns:
                for ys in heights:
                    own = zs is columns[0] and ys is heights[0]
                    for xt in lines[1:]:
                        self.pass_on(zs, x, ys, (y * 2 + c, z * wide + xt), own)
        if number == 3:
            for zs in columns:
                for xs in lines[1:]:
                    for ys in heights:
                        self.landed(zs, xs, ys, c)
            for zs in columns:
                for xs in lines:
                    for ys in heights:
                        own = zs is columns[0] and xs is lines[0] and ys is heights[0]
                        self.pass_on(zs, xs, ys, (y * 2 + 1 - c, z * wide + x), own)
        if number == 4:
            for zs in columns:
                for xs in lines:
                    for ys in heights:
                        self.landed(zs, xs, ys, 1 - c)
            self.keep.wait()


def spread_sends(sizes):
    wide, high, deep = sizes
    return deep - 1 + deep * (high - 1) + deep * high * (wide - 1) + deep * wide * high


class Reduce:
    def __init__(self, sizes, split, sender, in_ref, out_ref, scratch):
        self.sizes = sizes
        self.split = split
        self.place = place(sizes)
        self.sender = sender
        self.in_ref, self.out_ref = in_ref, out_ref
        (
            self.held,
            self.from_core,
            self.from_x_a,
            self.from_y_b,
            self.from_y_a,
            self.from_x_b,
            self.from_z,
            self.final,
            self.local_sem,
            self.core_sem,
            self.xa_sem,
            self.yb_sem,
            self.ya_sem,
            self.xb_sem,
            self.z_sem,
            self.done_sem,
        ) = scratch
        deep = sizes[2]
        z = self.place[2]
        far = list(range(deep // 2, deep)) + list(range(deep // 2 - 1, 0, -1))
        self.order = [(z + k) % deep for k in far] + [z]

    def local(self, step):
        c = self.place[3]
        source = self.in_ref.at[self.order[step], :, c]
        return pltpu.make_async_copy(source, self.held.at[step], self.local_sem.at[step])

    def start(self):
        wide, high, deep = self.sizes
        x, y, z, c = self.place
        x_first, y_first = self.split
        pieces = x_first + y_first
        for step in range(deep):
            self.local(step).start()
            self.sender.send(
                self.in_ref.at[self.order[step], :, 1 - c],
                self.from_core.at[step],
                self.core_sem.at[step],
                (y * 2 + 1 - c, z * wide + x),
            )

    def merge(self, target, extras):
        total = target[...].astype(jnp.float32)
        for extra in extras:
            total = total + extra[...].astype(jnp.float32)
        target[...] = total.astype(target.dtype)

    def first(self, step):
        wide, high, deep = self.sizes
        x, y, z, c = self.place
        x_first, y_first = self.split
        pieces = x_first + y_first
        self.local(step).wait()
        self.sender.arrive(self.from_core.at[step], self.core_sem.at[step])

        def body(i, carry):
            xi, yi, hi = i // (pieces * high), i // pieces % high, i % pieces
            self.merge(self.held.at[step, xi, yi, hi], [self.from_core.at[step, xi, yi, hi]])
            return carry

        lax.fori_loop(0, wide * high * pieces, body, 0)
        for k in range(1, wide):
            xt = (x + k) % wide
            self.sender.send(
                self.held.at[step, xt, :, :x_first],
                self.from_x_a.at[k - 1, step],
                self.xa_sem.at[k - 1, step],
                (y * 2 + c, z * wide + xt),
            )
        for k in range(1, high):
            yt = (y + k) % high
            self.sender.send(
                self.held.at[step, :, yt, x_first:],
                self.from_y_b.at[k - 1, step],
                self.yb_sem.at[k - 1, step],
                (yt * 2 + c, z * wide + x),
            )

    def second(self, step):
        wide, high, deep = self.sizes
        x, y, z, c = self.place
        x_first, y_first = self.split
        pieces = x_first + y_first
        for k in range(1, wide):
            self.sender.arrive(self.from_x_a.at[k - 1, step], self.xa_sem.at[k - 1, step])

        def body_a(i, carry):
            yt, h = (y + 1 + i // x_first) % high, i % x_first
            extras = [self.from_x_a.at[k, step, yt, h] for k in range(wide - 1)]
            self.merge(self.held.at[step, x, yt, h], extras)
            return carry

        lax.fori_loop(0, high * x_first, body_a, 0)
        for k in range(1, high):
            yt = (y + k) % high
            self.sender.send(
                self.held.at[step, x, yt, :x_first],
                self.from_y_a.at[k - 1, step],
                self.ya_sem.at[k - 1, step],
                (yt * 2 + c, z * wide + x),
            )
        for k in range(1, high):
            self.sender.arrive(self.from_y_b.at[k - 1, step], self.yb_sem.at[k - 1, step])

        def body_b(i, carry):
            xt, h = (x + 1 + i // y_first) % wide, i % y_first
            extras = [self.from_y_b.at[k, step, xt, h] for k in range(high - 1)]
            self.merge(self.held.at[step, xt, y, x_first + h], extras)
            return carry

        lax.fori_loop(0, wide * y_first, body_b, 0)
        for k in range(1, wide):
            xt = (x + k) % wide
            self.sender.send(
                self.held.at[step, xt, y, x_first:],
                self.from_x_b.at[k - 1, step],
                self.xb_sem.at[k - 1, step],
                (y * 2 + c, z * wide + xt),
            )

    def third(self, step):
        wide, high, deep = self.sizes
        x, y, z, c = self.place
        x_first, y_first = self.split
        pieces = x_first + y_first
        for k in range(1, high):
            self.sender.arrive(self.from_y_a.at[k - 1, step], self.ya_sem.at[k - 1, step])
        for h in range(x_first):
            extras = [self.from_y_a.at[k, step, h] for k in range(high - 1)]
            self.merge(self.held.at[step, x, y, h], extras)
        for k in range(1, wide):
            self.sender.arrive(self.from_x_b.at[k - 1, step], self.xb_sem.at[k - 1, step])
        for h in range(y_first):
            extras = [self.from_x_b.at[k, step, h] for k in range(wide - 1)]
            self.merge(self.held.at[step, x, y, x_first + h], extras)
        if step < deep - 1:
            self.sender.send(
                self.held.at[step, x, y],
                self.from_z.at[step],
                self.z_sem.at[step],
                (y * 2 + c, self.order[step] * wide + x),
            )

    def turn(self, number):
        deep = self.sizes[2]
        if number < deep:
            self.first(number)
        if 0 <= number - 1 < deep:
            self.second(number - 1)
        if 0 <= number - 2 < deep:
            self.third(number - 2)

    def total(self):
        wide, high, deep = self.sizes
        x, y, z, c = self.place
        x_first, y_first = self.split
        pieces = x_first + y_first
        for step in range(deep - 1):
            self.sender.arrive(self.from_z.at[step], self.z_sem.at[step])
        for h in range(pieces):
            total = self.held[deep - 1, x, y, h].astype(jnp.float32)
            for step in range(deep - 1):
                total = total + self.from_z[step, h].astype(jnp.float32)
            self.final[h] = total.astype(self.final.dtype)
        spot, recv = self.out_ref.at[c, y], self.done_sem.at[c, y]
        pltpu.make_async_copy(self.final, spot, self.local_sem.at[deep]).start()
        for k in range(1, high):
            to = ((y + k) % high * 2 + c, z * wide + x)
            self.sender.send(self.final, spot, recv, to)
        self.sender.send(self.final, spot, recv, (y * 2 + 1 - c, z * wide + x))

    def last(self):
        wide, high, deep = self.sizes
        x, y, z, c = self.place
        x_first, y_first = self.split
        pieces = x_first + y_first
        for k in range(1, high):
            yt = (y + k) % high
            spot, recv = self.out_ref.at[c, yt], self.done_sem.at[c, yt]
            self.sender.arrive(spot, recv)
            self.sender.send(spot, spot, recv, (y * 2 + 1 - c, z * wide + x))
        for k in range(high):
            yt = (y + k) % high
            self.sender.arrive(self.out_ref.at[1 - c, yt], self.done_sem.at[1 - c, yt])
        own = self.out_ref.at[c, y]
        pltpu.make_async_copy(self.final, own, self.local_sem.at[deep]).wait()


def reduce_sends(sizes):
    wide, high, deep = sizes
    return deep + deep * 2 * (wide - 1 + high - 1) + deep - 1 + 2 * (high - 1) + 1


def reduce_scratch(sizes, split, rows, width, kind):
    wide, high, deep = sizes
    x_first, y_first = split
    pieces = x_first + y_first
    tail = (rows, width)
    dma = pltpu.SemaphoreType.DMA
    return [
        pltpu.VMEM((deep, wide, high, pieces) + tail, kind),
        pltpu.VMEM((deep, wide, high, pieces) + tail, kind),
        pltpu.VMEM((wide - 1, deep, high, x_first) + tail, kind),
        pltpu.VMEM((high - 1, deep, wide, y_first) + tail, kind),
        pltpu.VMEM((high - 1, deep, x_first) + tail, kind),
        pltpu.VMEM((wide - 1, deep, y_first) + tail, kind),
        pltpu.VMEM((deep - 1, pieces) + tail, kind),
        pltpu.VMEM((pieces,) + tail, kind),
        dma((deep + 1,)),
        dma((deep,)),
        dma((wide - 1, deep)),
        dma((high - 1, deep)),
        dma((high - 1, deep)),
        dma((wide - 1, deep)),
        dma((deep - 1,)),
        dma((2, high)),
    ]


reduce_parts = 16


class Outer:
    def __init__(self, sizes, sender, left, right, lefts, rights, left_sem, right_sem):
        self.sizes = sizes
        self.place = place(sizes)
        self.sender = sender
        self.left, self.right = left, right
        self.lefts, self.rights = lefts, rights
        self.left_sem, self.right_sem = left_sem, right_sem
        x, y, z, c = self.place
        self.count = sizes[0] * sizes[2]
        self.me = z * sizes[0] + x

    def own(self, part):
        share = self.lefts.shape[2]
        return self.left.at[:, pl.ds(pl.multiple_of(part * share, 16), share)]

    def start(self):
        x, y, z, c = self.place
        me = self.me
        for k in range(1, self.count):
            to = (me + k) % self.count
            self.sender.send(self.own(to), self.lefts.at[me], self.left_sem.at[me], (y * 2 + c, to))
            self.sender.send(self.right, self.rights.at[me], self.right_sem.at[me], (y * 2 + c, to))
        self.lefts[me] = self.own(me)[...]
        self.rights[me] = self.right[...]

    def multiply(self, target):
        for k in range(1, self.count):
            source = (self.me + k) % self.count
            self.sender.arrive(self.lefts.at[source], self.left_sem.at[source])
            self.sender.arrive(self.rights.at[source], self.right_sem.at[source])
        share = self.lefts.shape[2]
        latents = self.right.shape[0]
        taps = lanes // latents
        lane = lax.broadcasted_iota(jnp.int32, (share, lanes), 1) // latents
        rights = jnp.concatenate(
            [self.rights[source] for source in range(self.count) for _ in range(taps)], axis=0
        )
        for group in range(self.left.shape[0]):
            pieces = []
            for source in range(self.count):
                block = self.lefts[source, group].astype(jnp.float32)
                pieces.append(
                    jnp.concatenate(
                        [jnp.where(lane == tap, block, 0.0) for tap in range(taps)], axis=0
                    ).astype(jnp.bfloat16)
                )
            value = dot(jnp.concatenate(pieces, axis=1), rights)
            target[group * taps : (group + 1) * taps] = value.reshape(taps, share, -1)


class OuterSum:
    def __init__(self, sizes, sender, partials, out_ref, scratch):
        self.sizes = sizes
        self.place = place(sizes)
        self.sender = sender
        self.partials, self.out_ref = partials, out_ref
        self.peer, self.low, self.peers, self.core_sem, self.y_sem, self.out_sem, self.last_sem = scratch
        self.taps = partials.shape[1] // sizes[1]

    def to_core(self):
        wide, high, deep = self.sizes
        x, y, z, c = self.place
        to = (y * 2 + 1 - c, z * wide + x)
        self.sender.send(self.partials.at[1 - c], self.peer, self.core_sem, to)

    def to_y(self):
        wide, high, deep = self.sizes
        x, y, z, c = self.place
        self.sender.arrive(self.peer, self.core_sem)
        total = self.partials[c] + self.peer[...]
        self.partials[c] = total
        self.low[...] = total.astype(self.low.dtype)
        for k in range(1, high):
            yt = (y + k) % high
            self.sender.send(
                self.low.at[pl.ds(yt * self.taps, self.taps)],
                self.peers.at[k - 1],
                self.y_sem.at[k - 1],
                (yt * 2 + c, z * wide + x),
            )

    def back_y(self):
        wide, high, deep = self.sizes
        x, y, z, c = self.place
        mine = pl.ds(y * self.taps, self.taps)
        total = self.partials[c, mine]
        for k in range(1, high):
            self.sender.arrive(self.peers.at[k - 1], self.y_sem.at[k - 1])
            total = total + self.peers[k - 1].astype(jnp.float32)
        spot = self.out_ref.at[c, mine]
        spot[...] = total
        for k in range(1, high):
            to = ((y + k) % high * 2 + c, z * wide + x)
            self.sender.send(spot, spot, self.out_sem.at[y], to)

    def back_core(self):
        wide, high, deep = self.sizes
        x, y, z, c = self.place
        for k in range(1, high):
            yt = (y + k) % high
            spot = self.out_ref.at[c, pl.ds(yt * self.taps, self.taps)]
            self.sender.arrive(spot, self.out_sem.at[yt])
        to = (y * 2 + 1 - c, z * wide + x)
        self.sender.send(self.out_ref.at[c], self.out_ref.at[c], self.last_sem, to)

    def last(self):
        c = self.place[3]
        self.sender.arrive(self.out_ref.at[1 - c], self.last_sem)


def outer_sends(sizes):
    wide, high, deep = sizes
    return 4 * (wide * deep - 1) + 2 * high


def outer_left(taps):
    per = lanes // taps[0].shape[0]
    turned = [tap.T for tap in taps]
    return [
        jnp.concatenate(turned[start : start + per], axis=1).astype(jnp.bfloat16)
        for start in range(0, len(taps), per)
    ]


margin = 32
lanes = 128


def elu_slope(values):
    return jnp.where(values > 0, 1.0, jnp.exp(jnp.minimum(values, 0.0)))


def elu(values):
    return jnp.where(values > 0, values, jnp.exp(jnp.minimum(values, 0.0)) - 1.0)


def dot(left, right):
    return jnp.dot(left, right, preferred_element_type=jnp.float32)


def dot_last(left, right):
    return lax.dot_general(
        left, right, (((1,), (1,)), ((), ())), preferred_element_type=jnp.float32
    )


def dot_rows(left, right):
    return lax.dot_general(
        left, right, (((0,), (0,)), ((), ())), preferred_element_type=jnp.float32
    )


def spread_taps(target, source, ids, width, sign, dilation, length):
    block = 64

    def body(step, carry):
        base = pl.multiple_of(step * block, block)
        window = ids[pl.ds(base, block + 2 * margin), :]
        own = window[margin : margin + block]
        for tap in range(KERNEL):
            start = margin + sign * (tap - KERNEL // 2) * dilation
            match = window[start : start + block] == own
            for piece in range(width // lanes):
                columns = slice(piece * lanes, (piece + 1) * lanes)
                values = source[pl.ds(base, block + 2 * margin), columns][start : start + block]
                spot = tap * width + piece * lanes
                target[pl.ds(base, block), spot : spot + lanes] = jnp.where(
                    match, values, 0.0
                ).astype(jnp.bfloat16)
        return carry

    lax.fori_loop(0, length // block, body, 0)


def forward_unit(unit, stream, follow, ids, weights, scratch, length, own):
    dilated, pointwise = weights
    padded, columns, hidden, excited, active = scratch
    channels = stream.shape[1]
    values = elu(stream[...])
    padded[margin : margin + length, :] = values
    active[unit] = values[own].astype(jnp.bfloat16)
    spread_taps(columns, padded, ids, channels, 1, dilation_list[unit], length)
    kernel = dilated[unit * KERNEL : (unit + 1) * KERNEL].reshape(KERNEL * channels, -1)
    value = dot(columns[...], kernel)
    hidden[unit] = value
    lifted = elu(value).astype(jnp.bfloat16)
    excited[unit] = lifted
    follow[...] = stream[...] + dot_last(lifted, pointwise[unit])


def backward_unit(unit, grad, stream, ids, weights, scratch, length, own):
    dilated, pointwise = weights
    padded, columns, hidden, excited, active = scratch
    width = hidden.shape[2]
    low = grad[...].astype(jnp.bfloat16)
    grad_hidden = dot(low, pointwise[unit]) * elu_slope(hidden[unit])
    pointwise[unit] = dot(
        grad[own, :].T.astype(jnp.bfloat16), excited[unit, own, :]
    ).astype(jnp.bfloat16)
    padded[margin : margin + length, :width] = grad_hidden.astype(jnp.bfloat16).astype(jnp.float32)
    spread_taps(columns, padded, ids, width, -1, dilation_list[unit], length)
    turned = active[unit].astype(jnp.float32).T.astype(jnp.bfloat16)
    total = None
    for tap in range(KERNEL):
        piece = slice(tap * width, (tap + 1) * width)
        part = dot_last(columns[:, piece], dilated[unit * KERNEL + tap])
        total = part if total is None else total + part
        dilated[unit * KERNEL + tap] = dot(turned, columns[own, piece]).astype(jnp.bfloat16)
    grad[...] = grad[...] + total * elu_slope(stream[...])


class Mover:
    def __init__(self, side, geometry, gathered, packed, weights, sems):
        self.seq, self.share, self.blocks = geometry
        self.base = side * self.blocks
        width = gathered.shape[-1]
        self.gathered = gathered.reshape(self.seq, -1, self.share, width)
        self.packed = packed
        self.weights = weights
        self.sems = sems

    def block_start(self, kind):
        return (0, 3 * KERNEL, 3 * KERNEL + 3, 3 * KERNEL + 4)[kind]

    def load(self, kind, owner):
        rows = self.weights[kind]
        start = self.base + self.block_start(kind)
        source = self.gathered.at[owner, pl.ds(start, rows.shape[0])]
        target = rows.at[:, pl.ds(pl.multiple_of(owner * self.share, 16), self.share)]
        return pltpu.make_async_copy(source, target, self.sems.at[kind, owner])

    def start_loads(self, kind):
        for owner in range(self.seq):
            self.load(kind, owner).start()

    def load_owner(self, owner):
        for kind in (2, 3, 0, 1):
            self.load(kind, owner).start()

    def wait_loads(self, kind):
        for owner in range(self.seq):
            self.load(kind, owner).wait()

    def store(self, kind, owner, first, size):
        rows = self.weights[kind]
        start = self.block_start(kind) + first
        source = rows.at[first : first + size, pl.ds(owner * self.share, self.share)]
        target = self.packed.at[owner, pl.ds(start, size)]
        return pltpu.make_async_copy(source, target, self.sems.at[4 + kind, owner])


def load_group(rows, seq, share):
    width = rows.shape[-1]
    part = width // seq
    value = rows.astype(jnp.float32).reshape(seq, GROUPS, part, width)
    return [value[:, g].reshape(width, width).astype(jnp.bfloat16) for g in range(GROUPS)]


def store_group(grads, seq, share):
    width = grads[0].shape[-1]
    part = width // seq
    value = jnp.stack([grad.reshape(seq, part, width) for grad in grads], axis=1)
    return value.reshape(seq, GROUPS * part, width).astype(jnp.bfloat16)


def put_tap(tiles, tap, value):
    latents = value.shape[0]
    for piece in range(tiles.shape[0]):
        tiles[piece, pl.ds(tap, latents, stride=STRIDE), :] = value[
            :, piece * lanes : (piece + 1) * lanes
        ]


def take_tap(tiles, tap, latents):
    return jnp.concatenate(
        [tiles[piece, pl.ds(tap, latents, stride=STRIDE), :] for piece in range(tiles.shape[0])],
        axis=1,
    )


def to_tiles(tiles, value):
    for piece in range(tiles.shape[0]):
        tiles[piece] = value[:, piece * lanes : (piece + 1) * lanes]


def from_tiles(tiles):
    return jnp.concatenate([tiles[piece] for piece in range(tiles.shape[0])], axis=1)


def set_edges(padded, length):
    zero = jnp.zeros((margin, padded.shape[1]), jnp.float32)
    padded[:margin, :] = zero
    padded[margin + length :, :] = zero


def front_kernel(
    sizes,
    geometry,
    length,
    enc_dilated,
    enc_point,
    enc_group,
    enc_strided,
    dec_dilated,
    dec_point,
    dec_group,
    dec_strided,
    numbers_own,
    frames_own,
    cot_own,
    books_ref,
    gathered,
    frames_long,
    ids_ref,
    decoded_ref,
    grad_quant_ref,
    picks_ref,
    packed,
    left_ref,
    right_ref,
    shard_ref,
    wide_dilated,
    wide_point,
    wide_group,
    wide_strided,
    code_ref,
    cot_ref,
    dilated,
    pointwise,
    group,
    strided,
    streams,
    padded,
    columns,
    hidden,
    excited,
    active,
    tiles,
    sems,
    edge_sem,
    keep_sem,
    recv_sem,
    send_sem,
):
    seq, share, blocks = geometry
    wide, high, deep = sizes
    x, y, z, c = place(sizes)
    me = z * wide + x
    masters = ((enc_dilated, enc_point, enc_group, enc_strided),) + (
        (dec_dilated, dec_point, dec_group, dec_strided),
    )
    wides = (wide_dilated, wide_point, wide_group, wide_strided)
    reads = [
        [
            pltpu.make_async_copy(source, target.at[side], keep_sem.at[5 + 4 * side + number])
            for number, (source, target) in enumerate(zip(masters[side], wides))
        ]
        for side in range(2)
    ]
    for side in (1, 0):
        for copy in reads[side]:
            copy.start()
    greet(sizes)
    sender = Sender(send_sem, (y * 2 + 1 - c, me))
    gathers = [
        Gather(
            sizes,
            sender,
            shard_ref.at[side].reshape(2, high, 2, -1, shard_ref.shape[-1]),
            gathered.at[:, :, side],
            recv_sem.at[side],
        )
        for side in range(2)
    ]
    encoder, decoder = gathers

    def pack(side):
        dil, point, both = wide_dilated[side], wide_point[side], wide_group[side]
        width = shard_ref.shape[-1]
        low = jnp.bfloat16
        at = 0
        for value in (dil, point, both.reshape(1, share, width)):
            shard_ref[side, at : at + value.shape[0]] = value.astype(low)
            at += value.shape[0]
        for part in range(2):
            value = wide_strided[side, :, :, part * width : (part + 1) * width]
            shard_ref[side, at : at + value.shape[0]] = value.astype(low)
            at += value.shape[0]
        if at < blocks:
            shard_ref[side, at:] = jnp.zeros((blocks - at, share, width), low)

    for copy in reads[1]:
        copy.wait()
    pack(1)
    decoder.own_z()
    decoder.own_x()
    keeps = [
        pltpu.make_async_copy(
            gathers[side].in_ref, gathered.at[z, x, side], keep_sem.at[13 + side]
        )
        for side in range(2)
    ]
    keeps[1].start()
    for copy in reads[0]:
        copy.wait()
    pack(0)
    keeps[0].start()
    own = length // 2
    half = length // 4
    reach = half // STRIDE
    near = 80
    set_edges(padded, length)
    blank = jnp.zeros((half - near, cot_ref.shape[1]), jnp.float32)
    cot_ref[: half - near, :] = blank
    cot_ref[length - (half - near) :, :] = blank
    outside = jnp.full((margin, lanes), -1, jnp.int32)
    ids_ref[:margin, :] = outside
    ids_ref[margin + length :, :] = outside
    ids_own = numbers_own.at[:own]
    code_own = numbers_own.at[own:].reshape(code_ref.shape[0], own // STRIDE, lanes)
    own_copies = [
        pltpu.make_async_copy(frames_own, frames_long.at[half : half + own], keep_sem.at[1]),
        pltpu.make_async_copy(cot_own, cot_ref.at[half : half + own], keep_sem.at[2]),
        pltpu.make_async_copy(
            ids_own, ids_ref.at[margin + half : margin + half + own], keep_sem.at[3]
        ),
        pltpu.make_async_copy(code_own, code_ref.at[:, reach : reach + own // STRIDE], keep_sem.at[4]),
    ]
    for copy in own_copies:
        copy.start()
    edges = [
        (frames_own.at[own - half :], frames_long.at[:half]),
        (cot_own.at[own - near :], cot_ref.at[half - near : half]),
        (ids_own.at[own - half :], ids_ref.at[margin : margin + half]),
        (code_own.at[:, own // STRIDE - reach :], code_ref.at[:, :reach]),
        (frames_own.at[:half], frames_long.at[half + own :]),
        (cot_own.at[:near], cot_ref.at[half + own : half + own + near]),
        (ids_own.at[:half], ids_ref.at[margin + half + own : margin + length]),
        (code_own.at[:, :reach], code_ref.at[:, reach + own // STRIDE :]),
    ]
    edge_copies = []
    for number, (src, dst) in enumerate(edges):
        other = (me + (1 if number < len(edges) // 2 else seq - 1)) % seq
        copy = pltpu.make_async_remote_copy(
            src_ref=src,
            dst_ref=dst,
            send_sem=edge_sem.at[0, number],
            recv_sem=edge_sem.at[1, number],
            device_id=(y * 2 + c, other),
            device_id_type=MESH,
        )
        copy.start()
        edge_copies.append(copy)
    for number in (3, 7):
        edge_copies[number].wait()
    own_copies[3].wait()
    latents = length // STRIDE
    codes = books_ref.shape[2]
    width = books_ref.shape[3]
    tile_range = lax.broadcasted_iota(jnp.int32, (latents, lanes), 1)
    quantized = []
    for g in range(GROUPS):
        picked = []
        for level in range(LEVELS):
            entry = g * LEVELS + level
            chosen = code_ref[entry]
            hot = jnp.concatenate(
                [
                    (chosen == tile_range + tile * lanes).astype(jnp.float32)
                    for tile in range(codes // lanes)
                ],
                axis=1,
            )
            pick = jnp.dot(hot, books_ref[g, level], precision=lax.Precision.HIGHEST)
            picks_ref[entry] = pick
            picked.append(pick)
        quantized.append((picked[0] + picked[1]).astype(jnp.bfloat16))
    for k in range(1, deep):
        decoder.from_z(k)
    encoder.own_z()
    for k in range(deep):
        decoder.second(k)
    encoder.own_x()
    for k in range(deep):
        decoder.third(k)
        if k > 0:
            encoder.from_z(k)
    for number, copy in enumerate(edge_copies):
        if number not in (3, 7):
            copy.wait()
    for copy in own_copies[:3]:
        copy.wait()

    @pl.when(me == 0)
    def _():
        ids_ref[margin : margin + half, :] = jnp.full((half, lanes), -1, jnp.int32)

    @pl.when(me == seq - 1)
    def _():
        ids_ref[margin + half + own : margin + length, :] = jnp.full((half, lanes), -1, jnp.int32)

    weights = (dilated, pointwise, group, strided)
    mover = Mover(1, geometry, gathered, packed, weights, sems)
    for copy in keeps:
        copy.wait()
    mover.load_owner(me)
    decoder.last(mover.load_owner)
    pump = [functools.partial(encoder.second, k) for k in range(deep)]
    pump += [functools.partial(encoder.third, k) for k in range(deep)]
    first, last = length // 4, 3 * length // 4
    mover.wait_loads(2)
    out_weights = load_group(group[0], seq, share)
    mixed = [dot(quantized[g], out_weights[g]) for g in range(GROUPS)]
    lifted = [elu(value).astype(jnp.bfloat16) for value in mixed]
    mover.wait_loads(3)
    for tap in range(STRIDE):
        value = dot_last(lifted[0], strided[tap]) + dot_last(lifted[1], strided[STRIDE + tap])
        put_tap(tiles, tap, value)
    streams[0] = from_tiles(tiles)
    mover.wait_loads(0)
    mover.wait_loads(1)
    scratch = (padded, columns, hidden, excited, active)
    pump.pop(0)()
    for unit in range(3):
        forward_unit(
            unit, streams.at[unit], streams.at[unit + 1], ids_ref, (dilated, pointwise), scratch,
            length, slice(first, last),
        )
        pump.pop(0)()
    decoded_ref[...] = streams[3, first:last, :].astype(jnp.bfloat16)
    grad = streams.at[3]
    grad[...] = cot_ref[...]

    for unit in (2, 1, 0):
        backward_unit(
            unit, grad, streams.at[unit], ids_ref, (dilated, pointwise), scratch, length,
            slice(first, last),
        )
        for owner in range(seq):
            mover.store(0, owner, unit * KERNEL, KERNEL).start()
        if pump:
            pump.pop(0)()
    for owner in range(seq):
        mover.store(1, owner, 0, 3).start()
    own = slice(first // STRIDE, last // STRIDE)
    grad_lifted = [None, None]
    own_taps = []
    to_tiles(tiles, grad[...])
    for tap in range(STRIDE):
        part = take_tap(tiles, tap, latents)
        low = part.astype(jnp.bfloat16)
        own_taps.append(part[own])
        for half in range(2):
            value = dot(low, strided[half * STRIDE + tap])
            grad_lifted[half] = value if tap == 0 else grad_lifted[half] + value
    for number, value in enumerate(outer_left(own_taps)):
        left_ref[number] = value
    right_ref[...] = jnp.concatenate([lifted[0][own], lifted[1][own]], axis=1)
    group_grads = []
    for g in range(GROUPS):
        low = (grad_lifted[g] * elu_slope(mixed[g])).astype(jnp.bfloat16)
        group_grads.append(dot_rows(quantized[g][own], low[own]))
        grad_quant_ref[g] = dot_last(low, out_weights[g])
    group[0] = store_group(group_grads, seq, share).reshape(group.shape[1:])
    for owner in range(seq):
        mover.store(2, owner, 0, 1).start()
    while pump:
        pump.pop(0)()
    finish_stores(mover, seq)
    encoder.last()
    sender.finish()


def finish_stores(mover, seq):
    for owner in range(seq):
        for unit in range(3):
            mover.store(0, owner, unit * KERNEL, KERNEL).wait()
        mover.store(1, owner, 0, 3).wait()
        mover.store(2, owner, 0, 1).wait()


def back_kernel(
    sizes,
    split,
    geometry,
    length,
    frames_ref,
    ids_ref,
    grad_quant_ref,
    picks_ref,
    digits_ref,
    left_ref,
    right_ref,
    gathered,
    partial_ref,
    frames_grad_ref,
    packed,
    share_decoder,
    share_encoder,
    all_ref,
    strided_out,
    dilated,
    pointwise,
    group,
    strided,
    streams,
    padded,
    columns,
    hidden,
    excited,
    active,
    tiles,
    sems,
    *refs,
):
    seq, share, blocks = geometry
    x, y, z, c = place(sizes)
    me = z * sizes[0] + x
    weights = (dilated, pointwise, group, strided)
    mover = Mover(0, geometry, gathered, packed, weights, sems)
    for kind in (0, 1, 3, 2):
        mover.start_loads(kind)
    greet(sizes, row=True)
    sender = Sender(refs[-1], (y * 2 + 1 - c, me))
    packed_view = packed.reshape(partial_ref.shape)
    other = Reduce(sizes, split, sender, partial_ref, share_decoder, refs[:reduce_parts])
    side = Reduce(sizes, split, sender, packed_view, share_encoder, refs[reduce_parts : 2 * reduce_parts])
    rows_ref, keep_sem, row_sem = refs[2 * reduce_parts : 2 * reduce_parts + 3]
    spread = Spread(sizes, sender, rows_ref, all_ref, row_sem, keep_sem)
    extra = refs[2 * reduce_parts + 3 : -1]
    left_own, right_own, lefts, rights, partials = extra[:5]
    left_sem, right_sem = extra[5:7]
    down, up = [
        Outer(
            sizes, sender, left, right, lefts.at[side], rights.at[side], left_sem.at[side],
            right_sem.at[side],
        )
        for side, (left, right) in enumerate(((left_own, right_own), (left_ref, right_ref)))
    ]
    both = OuterSum(sizes, sender, partials, strided_out, extra[7:])
    other.start()
    up.start()
    turns = sizes[2] + 2
    pump = [functools.partial(other.turn, number) for number in range(turns)]
    pump += [other.total, other.last]
    for spot in (1, 3, 5, 6):
        pump.insert(spot, lambda: None)
    set_edges(padded, length)
    own_frames = frames_grad_ref.shape[0]
    first = (length - own_frames) // 2
    last = first + own_frames
    skip = (frames_ref.shape[0] - length) // 2
    ids_ref = ids_ref.at[skip : skip + length + 2 * margin]
    latents = length // STRIDE
    own = slice(first // STRIDE, last // STRIDE)
    width = picks_ref.shape[2]
    streams[0] = frames_ref[skip : skip + length, :].astype(jnp.float32)
    mover.wait_loads(0)
    mover.wait_loads(1)
    scratch = (padded, columns, hidden, excited, active)
    for unit in range(3):
        forward_unit(
            unit, streams.at[unit], streams.at[unit + 1], ids_ref, (dilated, pointwise), scratch,
            length, slice(first, last),
        )
        pump.pop(0)()
    to_tiles(tiles, elu(streams[3]))
    mover.wait_loads(3)
    mover.wait_loads(2)
    in_weights = load_group(group[0], seq, share)
    latent = [None, None]
    for tap in range(STRIDE):
        low = take_tap(tiles, tap, latents).astype(jnp.bfloat16)
        for half in range(2):
            value = dot(low, strided[half * STRIDE + tap])
            latent[half] = value if tap == 0 else latent[half] + value
    group_grads = []
    grad_latent = []
    for g in range(GROUPS):
        low = latent[g].astype(jnp.bfloat16)
        first_part = dot(low, in_weights[g])
        wanted = slice(skip // STRIDE, skip // STRIDE + latents)
        pick = [picks_ref[g * LEVELS + level, wanted, :] for level in range(LEVELS)]
        second_part = first_part - pick[0]
        rows_ref[:, g * width : (g + 1) * width] = first_part[own].astype(jnp.bfloat16)
        grad_first = grad_quant_ref[g, wanted, :] + 2.0 * commit_weight * (
            second_part + (second_part - pick[1])
        )
        low_first = grad_first.astype(jnp.bfloat16)
        group_grads.append(dot_rows(low[own], low_first[own]))
        grad_latent.append(dot_last(low_first, in_weights[g]).astype(jnp.bfloat16))
    group[0] = store_group(group_grads, seq, share).reshape(group.shape[1:])
    rows_ref[:, GROUPS * width :] = digits_ref[...]
    spread.stage(0)
    for owner in range(seq):
        mover.store(2, owner, 0, 1).start()
    own_taps = []
    for tap in range(STRIDE):
        own_taps.append(take_tap(tiles, tap, latents)[own])
        value = dot_last(grad_latent[0], strided[tap]) + dot_last(
            grad_latent[1], strided[STRIDE + tap]
        )
        put_tap(tiles, tap, value)
    for number, value in enumerate(outer_left(own_taps)):
        left_own[number] = value
    right_own[...] = jnp.concatenate([grad_latent[0][own], grad_latent[1][own]], axis=1)
    down.start()
    grad = streams.at[3]
    grad[...] = from_tiles(tiles) * elu_slope(grad[...])
    pump.pop(0)()

    for unit in (2, 1, 0):
        backward_unit(
            unit, grad, streams.at[unit], ids_ref, (dilated, pointwise), scratch, length,
            slice(first, last),
        )
        for owner in range(seq):
            mover.store(0, owner, unit * KERNEL, KERNEL).start()
        if pump:
            pump.pop(0)()
    for owner in range(seq):
        mover.store(1, owner, 0, 3).start()
    frames_grad_ref[...] = grad[first:last, :]
    finish_stores(mover, seq)
    side.start()
    outer = [both.to_core, both.to_y, both.back_y, both.back_core, both.last]
    up.multiply(partials.at[1])
    for number in range(turns):
        if pump:
            pump.pop(0)()
        side.turn(number)
        if number == 0:
            down.multiply(partials.at[0])
        outer.pop(0)() if outer else None
        if number >= turns - 2:
            spread.stage(number - turns + 3)
    side.total()
    spread.stage(3)
    side.last()
    spread.stage(4)
    sender.finish()


def side_scratch(seq, share, length, own, channels, hidden):
    bf, f32 = jnp.bfloat16, jnp.float32
    group_rows = GROUPS * hidden // seq
    mats = [
        pltpu.VMEM((3 * KERNEL, channels, hidden), bf),
        pltpu.VMEM((3, channels, hidden), bf),
        pltpu.VMEM((1, seq * group_rows, hidden), bf),
        pltpu.VMEM((2 * STRIDE, channels, hidden), bf),
    ]
    return mats + [
        pltpu.VMEM((4, length, channels), f32),
        pltpu.VMEM((length + 2 * margin, channels), f32),
        pltpu.VMEM((length, KERNEL * channels), bf),
        pltpu.VMEM((3, length, hidden), f32),
        pltpu.VMEM((3, length, hidden), bf),
        pltpu.VMEM((3, own, channels), bf),
        pltpu.VMEM((channels // lanes, length, lanes), f32),
        pltpu.SemaphoreType.DMA((8, seq)),
    ]


def split_terms(value, count):
    terms = []
    for number in range(count):
        term = value.astype(jnp.bfloat16)
        terms.append(term)
        if number < count - 1:
            value = value - term.astype(jnp.float32)
    return terms


def product(left, right):
    def pair(i, j):
        return jnp.dot(left[i], right[j], preferred_element_type=jnp.float32)

    low = pair(0, 1) + pair(1, 0)
    if len(left) > 2:
        low = low + (pair(1, 1) + pair(0, 2) + pair(2, 0))
    return pair(0, 0) + low


def gram_of(left, right):
    return product(split_terms(left.T, 3), split_terms(right, 3))


def solve_mixing(gram):
    size = gram.shape[0]
    eye = (
        lax.broadcasted_iota(jnp.int32, (size, size), 0)
        == lax.broadcasted_iota(jnp.int32, (size, size), 1)
    ).astype(jnp.float32)
    scale = 1.0 / (jnp.sqrt(jnp.sum(gram * eye)) + norm_floor)
    current = gram * (scale * scale)
    total = None
    for repeat in range(NS_STEPS):
        terms = 3 if repeat < 2 else 2
        parts = split_terms(current, terms)
        factor = coef_first * eye + coef_second * current + coef_third * product(parts, parts)
        factors = split_terms(factor, terms)
        if total is None:
            total = factor
        else:
            total = product(split_terms(total, 2), factors[:2])
        if repeat < NS_STEPS - 1:
            half = split_terms(product(parts, factors), terms)
            current = product(half, factors)
    return total * scale


def solve_pair(corner, side, other):
    size = corner.shape[0]
    eye = (
        lax.broadcasted_iota(jnp.int32, (size, size), 0)
        == lax.broadcasted_iota(jnp.int32, (size, size), 1)
    ).astype(jnp.float32)
    scale = 1.0 / (jnp.sqrt(jnp.sum((corner + other) * eye)) + norm_floor)
    current = [value * (scale * scale) for value in (corner, side, other)]

    def whole(blocks, terms):
        parts = [split_terms(value, terms) for value in blocks]
        turned = split_terms(blocks[1].T, terms)
        top = [jnp.concatenate([p, q], axis=1) for p, q in zip(parts[0], parts[1])]
        low = [jnp.concatenate([p, q], axis=1) for p, q in zip(turned, parts[2])]
        return top, low

    def times(left, right):
        rows = [jnp.concatenate([p, q], axis=0) for p, q in zip(*right)]
        top = product(left[0], rows)
        low = product(left[1], [value[:, size:] for value in rows])
        return [top[:, :size], top[:, size:], low]

    total = None
    for repeat in range(NS_STEPS):
        terms = 3 if repeat < 2 else 2
        parts = whole(current, terms)
        square = times(parts, parts)
        factor = [
            coef_second * value + coef_third * double for value, double in zip(current, square)
        ]
        factor = [factor[0] + coef_first * eye, factor[1], factor[2] + coef_first * eye]
        factors = whole(factor, terms)
        if total is None:
            total = factor
        else:
            total = times(whole(total, 2), [values[:2] for values in factors])
        if repeat < NS_STEPS - 1:
            half = whole(times(parts, factors), terms)
            current = times(half, factors)
    return [value * scale for value in total]


def mixing_kernel(
    sizes,
    share,
    enc_dilated,
    enc_point,
    enc_group,
    enc_strided,
    dec_dilated,
    dec_point,
    dec_group,
    dec_strided,
    enc_dilated_w,
    enc_strided_w,
    dec_dilated_w,
    dec_strided_w,
    row_ref,
    books_ref,
    buffered_ref,
    marks_ref,
    enc_point_w,
    enc_group_w,
    dec_point_w,
    dec_group_w,
    enc_point_next,
    enc_group_next,
    dec_point_next,
    dec_group_next,
    enc_dilated_next,
    enc_strided_next,
    dec_dilated_next,
    dec_strided_next,
    books_next,
    small_ref,
    mix_ref,
    dilated,
    point,
    group,
    strided,
    dilated_w,
    strided_w,
    blocks,
    corner,
    slots,
    point_all,
    group_all,
    work,
    point_done,
    group_done,
    load_sem,
    send_sem,
    slot_sem,
    rows_sem,
    mix_sem,
    core_sem,
    small_sem,
    corner_sem,
    all_ref,
    books,
    first_books,
    buffered,
    code_sem,
):
    wide, high, deep = sizes
    x, y, z, c = place(sizes)
    count = wide * deep
    me = z * wide + x
    row = y * 2 + c
    middle = count // 2
    partner = (y * 2 + 1 - c, me)
    others = [(row, (me + k) % count) for k in range(1, count)]
    others += [
        ((y + j) % high * 2 + c, z * wide + (x + i) % wide)
        for i in range(wide)
        for j in range(1, high)
    ] + [partner]
    pending = []

    def remote(src, dst, number, recv, to):
        return pltpu.make_async_remote_copy(
            src_ref=src,
            dst_ref=dst,
            send_sem=send_sem.at[number],
            recv_sem=recv,
            device_id=to,
            device_id_type=MESH,
        )

    def send(when, src, dst, recv, to):
        number = len(pending)
        pending.append((when, src, dst, recv, to))

        @pl.when(when)
        def _():
            remote(src, dst, number, recv, to).start()

    def arrive(dst, recv):
        remote(dst, dst, 0, recv, partner).wait_recv()

    first_set = y == 0
    second_set = y == 1

    def load(number, source, target):
        return pltpu.make_async_copy(source, target, load_sem.at[number])

    own_loads = [
        (enc_dilated, dilated.at[0]),
        (dec_dilated, dilated.at[1]),
        (enc_strided, strided.at[0]),
        (dec_strided, strided.at[1]),
        (enc_point, point.at[0]),
        (dec_point, point.at[1]),
        (enc_group, group.at[0]),
        (dec_group, group.at[1]),
        (enc_dilated_w, dilated_w.at[0]),
        (dec_dilated_w, dilated_w.at[1]),
        (enc_strided_w, strided_w.at[0]),
        (dec_strided_w, strided_w.at[1]),
    ]
    for number, (source, target) in enumerate(own_loads):
        load(number, source, target).start()
    code_share = books.shape[2]
    own_books = books_ref.at[:, :, pl.ds(pl.multiple_of(me * code_share, 8), code_share)]
    code_loads = [
        pltpu.make_async_copy(row_ref, all_ref, code_sem.at[0]),
        pltpu.make_async_copy(own_books, books, code_sem.at[1]),
        pltpu.make_async_copy(buffered_ref, buffered, code_sem.at[2]),
        pltpu.make_async_copy(books_ref.at[:, 0], first_books, code_sem.at[3]),
    ]
    for copy in code_loads:
        copy.start()
    barrier = pltpu.get_barrier_semaphore()
    for other in others:
        pl.semaphore_signal(barrier, inc=1, device_id=other, device_id_type=MESH)
    pl.semaphore_wait(barrier, len(others))

    for number in (4, 5, 6, 7, 2, 3, 0, 1):
        load(number, *own_loads[number]).wait()

    block_at = [middle - 2 + number + c for number in range(3)]
    strided_at = block_at[1]
    small_at = [(middle + c + offset + count) % count for offset in (1, 2, 3, -3, -4)]
    point_at, group_at = small_at[:3], small_at[3:]
    part = share // GROUPS
    piece = blocks.shape[1] // (wide * high)

    for unit in range(3):
        at = point_at[unit]
        rows = pl.ds(pl.multiple_of(me * share, 8), share)
        send(
            second_set & (me != at),
            point.at[c, unit],
            point_all.at[rows],
            rows_sem.at[me],
            (row, at),
        )

        @pl.when(second_set & (me == at))
        def _():
            point_all[rows, :] = point[c, unit]

    for g in range(GROUPS):
        at = group_at[g]
        rows = pl.ds(pl.multiple_of(me * part, 8), part)
        send(
            second_set & (me != at),
            group.at[c, g],
            group_all.at[rows],
            rows_sem.at[me],
            (row, at),
        )

        @pl.when(second_set & (me == at))
        def _():
            group_all[rows, :] = group[c, g]

    block = blocks.shape[1]

    @pl.when(first_set)
    def _():
        for unit in range(3):
            value = dilated[c, unit * KERNEL : (unit + 1) * KERNEL].reshape(KERNEL * share, block)
            blocks[unit] = gram_of(value, value)

    @pl.when(second_set)
    def _():
        value = strided[c].reshape(-1, 2 * block)
        left, right = value[:, :block], value[:, block:]
        blocks[0] = gram_of(left, left)
        blocks[1] = gram_of(left, right)
        blocks[2] = gram_of(right, right)

    for number in range(3):
        at = block_at[number]
        send(
            (first_set | second_set) & (me != at),
            blocks.at[number],
            slots.at[number, me],
            slot_sem.at[number, me],
            (row, at),
        )

    for copy in code_loads:
        copy.wait()
    renew_codes(me, all_ref, books, first_books, buffered, marks_ref, books_next)

    def summed(number):
        total = blocks[number]
        for k in range(1, count):
            source = (me + k) % count
            arrive(slots.at[number, source], slot_sem.at[number, source])
            total = total + slots[number, source]
        return total

    for number in range(3):

        @pl.when((first_set | second_set) & (me == block_at[number]))
        def _():
            work[...] = summed(number)

    for number in (0, 2):
        send(
            second_set & (me == block_at[number]),
            work,
            corner.at[number // 2],
            corner_sem.at[number // 2],
            (row, strided_at),
        )

    @pl.when(second_set & (me == strided_at))
    def _():
        for number in range(2):
            arrive(corner.at[number], corner_sem.at[number])
        solved = solve_pair(corner[0], work[...], corner[1])
        for number in range(3):
            mix_ref[1, c, number] = solved[number]

    def piece_of(which, number, xs, ys):
        rows = pl.ds(pl.multiple_of((xs * high + ys) * piece, 8), piece)
        return (
            mix_ref.at[which, c, number, rows],
            mix_sem.at[which, c, number, xs * high + ys],
        )

    def hand_first(which, number, at):
        owner = (y == which) & (me == at)
        for i in range(wide):
            for j in range(high):
                if i == 0 and j == 0:
                    continue
                xt, yt = (x + i) % wide, (y + j) % high
                spot, recv = piece_of(which, number, xt, yt)
                send(owner, spot, spot, recv, (yt * 2 + c, z * wide + xt))

    for number in range(3):
        hand_first(1, number, strided_at)

    is_point = second_set & (
        (me == point_at[0]) | (me == point_at[1]) | (me == point_at[2])
    )
    is_group = second_set & ((me == group_at[0]) | (me == group_at[1]))
    is_dilated = first_set & (
        (me == block_at[0]) | (me == block_at[1]) | (me == block_at[2])
    )

    @pl.when(is_point)
    def _():
        for k in range(1, count):
            source = (me + k) % count
            rows = pl.ds(pl.multiple_of(source * share, 8), share)
            arrive(point_all.at[rows], rows_sem.at[source])
        work[...] = gram_of(point_all[...], point_all[...])

    @pl.when(is_group)
    def _():
        for k in range(1, count):
            source = (me + k) % count
            rows = pl.ds(pl.multiple_of(source * part, 8), part)
            arrive(group_all.at[rows], rows_sem.at[source])
        work[...] = gram_of(group_all[...], group_all[...])

    @pl.when(is_dilated | is_point | is_group)
    def _():
        work[...] = solve_mixing(work[...])

    for unit in range(3):

        @pl.when(first_set & (me == block_at[unit]))
        def _():
            mix_ref[0, c, unit] = work[...]

        hand_first(0, unit, block_at[unit])

    @pl.when(is_point)
    def _():
        point_done[...] = product(split_terms(point_all[...], 3), split_terms(work[...], 3))

    @pl.when(is_group)
    def _():
        group_done[...] = product(split_terms(group_all[...], 3), split_terms(work[...], 3))

    for unit in range(3):
        at = point_at[unit]
        for k in range(1, count):
            target = (me + k) % count
            rows = pl.ds(pl.multiple_of(target * share, 8), share)
            send(
                second_set & (me == at),
                point_done.at[rows],
                small_ref.at[c, unit],
                small_sem.at[unit],
                (row, target),
            )

        @pl.when(second_set & (me == at))
        def _():
            small_ref[c, unit] = point_done[pl.ds(pl.multiple_of(me * share, 8), share), :]

    for g in range(GROUPS):
        at = group_at[g]
        spot = small_ref.at[c, 3, g * part : (g + 1) * part]
        for k in range(1, count):
            target = (me + k) % count
            rows = pl.ds(pl.multiple_of(target * part, 8), part)
            send(
                second_set & (me == at),
                group_done.at[rows],
                spot,
                small_sem.at[3 + g],
                (row, target),
            )

        @pl.when(second_set & (me == at))
        def _():
            spot[...] = group_done[pl.ds(pl.multiple_of(me * part, 8), part), :]

    always = y >= 0

    def hand_down(which, number, at):
        owner = (y == which) & (me == at)
        in_plane = z == at // wide
        spot, recv = piece_of(which, number, x, y)

        @pl.when(jnp.logical_not(owner))
        def _():
            arrive(spot, recv)

        for k in range(1, deep):
            send(in_plane, spot, spot, recv, (row, (z + k) % deep * wide + x))

    def hand_across(which, number, at):
        spot, recv = piece_of(which, number, x, y)
        for i in range(wide):
            for j in range(high):
                if i == 0 and j == 0:
                    continue
                xt, yt = (x + i) % wide, (y + j) % high
                target = z * wide + xt
                wants = jnp.logical_not((yt == which) & (target == at))
                send(wants, spot, spot, recv, (yt * 2 + c, target))

    def hand_over(which, number, at):
        owner = (y == which) & (me == at)

        @pl.when(jnp.logical_not(owner))
        def _():
            for i in range(wide):
                for j in range(high):
                    if i == 0 and j == 0:
                        continue
                    arrive(*piece_of(which, number, (x + i) % wide, (y + j) % high))

        spot = mix_ref.at[which, c, number]
        send(always, spot, spot, core_sem.at[which, c, number], partner)

    strided_ats = [strided_at] * 3
    for which, ats in ((0, block_at), (1, strided_ats)):
        for step in (hand_down, hand_across):
            for number in range(3):
                step(which, number, ats[number])
    for unit in range(3):

        @pl.when(second_set & (me != point_at[unit]))
        def _():
            arrive(small_ref.at[c, unit], small_sem.at[unit])

    for g in range(GROUPS):

        @pl.when(second_set & (me != group_at[g]))
        def _():
            arrive(small_ref.at[c, 3, g * part : (g + 1) * part], small_sem.at[3 + g])

    for k in range(1, high):
        send(
            second_set,
            small_ref.at[c],
            small_ref.at[c],
            small_sem.at[5],
            ((y + k) % high * 2 + c, me),
        )

    @pl.when(jnp.logical_not(second_set))
    def _():
        arrive(small_ref.at[c], small_sem.at[5])

    send(always, small_ref.at[c], small_ref.at[c], small_sem.at[6], partner)
    for which, ats in ((0, block_at), (1, strided_ats)):
        for number in range(3):
            hand_over(which, number, ats[number])
    for unit in range(3):
        arrive(mix_ref.at[0, 1 - c, unit], core_sem.at[0, 1 - c, unit])
    for number in range(8, 12):
        load(number, *own_loads[number]).wait()
    for side, target in enumerate((enc_dilated_next, dec_dilated_next)):
        for unit in range(3):
            taps = slice(unit * KERNEL, (unit + 1) * KERNEL)
            rows = dilated[side, taps].reshape(KERNEL * share, block)
            moved = product(split_terms(rows, 2), split_terms(mix_ref[0, side, unit], 2))
            target[taps] = dilated_w[side, taps] - update_rate * moved.reshape(
                KERNEL, share, block
            )
    arrive(small_ref.at[1 - c], small_sem.at[6])
    for side, (weight, target) in enumerate(
        ((enc_point_w, enc_point_next), (dec_point_w, dec_point_next))
    ):
        target[...] = weight[...] - update_rate * small_ref[side, :3]
    for side, (weight, target) in enumerate(
        ((enc_group_w, enc_group_next), (dec_group_w, dec_group_next))
    ):
        for g in range(GROUPS):
            step = small_ref[side, 3, g * part : (g + 1) * part, :]
            target[g] = weight[g] - update_rate * step
    for number in range(3):
        arrive(mix_ref.at[1, 1 - c, number], core_sem.at[1, 1 - c, number])
    for side, target in enumerate((enc_strided_next, dec_strided_next)):
        corners = [split_terms(mix_ref[1, side, number], 2) for number in range(3)]
        turned = split_terms(mix_ref[1, side, 1].T, 2)
        rows = strided[side].reshape(-1, 2 * block)
        left, right = split_terms(rows[:, :block], 2), split_terms(rows[:, block:], 2)
        low = product(left, corners[0]) + product(right, turned)
        top = product(left, corners[1]) + product(right, corners[2])
        shape = (strided.shape[1], share, block)
        target[:, :, :block] = strided_w[side, :, :, :block] - update_rate * low.reshape(shape)
        target[:, :, block:] = strided_w[side, :, :, block:] - update_rate * top.reshape(shape)

    for number, (when, src, dst, recv, to) in enumerate(pending):

        @pl.when(when)
        def _():
            remote(src, dst, number, recv, to).wait_send()


def renew_codes(me, all_ref, books, first_books, buffered, marks_ref, books_next):
    groups, levels, share, width = books.shape
    entries = groups * levels
    codes = first_books.shape[1]
    slot_range = lax.broadcasted_iota(jnp.int32, (share, buffered.shape[1]), 1)
    deep, wide, high, _, length, _ = all_ref.shape
    size = wide * high * 2 * length
    every = lax.broadcasted_iota(jnp.int32, (codes, size), 0).astype(jnp.float32)
    own_range = lax.broadcasted_iota(jnp.int32, (share, size), 0) + me * share
    own_range = own_range.astype(jnp.float32)
    ones = jnp.ones((size, lanes), jnp.bfloat16)
    sums = [None] * entries
    counts = [None] * entries
    pairs = [None] * groups

    def add(target, number, value):
        target[number] = value if target[number] is None else target[number] + value

    def chosen(digits, entry, choices):
        code = digits[entry : entry + 1] * 32.0 + digits[entries + entry : entries + entry + 1]
        return (code == choices).astype(jnp.float32).astype(jnp.bfloat16)

    for zs in range(deep):
        rows = all_ref[zs].reshape(size, -1)
        digits = rows[:, groups * width :].astype(jnp.float32).T
        for g in range(groups):
            values = rows[:, g * width : (g + 1) * width]
            for level in range(levels):
                entry = g * levels + level
                hot = chosen(digits, entry, own_range)
                add(sums, entry, dot(hot, values))
                add(counts, entry, dot(hot, ones))
            add(pairs, g, dot_last(hot, chosen(digits, g * levels, every)))
    for entry in range(entries):
        g, level = entry // levels, entry % levels
        if level == 1:
            both = split_terms(pairs[g], 2)
            taken = product(both, split_terms(first_books[g], 2))
            sums[entry] = sums[entry] - taken
        count = jnp.concatenate([counts[entry]] * (width // lanes), axis=1)
        own = books[g, level]
        mean = sums[entry] / jnp.maximum(count, 1.0)
        updated = own + code_rate * jnp.minimum(count, 1.0) * (mean - own)
        hot = (marks_ref[:, entry : entry + 1] == slot_range).astype(jnp.bfloat16)
        replaced = None
        for term in split_terms(buffered[g], 3):
            part = dot(hot, term)
            replaced = part if replaced is None else replaced + part
        dead = marks_ref[:, entries + entry : entries + entry + 1] == 1
        books_next[g, level] = jnp.where(dead, replaced, updated)


def solve_all(views, weights, codes, small_weights, sizes, collective_id):
    wide, high, deep = sizes
    count = wide * deep
    share, block = views[0].shape[1:]
    part = share // GROUPS
    f32 = jnp.float32
    dma = pltpu.SemaphoreType.DMA
    sends = 5 + 3 + 2 + 5 * (count - 1) + (high - 1) + 1 + 6 * (deep + 2 * (wide * high - 1))
    all_rows, books, buffered, marks = codes
    own_books = books.shape[:2] + (books.shape[2] // count,) + books.shape[3:]
    vmem = pl.BlockSpec(memory_space=pltpu.VMEM)
    return pl.pallas_call(
        functools.partial(mixing_kernel, sizes, share),
        out_shape=tuple(jax.ShapeDtypeStruct(weight.shape, f32) for weight in small_weights)
        + tuple(jax.ShapeDtypeStruct(weight.shape, f32) for weight in weights)
        + (jax.ShapeDtypeStruct(own_books, f32),),
        in_specs=[pl.BlockSpec(memory_space=pl.ANY)] * 15 + [vmem] * 5,
        out_specs=(vmem,) * 9,
        scratch_shapes=[
            pltpu.VMEM((2, 4, share, block), f32),
            pltpu.VMEM((2, 2, 3, block, block), f32),
            pltpu.VMEM((2,) + views[0].shape, f32),
            pltpu.VMEM((2,) + views[1].shape, f32),
            pltpu.VMEM((2,) + views[2].shape, f32),
            pltpu.VMEM((2,) + views[3].shape, f32),
            pltpu.VMEM((2,) + views[0].shape, f32),
            pltpu.VMEM((2,) + views[3].shape, f32),
            pltpu.VMEM((3, block, block), f32),
            pltpu.VMEM((2, block, block), f32),
            pltpu.VMEM((3, count, block, block), f32),
            pltpu.VMEM((count * share, block), f32),
            pltpu.VMEM((count * part, block), f32),
            pltpu.VMEM((block, block), f32),
            pltpu.VMEM((count * share, block), f32),
            pltpu.VMEM((count * part, block), f32),
            dma((12,)),
            dma((sends,)),
            dma((3, count)),
            dma((count,)),
            dma((2, 2, 3, wide * high)),
            dma((2, 2, 3)),
            dma((7,)),
            dma((2,)),
            pltpu.VMEM(all_rows.shape, all_rows.dtype),
            pltpu.VMEM(own_books, f32),
            pltpu.VMEM(books.shape[:1] + books.shape[2:], f32),
            pltpu.VMEM(buffered.shape, f32),
            dma((4,)),
        ],
        compiler_params=pltpu.CompilerParams(
            collective_id=collective_id, has_side_effects=True, vmem_limit_bytes=60 * 2**20
        ),
    )(*views, *weights, *codes, *small_weights)


def velocity_kernel(share_encoder, share_decoder, strided_sums, *refs):
    moments, outs = refs[:8], refs[8:]
    for side, rows in enumerate((share_encoder, share_decoder)):
        dilated, point, group, strided = range(4 * side, 4 * side + 4)
        at = 0
        for number in (dilated, point):
            size = moments[number].shape[0]
            step = rows[at : at + size].astype(jnp.float32)
            outs[number][...] = moment_decay * moments[number][...] + step
            at += size
        step = rows[at].astype(jnp.float32).reshape(moments[group].shape)
        outs[group][...] = moment_decay * moments[group][...] + step
        outs[strided][...] = moment_decay * moments[strided][...] + strided_sums[side]


def new_velocities(side_shares, moments):
    vmem = pl.BlockSpec(memory_space=pltpu.VMEM)
    return pl.pallas_call(
        velocity_kernel,
        out_shape=tuple(jax.ShapeDtypeStruct(moment.shape, jnp.float32) for moment in moments),
        in_specs=[vmem] * (len(side_shares) + len(moments)),
        out_specs=(vmem,) * len(moments),
        compiler_params=pltpu.CompilerParams(vmem_limit_bytes=60 * 2**20),
    )(*side_shares, *moments)


def per_device(
    frames,
    cotangent,
    segment_ids,
    code_index,
    codebooks,
    dead_codes,
    code_slots,
    buffered,
    encoder_dilated,
    encoder_pointwise,
    down_weight,
    group_in,
    group_out,
    up_weight,
    decoder_dilated,
    decoder_pointwise,
    encoder_dilated_moment,
    encoder_pointwise_moment,
    down_moment,
    group_in_moment,
    group_out_moment,
    up_moment,
    decoder_dilated_moment,
    decoder_pointwise_moment,
):
    masters = (
        encoder_dilated,
        encoder_pointwise,
        down_weight,
        group_in,
        group_out,
        up_weight,
        decoder_dilated,
        decoder_pointwise,
    )
    olds = (
        encoder_dilated_moment,
        encoder_pointwise_moment,
        down_moment,
        group_in_moment,
        group_out_moment,
        up_moment,
        decoder_dilated_moment,
        decoder_pointwise_moment,
    )
    count = lax.axis_size("seq")
    sizes = line_sizes(count, lax.axis_size("dp"))
    sides = ((0, 1, 3, 2), (6, 7, 4, 5))
    side_rows = whole_rows(masters, sizes[1])
    wide, high, deep = sizes
    _, length, channels = frames.shape
    long = 2 * length
    latent_len = long // STRIDE
    place_seq = lax.axis_index("seq")
    hidden = encoder_dilated.shape[-1]
    share = masters[0].shape[2]
    blocks = side_rows // share
    geometry = (count, share, blocks)
    rows = side_rows // (4 * high)
    low, f32 = jnp.bfloat16, jnp.float32
    dma = pltpu.SemaphoreType.DMA
    entries = GROUPS * LEVELS
    numbers_own = jnp.concatenate([segment_ids[0], code_index[0].reshape(-1, entries).T.reshape(-1)])
    numbers_own = jnp.broadcast_to(numbers_own[:, None], numbers_own.shape + (lanes,))
    vmem = pl.BlockSpec(memory_space=pltpu.VMEM)
    anywhere = pl.BlockSpec(memory_space=pl.ANY)
    grad_rows, split = reduce_rows(masters, high)
    pieces = sum(split)
    grad_blocks = grad_rows // share
    partial_type = jax.ShapeDtypeStruct((count, grad_blocks, share, hidden), low)
    latents = length // STRIDE
    taps = masters[2].shape[0]
    left_type = jax.ShapeDtypeStruct((taps * latents // lanes, channels, lanes), low)
    right_type = jax.ShapeDtypeStruct((latents, channels), low)
    scratch = side_scratch(count, share, long, length, channels, hidden)
    inner = length + 2 * 96
    inner_scratch = side_scratch(count, share, inner, length, channels, hidden)
    flat = [masters[i].reshape((-1,) + masters[i].shape[-2:]) for side in sides for i in side]
    packed_shape = (2, high, 2, rows, hidden)
    piece_rows = grad_rows // (2 * high * pieces)
    reduce_shape = (2, high, pieces, piece_rows, hidden)
    both = [pltpu.VMEM((2,) + array.shape, f32) for array in flat[:4]]
    gathered, frames_long, ids, decoded, grad_quant, picks, partial, left, right = pl.pallas_call(
        functools.partial(front_kernel, sizes, geometry, long),
        out_shape=(
            jax.ShapeDtypeStruct((deep, wide, 2) + packed_shape, low),
            jax.ShapeDtypeStruct((long, channels), frames.dtype),
            jax.ShapeDtypeStruct((long + 2 * margin, lanes), jnp.int32),
            jax.ShapeDtypeStruct((length, channels), low),
            jax.ShapeDtypeStruct((GROUPS, latent_len, hidden), f32),
            jax.ShapeDtypeStruct((entries, latent_len, hidden), f32),
            partial_type,
            left_type,
            right_type,
        ),
        in_specs=[anywhere] * 11 + [vmem],
        out_specs=(anywhere, vmem, vmem, vmem, vmem, vmem, anywhere, vmem, vmem),
        scratch_shapes=[pltpu.VMEM((2, blocks, share, hidden), low)]
        + both
        + [
            pltpu.VMEM((entries, latent_len, lanes), jnp.int32),
            pltpu.VMEM((long, channels), f32),
        ]
        + scratch
        + [
            dma((2, 8)),
            dma((15,)),
            dma((2, deep, wide, 2, high, 2)),
            dma((2 * gather_sends(sizes),)),
        ],
        compiler_params=pltpu.CompilerParams(
            collective_id=0, has_side_effects=True, vmem_limit_bytes=60 * 2**20
        ),
    )(*flat, numbers_own, frames[0], cotangent[0], codebooks)
    own_codes_low = code_index[0].reshape(-1, entries)
    digits = jnp.concatenate([own_codes_low // 32, own_codes_low % 32], axis=1)
    digits = jnp.pad(digits, ((0, 0), (0, lanes - digits.shape[1]))).astype(low)
    rows_own = (length // STRIDE, GROUPS * hidden + lanes)
    grad, _, share_decoder, share_encoder, all_rows, strided_sums = pl.pallas_call(
        functools.partial(back_kernel, sizes, split, geometry, inner),
        out_shape=(
            jax.ShapeDtypeStruct((length, channels), f32),
            partial_type,
            jax.ShapeDtypeStruct(reduce_shape, low),
            jax.ShapeDtypeStruct(reduce_shape, low),
            jax.ShapeDtypeStruct((deep, wide, high, 2) + rows_own, low),
            jax.ShapeDtypeStruct((2, taps, share, channels), f32),
        ),
        in_specs=[vmem] * 7 + [anywhere, anywhere],
        out_specs=(vmem, anywhere, anywhere, anywhere, anywhere, vmem),
        scratch_shapes=inner_scratch
        + reduce_scratch(sizes, split, piece_rows, hidden, low)
        + reduce_scratch(sizes, split, piece_rows, hidden, low)
        + [
            pltpu.VMEM(rows_own, low),
            dma,
            dma((deep, wide, high, 2)),
            pltpu.VMEM(left_type.shape, low),
            pltpu.VMEM(right_type.shape, low),
            pltpu.VMEM((2, count, left_type.shape[0], share, lanes), low),
            pltpu.VMEM((2, count) + right_type.shape, low),
            pltpu.VMEM((2, taps, share, channels), f32),
            dma((2, count)),
            dma((2, count)),
            pltpu.VMEM((taps, share, channels), f32),
            pltpu.VMEM((taps, share, channels), low),
            pltpu.VMEM((high - 1, taps // high, share, channels), low),
            dma,
            dma((high - 1,)),
            dma((high,)),
            dma,
            dma((2 * reduce_sends(sizes) + spread_sends(sizes) + outer_sends(sizes),)),
        ],
        compiler_params=pltpu.CompilerParams(
            collective_id=1, has_side_effects=True, vmem_limit_bytes=63 * 2**20
        ),
    )(
        frames_long, ids, grad_quant, picks, digits, left, right, gathered,
        partial.reshape((deep, wide) + reduce_shape),
    )
    decoded = decoded[None]
    grad = grad[None]
    side_shares = (
        share_encoder.reshape(grad_blocks, share, hidden),
        share_decoder.reshape(grad_blocks, share, hidden),
        strided_sums,
    )
    order = [i for side in sides for i in side]
    moments = [olds[i].reshape((-1,) + olds[i].shape[-2:]) for i in order]
    views = new_velocities(side_shares, moments)
    velocities = [None] * 8
    for i, view in zip(order, views):
        velocities[i] = view.reshape(olds[i].shape)
    flat = [masters[i].reshape((-1,) + masters[i].shape[-2:]) for i in (0, 2, 6, 5)]
    marks = jnp.concatenate(
        [code_slots.reshape(entries, -1).T, dead_codes.reshape(entries, -1).T], axis=1
    )
    small = [i for side in sides for i in side[1:3]]
    *moved, new_codebooks = solve_all(
        views,
        flat,
        (all_rows, codebooks, buffered, marks),
        [masters[i] for i in small],
        sizes,
        2,
    )
    nexts = [None] * 8
    for i, value in zip(small + [0, 2, 6, 5], moved):
        nexts[i] = value.reshape(masters[i].shape)
    return (
        decoded,
        grad,
        new_codebooks,
        velocities[0],
        velocities[1],
        velocities[2],
        velocities[3],
        velocities[4],
        velocities[5],
        velocities[6],
        velocities[7],
        nexts[0],
        nexts[1],
        nexts[2],
        nexts[3],
        nexts[4],
        nexts[5],
        nexts[6],
        nexts[7],
    )


def solution(mesh):
    in_specs = (
        P("dp", "seq", None),
        P("dp", "seq", None),
        P("dp", "seq"),
        P("dp", "seq", None, None),
        P(),
        P(None, None, "seq"),
        P(None, None, "seq"),
        P(),
        P(None, None, "seq", None),
        P(None, "seq", None),
        P(None, "seq", None),
        P(None, "seq", None),
        P(None, "seq", None),
        P(None, "seq", None),
        P(None, None, "seq", None),
        P(None, "seq", None),
        P(None, None, "seq", None),
        P(None, "seq", None),
        P(None, "seq", None),
        P(None, "seq", None),
        P(None, "seq", None),
        P(None, "seq", None),
        P(None, None, "seq", None),
        P(None, "seq", None),
    )
    out_specs = (
        P("dp", "seq", None),
        P("dp", "seq", None),
        P(None, None, "seq", None),
        P(None, None, "seq", None),
        P(None, "seq", None),
        P(None, "seq", None),
        P(None, "seq", None),
        P(None, "seq", None),
        P(None, "seq", None),
        P(None, None, "seq", None),
        P(None, "seq", None),
        P(None, None, "seq", None),
        P(None, "seq", None),
        P(None, "seq", None),
        P(None, "seq", None),
        P(None, "seq", None),
        P(None, "seq", None),
        P(None, None, "seq", None),
        P(None, "seq", None),
    )
    return jax.shard_map(
        per_device, mesh=mesh, in_specs=in_specs, out_specs=out_specs, check_vma=False
    )
```
